32 devices in a mesh: shard: 8 (over y, x, core), seq: 4 (over z).
Axes of the slice: x: 2, y: 2, z: 4, core: 2. Of those that a mesh axis runs over, the one named last changes fastest.
Arguments:
- tokens: bfloat16 [8, 28, 112, 512], P('shard', 'seq'), may hold values from -6 to 6
- regions: int32 [8, 28, 112], P('shard'), may hold values from 0 to 8, as said below
- cotangent: bfloat16 [8, 28, 112, 512], P('shard', 'seq'), may hold values from -6 to 6
- gain_one: bfloat16 [512], P('shard'), may hold values from 0.5 to 1.5
- bias_one: bfloat16 [512], P('shard'), may hold values from -1 to 1
- w_qkv: bfloat16 [512, 1536], P('shard'), may hold values from -0.25 to 0.25
- bias_qv: bfloat16 [2, 512], P(None, 'shard'), may hold values from -1 to 1
- table: bfloat16 [169, 16], P(None, 'shard'), may hold values from -4 to 4
- w_proj: bfloat16 [512, 512], P('shard'), may hold values from -1 to 1
- bias_proj: bfloat16 [512], P('shard'), may hold values from -1 to 1
- gain_two: bfloat16 [512], P('shard'), may hold values from 0.5 to 1.5
- bias_two: bfloat16 [512], P('shard'), may hold values from -1 to 1
- w_in: bfloat16 [512, 2048], P('shard'), may hold values from -0.25 to 0.25
- bias_in: bfloat16 [2048], P('shard'), may hold values from -1 to 1
- w_out: bfloat16 [2048, 512], P('shard'), may hold values from -0.125 to 0.125
- bias_out: bfloat16 [512], P('shard'), may hold values from -1 to 1
Outputs:
- output: float32 [8, 28, 112, 512], P('shard', 'seq')
- grad_tokens: float32 [8, 28, 112, 512], P('shard', 'seq')
- grad_gain_one: float32 [512], P('shard')
- grad_bias_one: float32 [512], P('shard')
- grad_w_qkv: float32 [512, 1536], P('shard')
- grad_bias_qv: float32 [2, 512], P(None, 'shard')
- grad_table: float32 [169, 16], P(None, 'shard')
- grad_w_proj: float32 [512, 512], P('shard')
- grad_bias_proj: float32 [512], P('shard')
- grad_gain_two: float32 [512], P('shard')
- grad_bias_two: float32 [512], P('shard')
- grad_w_in: float32 [512, 2048], P('shard')
- grad_bias_in: float32 [2048], P('shard')
- grad_w_out: float32 [2048, 512], P('shard')
- grad_bias_out: float32 [512], P('shard')
The draws below stay inside these ranges and needn't reach their ends.
Inputs may be any that keep to these rules, and one draw needn't show every extreme that they name: `regions`: tokens of one window attend to each other only where their labels are equal.
All inputs are finite; a program needn't handle non-finite values.
Results may differ from the reference program's by a relative error of at most 0.019.
Values may be sent and summed in bfloat16 or wider, within the bound.
No kernel may reach another device: no remote copies, remote signals or barrier semaphores. Data moves between devices by JAX's collectives and lax.ppermute only.
A program may use at most 128 MiB of HBM per device.

```python
import jax
import jax.numpy as jnp
from jax import lax

D = 512
HEADS = 16
HEAD = 32
FF = 2048
WIN = 7
SHIFT = 3
TABLE = 169
WIDTH = 112
HEIGHT = 28
IMAGES = 8


def draw_regions(key, part):
    key = jax.random.fold_in(key, 11)
    cuts = jax.random.randint(key, (IMAGES, 2), 1, WIN)
    row_places = jnp.arange(HEIGHT, dtype=jnp.int32)
    col_places = jnp.arange(WIDTH, dtype=jnp.int32)
    row_band = (row_places[None, :] >= HEIGHT - WIN).astype(jnp.int32) + (row_places[None, :] >= HEIGHT - cuts[:, 0:1]).astype(jnp.int32)
    col_band = (col_places[None, :] >= WIDTH - WIN).astype(jnp.int32) + (col_places[None, :] >= WIDTH - cuts[:, 1:2]).astype(jnp.int32)
    return (3 * row_band[:, :, None] + col_band[:, None, :]).astype(jnp.int32)


def steps_of(stream_key, extent, cuts, least, high):
    def one(axis_at, parts):
        draws = jax.random.uniform(jax.random.fold_in(jax.random.fold_in(stream_key, 6), axis_at), (parts,), jnp.float32, least / len(cuts), high / len(cuts))
        return jnp.repeat(jnp.exp(draws), extent[axis_at] // parts).reshape((-1,) + (1,) * (len(extent) - axis_at - 1))

    factor_of = one(*cuts[0])
    for cut in cuts[1:]:
        factor_of = factor_of * one(*cut)
    return factor_of


def normal_values(own_key, extent, deviation, limit, cuts=(), held_as=jnp.bfloat16):
    array = deviation * jax.random.normal(own_key, extent, jnp.float32)
    if cuts:
        array = array * steps_of(own_key, extent, cuts, -0.22, 0.18)
    return jnp.clip(array, -limit, limit).astype(held_as)


def setup_inputs(seed: int = 0) -> dict:
    arg_keys = jax.random.split(jax.random.key(seed), 17)
    return {
        "tokens": normal_values(arg_keys[0], (IMAGES, HEIGHT, WIDTH, D), 1.0, 6.0, ((0, 8), (1, 4))),
        "regions": draw_regions(jax.random.fold_in(arg_keys[16], 71), 0),
        "cotangent": normal_values(arg_keys[2], (IMAGES, HEIGHT, WIDTH, D), 1.0, 6.0, ((0, 8), (1, 4))),
        "gain_one": jnp.clip(1.0 + 0.1 * jax.random.normal(arg_keys[3], (D,), jnp.float32), 0.5, 1.5).astype(jnp.bfloat16),
        "bias_one": normal_values(arg_keys[4], (D,), 0.2, 1.0, ((0, 8),)),
        "w_qkv": normal_values(arg_keys[5], (D, 3 * D), D ** -0.5, 0.25, ((0, 8),)),
        "bias_qv": normal_values(arg_keys[6], (2, D), 0.2, 1.0, ((1, 8),)),
        "table": normal_values(arg_keys[7], (TABLE, HEADS), 1.0, 4.0, ((1, 8),)),
        "w_proj": normal_values(arg_keys[8], (D, D), (D // 16) ** -0.5, 1.0, ((0, 8),)),
        "bias_proj": normal_values(arg_keys[9], (D,), 0.2, 1.0, ((0, 8),)),
        "gain_two": jnp.clip(1.0 + 0.1 * jax.random.normal(arg_keys[10], (D,), jnp.float32), 0.5, 1.5).astype(jnp.bfloat16),
        "bias_two": normal_values(arg_keys[11], (D,), 0.2, 1.0, ((0, 8),)),
        "w_in": normal_values(arg_keys[12], (D, FF), D ** -0.5, 0.25, ((0, 8),)),
        "bias_in": normal_values(arg_keys[13], (FF,), 0.2, 1.0, ((0, 8),)),
        "w_out": normal_values(arg_keys[14], (FF, D), FF ** -0.5, 0.125, ((0, 8),)),
        "bias_out": normal_values(arg_keys[15], (D,), 0.2, 1.0, ((0, 8),)),
    }


@jax.custom_vjp
def low(v):
    return lax.optimization_barrier(v.astype(jnp.bfloat16)).astype(jnp.float32)

@jax.custom_vjp
def low_back(v):
    return v

def low_keep(v):
    return (low(v), None)

def low_pass(kept, grad):
    return (grad,)

def back_keep(v):
    return (v, None)

def back_low(kept, grad):
    return (low(grad),)
low.defvjp(low_keep, low_pass)
low_back.defvjp(back_keep, back_low)
EPS = 1e-05

def normalize(values, gain, offset):
    average = lax.optimization_barrier(jnp.mean(values, -1, keepdims=True))
    centered = values - average
    variance = lax.optimization_barrier(jnp.mean(centered * centered, -1, keepdims=True))
    return centered * lax.rsqrt(variance + EPS) * gain + offset

def matmul(left, right):
    return jnp.dot(left, right, precision=lax.Precision.HIGHEST, preferred_element_type=jnp.float32)

def to_windows(tensor):
    depth = tensor.shape[-1]
    tensor = tensor.reshape(HEIGHT // WIN, WIN, WIDTH // WIN, WIN, depth)
    return tensor.transpose(0, 2, 1, 3, 4).reshape(-1, WIN * WIN, depth)

def from_windows(tensor):
    depth = tensor.shape[-1]
    tensor = tensor.reshape(HEIGHT // WIN, WIDTH // WIN, WIN, WIN, depth)
    return tensor.transpose(0, 2, 1, 3, 4).reshape(HEIGHT, WIDTH, depth)

def relative_index():
    position = jnp.arange(WIN * WIN, dtype=jnp.int32)
    pos_row = position // WIN
    pos_col = position % WIN
    return ((pos_row[:, None] - pos_row[None, :] + WIN - 1) * (2 * WIN - 1) + pos_col[:, None] - pos_col[None, :] + WIN - 1).astype(jnp.int32)

def forward(image, labels, params):
    gain_one, bias_one, w_qkv, bias_qv, table, w_proj, bias_proj, gain_two, bias_two, w_in, bias_in, w_out, bias_out = params
    normed = low_back(low(normalize(image, gain_one, bias_one)))
    shifted = jnp.roll(normed, (-SHIFT, -SHIFT), (0, 1)).reshape(-1, D)
    query_all = low_back(low(matmul(shifted, w_qkv[:, :D]) + bias_qv[0]))
    key_all = low_back(low(matmul(shifted, w_qkv[:, D:2 * D])))
    value_all = low_back(low(matmul(shifted, w_qkv[:, 2 * D:]) + bias_qv[1]))

    def split_heads(tensor):
        return to_windows(tensor.reshape(HEIGHT, WIDTH, D)).reshape(-1, WIN * WIN, HEADS, HEAD)
    query_win = split_heads(query_all)
    key_win = split_heads(key_all)
    value_win = split_heads(value_all)
    logits = jnp.einsum('nqhe,nkhe->nhqk', query_win, key_win, precision=lax.Precision.HIGHEST) * HEAD ** (-0.5)
    rel_bias = table[relative_index()].transpose(2, 0, 1)
    labels_win = to_windows(labels[:, :, None]).reshape(-1, WIN * WIN)
    penalty = jnp.where(labels_win[:, :, None] != labels_win[:, None, :], -100.0, 0.0).astype(jnp.float32)
    logits = low_back(logits + rel_bias[None] + penalty[:, None])
    attention = low(jax.nn.softmax(logits, axis=-1))
    attended = jnp.einsum('nhqk,nkhe->nqhe', attention, value_win, precision=lax.Precision.HIGHEST)
    attended = low_back(low(attended)).reshape(-1, WIN * WIN, D)
    restored = jnp.roll(from_windows(attended), (SHIFT, SHIFT), (0, 1)).reshape(-1, D)
    branch = low_back(matmul(restored, w_proj) + bias_proj)
    mixed = image.reshape(-1, D) + branch
    normed_two = low(normalize(mixed, gain_two, bias_two))
    hidden = low_back(matmul(normed_two, w_in) + bias_in)
    activated = low(jax.nn.gelu(hidden, approximate=False))
    result = low_back(matmul(activated, w_out) + bias_out)
    return (mixed + result).reshape(HEIGHT, WIDTH, D)

def reference(tokens, regions, cotangent, gain_one, bias_one, w_qkv, bias_qv, table, w_proj, bias_proj, gain_two, bias_two, w_in, bias_in, w_out, bias_out):
    params = tuple((tensor.astype(jnp.float32) for tensor in (gain_one, bias_one, w_qkv, bias_qv, table, w_proj, bias_proj, gain_two, bias_two, w_in, bias_in, w_out, bias_out)))
    zeros_init = tuple((jnp.zeros(tensor.shape, jnp.float32) for tensor in params))

    def per_image(totals, slices):
        image, labels, grad_result = slices

        def apply_layer(image_in, *weights):
            return forward(image_in, labels, weights)
        result, pullback = jax.vjp(apply_layer, image.astype(jnp.float32), *params)
        grads = pullback(grad_result.astype(jnp.float32))
        return (tuple((total + grad for total, grad in zip(totals, grads[1:]))), (result, grads[0]))
    totals, (results, grad_images) = lax.scan(per_image, zeros_init, (tokens, regions, cotangent))
    return (results, grad_images, totals[0], totals[1], totals[2], totals[3], totals[4], totals[5], totals[6], totals[7], totals[8], totals[9], totals[10], totals[11], totals[12])
```

```python
import jax
import jax.numpy as jnp
from jax import lax
from jax.experimental import pallas as pl
from jax.experimental.pallas import tpu as pltpu
from jax.sharding import PartitionSpec as P

D = 512
HEADS = 16
HEAD = 32
WIN = 7
SHIFT = 3
FF = 2048
WIDTH = 112
WINDOWS = WIDTH // WIN
SLOT = 8
PLACES = WIN * SLOT
GROUP = 8
GROUPS = HEADS // GROUP
FEAT = GROUP * HEAD
LANES = 64 * GROUP
TOKENS = WIN * WIDTH
PADDED = WINDOWS * PLACES
TAB = 1536
TAB_USED = 768
SMALL = 16
EPS = 1e-05
SCALE = HEAD**-0.5
BF = jnp.bfloat16
F32 = jnp.float32
VMEM_LIMIT = 60 * 1024 * 1024


def shifted_2(value, axis, by):
    peers = lax.axis_size(axis)
    return lax.ppermute(value, axis, [(i, (i + by) % peers) for i in range(peers)])


def dot(left, right, dims=((1,), (0,))):
    return lax.dot_general(left, right, (dims, ((), ())), preferred_element_type=F32)


def dot_nt(left, right):
    return dot(left, right, ((1,), (1,)))


def dot_tn(left, right):
    return dot(left, right, ((0,), (0,)))


def iota(shape, axis):
    return lax.broadcasted_iota(jnp.int32, shape, axis)


def one_hot(condition):
    return jnp.where(condition, 1.0, 0.0).astype(BF)


def column_places():
    slot = iota((WINDOWS * SLOT, WIDTH), 0)
    column = iota((WINDOWS * SLOT, WIDTH), 1)
    place = slot & (SLOT - 1)
    wanted = (slot >> 3) * WIN + place + SHIFT
    wanted = jnp.where(wanted >= WIDTH, wanted - WIDTH, wanted)
    return one_hot((wanted == column) & (place < WIN))


def places_column():
    slot = iota((WIDTH, WINDOWS * SLOT), 1)
    column = iota((WIDTH, WINDOWS * SLOT), 0)
    place = slot & (SLOT - 1)
    wanted = (slot >> 3) * WIN + place + SHIFT
    wanted = jnp.where(wanted >= WIDTH, wanted - WIDTH, wanted)
    return one_hot((wanted == column) & (place < WIN))


def spread_matrix():
    return one_hot((iota((LANES, PLACES), 0) >> 3) == iota((LANES, PLACES), 1))


def fold_matrix():
    return one_hot((iota((PLACES, LANES), 1) >> 3) == iota((PLACES, LANES), 0))


def head_mask(value):
    row = iota((LANES, FEAT), 0) & (GROUP - 1)
    feature = iota((LANES, FEAT), 1) >> 5
    return jnp.where(row == feature, value, 0.0).astype(F32)


def table_pick(row_axis, backwards):
    shape = (TAB_USED, LANES) if row_axis == 0 else (LANES, TAB_USED)
    lane = iota(shape, row_axis)
    pair = iota(shape, 1 - row_axis)
    place = pair >> 3
    row, column = place >> 3, place & (SLOT - 1)
    entry = row * (2 * WIN - 1) + column
    if backwards:
        entry = (WIN - 1) * 2 * WIN - entry
    match = ((lane >> 3) == entry) & ((lane & 7) == (pair & 7))
    return one_hot(match & (column < WIN) & (row < WIN))


def norm_stats(values):
    average = jnp.mean(values, -1, keepdims=True)
    centered = values - average
    variance = jnp.mean(centered * centered, -1, keepdims=True)
    scale = lax.rsqrt(variance + EPS)
    return centered * scale, scale


def norm_back(grad, normed, scale, gain):
    scaled = grad * gain
    first = jnp.mean(scaled, -1, keepdims=True)
    second = jnp.mean(scaled * normed, -1, keepdims=True)
    return scale * (scaled - first - normed * second)


def whole(memory=pltpu.VMEM):
    return pl.BlockSpec(memory_space=memory)


def kernel_call(body, outs, ins, scratch=(), flops=0, smem=0):
    size = sum(a.size * a.dtype.itemsize for a in list(ins) + list(outs))
    return pl.pallas_call(
        body,
        out_shape=tuple(outs),
        in_specs=[whole(pltpu.SMEM)] * smem + [whole()] * (len(ins) - smem),
        out_specs=tuple(whole() for _ in outs),
        scratch_shapes=list(scratch),
        cost_estimate=pl.CostEstimate(flops=flops, bytes_accessed=size, transcendentals=0),
        compiler_params=pltpu.CompilerParams(vmem_limit_bytes=VMEM_LIMIT),
    )(*ins)


def like(shape, dtype):
    return jax.ShapeDtypeStruct(shape, dtype)


def pack_body(
    me_ref, g1, b1, wqkv, bqv, table, wproj, bproj, g2, b2, win, bin_, wout, bout, attn, mlp
):
    depth = wqkv.shape[0]
    me = me_ref[0]

    def place(vector, lanes):
        w = vector.shape[1]
        pick = one_hot(iota((w, lanes), 1) == iota((w, lanes), 0) + me * w)
        wide = jnp.broadcast_to(vector, (8, w))
        return dot(wide.astype(BF), pick)[0:1]

    for c in range(3):
        attn[c * depth : (c + 1) * depth, :] = wqkv[:, c * D : (c + 1) * D]
    attn[3 * depth : 4 * depth, :] = wproj[...]
    rows = [
        place(g1[...], D),
        place(b1[...], D),
        place(bqv[0:1, :], D),
        place(bqv[1:2, :], D),
        place(bproj[...], D),
    ]
    entries, held = table.shape
    lane = iota((entries, TAB), 1)
    entry = iota((entries, TAB), 0)
    spot = entry * GROUP + TAB - (WIN - 1) * 2 * WIN * GROUP
    spot = jnp.where(spot >= TAB, spot - TAB, spot)
    values = table[...].astype(F32)
    groups = [jnp.zeros((1, TAB), F32) for _ in range(GROUPS)]
    for h in range(held):
        head = me * held + h
        inside = lane == spot + (head & (GROUP - 1))
        row = jnp.sum(jnp.where(inside, values[:, h : h + 1], 0.0), 0, keepdims=True)
        for g in range(GROUPS):
            groups[g] = groups[g] + jnp.where((head >> 3) == g, row, 0.0)
    for g in range(GROUPS):
        rows += [groups[g][:, c * D : (c + 1) * D] for c in range(TAB // D)]
    rows += [jnp.zeros((SMALL - len(rows), D), F32)]
    attn[4 * depth :, :] = jnp.concatenate(rows, 0).astype(BF)

    for c in range(FF // D):
        mlp[c * depth : (c + 1) * depth, :] = win[:, c * D : (c + 1) * D]
    mlp[4 * depth : 8 * depth, :] = wout[...]
    hidden_bias = place(bin_[...], FF)
    rows = [place(g2[...], D), place(b2[...], D), place(bout[...], D)]
    rows += [hidden_bias[:, c * D : (c + 1) * D] for c in range(FF // D)]
    rows += [jnp.zeros((SMALL - len(rows), D), F32)]
    mlp[8 * depth :, :] = jnp.concatenate(rows, 0).astype(BF)


def unpack_body(
    me_ref, attn, mlp, g1, b1, wqkv, bqv, table, wproj, bproj, g2, b2, win, bin_, wout, bout
):
    depth = wqkv.shape[0]
    me = me_ref[0]

    def mine(row, w):
        lanes = row.shape[1]
        pick = one_hot(iota((lanes, w), 0) == iota((lanes, w), 1) + me * w)
        wide = jnp.broadcast_to(row, (8, lanes))
        return dot(wide.astype(BF), pick)[0:1]

    for c in range(3):
        wqkv[:, c * D : (c + 1) * D] = attn[c * depth : (c + 1) * depth, :].astype(F32)
    wproj[...] = attn[3 * depth : 4 * depth, :].astype(F32)
    small = attn[4 * depth :, :].astype(F32)
    w = D * depth // D
    g1[...] = mine(small[0:1], w)
    b1[...] = mine(small[1:2], w)
    bqv[0:1, :] = mine(small[2:3], w)
    bqv[1:2, :] = mine(small[3:4], w)
    bproj[...] = mine(small[4:5], w)
    entries, held = table.shape
    lane = iota((entries, TAB), 1)
    spot = (entries - 1 - iota((entries, TAB), 0)) * GROUP
    parts = TAB // D
    rows = [
        jnp.concatenate([small[5 + g * parts + c : 6 + g * parts + c] for c in range(parts)], 1)
        for g in range(GROUPS)
    ]
    which = iota((entries, held), 1)
    total = jnp.zeros((entries, held), F32)
    for h in range(held):
        head = me * held + h
        row = rows[0]
        for g in range(1, GROUPS):
            row = jnp.where((head >> 3) == g, rows[g], row)
        inside = lane == spot + (head & (GROUP - 1))
        column = jnp.sum(jnp.where(inside, row, 0.0), 1, keepdims=True)
        total = jnp.where(which == h, column, total)
    table[...] = total

    for c in range(FF // D):
        win[:, c * D : (c + 1) * D] = mlp[c * depth : (c + 1) * depth, :].astype(F32)
    wout[...] = mlp[4 * depth : 8 * depth, :].astype(F32)
    small = mlp[8 * depth :, :].astype(F32)
    g2[...] = mine(small[0:1], w)
    b2[...] = mine(small[1:2], w)
    bout[...] = mine(small[2:3], w)
    bin_[...] = mine(
        jnp.concatenate([small[3 + c : 4 + c] for c in range(FF // D)], 1), w * FF // D
    )


def block_of(slab, c, depth):
    return slab[:, c * depth : (c + 1) * depth, :].reshape(D, D)


def smalls_of(slab, start):
    return jnp.sum(slab[:, start:, :].astype(F32), 0)


def attn_forward_body(
    tokens,
    halo,
    slab,
    reg_rows,
    reg_lanes,
    mixed,
    normed_win,
    query,
    key,
    value,
    probs,
    restored,
    wide,
    spread,
    fold,
    mask,
    bias,
):
    depth = (slab.shape[1] - SMALL) // 4
    small = smalls_of(slab, 4 * depth)
    gain, offset = small[0:1], small[1:2]
    bias_q, bias_v, bias_o = small[2:3], small[3:4], small[4:5]
    spread[...] = spread_matrix()
    fold[...] = fold_matrix()
    mask[...] = head_mask(1.0)
    pick = table_pick(0, False)
    parts = TAB // D
    empty = (iota((PLACES, LANES), 0) & (SLOT - 1)) == WIN
    for g in range(GROUPS):
        row = jnp.concatenate([small[5 + g * parts + c : 6 + g * parts + c] for c in range(parts)], 1)
        row = jnp.broadcast_to(row, (SLOT, TAB))
        row = pltpu.roll(row, 0, 1, stride=GROUP, stride_axis=0)
        turned = [
            pltpu.roll(row, (2 * WIN - 1) * GROUP * r, 1)[:, :TAB_USED] for r in range(WIN)
        ]
        picked = dot(jnp.concatenate(turned, 0).astype(BF), pick)
        bias[g] = jnp.where(empty, -1e30, picked)

    columns = column_places()
    own = WIN - SHIFT
    for r in range(WIN):
        x = (tokens[SHIFT + r] if r < own else halo[r - own]).astype(F32)
        normed, _ = norm_stats(x)
        low = (normed * gain + offset).astype(BF)
        wide[:, r] = dot(columns, low).reshape(WINDOWS, SLOT, D)
    normed_win[...] = wide[...].reshape(PADDED, D).astype(BF)
    query[...] = (dot(normed_win[...], block_of(slab, 0, depth)) + bias_q).astype(BF)
    key[...] = dot(normed_win[...], block_of(slab, 1, depth)).astype(BF)
    value[...] = (dot(normed_win[...], block_of(slab, 2, depth)) + bias_v).astype(BF)

    def pair(n, carry):
        rows = pl.ds(pl.multiple_of(n * 2 * PLACES, 2 * PLACES), 2 * PLACES)
        for g in range(GROUPS):
            feats = slice(g * FEAT, (g + 1) * FEAT)
            q2 = query[rows, feats].astype(F32)
            k2 = key[rows, feats].astype(F32)
            v2 = value[rows, feats].astype(F32)
            held = []
            for s in range(2):
                w = 2 * n + s
                part = slice(s * PLACES, (s + 1) * PLACES)
                q, k, v = (a[part].astype(BF) for a in (q2, k2, v2))
                q_big = (dot(spread[...], q) * mask[...]).astype(BF)
                penalty = jnp.where(reg_rows[w][:, 0:1] != reg_lanes[w], -100.0, 0.0)
                logits = dot_nt(k, q_big) * SCALE + bias[g] + penalty
                top = jnp.max(logits, 0, keepdims=True)
                powers = jnp.exp(logits - top)
                p = powers * (1.0 / jnp.sum(powers, 0, keepdims=True))
                held.append(p)
                o_big = (dot_tn(p.astype(BF), v) * mask[...]).astype(BF)
                o = dot(fold[...], o_big)
                wide[w, :, :, feats] = o.reshape(WIN, SLOT, FEAT)
            probs[n, g] = jnp.concatenate(held, 0).astype(BF)
        return carry

    lax.fori_loop(0, WINDOWS // 2, pair, 0)
    back = places_column()
    for r in range(WIN):
        here = wide[:, r].reshape(WINDOWS * SLOT, D).astype(BF)
        restored[r * WIDTH : (r + 1) * WIDTH, :] = dot(back, here).astype(BF)
    branch = dot(restored[...], block_of(slab, 3, depth)) + bias_o
    for r in range(WIN):
        x = (tokens[SHIFT + r] if r < own else halo[r - own]).astype(F32)
        part = slice(r * WIDTH, (r + 1) * WIDTH)
        mixed[part, :] = x + branch[part]


def gelu_parts(h):
    size = jnp.abs(h) * (0.5**0.5)
    t = 1.0 / (1.0 + 0.3275911 * size)
    bell = jnp.exp(-0.5 * h * h)
    poly = t * (
        0.254829592
        + t * (-0.284496736 + t * (1.421413741 + t * (-1.453152027 + t * 1.061405429)))
    )
    tail = 0.5 * poly * bell
    upto = jnp.where(h >= 0, 1.0 - tail, tail)
    return upto, bell * 0.3989422804014327


def mlp_body(
    mixed, cotangent, halo, slab, kept, sent, grad_mixed, grads, normed_low, cot, out_sum, back_sum
):
    shards, height = slab.shape[:2]
    depth = (height - SMALL) // 8
    span = shards * D // FF
    small = smalls_of(slab, 8 * depth)
    gain, offset, bias_o = small[0:1], small[1:2], small[2:3]
    own = WIN - SHIFT
    for r in range(WIN):
        part = slice(r * WIDTH, (r + 1) * WIDTH)
        cot[part, :] = cotangent[SHIFT + r] if r < own else halo[r - own]
    normed, _ = norm_stats(mixed[...])
    normed_low[...] = (normed * gain + offset).astype(BF)
    vectors = []
    for c in range(FF // D):
        w_in = block_of(slab, c, depth)
        w_out = slab[c * span : (c + 1) * span, 4 * depth : 8 * depth, :].reshape(D, D)
        hidden = dot(normed_low[...], w_in) + small[3 + c : 4 + c]
        upto, density = gelu_parts(hidden)
        active = (hidden * upto).astype(BF)
        slope = upto + hidden * density
        grad = (dot_nt(cot[...], w_out) * slope).astype(BF)
        forward = dot(active, w_out)
        backward = dot_nt(grad, w_in)
        if c == 0:
            out_sum[...] = forward
            back_sum[...] = backward
        else:
            out_sum[...] += forward
            back_sum[...] += backward
        vectors.append(jnp.sum(grad.astype(F32), 0, keepdims=True))
        grads[:, c * depth : (c + 1) * depth, :] = (
            dot_tn(normed_low[...], grad).astype(BF).reshape(shards, depth, D)
        )
        grads[c * span : (c + 1) * span, 4 * depth : 8 * depth, :] = (
            dot_tn(active, cot[...]).astype(BF).reshape(span, 4 * depth, D)
        )
    result = mixed[...] + out_sum[...] + bias_o
    kept[...] = result[: own * WIDTH]
    sent[...] = result[own * WIDTH :].astype(BF)
    normed, scale = norm_stats(mixed[...])
    g = back_sum[...]
    rows = [
        jnp.sum(g * normed, 0, keepdims=True),
        jnp.sum(g, 0, keepdims=True),
        jnp.sum(cot[...].astype(F32), 0, keepdims=True),
    ] + vectors
    rows += [jnp.zeros((SMALL - len(rows), D), F32)]
    grads[:, 8 * depth :, :] = jnp.broadcast_to(
        jnp.concatenate(rows, 0).astype(BF)[None], (shards, SMALL, D)
    )
    grad_mixed[...] = cot[...].astype(F32) + norm_back(g, normed, scale, gain)


def attn_backward_body(
    grad_mixed,
    tokens,
    halo,
    slab,
    normed_win,
    query,
    key,
    value,
    probs,
    restored,
    kept,
    sent,
    grads,
    wide,
    grad_qkv,
    spread,
    fold,
    mask,
    pairs,
):
    shards = slab.shape[0]
    depth = (slab.shape[1] - SMALL) // 4
    small = smalls_of(slab, 4 * depth)
    gain = small[0:1]
    spread[...] = spread_matrix()
    fold[...] = fold_matrix()
    mask[...] = head_mask(1.0)
    pairs[...] = jnp.zeros_like(pairs)
    own = WIN - SHIFT

    def store(c, grad):
        grads[:, c * depth : (c + 1) * depth, :] = grad.astype(BF).reshape(shards, depth, D)

    branch = grad_mixed[...].astype(BF)
    bias_o = jnp.sum(branch.astype(F32), 0, keepdims=True)
    store(3, dot_tn(restored[...], branch))
    grad_att = dot_nt(branch, block_of(slab, 3, depth)).astype(BF)
    columns = column_places()
    for r in range(WIN):
        wide[:, r] = dot(columns, grad_att[r * WIDTH : (r + 1) * WIDTH]).reshape(WINDOWS, SLOT, D)

    def pair(n, carry):
        rows = pl.ds(pl.multiple_of(n * 2 * PLACES, 2 * PLACES), 2 * PLACES)
        for g in range(GROUPS):
            feats = slice(g * FEAT, (g + 1) * FEAT)
            q2 = query[rows, feats].astype(F32)
            k2 = key[rows, feats].astype(F32)
            v2 = value[rows, feats].astype(F32)
            p2 = probs[n, g].astype(F32)
            held = []
            for s in range(2):
                w = 2 * n + s
                part = slice(s * PLACES, (s + 1) * PLACES)
                q, k, v, p_low = (a[part].astype(BF) for a in (q2, k2, v2, p2))
                p = p2[part]
                go = wide[w, :, :, feats].reshape(PLACES, FEAT).astype(BF)
                go_big = (dot(spread[...], go) * mask[...]).astype(BF)
                q_big = (dot(spread[...], q) * mask[...]).astype(BF)
                dp = dot_nt(v, go_big)
                dv = dot(p_low, go_big)
                inner = jnp.sum(p * dp, 0, keepdims=True)
                ds = (p * (dp - inner)).astype(BF)
                pairs[g] += ds.astype(F32)
                dk = dot(ds, q_big) * SCALE
                dq_big = (dot_tn(ds, k) * (mask[...] * SCALE)).astype(BF)
                dq = dot(fold[...], dq_big)
                held.append((dq, dk, dv))
            for c in range(3):
                both = jnp.concatenate([held[0][c], held[1][c]], 0).astype(BF)
                grad_qkv[rows, c * D + g * FEAT : c * D + (g + 1) * FEAT] = both
        return carry

    lax.fori_loop(0, WINDOWS // 2, pair, 0)
    vectors = []
    for c in range(3):
        g = grad_qkv[:, c * D : (c + 1) * D]
        if c != 1:
            vectors.append(jnp.sum(g.astype(F32), 0, keepdims=True))
        store(c, dot_tn(normed_win[...], g))
        part = dot_nt(g, block_of(slab, c, depth))
        total = part if c == 0 else total + part
    wide[...] = total.reshape(WINDOWS, WIN, SLOT, D)
    back = places_column()
    gain_sum = jnp.zeros((1, D), F32)
    bias_sum = jnp.zeros((1, D), F32)
    for r in range(WIN):
        here = wide[:, r].reshape(WINDOWS * SLOT, D).astype(BF)
        g = dot(back, here)
        x = (tokens[SHIFT + r] if r < own else halo[r - own]).astype(F32)
        normed, scale = norm_stats(x)
        gain_sum += jnp.sum(g * normed, 0, keepdims=True)
        bias_sum += jnp.sum(g, 0, keepdims=True)
        grad = grad_mixed[r * WIDTH : (r + 1) * WIDTH, :] + norm_back(g, normed, scale, gain)
        if r < own:
            kept[r * WIDTH : (r + 1) * WIDTH, :] = grad
        else:
            sent[(r - own) * WIDTH : (r - own + 1) * WIDTH, :] = grad.astype(BF)

    pick = table_pick(1, True)
    rows = [gain_sum, bias_sum, vectors[0], vectors[1], bias_o]
    for g in range(GROUPS):
        high = pairs[g].astype(BF)
        low = (pairs[g] - high.astype(F32)).astype(BF)
        laid = dot(high, pick) + dot(low, pick)
        laid = jnp.concatenate([laid, jnp.zeros((PLACES, TAB - TAB_USED), F32)], 1)
        total = jnp.zeros((SLOT, TAB), F32)
        for r in range(WIN):
            total += pltpu.roll(
                laid[r * SLOT : (r + 1) * SLOT], (2 * WIN - 1) * GROUP * r, 1
            )
        total = pltpu.roll(total, 0, 1, stride=GROUP, stride_axis=0)
        row = jnp.sum(total, 0, keepdims=True)
        rows += [row[:, c * D : (c + 1) * D] for c in range(TAB // D)]
    rows += [jnp.zeros((SMALL - len(rows), D), F32)]
    grads[:, 4 * depth :, :] = jnp.broadcast_to(
        jnp.concatenate(rows, 0).astype(BF)[None], (shards, SMALL, D)
    )


def region_views(regions, rows, place):
    here = lax.dynamic_slice_in_dim(regions[0], place * rows, rows, 0)
    windows = here.reshape(WIN, WINDOWS, WIN).transpose(1, 0, 2)
    windows = jnp.pad(windows, ((0, 0), (0, 0), (0, SLOT - WIN))).astype(F32)
    windows = windows.reshape(WINDOWS, PLACES)
    by_row = jnp.broadcast_to(windows[:, :, None], (WINDOWS, PLACES, 128))
    by_lane = jnp.pad(jnp.repeat(windows, GROUP, 1), ((0, 0), (0, LANES - PLACES * GROUP)))
    return by_row, by_lane[:, None, :]


def per_device(
    tokens,
    regions,
    cotangent,
    gain_one,
    bias_one,
    w_qkv,
    bias_qv,
    table,
    w_proj,
    bias_proj,
    gain_two,
    bias_two,
    w_in,
    bias_in,
    w_out,
    bias_out,
):
    images, local_rows, columns, _ = tokens.shape
    assert images == 1 and local_rows == WIN and columns == WIDTH
    shards = lax.axis_size("shard")
    me = lax.axis_index("shard").astype(jnp.int32).reshape(1)
    depth = D // shards
    own = WIN - SHIFT
    params = (
        gain_one[None],
        bias_one[None],
        w_qkv,
        bias_qv,
        table,
        w_proj,
        bias_proj[None],
        gain_two[None],
        bias_two[None],
        w_in,
        bias_in[None],
        w_out,
        bias_out[None],
    )
    attn_slab, mlp_slab = kernel_call(
        pack_body,
        [like((4 * depth + SMALL, D), BF), like((8 * depth + SMALL, D), BF)],
        (me,) + params,
        smem=1,
    )
    attn_all = lax.all_gather(attn_slab, "shard")
    mlp_all = lax.all_gather(mlp_slab, "shard")
    tokens_here = tokens[0]
    token_halo = shifted_2(tokens_here[:SHIFT], "seq", -1)
    cot_here = cotangent[0]
    cot_halo = shifted_2(cot_here[:SHIFT], "seq", -1)
    by_row, by_lane = region_views(regions, local_rows, lax.axis_index("seq"))

    mixed, normed_win, query, key, value, probs, restored = kernel_call(
        attn_forward_body,
        [
            like((TOKENS, D), F32),
            like((PADDED, D), BF),
            like((PADDED, D), BF),
            like((PADDED, D), BF),
            like((PADDED, D), BF),
            like((WINDOWS // 2, GROUPS, 2 * PLACES, LANES), BF),
            like((TOKENS, D), BF),
        ],
        (tokens_here, token_halo, attn_all, by_row, by_lane),
        scratch=[
            pltpu.VMEM((WINDOWS, WIN, SLOT, D), F32),
            pltpu.VMEM((LANES, PLACES), BF),
            pltpu.VMEM((PLACES, LANES), BF),
            pltpu.VMEM((LANES, FEAT), F32),
            pltpu.VMEM((GROUPS, PLACES, LANES), F32),
        ],
        flops=5_000_000_000,
    )
    out_kept, out_sent, grad_mixed, mlp_grads = kernel_call(
        mlp_body,
        [
            like((own * WIDTH, D), F32),
            like((SHIFT * WIDTH, D), BF),
            like((TOKENS, D), F32),
            like(mlp_all.shape, BF),
        ],
        (mixed, cot_here, cot_halo, mlp_all),
        scratch=[
            pltpu.VMEM((TOKENS, D), BF),
            pltpu.VMEM((TOKENS, D), BF),
            pltpu.VMEM((TOKENS, D), F32),
            pltpu.VMEM((TOKENS, D), F32),
        ],
        flops=10_000_000_000,
    )
    mlp_share = lax.psum_scatter(mlp_grads, "shard", scatter_dimension=0)
    out_halo = shifted_2(out_sent, "seq", 1)
    tok_kept, tok_sent, attn_grads = kernel_call(
        attn_backward_body,
        [
            like((own * WIDTH, D), F32),
            like((SHIFT * WIDTH, D), BF),
            like(attn_all.shape, BF),
        ],
        (
            grad_mixed,
            tokens_here,
            token_halo,
            attn_all,
            normed_win,
            query,
            key,
            value,
            probs,
            restored,
        ),
        scratch=[
            pltpu.VMEM((WINDOWS, WIN, SLOT, D), F32),
            pltpu.VMEM((PADDED, 3 * D), BF),
            pltpu.VMEM((LANES, PLACES), BF),
            pltpu.VMEM((PLACES, LANES), BF),
            pltpu.VMEM((LANES, FEAT), F32),
            pltpu.VMEM((GROUPS, PLACES, LANES), F32),
        ],
        flops=10_000_000_000,
    )
    attn_share = lax.psum_scatter(attn_grads, "shard", scatter_dimension=0)
    tok_halo = shifted_2(tok_sent, "seq", 1)
    attn_total, mlp_total = lax.psum((attn_share, mlp_share), "seq")
    shapes = [like(p.shape, F32) for p in params]
    summed = kernel_call(unpack_body, shapes, (me, attn_total, mlp_total), smem=1)

    def joined(halo, kept):
        return jnp.concatenate([halo.astype(F32), kept], 0).reshape(tokens.shape)

    grads = [s.reshape(p.shape) for s, p in zip(
        summed,
        (
            gain_one,
            bias_one,
            w_qkv,
            bias_qv,
            table,
            w_proj,
            bias_proj,
            gain_two,
            bias_two,
            w_in,
            bias_in,
            w_out,
            bias_out,
        ),
    )]
    return (joined(out_halo, out_kept), joined(tok_halo, tok_kept), *grads)


def solution(mesh):
    return jax.shard_map(
        per_device,
        mesh=mesh,
        in_specs=(
            P("shard", "seq", None, None),
            P("shard", None, None),
            P("shard", "seq", None, None),
            P("shard"),
            P("shard"),
            P("shard", None),
            P(None, "shard"),
            P(None, "shard"),
            P("shard", None),
            P("shard"),
            P("shard"),
            P("shard"),
            P("shard", None),
            P("shard"),
            P("shard", None),
            P("shard"),
        ),
        out_specs=(
            P("shard", "seq", None, None),
            P("shard", "seq", None, None),
            P("shard"),
            P("shard"),
            P("shard", None),
            P(None, "shard"),
            P(None, "shard"),
            P("shard", None),
            P("shard"),
            P("shard"),
            P("shard"),
            P("shard", None),
            P("shard"),
            P("shard", None),
            P("shard"),
        ),
        check_vma=False,
    )
```

```python
import jax
import jax.numpy as jnp
from jax import lax
from jax.experimental import pallas as pl
from jax.experimental.pallas import tpu as pltpu
from jax.sharding import PartitionSpec as P

D = 512
HEADS = 16
HEAD = 32
WIN = 7
SHIFT = 3
FF = 2048
WIDTH = 112
WINDOWS = WIDTH // WIN
SLOT = 8
PLACES = WIN * SLOT
GROUP = 8
GROUPS = HEADS // GROUP
FEAT = GROUP * HEAD
LANES = 64 * GROUP
TOKENS = WIN * WIDTH
PADDED = WINDOWS * PLACES
TAB = 1536
TAB_USED = 768
SMALL = 32
EPS = 1e-05
SCALE = HEAD**-0.5
BF = jnp.bfloat16
F32 = jnp.float32
VMEM_LIMIT = 60 * 1024 * 1024


def shifted_2(value, axis, by):
    peers = lax.axis_size(axis)
    return lax.ppermute(value, axis, [(i, (i + by) % peers) for i in range(peers)])


def dot(left, right, dims=((1,), (0,))):
    return lax.dot_general(left, right, (dims, ((), ())), preferred_element_type=F32)


def dot_nt(left, right):
    return dot(left, right, ((1,), (1,)))


def dot_tn(left, right):
    return dot(left, right, ((0,), (0,)))


def iota(shape, axis):
    return lax.broadcasted_iota(jnp.int32, shape, axis)


def one_hot(condition):
    return jnp.where(condition, 1.0, 0.0).astype(BF)


def column_places():
    slot = iota((WINDOWS * SLOT, WIDTH), 0)
    column = iota((WINDOWS * SLOT, WIDTH), 1)
    place = slot & (SLOT - 1)
    wanted = (slot >> 3) * WIN + place + SHIFT
    wanted = jnp.where(wanted >= WIDTH, wanted - WIDTH, wanted)
    return one_hot((wanted == column) & (place < WIN))


def places_column():
    slot = iota((WIDTH, WINDOWS * SLOT), 1)
    column = iota((WIDTH, WINDOWS * SLOT), 0)
    place = slot & (SLOT - 1)
    wanted = (slot >> 3) * WIN + place + SHIFT
    wanted = jnp.where(wanted >= WIDTH, wanted - WIDTH, wanted)
    return one_hot((wanted == column) & (place < WIN))


def spread_matrix():
    return one_hot((iota((LANES, PLACES), 0) >> 3) == iota((LANES, PLACES), 1))


def fold_matrix():
    return one_hot((iota((PLACES, LANES), 1) >> 3) == iota((PLACES, LANES), 0))


def head_mask(value):
    row = iota((LANES, FEAT), 0) & (GROUP - 1)
    feature = iota((LANES, FEAT), 1) >> 5
    return jnp.where(row == feature, value, 0.0).astype(F32)


def table_pick(row_axis, backwards):
    shape = (TAB_USED, LANES) if row_axis == 0 else (LANES, TAB_USED)
    lane = iota(shape, row_axis)
    pair = iota(shape, 1 - row_axis)
    place = pair >> 3
    row, column = place >> 3, place & (SLOT - 1)
    entry = row * (2 * WIN - 1) + column
    if backwards:
        entry = (WIN - 1) * 2 * WIN - entry
    match = ((lane >> 3) == entry) & ((lane & 7) == (pair & 7))
    return one_hot(match & (column < WIN) & (row < WIN))


def norm_stats(values):
    average = jnp.mean(values, -1, keepdims=True)
    centered = values - average
    variance = jnp.mean(centered * centered, -1, keepdims=True)
    scale = lax.rsqrt(variance + EPS)
    return centered * scale, scale


def norm_back(grad, normed, scale, gain):
    scaled = grad * gain
    first = jnp.mean(scaled, -1, keepdims=True)
    second = jnp.mean(scaled * normed, -1, keepdims=True)
    return scale * (scaled - first - normed * second)


def whole(memory=pltpu.VMEM):
    return pl.BlockSpec(memory_space=memory)


def kernel_call(body, outs, ins, scratch=(), flops=0, smem=0, apart=0):
    size = sum(a.size * a.dtype.itemsize for a in list(ins) + list(outs))
    return pl.pallas_call(
        body,
        out_shape=tuple(outs),
        in_specs=[whole(pltpu.SMEM)] * smem
        + [whole()] * (len(ins) - smem - apart)
        + [whole(pl.ANY)] * apart,
        out_specs=tuple(whole() for _ in outs),
        scratch_shapes=list(scratch),
        cost_estimate=pl.CostEstimate(flops=flops, bytes_accessed=size, transcendentals=0),
        compiler_params=pltpu.CompilerParams(vmem_limit_bytes=VMEM_LIMIT),
    )(*ins)


def like(shape, dtype):
    return jax.ShapeDtypeStruct(shape, dtype)


def place(vector, lanes, me):
    w = vector.shape[1]
    pick = one_hot(iota((w, lanes), 1) == iota((w, lanes), 0) + me * w)
    wide = jnp.broadcast_to(vector, (8, w))
    return dot(wide.astype(BF), pick)[0:1]


def mine(row, w, me):
    lanes = row.shape[1]
    pick = one_hot(iota((lanes, w), 0) == iota((lanes, w), 1) + me * w)
    wide = jnp.broadcast_to(row, (8, lanes))
    return dot(wide.astype(BF), pick)[0:1]


def padded(rows, height):
    total = sum(r.shape[0] for r in rows)
    return jnp.concatenate(rows + [jnp.zeros((height - total, D), F32)], 0).astype(BF)


def pack_attn_body(me_ref, g1, b1, wqkv, bqv, table, wproj, bproj, attn):
    depth = wqkv.shape[0]
    me = me_ref[0]
    for c in range(3):
        attn[c * depth : (c + 1) * depth, :] = wqkv[:, c * D : (c + 1) * D]
    attn[3 * depth : 4 * depth, :] = wproj[...]
    rows = [
        place(v, D, me) for v in (g1[...], b1[...], bqv[0:1, :], bqv[1:2, :], bproj[...])
    ]
    held, entries = table.shape
    lane = iota((entries, TAB), 1)
    spot = iota((entries, TAB), 0) * GROUP + TAB - (WIN - 1) * 2 * WIN * GROUP
    spot = jnp.where(spot >= TAB, spot - TAB, spot)
    values = table[...].astype(F32).T
    groups = [jnp.zeros((1, TAB), F32) for _ in range(GROUPS)]
    for h in range(held):
        head = me * held + h
        inside = lane == spot + (head & (GROUP - 1))
        row = jnp.sum(jnp.where(inside, values[:, h : h + 1], 0.0), 0, keepdims=True)
        for g in range(GROUPS):
            groups[g] = groups[g] + jnp.where((head >> 3) == g, row, 0.0)
    for g in range(GROUPS):
        rows += [groups[g][:, c * D : (c + 1) * D] for c in range(TAB // D)]
    attn[4 * depth :, :] = padded(rows, SMALL)


def pack_mlp_body(me_ref, g2, b2, win, bin_, wout, bout, mlp):
    depth = win.shape[0]
    me = me_ref[0]
    for c in range(FF // D):
        mlp[c * depth : (c + 1) * depth, :] = win[:, c * D : (c + 1) * D]
    mlp[4 * depth : 8 * depth, :] = wout[...]
    hidden_bias = place(bin_[...], FF, me)
    rows = [place(v, D, me) for v in (g2[...], b2[...], bout[...])]
    rows += [hidden_bias[:, c * D : (c + 1) * D] for c in range(FF // D)]
    mlp[8 * depth :, :] = padded(rows, SMALL)


def unpack_body(
    me_ref,
    attn_half,
    attn_back,
    mlp_half,
    mlp_back,
    g1,
    b1,
    wqkv,
    bqv,
    table,
    wproj,
    bproj,
    g2,
    b2,
    win,
    bin_,
    wout,
    bout,
    attn,
    mlp,
):
    depth = wqkv.shape[0]
    me = me_ref[0]
    late = me_ref[1]
    for half, back, both in ((attn_half, attn_back, attn), (mlp_half, mlp_back, mlp)):
        rows = half.shape[0]
        both[pl.ds(pl.multiple_of(late * rows, 16), rows), :] = half[...]
        both[pl.ds(pl.multiple_of((1 - late) * rows, 16), rows), :] = back[...]
    for c in range(3):
        wqkv[:, c * D : (c + 1) * D] = attn[c * depth : (c + 1) * depth, :].astype(F32)
    small = attn[3 * depth :, :].astype(F32)
    g1[...] = mine(small[0:1], depth, me)
    b1[...] = mine(small[1:2], depth, me)
    bqv[0:1, :] = mine(small[2:3], depth, me)
    bqv[1:2, :] = mine(small[3:4], depth, me)
    held, entries = table.shape
    lane = iota((entries, TAB), 1)
    spot = (entries - 1 - iota((entries, TAB), 0)) * GROUP
    parts = TAB // D
    rows = [
        jnp.concatenate([small[4 + g * parts + c : 5 + g * parts + c] for c in range(parts)], 1)
        for g in range(GROUPS)
    ]
    which = iota((entries, held), 1)
    total = jnp.zeros((entries, held), F32)
    for h in range(held):
        head = me * held + h
        row = rows[0]
        for g in range(1, GROUPS):
            row = jnp.where((head >> 3) == g, rows[g], row)
        inside = lane == spot + (head & (GROUP - 1))
        column = jnp.sum(jnp.where(inside, row, 0.0), 1, keepdims=True)
        total = jnp.where(which == h, column, total)
    table[...] = total.T

    for c in range(FF // D):
        win[:, c * D : (c + 1) * D] = mlp[c * depth : (c + 1) * depth, :].astype(F32)
    wout[...] = mlp[4 * depth : 8 * depth, :].astype(F32)
    wproj[...] = mlp[8 * depth : 9 * depth, :].astype(F32)
    small = mlp[9 * depth :, :].astype(F32)
    g2[...] = mine(small[0:1], depth, me)
    b2[...] = mine(small[1:2], depth, me)
    bout[...] = mine(small[2:3], depth, me)
    bproj[...] = mine(small[3:4], depth, me)
    hidden = jnp.concatenate([small[4 + c : 5 + c] for c in range(FF // D)], 1)
    bin_[...] = mine(hidden, depth * FF // D, me)


def put_shares(me, same, other, start, values, first=0):
    core, chip = me & 1, me >> 1
    rows = values.shape[1]
    for c in range(values.shape[0] // 2):
        one, two = values[2 * c], values[2 * c + 1]
        q = (first // 2 + c) ^ chip
        same[q, start : start + rows, :] = jnp.where(core == 0, one, two).astype(BF)
        other[q, start : start + rows, :] = jnp.where(core == 0, two, one).astype(BF)


def put_smalls(same, other, start, rows):
    block = padded(rows, SMALL)
    for q in range(same.shape[0]):
        same[q, start:, :] = block
        other[q, start:, :] = block


def add_cores_body(same, came, *sums):
    for q, total in enumerate(sums):
        total[...] = (same[q].astype(F32) + came[q].astype(F32)).astype(BF)


def add_chips_body(me_ref, *refs):
    parts, (keep, send) = refs[:-2], refs[-2:]
    half = keep.shape[0]
    late = me_ref[1]
    for place_at, target in ((late, keep), (1 - late, send)):
        rows = pl.ds(pl.multiple_of(place_at * half, 16), half)
        total = parts[0][rows, :].astype(F32)
        for part in parts[1:]:
            total += part[rows, :].astype(F32)
        target[...] = total.astype(BF)


def exchange(value, axis, mask):
    peers = lax.axis_size(axis)
    return lax.ppermute(value, axis, [(i, i ^ mask) for i in range(peers)])


def gather_pieces(slab):
    chips = lax.axis_size("shard") // 2
    pieces = [None] * (2 * chips)
    for q in range(chips):
        pieces[2 * q] = exchange(slab, "shard", 2 * q) if q else slab
    for q in range(chips):
        pieces[2 * q + 1] = exchange(pieces[2 * q], "shard", 1)
    return pieces


def add_cores(same, other):
    came = exchange(other, "shard", 1)
    chips, rows, _ = same.shape
    return kernel_call(add_cores_body, [like((rows, D), BF)] * chips, (same, came))


def add_chips(where, sums):
    parts = [sums[0]] + [exchange(sums[q], "shard", 2 * q) for q in range(1, len(sums))]
    rows = sums[0].shape[0]
    return kernel_call(add_chips_body, [like((rows // 2, D), BF)] * 2, (where, *parts), smem=1)


def add_pair(here, came):
    return (here.astype(F32) + came.astype(F32)).astype(BF)


def add_seq(keep, send):
    half = add_pair(keep, exchange(send, "seq", 1))
    reach = 2
    while reach < lax.axis_size("seq"):
        half = add_pair(half, exchange(half, "seq", reach))
        reach *= 2
    return half, exchange(half, "seq", 1)


def block_of(slab, c, depth):
    return slab[:, c * depth : (c + 1) * depth, :].reshape(D, D)


def smalls_of(slab, start):
    return jnp.sum(slab[:, start:, :].astype(F32), 0)


def load_pieces(me, pieces, slab, sems):
    copies = [
        pltpu.make_async_copy(piece, slab.at[me ^ p], sems.at[p]) for p, piece in enumerate(pieces)
    ]
    for copy in copies:
        copy.start()
    return copies


def attn_forward_body(me_ref, tokens, halo, reg_rows, reg_lanes, *refs):
    shards = len(refs) - 14
    pieces = refs[:shards]
    (
        mixed,
        normed_win,
        query,
        key,
        value,
        probs,
        restored,
        slab,
        wide,
        spread,
        fold,
        mask,
        bias,
        sems,
    ) = refs[shards:]
    copies = load_pieces(me_ref[0], pieces, slab, sems)
    depth = (slab.shape[1] - SMALL) // 4
    for copy in copies:
        copy.wait()
    small = smalls_of(slab, 4 * depth)
    gain, offset = small[0:1], small[1:2]
    bias_q, bias_v, bias_o = small[2:3], small[3:4], small[4:5]
    spread[...] = spread_matrix()
    fold[...] = fold_matrix()
    mask[...] = head_mask(1.0)
    pick = table_pick(0, False)
    parts = TAB // D
    empty = (iota((PLACES, LANES), 0) & (SLOT - 1)) == WIN
    for g in range(GROUPS):
        row = jnp.concatenate([small[5 + g * parts + c : 6 + g * parts + c] for c in range(parts)], 1)
        row = jnp.broadcast_to(row, (SLOT, TAB))
        row = pltpu.roll(row, 0, 1, stride=GROUP, stride_axis=0)
        turned = [
            pltpu.roll(row, (2 * WIN - 1) * GROUP * r, 1)[:, :TAB_USED] for r in range(WIN)
        ]
        picked = dot(jnp.concatenate(turned, 0).astype(BF), pick)
        bias[g] = jnp.where(empty, -1e30, picked)

    columns = column_places()
    own = WIN - SHIFT
    for r in range(WIN):
        x = (tokens[SHIFT + r] if r < own else halo[r - own]).astype(F32)
        normed, _ = norm_stats(x)
        low = (normed * gain + offset).astype(BF)
        wide[:, r] = dot(columns, low).reshape(WINDOWS, SLOT, D)
    normed_win[...] = wide[...].reshape(PADDED, D).astype(BF)
    query[...] = (dot(normed_win[...], block_of(slab, 0, depth)) + bias_q).astype(BF)
    key[...] = dot(normed_win[...], block_of(slab, 1, depth)).astype(BF)
    value[...] = (dot(normed_win[...], block_of(slab, 2, depth)) + bias_v).astype(BF)

    def pair(n, carry):
        rows = pl.ds(pl.multiple_of(n * 2 * PLACES, 2 * PLACES), 2 * PLACES)
        for g in range(GROUPS):
            feats = slice(g * FEAT, (g + 1) * FEAT)
            q2 = query[rows, feats].astype(F32)
            k2 = key[rows, feats].astype(F32)
            v2 = value[rows, feats].astype(F32)
            held = []
            for s in range(2):
                w = 2 * n + s
                part = slice(s * PLACES, (s + 1) * PLACES)
                q, k, v = (a[part].astype(BF) for a in (q2, k2, v2))
                q_big = (dot(spread[...], q) * mask[...]).astype(BF)
                penalty = jnp.where(reg_rows[w][:, 0:1] != reg_lanes[w], -100.0, 0.0)
                logits = dot_nt(k, q_big) * SCALE + bias[g] + penalty
                top = jnp.max(logits, 0, keepdims=True)
                powers = jnp.exp(logits - top)
                p = powers * (1.0 / jnp.sum(powers, 0, keepdims=True))
                held.append(p)
                o_big = (dot_tn(p.astype(BF), v) * mask[...]).astype(BF)
                o = dot(fold[...], o_big)
                wide[w, :, :, feats] = o.reshape(WIN, SLOT, FEAT)
            probs[n, g] = jnp.concatenate(held, 0).astype(BF)
        return carry

    lax.fori_loop(0, WINDOWS // 2, pair, 0)
    back = places_column()
    for r in range(WIN):
        here = wide[:, r].reshape(WINDOWS * SLOT, D).astype(BF)
        restored[r * WIDTH : (r + 1) * WIDTH, :] = dot(back, here).astype(BF)
    branch = dot(restored[...], block_of(slab, 3, depth)) + bias_o
    for r in range(WIN):
        x = (tokens[SHIFT + r] if r < own else halo[r - own]).astype(F32)
        part = slice(r * WIDTH, (r + 1) * WIDTH)
        mixed[part, :] = x + branch[part]


def gelu_parts(h):
    size = jnp.abs(h) * (0.5**0.5)
    t = 1.0 / (1.0 + 0.3275911 * size)
    bell = jnp.exp(-0.5 * h * h)
    poly = t * (
        0.254829592
        + t * (-0.284496736 + t * (1.421413741 + t * (-1.453152027 + t * 1.061405429)))
    )
    tail = 0.5 * poly * bell
    upto = jnp.where(h >= 0, 1.0 - tail, tail)
    return upto, bell * 0.3989422804014327


def mlp_body(
    me_ref,
    mixed,
    cotangent,
    halo,
    slab,
    attn_slab,
    restored,
    kept,
    sent,
    grad_mixed,
    grad_win,
    same,
    other,
    normed_low,
    cot,
    out_sum,
    back_sum,
    wide,
):
    me = me_ref[0]
    shards, height = slab.shape[:2]
    depth = (height - SMALL) // 8
    span = shards * D // FF
    small = smalls_of(slab, 8 * depth)
    gain, offset, bias_o = small[0:1], small[1:2], small[2:3]
    own = WIN - SHIFT
    for r in range(WIN):
        part = slice(r * WIDTH, (r + 1) * WIDTH)
        cot[part, :] = cotangent[SHIFT + r] if r < own else halo[r - own]
    normed, _ = norm_stats(mixed[...])
    normed_low[...] = (normed * gain + offset).astype(BF)
    vectors = []
    for c in range(FF // D):
        w_in = block_of(slab, c, depth)
        w_out = slab[c * span : (c + 1) * span, 4 * depth : 8 * depth, :].reshape(D, D)
        hidden = dot(normed_low[...], w_in) + small[3 + c : 4 + c]
        upto, density = gelu_parts(hidden)
        active = (hidden * upto).astype(BF)
        slope = upto + hidden * density
        grad = (dot_nt(cot[...], w_out) * slope).astype(BF)
        forward = dot(active, w_out)
        backward = dot_nt(grad, w_in)
        if c == 0:
            out_sum[...] = forward
            back_sum[...] = backward
        else:
            out_sum[...] += forward
            back_sum[...] += backward
        vectors.append(jnp.sum(grad.astype(F32), 0, keepdims=True))
        put_shares(
            me, same, other, c * depth, dot_tn(normed_low[...], grad).reshape(shards, depth, D)
        )
        put_shares(
            me,
            same,
            other,
            4 * depth,
            dot_tn(active, cot[...]).reshape(span, 4 * depth, D),
            c * span,
        )
    result = mixed[...] + out_sum[...] + bias_o
    kept[...] = result[: own * WIDTH]
    sent[...] = result[own * WIDTH :].astype(BF)
    normed, scale = norm_stats(mixed[...])
    g = back_sum[...]
    gain_sum = jnp.sum(g * normed, 0, keepdims=True)
    offset_sum = jnp.sum(g, 0, keepdims=True)
    cot_sum = jnp.sum(cot[...].astype(F32), 0, keepdims=True)
    grad_mixed[...] = cot[...].astype(F32) + norm_back(g, normed, scale, gain)

    branch = grad_mixed[...].astype(BF)
    branch_sum = jnp.sum(branch.astype(F32), 0, keepdims=True)
    proj = dot_tn(restored[...], branch).reshape(shards, depth, D)
    put_shares(me, same, other, 8 * depth, proj)
    put_smalls(same, other, 9 * depth, [gain_sum, offset_sum, cot_sum, branch_sum] + vectors)
    grad_att = dot_nt(branch, block_of(attn_slab, 3, depth)).astype(BF)
    columns = column_places()
    for r in range(WIN):
        wide[:, r] = dot(columns, grad_att[r * WIDTH : (r + 1) * WIDTH]).reshape(WINDOWS, SLOT, D)
    grad_win[...] = wide[...].reshape(PADDED, D).astype(BF)


def attn_pairs(first, last, query, key, value, probs, grad_win, out, spread, fold, mask, pairs):
    spread[...] = spread_matrix()
    fold[...] = fold_matrix()
    mask[...] = head_mask(1.0)

    def pair(n, carry):
        rows = pl.ds(pl.multiple_of(n * 2 * PLACES, 2 * PLACES), 2 * PLACES)
        for g in range(GROUPS):
            feats = slice(g * FEAT, (g + 1) * FEAT)
            q2 = query[rows, feats].astype(F32)
            k2 = key[rows, feats].astype(F32)
            v2 = value[rows, feats].astype(F32)
            go2 = grad_win[rows, feats].astype(F32)
            p2 = probs[n, g].astype(F32)
            held = []
            for s in range(2):
                part = slice(s * PLACES, (s + 1) * PLACES)
                q, k, v, go, p_low = (a[part].astype(BF) for a in (q2, k2, v2, go2, p2))
                p = p2[part]
                go_big = (dot(spread[...], go) * mask[...]).astype(BF)
                q_big = (dot(spread[...], q) * mask[...]).astype(BF)
                dp = dot_nt(v, go_big)
                dv = dot(p_low, go_big)
                inner = jnp.sum(p * dp, 0, keepdims=True)
                ds = (p * (dp - inner)).astype(BF)
                pairs[g] += ds.astype(F32)
                dk = dot(ds, q_big) * SCALE
                dq_big = (dot_tn(ds, k) * (mask[...] * SCALE)).astype(BF)
                dq = dot(fold[...], dq_big)
                held.append((dq, dk, dv))
            to = pl.ds(pl.multiple_of((n - first) * 2 * PLACES, 2 * PLACES), 2 * PLACES)
            for c in range(3):
                both = jnp.concatenate([held[0][c], held[1][c]], 0).astype(BF)
                out[to, c * D + g * FEAT : c * D + (g + 1) * FEAT] = both
        return carry

    lax.fori_loop(first, last, pair, 0)


def attn_first_body(query, key, value, probs, grad_win, out, pairs, spread, fold, mask):
    pairs[...] = jnp.zeros_like(pairs)
    last = out.shape[0] // (2 * PLACES)
    attn_pairs(0, last, query, key, value, probs, grad_win, out, spread, fold, mask, pairs)


def attn_last_body(
    me_ref,
    query,
    key,
    value,
    probs,
    grad_win,
    grad_early,
    pairs_early,
    grad_mixed,
    tokens,
    halo,
    slab,
    normed_win,
    kept,
    sent,
    same,
    other,
    grad_late,
    spread,
    fold,
    mask,
    pairs,
    wide,
):
    me = me_ref[0]
    pairs[...] = pairs_early[...]
    early = grad_early.shape[0]
    attn_pairs(
        early // (2 * PLACES),
        WINDOWS // 2,
        query,
        key,
        value,
        probs,
        grad_win,
        grad_late,
        spread,
        fold,
        mask,
        pairs,
    )
    shards = slab.shape[0]
    depth = (slab.shape[1] - SMALL) // 4
    small = smalls_of(slab, 4 * depth)
    gain = small[0:1]
    own = WIN - SHIFT
    vectors = []
    for c in range(3):
        cols = slice(c * D, (c + 1) * D)
        g = jnp.concatenate([grad_early[:, cols], grad_late[:, cols]], 0)
        if c != 1:
            vectors.append(jnp.sum(g.astype(F32), 0, keepdims=True))
        put_shares(
            me, same, other, c * depth, dot_tn(normed_win[...], g).reshape(shards, depth, D)
        )
        part = dot_nt(g, block_of(slab, c, depth))
        total = part if c == 0 else total + part
    wide[...] = total.reshape(WINDOWS, WIN, SLOT, D)
    back = places_column()
    gain_sum = jnp.zeros((1, D), F32)
    bias_sum = jnp.zeros((1, D), F32)
    for r in range(WIN):
        here = wide[:, r].reshape(WINDOWS * SLOT, D).astype(BF)
        g = dot(back, here)
        x = (tokens[SHIFT + r] if r < own else halo[r - own]).astype(F32)
        normed, scale = norm_stats(x)
        gain_sum += jnp.sum(g * normed, 0, keepdims=True)
        bias_sum += jnp.sum(g, 0, keepdims=True)
        grad = grad_mixed[r * WIDTH : (r + 1) * WIDTH, :] + norm_back(g, normed, scale, gain)
        if r < own:
            kept[r * WIDTH : (r + 1) * WIDTH, :] = grad
        else:
            sent[(r - own) * WIDTH : (r - own + 1) * WIDTH, :] = grad.astype(BF)

    pick = table_pick(1, True)
    rows = [gain_sum, bias_sum, vectors[0], vectors[1]]
    for g in range(GROUPS):
        high = pairs[g].astype(BF)
        low = (pairs[g] - high.astype(F32)).astype(BF)
        laid = dot(high, pick) + dot(low, pick)
        laid = jnp.concatenate([laid, jnp.zeros((PLACES, TAB - TAB_USED), F32)], 1)
        total = jnp.zeros((SLOT, TAB), F32)
        for r in range(WIN):
            total += pltpu.roll(
                laid[r * SLOT : (r + 1) * SLOT], (2 * WIN - 1) * GROUP * r, 1
            )
        total = pltpu.roll(total, 0, 1, stride=GROUP, stride_axis=0)
        row = jnp.sum(total, 0, keepdims=True)
        rows += [row[:, c * D : (c + 1) * D] for c in range(TAB // D)]
    put_smalls(same, other, 3 * depth, rows)


def region_views(regions, rows, place):
    here = lax.dynamic_slice_in_dim(regions[0], place * rows, rows, 0)
    windows = here.reshape(WIN, WINDOWS, WIN).transpose(1, 0, 2)
    windows = jnp.pad(windows, ((0, 0), (0, 0), (0, SLOT - WIN))).astype(F32)
    windows = windows.reshape(WINDOWS, PLACES)
    by_row = jnp.broadcast_to(windows[:, :, None], (WINDOWS, PLACES, 128))
    by_lane = jnp.pad(jnp.repeat(windows, GROUP, 1), ((0, 0), (0, LANES - PLACES * GROUP)))
    return by_row, by_lane[:, None, :]


def per_device(
    tokens,
    regions,
    cotangent,
    gain_one,
    bias_one,
    w_qkv,
    bias_qv,
    table,
    w_proj,
    bias_proj,
    gain_two,
    bias_two,
    w_in,
    bias_in,
    w_out,
    bias_out,
):
    images, local_rows, columns, _ = tokens.shape
    assert images == 1 and local_rows == WIN and columns == WIDTH
    shards = lax.axis_size("shard")
    me = lax.axis_index("shard").astype(jnp.int32)
    seq = lax.axis_index("seq").astype(jnp.int32)
    where = jnp.stack([me, seq & 1])
    chips = shards // 2
    depth = D // shards
    own = WIN - SHIFT
    attn_params = (
        gain_one[None],
        bias_one[None],
        w_qkv,
        bias_qv,
        table.T,
        w_proj,
        bias_proj[None],
    )
    mlp_params = (gain_two[None], bias_two[None], w_in, bias_in[None], w_out, bias_out[None])
    (attn_slab,) = kernel_call(
        pack_attn_body, [like((4 * depth + SMALL, D), BF)], (where,) + attn_params, smem=1
    )
    pieces = gather_pieces(attn_slab)
    (mlp_slab,) = kernel_call(
        pack_mlp_body, [like((8 * depth + SMALL, D), BF)], (where,) + mlp_params, smem=1
    )
    mlp_all = lax.all_gather(mlp_slab, "shard")
    tokens_here = tokens[0]
    token_halo = shifted_2(tokens_here[:SHIFT], "seq", -1)
    cot_here = cotangent[0]
    cot_halo = shifted_2(cot_here[:SHIFT], "seq", -1)
    by_row, by_lane = region_views(regions, local_rows, seq)

    mixed, normed_win, query, key, value, probs, restored, attn_all = kernel_call(
        attn_forward_body,
        [
            like((TOKENS, D), F32),
            like((PADDED, D), BF),
            like((PADDED, D), BF),
            like((PADDED, D), BF),
            like((PADDED, D), BF),
            like((WINDOWS // 2, GROUPS, 2 * PLACES, LANES), BF),
            like((TOKENS, D), BF),
            like((shards, *attn_slab.shape), BF),
        ],
        (where, tokens_here, token_halo, by_row, by_lane, *pieces),
        scratch=[
            pltpu.VMEM((WINDOWS, WIN, SLOT, D), F32),
            pltpu.VMEM((LANES, PLACES), BF),
            pltpu.VMEM((PLACES, LANES), BF),
            pltpu.VMEM((LANES, FEAT), F32),
            pltpu.VMEM((GROUPS, PLACES, LANES), F32),
            pltpu.SemaphoreType.DMA((shards,)),
        ],
        flops=5_000_000_000,
        smem=1,
        apart=shards,
    )
    out_kept, out_sent, grad_mixed, grad_win, mlp_same, mlp_other = kernel_call(
        mlp_body,
        [
            like((own * WIDTH, D), F32),
            like((SHIFT * WIDTH, D), BF),
            like((TOKENS, D), F32),
            like((PADDED, D), BF),
            like((chips, 9 * depth + SMALL, D), BF),
            like((chips, 9 * depth + SMALL, D), BF),
        ],
        (where, mixed, cot_here, cot_halo, mlp_all, attn_all, restored),
        scratch=[
            pltpu.VMEM((TOKENS, D), BF),
            pltpu.VMEM((TOKENS, D), BF),
            pltpu.VMEM((TOKENS, D), F32),
            pltpu.VMEM((TOKENS, D), F32),
            pltpu.VMEM((WINDOWS, WIN, SLOT, D), F32),
        ],
        flops=10_000_000_000,
        smem=1,
    )
    out_halo = shifted_2(out_sent, "seq", 1)
    scratch = [
        pltpu.VMEM((LANES, PLACES), BF),
        pltpu.VMEM((PLACES, LANES), BF),
        pltpu.VMEM((LANES, FEAT), F32),
    ]
    early, pairs_early = kernel_call(
        attn_first_body,
        [like((PADDED // 2, 3 * D), BF), like((GROUPS, PLACES, LANES), F32)],
        (query, key, value, probs, grad_win),
        scratch=scratch,
        flops=5_000_000_000,
    )
    mlp_sums = add_cores(mlp_same, mlp_other)
    *mlp_sums, early = lax.optimization_barrier((*mlp_sums, early))
    tok_kept, tok_sent, attn_same, attn_other = kernel_call(
        attn_last_body,
        [
            like((own * WIDTH, D), F32),
            like((SHIFT * WIDTH, D), BF),
            like((chips, 3 * depth + SMALL, D), BF),
            like((chips, 3 * depth + SMALL, D), BF),
        ],
        (
            where,
            query,
            key,
            value,
            probs,
            grad_win,
            early,
            pairs_early,
            grad_mixed,
            tokens_here,
            token_halo,
            attn_all,
            normed_win,
        ),
        scratch=[
            pltpu.VMEM((PADDED // 2, 3 * D), BF),
            *scratch,
            pltpu.VMEM((GROUPS, PLACES, LANES), F32),
            pltpu.VMEM((WINDOWS, WIN, SLOT, D), F32),
        ],
        flops=10_000_000_000,
        smem=1,
    )
    mlp_parts = add_chips(where, mlp_sums)
    mlp_total = add_seq(*mlp_parts)
    attn_total = add_seq(*add_chips(where, add_cores(attn_same, attn_other)))
    tok_halo = shifted_2(tok_sent, "seq", 1)
    shapes = [like(p.shape, F32) for p in attn_params + mlp_params]
    summed = list(
        kernel_call(
            unpack_body,
            shapes,
            (where, *attn_total, *mlp_total),
            scratch=[
                pltpu.VMEM((3 * depth + SMALL, D), BF),
                pltpu.VMEM((9 * depth + SMALL, D), BF),
            ],
            smem=1,
        )
    )
    summed[4] = summed[4].T

    def joined(halo, kept):
        return jnp.concatenate([halo.astype(F32), kept], 0).reshape(tokens.shape)

    targets = (
        gain_one,
        bias_one,
        w_qkv,
        bias_qv,
        table,
        w_proj,
        bias_proj,
        gain_two,
        bias_two,
        w_in,
        bias_in,
        w_out,
        bias_out,
    )
    grads = [g.reshape(p.shape) for g, p in zip(summed, targets)]
    return (joined(out_halo, out_kept), joined(tok_halo, tok_kept), *grads)


def solution(mesh):
    return jax.shard_map(
        per_device,
        mesh=mesh,
        in_specs=(
            P("shard", "seq", None, None),
            P("shard", None, None),
            P("shard", "seq", None, None),
            P("shard"),
            P("shard"),
            P("shard", None),
            P(None, "shard"),
            P(None, "shard"),
            P("shard", None),
            P("shard"),
            P("shard"),
            P("shard"),
            P("shard", None),
            P("shard"),
            P("shard", None),
            P("shard"),
        ),
        out_specs=(
            P("shard", "seq", None, None),
            P("shard", "seq", None, None),
            P("shard"),
            P("shard"),
            P("shard", None),
            P(None, "shard"),
            P(None, "shard"),
            P("shard", None),
            P("shard"),
            P("shard"),
            P("shard"),
            P("shard", None),
            P("shard"),
            P("shard", None),
            P("shard"),
        ),
        check_vma=False,
    )
```

```python
import jax
import jax.numpy as jnp
from jax import lax
from jax.experimental import pallas as pl
from jax.experimental.pallas import tpu as pltpu
from jax.sharding import PartitionSpec as P

D = 512
HEADS = 16
HEAD = 32
WIN = 7
SHIFT = 3
FF = 2048
WIDTH = 112
WINDOWS = WIDTH // WIN
SLOT = 8
PLACES = WIN * SLOT
GROUP = 8
GROUPS = HEADS // GROUP
FEAT = GROUP * HEAD
LANES = 64 * GROUP
TOKENS = WIN * WIDTH
PADDED = WINDOWS * PLACES
TAB = 1536
TAB_USED = 768
SMALL = 32
EPS = 1e-05
SCALE = HEAD**-0.5
BF = jnp.bfloat16
F32 = jnp.float32
VMEM_LIMIT = 60 * 1024 * 1024


def shifted_2(value, axis, by):
    peers = lax.axis_size(axis)
    return lax.ppermute(value, axis, [(i, (i + by) % peers) for i in range(peers)])


def dot(left, right, dims=((1,), (0,))):
    return lax.dot_general(left, right, (dims, ((), ())), preferred_element_type=F32)


def dot_nt(left, right):
    return dot(left, right, ((1,), (1,)))


def dot_tn(left, right):
    return dot(left, right, ((0,), (0,)))


def iota(shape, axis):
    return lax.broadcasted_iota(jnp.int32, shape, axis)


def one_hot(condition):
    return jnp.where(condition, 1.0, 0.0).astype(BF)


def column_places():
    slot = iota((WINDOWS * SLOT, WIDTH), 0)
    column = iota((WINDOWS * SLOT, WIDTH), 1)
    place = slot & (SLOT - 1)
    wanted = (slot >> 3) * WIN + place + SHIFT
    wanted = jnp.where(wanted >= WIDTH, wanted - WIDTH, wanted)
    return one_hot((wanted == column) & (place < WIN))


def places_column():
    slot = iota((WIDTH, WINDOWS * SLOT), 1)
    column = iota((WIDTH, WINDOWS * SLOT), 0)
    place = slot & (SLOT - 1)
    wanted = (slot >> 3) * WIN + place + SHIFT
    wanted = jnp.where(wanted >= WIDTH, wanted - WIDTH, wanted)
    return one_hot((wanted == column) & (place < WIN))


def fold_matrix():
    return one_hot((iota((PLACES, LANES), 1) >> 3) == iota((PLACES, LANES), 0))


def head_mask():
    shape = (GROUP, FEAT)
    return jnp.where(iota(shape, 0) == (iota(shape, 1) >> 5), 1.0, 0.0).astype(F32)


def spread(values, mask):
    rows = [jnp.broadcast_to(values[i : i + 1], (GROUP, FEAT)) * mask for i in range(PLACES)]
    rows.append(jnp.zeros((LANES - PLACES * GROUP, FEAT), F32))
    return jnp.concatenate(rows, 0).astype(BF)


def own_heads(values, mask):
    return (values.reshape(LANES // GROUP, GROUP, FEAT) * mask[None]).reshape(LANES, FEAT)


def table_pick(row_axis, backwards):
    shape = (TAB_USED, LANES) if row_axis == 0 else (LANES, TAB_USED)
    lane = iota(shape, row_axis)
    pair = iota(shape, 1 - row_axis)
    place = pair >> 3
    row, column = place >> 3, place & (SLOT - 1)
    entry = row * (2 * WIN - 1) + column
    if backwards:
        entry = (WIN - 1) * 2 * WIN - entry
    match = ((lane >> 3) == entry) & ((lane & 7) == (pair & 7))
    return one_hot(match & (column < WIN) & (row < WIN))


def norm_stats(values):
    average = jnp.mean(values, -1, keepdims=True)
    centered = values - average
    variance = jnp.mean(centered * centered, -1, keepdims=True)
    scale = lax.rsqrt(variance + EPS)
    return centered * scale, scale


def norm_back(grad, normed, scale, gain):
    scaled = grad * gain
    first = jnp.mean(scaled, -1, keepdims=True)
    second = jnp.mean(scaled * normed, -1, keepdims=True)
    return scale * (scaled - first - normed * second)


def whole(memory=pltpu.VMEM):
    return pl.BlockSpec(memory_space=memory)


def kernel_call(
    body, outs, ins, scratch=(), flops=0, smem=0, apart=0, grid=None, in_blocks=None, out_blocks=None
):
    size = sum(a.size * a.dtype.itemsize for a in list(ins) + list(outs))
    in_specs = [whole(pltpu.SMEM)] * smem
    in_specs += in_blocks or [whole()] * (len(ins) - smem - apart) + [whole(pl.ANY)] * apart
    options = {"grid": grid} if grid else {}
    return pl.pallas_call(
        body,
        out_shape=tuple(outs),
        in_specs=in_specs,
        out_specs=tuple(out_blocks or [whole()] * len(outs)),
        scratch_shapes=list(scratch),
        cost_estimate=pl.CostEstimate(flops=flops, bytes_accessed=size, transcendentals=0),
        compiler_params=pltpu.CompilerParams(vmem_limit_bytes=VMEM_LIMIT),
        **options,
    )(*ins)


def like(shape, dtype):
    return jax.ShapeDtypeStruct(shape, dtype)


def place(vector, lanes, me):
    w = vector.shape[1]
    pick = one_hot(iota((w, lanes), 1) == iota((w, lanes), 0) + me * w)
    wide = jnp.broadcast_to(vector, (8, w))
    return dot(wide.astype(BF), pick)[0:1]


def mine(row, w, me):
    lanes = row.shape[1]
    pick = one_hot(iota((lanes, w), 0) == iota((lanes, w), 1) + me * w)
    wide = jnp.broadcast_to(row, (8, lanes))
    return dot(wide.astype(BF), pick)[0:1]


def padded(rows, height):
    total = sum(r.shape[0] for r in rows)
    return jnp.concatenate(rows + [jnp.zeros((height - total, D), F32)], 0).astype(BF)


def pack_attn_body(me_ref, g1, b1, wqkv, bqv, table, attn):
    depth = wqkv.shape[0]
    me = me_ref[0]
    for c in range(3):
        attn[c * depth : (c + 1) * depth, :] = wqkv[:, c * D : (c + 1) * D]
    rows = [place(v, D, me) for v in (g1[...], b1[...], bqv[0:1, :], bqv[1:2, :])]
    held, entries = table.shape
    lane = iota((entries, TAB), 1)
    spot = iota((entries, TAB), 0) * GROUP + TAB - (WIN - 1) * 2 * WIN * GROUP
    spot = jnp.where(spot >= TAB, spot - TAB, spot)
    values = table[...].astype(F32).T
    groups = [jnp.zeros((1, TAB), F32) for _ in range(GROUPS)]
    for h in range(held):
        head = me * held + h
        inside = lane == spot + (head & (GROUP - 1))
        row = jnp.sum(jnp.where(inside, values[:, h : h + 1], 0.0), 0, keepdims=True)
        for g in range(GROUPS):
            groups[g] = groups[g] + jnp.where((head >> 3) == g, row, 0.0)
    for g in range(GROUPS):
        rows += [groups[g][:, c * D : (c + 1) * D] for c in range(TAB // D)]
    attn[3 * depth :, :] = padded(rows, SMALL)


def pack_mlp_body(me_ref, wproj, bproj, g2, b2, win, bin_, wout, bout, mlp):
    depth = win.shape[0]
    me = me_ref[0]
    for c in range(FF // D):
        mlp[c * depth : (c + 1) * depth, :] = win[:, c * D : (c + 1) * D]
    mlp[4 * depth : 8 * depth, :] = wout[...]
    mlp[8 * depth : 9 * depth, :] = wproj[...]
    hidden_bias = place(bin_[...], FF, me)
    rows = [place(v, D, me) for v in (g2[...], b2[...], bout[...], bproj[...])]
    rows += [hidden_bias[:, c * D : (c + 1) * D] for c in range(FF // D)]
    mlp[9 * depth :, :] = padded(rows, SMALL)


def join_halves(late, half, back, both):
    rows = half.shape[0]
    both[pl.ds(pl.multiple_of(late * rows, 16), rows), :] = half[...]
    both[pl.ds(pl.multiple_of((1 - late) * rows, 16), rows), :] = back[...]


def unpack_attn_body(me_ref, half, back, g1, b1, wqkv, bqv, table, attn):
    depth = wqkv.shape[0]
    me = me_ref[0]
    join_halves(me_ref[1], half, back, attn)
    for c in range(3):
        wqkv[:, c * D : (c + 1) * D] = attn[c * depth : (c + 1) * depth, :].astype(F32)
    small = attn[3 * depth :, :].astype(F32)
    g1[...] = mine(small[0:1], depth, me)
    b1[...] = mine(small[1:2], depth, me)
    bqv[0:1, :] = mine(small[2:3], depth, me)
    bqv[1:2, :] = mine(small[3:4], depth, me)
    held, entries = table.shape
    lane = iota((entries, TAB), 1)
    spot = (entries - 1 - iota((entries, TAB), 0)) * GROUP
    parts = TAB // D
    rows = [
        jnp.concatenate([small[4 + g * parts + c : 5 + g * parts + c] for c in range(parts)], 1)
        for g in range(GROUPS)
    ]
    which = iota((entries, held), 1)
    total = jnp.zeros((entries, held), F32)
    for h in range(held):
        head = me * held + h
        row = rows[0]
        for g in range(1, GROUPS):
            row = jnp.where((head >> 3) == g, rows[g], row)
        inside = lane == spot + (head & (GROUP - 1))
        column = jnp.sum(jnp.where(inside, row, 0.0), 1, keepdims=True)
        total = jnp.where(which == h, column, total)
    table[...] = total.T


def unpack_mlp_body(
    me_ref, half_a, back_a, half_b, back_b, wproj, bproj, g2, b2, win, bin_, wout, bout, a, b
):
    depth = win.shape[0]
    me = me_ref[0]
    join_halves(me_ref[1], half_a, back_a, a)
    join_halves(me_ref[1], half_b, back_b, b)
    for c in range(FF // D):
        win[:, c * D : (c + 1) * D] = a[c * depth : (c + 1) * depth, :].astype(F32)
    wout[...] = b[: 4 * depth, :].astype(F32)
    wproj[...] = b[4 * depth :, :].astype(F32)
    small = a[4 * depth :, :].astype(F32)
    g2[...] = mine(small[0:1], depth, me)
    b2[...] = mine(small[1:2], depth, me)
    bout[...] = mine(small[2:3], depth, me)
    bproj[...] = mine(small[3:4], depth, me)
    hidden = jnp.concatenate([small[4 + c : 5 + c] for c in range(FF // D)], 1)
    bin_[...] = mine(hidden, depth * FF // D, me)


def put_shares(me, same, other, start, values, first=0):
    core, chip = me & 1, me >> 1
    rows = values.shape[1]
    for c in range(values.shape[0] // 2):
        one, two = values[2 * c], values[2 * c + 1]
        q = (first // 2 + c) ^ chip
        same[q, start : start + rows, :] = jnp.where(core == 0, one, two).astype(BF)
        other[q, start : start + rows, :] = jnp.where(core == 0, two, one).astype(BF)


def put_smalls(same, other, start, rows):
    block = padded(rows, SMALL)
    for q in range(same.shape[0]):
        same[q, start:, :] = block
        other[q, start:, :] = block


def exchange(value, axis, mask):
    peers = lax.axis_size(axis)
    return lax.ppermute(value, axis, [(i, i ^ mask) for i in range(peers)])


def gather_pieces(slab):
    chips = lax.axis_size("shard") // 2
    pieces = [None] * (2 * chips)
    for q in range(chips):
        pieces[2 * q] = exchange(slab, "shard", 2 * q) if q else slab
    for q in range(chips):
        pieces[2 * q + 1] = exchange(pieces[2 * q], "shard", 1)
    return pieces


def add_pair(here, came):
    return (here.astype(F32) + came.astype(F32)).astype(BF)


def add_cores(same, other):
    came = exchange(other, "shard", 1)
    return [add_pair(same[q], came[q]) for q in range(same.shape[0])]


def add_chips(late, sums):
    parts = [sums[0]] + [exchange(sums[q], "shard", 2 * q) for q in range(1, len(sums))]
    half = sums[0].shape[0] // 2
    out = []
    for start in (late * half, (1 - late) * half):
        total = 0.0
        for part in parts:
            total += lax.dynamic_slice_in_dim(part, start, half, 0).astype(F32)
        out.append(total.astype(BF))
    return out


def seq_near(keep, send):
    return add_pair(keep, exchange(send, "seq", 1))


def seq_far(half):
    reach = 2
    while reach < lax.axis_size("seq"):
        half = add_pair(half, exchange(half, "seq", reach))
        reach *= 2
    return half


def tie(first, second):
    first, second = list(first), list(second)
    out = lax.optimization_barrier((*first, *second))
    return list(out[: len(first)]), list(out[len(first) :])


def block_of(slab, c, depth):
    return slab[:, c * depth : (c + 1) * depth, :].reshape(D, D)


def smalls_of(slab, start):
    return jnp.sum(slab[:, start:, :].astype(F32), 0)


def project_body(me_ref, tokens, halo, *refs):
    shards = len(refs) - 7
    pieces = refs[:shards]
    normed_win, query, key, value, slab, wide, sems = refs[shards:]
    copies = [
        pltpu.make_async_copy(piece, slab.at[me_ref[0] ^ p], sems.at[p])
        for p, piece in enumerate(pieces)
    ]
    for copy in copies:
        copy.start()
    columns = column_places()
    own = WIN - SHIFT
    for copy in copies:
        copy.wait()
    depth = (slab.shape[1] - SMALL) // 3
    small = smalls_of(slab, 3 * depth)
    gain, offset, bias_q, bias_v = (small[r : r + 1] for r in range(4))
    for r in range(WIN):
        x = (tokens[SHIFT + r] if r < own else halo[r - own]).astype(F32)
        normed, _ = norm_stats(x)
        low = (normed * gain + offset).astype(BF)
        wide[:, r] = dot(columns, low).reshape(WINDOWS, SLOT, D)
    normed_win[...] = wide[...].reshape(PADDED, D).astype(BF)
    query[...] = (dot(normed_win[...], block_of(slab, 0, depth)) + bias_q).astype(BF)
    key[...] = dot(normed_win[...], block_of(slab, 1, depth)).astype(BF)
    value[...] = (dot(normed_win[...], block_of(slab, 2, depth)) + bias_v).astype(BF)


def attn_forward_body(
    slab, reg_rows, reg_lanes, query, key, value, probs, restored, wide, fold, bias
):
    n = pl.program_id(0)

    @pl.when(n == 0)
    def _():
        depth = (slab.shape[1] - SMALL) // 3
        small = smalls_of(slab, 3 * depth)
        fold[...] = fold_matrix()
        pick = table_pick(0, False)
        parts = TAB // D
        empty = (iota((PLACES, LANES), 0) & (SLOT - 1)) == WIN
        for g in range(GROUPS):
            first = 4 + g * parts
            row = jnp.concatenate([small[first + c : first + c + 1] for c in range(parts)], 1)
            row = jnp.broadcast_to(row, (SLOT, TAB))
            row = pltpu.roll(row, 0, 1, stride=GROUP, stride_axis=0)
            turned = [
                pltpu.roll(row, (2 * WIN - 1) * GROUP * r, 1)[:, :TAB_USED] for r in range(WIN)
            ]
            picked = dot(jnp.concatenate(turned, 0).astype(BF), pick)
            bias[g] = jnp.where(empty, -1e30, picked)

    mask = head_mask()
    for g in range(GROUPS):
        feats = slice(g * FEAT, (g + 1) * FEAT)
        q2 = query[:, feats].astype(F32)
        k2 = key[:, feats].astype(F32)
        v2 = value[:, feats].astype(F32)
        held = []
        for s in range(2):
            part = slice(s * PLACES, (s + 1) * PLACES)
            k, v = k2[part].astype(BF), v2[part].astype(BF)
            q_big = spread(q2[part], mask)
            penalty = jnp.where(reg_rows[s][:, 0:1] != reg_lanes[s], -100.0, 0.0)
            logits = dot_nt(k, q_big) * SCALE + bias[g] + penalty
            top = jnp.max(logits, 0, keepdims=True)
            powers = jnp.exp(logits - top)
            p = powers * (1.0 / jnp.sum(powers, 0, keepdims=True))
            held.append(p)
            o_big = own_heads(dot_tn(p.astype(BF), v), mask).astype(BF)
            o = dot(fold[...], o_big)
            wide[2 * n + s, :, :, feats] = o.reshape(WIN, SLOT, FEAT)
        probs[0, g] = jnp.concatenate(held, 0).astype(BF)

    @pl.when(n == pl.num_programs(0) - 1)
    def _():
        back = places_column()
        for r in range(WIN):
            here = wide[:, r].reshape(WINDOWS * SLOT, D).astype(BF)
            restored[r * WIDTH : (r + 1) * WIDTH, :] = dot(back, here).astype(BF)


def gelu_parts(h):
    size = jnp.abs(h) * (0.5**0.5)
    t = 1.0 / (1.0 + 0.3275911 * size)
    bell = jnp.exp(-0.5 * h * h)
    poly = t * (
        0.254829592
        + t * (-0.284496736 + t * (1.421413741 + t * (-1.453152027 + t * 1.061405429)))
    )
    tail = 0.5 * poly * bell
    upto = jnp.where(h >= 0, 1.0 - tail, tail)
    return upto, bell * 0.3989422804014327


def mlp_body(
    me_ref,
    tokens,
    token_halo,
    cotangent,
    cot_halo,
    slab,
    restored,
    kept,
    sent,
    grad_mixed,
    grad_win,
    same_a,
    other_a,
    same_b,
    other_b,
    normed_low,
    cot,
    mixed,
    out_sum,
    back_sum,
    wide,
):
    me = me_ref[0]
    shards, height = slab.shape[:2]
    depth = (height - SMALL) // 9
    span = shards * D // FF
    small = smalls_of(slab, 9 * depth)
    gain, offset, bias_o, bias_proj = (small[r : r + 1] for r in range(4))
    own = WIN - SHIFT
    branch = dot(restored[...], block_of(slab, 8, depth)) + bias_proj
    for r in range(WIN):
        part = slice(r * WIDTH, (r + 1) * WIDTH)
        cot[part, :] = cotangent[SHIFT + r] if r < own else cot_halo[r - own]
        x = (tokens[SHIFT + r] if r < own else token_halo[r - own]).astype(F32)
        mixed[part, :] = x + branch[part]
    normed, _ = norm_stats(mixed[...])
    normed_low[...] = (normed * gain + offset).astype(BF)
    vectors = []
    for c in range(FF // D):
        w_in = block_of(slab, c, depth)
        w_out = slab[c * span : (c + 1) * span, 4 * depth : 8 * depth, :].reshape(D, D)
        hidden = dot(normed_low[...], w_in) + small[4 + c : 5 + c]
        upto, density = gelu_parts(hidden)
        active = (hidden * upto).astype(BF)
        slope = upto + hidden * density
        grad = (dot_nt(cot[...], w_out) * slope).astype(BF)
        forward = dot(active, w_out)
        backward = dot_nt(grad, w_in)
        if c == 0:
            out_sum[...] = forward
            back_sum[...] = backward
        else:
            out_sum[...] += forward
            back_sum[...] += backward
        vectors.append(jnp.sum(grad.astype(F32), 0, keepdims=True))
        put_shares(
            me, same_a, other_a, c * depth, dot_tn(normed_low[...], grad).reshape(shards, depth, D)
        )
        put_shares(
            me,
            same_b,
            other_b,
            0,
            dot_tn(active, cot[...]).reshape(span, 4 * depth, D),
            c * span,
        )
    result = mixed[...] + out_sum[...] + bias_o
    kept[...] = result[: own * WIDTH]
    sent[...] = result[own * WIDTH :].astype(BF)
    normed, scale = norm_stats(mixed[...])
    g = back_sum[...]
    gain_sum = jnp.sum(g * normed, 0, keepdims=True)
    offset_sum = jnp.sum(g, 0, keepdims=True)
    cot_sum = jnp.sum(cot[...].astype(F32), 0, keepdims=True)
    grad_mixed[...] = cot[...].astype(F32) + norm_back(g, normed, scale, gain)

    branch = grad_mixed[...].astype(BF)
    branch_sum = jnp.sum(branch.astype(F32), 0, keepdims=True)
    proj = dot_tn(restored[...], branch).reshape(shards, depth, D)
    put_shares(me, same_b, other_b, 4 * depth, proj)
    put_smalls(same_a, other_a, 4 * depth, [gain_sum, offset_sum, cot_sum, branch_sum] + vectors)
    grad_att = dot_nt(branch, block_of(slab, 8, depth)).astype(BF)
    columns = column_places()
    for r in range(WIN):
        wide[:, r] = dot(columns, grad_att[r * WIDTH : (r + 1) * WIDTH]).reshape(WINDOWS, SLOT, D)
    grad_win[...] = wide[...].reshape(PADDED, D).astype(BF)


def attn_backward_body(query, key, value, probs, grad_win, came, out, pairs, fold):
    @pl.when(pl.program_id(0) == 0)
    def _():
        fold[...] = fold_matrix()
        pairs[...] = came[...]

    mask = head_mask()
    for g in range(GROUPS):
        feats = slice(g * FEAT, (g + 1) * FEAT)
        q2 = query[:, feats].astype(F32)
        k2 = key[:, feats].astype(F32)
        v2 = value[:, feats].astype(F32)
        go2 = grad_win[:, feats].astype(F32)
        p2 = probs[0, g].astype(F32)
        held = []
        for s in range(2):
            part = slice(s * PLACES, (s + 1) * PLACES)
            k, v, p_low = (a[part].astype(BF) for a in (k2, v2, p2))
            p = p2[part]
            go_big = spread(go2[part], mask)
            q_big = spread(q2[part], mask)
            dp = dot_nt(v, go_big)
            dv = dot(p_low, go_big)
            inner = jnp.sum(p * dp, 0, keepdims=True)
            ds = (p * (dp - inner)).astype(BF)
            pairs[g] += ds.astype(F32)
            dk = dot(ds, q_big) * SCALE
            dq_big = own_heads(dot_tn(ds, k), mask * SCALE).astype(BF)
            dq = dot(fold[...], dq_big)
            held.append((dq, dk, dv))
        for c in range(3):
            both = jnp.concatenate([held[0][c], held[1][c]], 0).astype(BF)
            out[:, c * D + g * FEAT : c * D + (g + 1) * FEAT] = both


def attn_last_body(
    me_ref,
    grad_mixed,
    tokens,
    halo,
    slab,
    normed_win,
    pairs,
    *refs,
):
    grads = refs[:-5]
    kept, sent, same, other, wide = refs[-5:]
    me = me_ref[0]
    shards = slab.shape[0]
    depth = (slab.shape[1] - SMALL) // 3
    small = smalls_of(slab, 3 * depth)
    gain = small[0:1]
    own = WIN - SHIFT
    vectors = []
    for c in range(3):
        cols = slice(c * D, (c + 1) * D)
        g = jnp.concatenate([part[:, cols] for part in grads], 0)
        if c != 1:
            vectors.append(jnp.sum(g.astype(F32), 0, keepdims=True))
        put_shares(
            me, same, other, c * depth, dot_tn(normed_win[...], g).reshape(shards, depth, D)
        )
        part = dot_nt(g, block_of(slab, c, depth))
        total = part if c == 0 else total + part
    wide[...] = total.reshape(WINDOWS, WIN, SLOT, D)
    back = places_column()
    gain_sum = jnp.zeros((1, D), F32)
    bias_sum = jnp.zeros((1, D), F32)
    for r in range(WIN):
        here = wide[:, r].reshape(WINDOWS * SLOT, D).astype(BF)
        g = dot(back, here)
        x = (tokens[SHIFT + r] if r < own else halo[r - own]).astype(F32)
        normed, scale = norm_stats(x)
        gain_sum += jnp.sum(g * normed, 0, keepdims=True)
        bias_sum += jnp.sum(g, 0, keepdims=True)
        grad = grad_mixed[r * WIDTH : (r + 1) * WIDTH, :] + norm_back(g, normed, scale, gain)
        if r < own:
            kept[r * WIDTH : (r + 1) * WIDTH, :] = grad
        else:
            sent[(r - own) * WIDTH : (r - own + 1) * WIDTH, :] = grad.astype(BF)

    pick = table_pick(1, True)
    rows = [gain_sum, bias_sum, vectors[0], vectors[1]]
    for g in range(GROUPS):
        high = pairs[g].astype(BF)
        low = (pairs[g] - high.astype(F32)).astype(BF)
        laid = dot(high, pick) + dot(low, pick)
        laid = jnp.concatenate([laid, jnp.zeros((PLACES, TAB - TAB_USED), F32)], 1)
        total = jnp.zeros((SLOT, TAB), F32)
        for r in range(WIN):
            total += pltpu.roll(
                laid[r * SLOT : (r + 1) * SLOT], (2 * WIN - 1) * GROUP * r, 1
            )
        total = pltpu.roll(total, 0, 1, stride=GROUP, stride_axis=0)
        row = jnp.sum(total, 0, keepdims=True)
        rows += [row[:, c * D : (c + 1) * D] for c in range(TAB // D)]
    put_smalls(same, other, 3 * depth, rows)


def region_views(regions, rows, place):
    here = lax.dynamic_slice_in_dim(regions[0], place * rows, rows, 0)
    windows = here.reshape(WIN, WINDOWS, WIN).transpose(1, 0, 2)
    windows = jnp.pad(windows, ((0, 0), (0, 0), (0, SLOT - WIN))).astype(F32)
    windows = windows.reshape(WINDOWS, PLACES)
    by_row = jnp.broadcast_to(windows[:, :, None], (WINDOWS, PLACES, 128))
    by_lane = jnp.pad(jnp.repeat(windows, GROUP, 1), ((0, 0), (0, LANES - PLACES * GROUP)))
    return by_row, by_lane[:, None, :]


def per_device(
    tokens,
    regions,
    cotangent,
    gain_one,
    bias_one,
    w_qkv,
    bias_qv,
    table,
    w_proj,
    bias_proj,
    gain_two,
    bias_two,
    w_in,
    bias_in,
    w_out,
    bias_out,
):
    images, local_rows, columns, _ = tokens.shape
    assert images == 1 and local_rows == WIN and columns == WIDTH
    shards = lax.axis_size("shard")
    me = lax.axis_index("shard").astype(jnp.int32)
    seq = lax.axis_index("seq").astype(jnp.int32)
    where = jnp.stack([me, seq & 1])
    chips = shards // 2
    depth = D // shards
    own = WIN - SHIFT
    attn_params = (gain_one[None], bias_one[None], w_qkv, bias_qv, table.T)
    mlp_params = (
        w_proj,
        bias_proj[None],
        gain_two[None],
        bias_two[None],
        w_in,
        bias_in[None],
        w_out,
        bias_out[None],
    )
    late = seq & 1
    (attn_slab,) = kernel_call(
        pack_attn_body, [like((3 * depth + SMALL, D), BF)], (where,) + attn_params, smem=1
    )
    (attn_slab,), mlp_params = tie([attn_slab], mlp_params)
    pieces = gather_pieces(attn_slab)
    (mlp_slab,) = kernel_call(
        pack_mlp_body, [like((9 * depth + SMALL, D), BF)], (where, *mlp_params), smem=1
    )
    mlp_all = lax.all_gather(mlp_slab, "shard")
    tokens_here = tokens[0]
    token_halo = shifted_2(tokens_here[:SHIFT], "seq", -1)
    cot_here = cotangent[0]
    cot_halo = shifted_2(cot_here[:SHIFT], "seq", -1)
    by_row, by_lane = region_views(regions, local_rows, seq)

    normed_win, query, key, value, attn_all = kernel_call(
        project_body,
        [like((PADDED, D), BF)] * 4 + [like((shards, *attn_slab.shape), BF)],
        (where, tokens_here, token_halo, *pieces),
        scratch=[
            pltpu.VMEM((WINDOWS, WIN, SLOT, D), F32),
            pltpu.SemaphoreType.DMA((shards,)),
        ],
        flops=1_500_000_000,
        smem=1,
        apart=shards,
    )
    pair_rows = 2 * PLACES
    steps = WINDOWS // 2

    def rows_from(first, width=D):
        return pl.BlockSpec((pair_rows, width), lambda i: (first + i, 0))

    def probs_from(first):
        return pl.BlockSpec((1, GROUPS, pair_rows, LANES), lambda i: (first + i, 0, 0, 0))

    def fixed(shape):
        return pl.BlockSpec(shape, lambda i: (0,) * len(shape))

    probs, restored = kernel_call(
        attn_forward_body,
        [like((steps, GROUPS, pair_rows, LANES), BF), like((TOKENS, D), BF)],
        (attn_all, by_row, by_lane, query, key, value),
        grid=(steps,),
        in_blocks=[
            fixed(attn_all.shape),
            pl.BlockSpec((2, *by_row.shape[1:]), lambda i: (i, 0, 0)),
            pl.BlockSpec((2, *by_lane.shape[1:]), lambda i: (i, 0, 0)),
            rows_from(0),
            rows_from(0),
            rows_from(0),
        ],
        out_blocks=[probs_from(0), fixed((TOKENS, D))],
        scratch=[
            pltpu.VMEM((WINDOWS, WIN, SLOT, D), F32),
            pltpu.VMEM((PLACES, LANES), BF),
            pltpu.VMEM((GROUPS, PLACES, LANES), F32),
        ],
        flops=5_000_000_000,
    )
    share_a = like((chips, 4 * depth + SMALL, D), BF)
    share_b = like((chips, 5 * depth, D), BF)
    out_kept, out_sent, grad_mixed, grad_win, same_a, other_a, same_b, other_b = kernel_call(
        mlp_body,
        [
            like((own * WIDTH, D), F32),
            like((SHIFT * WIDTH, D), BF),
            like((TOKENS, D), F32),
            like((PADDED, D), BF),
            share_a,
            share_a,
            share_b,
            share_b,
        ],
        (where, tokens_here, token_halo, cot_here, cot_halo, mlp_all, restored),
        scratch=[
            pltpu.VMEM((TOKENS, D), BF),
            pltpu.VMEM((TOKENS, D), BF),
            pltpu.VMEM((TOKENS, D), F32),
            pltpu.VMEM((TOKENS, D), F32),
            pltpu.VMEM((TOKENS, D), F32),
            pltpu.VMEM((WINDOWS, WIN, SLOT, D), F32),
        ],
        flops=10_000_000_000,
        smem=1,
    )

    def backward(first, count, grad_win, came):
        return kernel_call(
            attn_backward_body,
            [like((count * pair_rows, 3 * D), BF), like((GROUPS, PLACES, LANES), F32)],
            (query, key, value, probs, grad_win, came),
            grid=(count,),
            in_blocks=[rows_from(first)] * 3
            + [probs_from(first), rows_from(first), fixed((GROUPS, PLACES, LANES))],
            out_blocks=[rows_from(0, 3 * D), fixed((GROUPS, PLACES, LANES))],
            scratch=[pltpu.VMEM((PLACES, LANES), BF)],
            flops=2_500_000_000,
        )

    none = jnp.zeros((GROUPS, PLACES, LANES), F32)
    count = steps // 4
    grads = []
    part, pairs = backward(0, count, grad_win, none)
    grads.append(part)
    sums_a, sums_b = add_cores(same_a, other_a), add_cores(same_b, other_b)
    sums, (pairs,) = tie(sums_a + sums_b, [pairs])
    sums_a, sums_b = sums[:chips], sums[chips:]
    part, pairs = backward(count, count, grad_win, pairs)
    grads.append(part)
    sums_b, (pairs,) = tie(sums_b, [pairs])
    part, pairs = backward(2 * count, count, grad_win, pairs)
    grads.append(part)
    halves_a, (pairs,) = tie(add_chips(late, sums_a), [pairs])
    part, pairs = backward(3 * count, count, grad_win, pairs)
    grads.append(part)
    (near_a,), (pairs,) = tie([seq_near(*halves_a)], [pairs])
    out_halo = shifted_2(out_sent, "seq", 1)
    tok_kept, tok_sent, attn_same, attn_other = kernel_call(
        attn_last_body,
        [
            like((own * WIDTH, D), F32),
            like((SHIFT * WIDTH, D), BF),
            like((chips, 3 * depth + SMALL, D), BF),
            like((chips, 3 * depth + SMALL, D), BF),
        ],
        (where, grad_mixed, tokens_here, token_halo, attn_all, normed_win, pairs, *grads),
        scratch=[pltpu.VMEM((WINDOWS, WIN, SLOT, D), F32)],
        flops=5_000_000_000,
        smem=1,
    )
    half_a = seq_far(near_a)
    back_a = exchange(half_a, "seq", 1)
    half_b = seq_far(seq_near(*add_chips(late, sums_b)))
    back_b = exchange(half_b, "seq", 1)
    half = seq_far(seq_near(*add_chips(late, add_cores(attn_same, attn_other))))
    back = exchange(half, "seq", 1)
    tok_halo = shifted_2(tok_sent, "seq", 1)
    mlp_grads = kernel_call(
        unpack_mlp_body,
        [like(p.shape, F32) for p in mlp_params],
        (where, half_a, back_a, half_b, back_b),
        scratch=[
            pltpu.VMEM((4 * depth + SMALL, D), BF),
            pltpu.VMEM((5 * depth, D), BF),
        ],
        smem=1,
    )
    attn_grads = kernel_call(
        unpack_attn_body,
        [like(p.shape, F32) for p in attn_params],
        (where, half, back),
        scratch=[pltpu.VMEM((3 * depth + SMALL, D), BF)],
        smem=1,
    )
    summed = [*attn_grads[:4], attn_grads[4].T, *mlp_grads]

    def joined(halo, kept):
        return jnp.concatenate([halo.astype(F32), kept], 0).reshape(tokens.shape)

    targets = (
        gain_one,
        bias_one,
        w_qkv,
        bias_qv,
        table,
        w_proj,
        bias_proj,
        gain_two,
        bias_two,
        w_in,
        bias_in,
        w_out,
        bias_out,
    )
    grads = [g.reshape(p.shape) for g, p in zip(summed, targets)]
    return (joined(out_halo, out_kept), joined(tok_halo, tok_kept), *grads)


def solution(mesh):
    return jax.shard_map(
        per_device,
        mesh=mesh,
        in_specs=(
            P("shard", "seq", None, None),
            P("shard", None, None),
            P("shard", "seq", None, None),
            P("shard"),
            P("shard"),
            P("shard", None),
            P(None, "shard"),
            P(None, "shard"),
            P("shard", None),
            P("shard"),
            P("shard"),
            P("shard"),
            P("shard", None),
            P("shard"),
            P("shard", None),
            P("shard"),
        ),
        out_specs=(
            P("shard", "seq", None, None),
            P("shard", "seq", None, None),
            P("shard"),
            P("shard"),
            P("shard", None),
            P(None, "shard"),
            P(None, "shard"),
            P("shard", None),
            P("shard"),
            P("shard"),
            P("shard"),
            P("shard", None),
            P("shard"),
            P("shard", None),
            P("shard"),
        ),
        check_vma=False,
    )
```

```python
import jax
import jax.numpy as jnp
from jax import lax
from jax.experimental import pallas as pl
from jax.experimental.pallas import tpu as pltpu
from jax.sharding import PartitionSpec as P

D = 512
HEADS = 16
HEAD = 32
WIN = 7
SHIFT = 3
FF = 2048
WIDTH = 112
WINDOWS = WIDTH // WIN
SLOT = 8
PLACES = WIN * SLOT
GROUP = 8
GROUPS = HEADS // GROUP
QUAD = 4
QUADS = HEADS // QUAD
FEAT = QUAD * HEAD
LANES = QUAD * PLACES
TOKENS = WIN * WIDTH
PADDED = WINDOWS * PLACES
TAB = 1536
TAB_USED = 768
SMALL = 32
EPS = 1e-05
SCALE = HEAD**-0.5
BF = jnp.bfloat16
F32 = jnp.float32
VMEM_LIMIT = 60 * 1024 * 1024


def shifted_2(value, axis, by):
    peers = lax.axis_size(axis)
    return lax.ppermute(value, axis, [(i, (i + by) % peers) for i in range(peers)])


def dot(left, right, dims=((1,), (0,))):
    return lax.dot_general(left, right, (dims, ((), ())), preferred_element_type=F32)


def dot_nt(left, right):
    return dot(left, right, ((1,), (1,)))


def dot_tn(left, right):
    return dot(left, right, ((0,), (0,)))


def iota(shape, axis):
    return lax.broadcasted_iota(jnp.int32, shape, axis)


def one_hot(condition):
    return jnp.where(condition, 1.0, 0.0).astype(BF)


def column_places():
    slot = iota((WINDOWS * SLOT, WIDTH), 0)
    column = iota((WINDOWS * SLOT, WIDTH), 1)
    place = slot & (SLOT - 1)
    wanted = (slot >> 3) * WIN + place + SHIFT
    wanted = jnp.where(wanted >= WIDTH, wanted - WIDTH, wanted)
    return one_hot((wanted == column) & (place < WIN))


def places_column():
    slot = iota((WIDTH, WINDOWS * SLOT), 1)
    column = iota((WIDTH, WINDOWS * SLOT), 0)
    place = slot & (SLOT - 1)
    wanted = (slot >> 3) * WIN + place + SHIFT
    wanted = jnp.where(wanted >= WIDTH, wanted - WIDTH, wanted)
    return one_hot((wanted == column) & (place < WIN))


def head_masks():
    feature = iota((1, FEAT), 1) >> 5
    return [jnp.where(feature == h, 1.0, 0.0).astype(F32) for h in range(QUAD)]


def spread(values, masks):
    return jnp.concatenate([values * mask for mask in masks], 0).astype(BF)


def own_heads(values):
    feature = iota((PLACES, FEAT), 1) >> 5
    out = values[:PLACES]
    for h in range(1, QUAD):
        out = jnp.where(feature == h, values[h * PLACES : (h + 1) * PLACES], out)
    return out


def table_pick(row_axis, quad, backwards):
    shape = (TAB_USED, LANES) if row_axis == 0 else (LANES, TAB_USED)
    lane = iota(shape, row_axis)
    pair = iota(shape, 1 - row_axis)
    head = jnp.zeros(shape, jnp.int32)
    for h in range(1, QUAD):
        head += jnp.where(pair >= h * PLACES, 1, 0)
    place = pair - head * PLACES
    row, column = place >> 3, place & (SLOT - 1)
    entry = row * (2 * WIN - 1) + column
    if backwards:
        entry = (WIN - 1) * 2 * WIN - entry
    held = head + quad % (GROUP // QUAD) * QUAD
    match = ((lane >> 3) == entry) & ((lane & 7) == held)
    return one_hot(match & (column < WIN))


def norm_stats(values):
    average = jnp.mean(values, -1, keepdims=True)
    centered = values - average
    variance = jnp.mean(centered * centered, -1, keepdims=True)
    scale = lax.rsqrt(variance + EPS)
    return centered * scale, scale


def norm_back(grad, normed, scale, gain):
    scaled = grad * gain
    first = jnp.mean(scaled, -1, keepdims=True)
    second = jnp.mean(scaled * normed, -1, keepdims=True)
    return scale * (scaled - first - normed * second)


def whole(memory=pltpu.VMEM):
    return pl.BlockSpec(memory_space=memory)


def kernel_call(
    body, outs, ins, scratch=(), smem=0, apart=0, grid=None, in_blocks=None, out_blocks=None
):
    in_specs = [whole(pltpu.SMEM)] * smem
    in_specs += in_blocks or [whole()] * (len(ins) - smem - apart) + [whole(pl.ANY)] * apart
    options = {"grid": grid} if grid else {}
    return pl.pallas_call(
        body,
        out_shape=tuple(outs),
        in_specs=in_specs,
        out_specs=tuple(out_blocks or [whole()] * len(outs)),
        scratch_shapes=list(scratch),
        cost_estimate=pl.CostEstimate(flops=1024, bytes_accessed=1024, transcendentals=0),
        compiler_params=pltpu.CompilerParams(vmem_limit_bytes=VMEM_LIMIT),
        **options,
    )(*ins)


def like(shape, dtype):
    return jax.ShapeDtypeStruct(shape, dtype)


def place(vector, lanes, me):
    w = vector.shape[1]
    pick = one_hot(iota((w, lanes), 1) == iota((w, lanes), 0) + me * w)
    wide = jnp.broadcast_to(vector, (8, w))
    return dot(wide.astype(BF), pick)[0:1]


def mine(row, w, me):
    lanes = row.shape[1]
    pick = one_hot(iota((lanes, w), 0) == iota((lanes, w), 1) + me * w)
    wide = jnp.broadcast_to(row, (8, lanes))
    return dot(wide.astype(BF), pick)[0:1]


def padded(rows, height):
    total = sum(r.shape[0] for r in rows)
    return jnp.concatenate(rows + [jnp.zeros((height - total, D), F32)], 0).astype(BF)


def pack_body(
    me_ref, g1, b1, wqkv, bqv, table, wproj, bproj, g2, b2, win, bin_, wout, bout, attn, mlp
):
    depth = wqkv.shape[0]
    me = me_ref[0]
    for c in range(3):
        attn[c * depth : (c + 1) * depth, :] = wqkv[:, c * D : (c + 1) * D]
    rows = [place(v, D, me) for v in (g1[...], b1[...], bqv[0:1, :], bqv[1:2, :])]
    held, entries = table.shape
    lane = iota((entries, TAB), 1)
    spot = iota((entries, TAB), 0) * GROUP + TAB - (WIN - 1) * 2 * WIN * GROUP
    spot = jnp.where(spot >= TAB, spot - TAB, spot)
    values = table[...].astype(F32).T
    groups = [jnp.zeros((1, TAB), F32) for _ in range(GROUPS)]
    for h in range(held):
        head = me * held + h
        inside = lane == spot + (head & (GROUP - 1))
        row = jnp.sum(jnp.where(inside, values[:, h : h + 1], 0.0), 0, keepdims=True)
        for g in range(GROUPS):
            groups[g] = groups[g] + jnp.where((head >> 3) == g, row, 0.0)
    for g in range(GROUPS):
        rows += [groups[g][:, c * D : (c + 1) * D] for c in range(TAB // D)]
    attn[3 * depth :, :] = padded(rows, SMALL)
    for c in range(FF // D):
        mlp[c * depth : (c + 1) * depth, :] = win[:, c * D : (c + 1) * D]
    mlp[4 * depth : 8 * depth, :] = wout[...]
    mlp[8 * depth : 9 * depth, :] = wproj[...]
    hidden_bias = place(bin_[...], FF, me)
    rows = [place(v, D, me) for v in (g2[...], b2[...], bout[...], bproj[...])]
    rows += [hidden_bias[:, c * D : (c + 1) * D] for c in range(FF // D)]
    mlp[9 * depth :, :] = padded(rows, SMALL)


def join_halves(late, half, back, both):
    rows = half.shape[0]
    both[pl.ds(pl.multiple_of(late * rows, 16), rows), :] = half[...]
    both[pl.ds(pl.multiple_of((1 - late) * rows, 16), rows), :] = back[...]


def unpack_attn_body(me_ref, half, back, g1, b1, wqkv, bqv, table, attn):
    depth = wqkv.shape[0]
    me = me_ref[0]
    join_halves(me_ref[1], half, back, attn)
    for c in range(3):
        wqkv[:, c * D : (c + 1) * D] = attn[c * depth : (c + 1) * depth, :].astype(F32)
    small = attn[3 * depth :, :].astype(F32)
    g1[...] = mine(small[0:1], depth, me)
    b1[...] = mine(small[1:2], depth, me)
    bqv[0:1, :] = mine(small[2:3], depth, me)
    bqv[1:2, :] = mine(small[3:4], depth, me)
    held, entries = table.shape
    lane = iota((entries, TAB), 1)
    spot = (entries - 1 - iota((entries, TAB), 0)) * GROUP
    parts = TAB // D
    rows = [
        jnp.concatenate([small[4 + g * parts + c : 5 + g * parts + c] for c in range(parts)], 1)
        for g in range(GROUPS)
    ]
    which = iota((entries, held), 1)
    total = jnp.zeros((entries, held), F32)
    for h in range(held):
        head = me * held + h
        row = rows[0]
        for g in range(1, GROUPS):
            row = jnp.where((head >> 3) == g, rows[g], row)
        inside = lane == spot + (head & (GROUP - 1))
        column = jnp.sum(jnp.where(inside, row, 0.0), 1, keepdims=True)
        total = jnp.where(which == h, column, total)
    table[...] = total.T


def unpack_mlp_body(
    me_ref, half_a, back_a, half_b, back_b, wproj, bproj, g2, b2, win, bin_, wout, bout, a, b
):
    depth = win.shape[0]
    me = me_ref[0]
    join_halves(me_ref[1], half_a, back_a, a)
    join_halves(me_ref[1], half_b, back_b, b)
    for c in range(FF // D):
        win[:, c * D : (c + 1) * D] = a[c * depth : (c + 1) * depth, :].astype(F32)
    wout[...] = b[: 4 * depth, :].astype(F32)
    wproj[...] = b[4 * depth :, :].astype(F32)
    small = a[4 * depth :, :].astype(F32)
    g2[...] = mine(small[0:1], depth, me)
    b2[...] = mine(small[1:2], depth, me)
    bout[...] = mine(small[2:3], depth, me)
    bproj[...] = mine(small[3:4], depth, me)
    hidden = jnp.concatenate([small[4 + c : 5 + c] for c in range(FF // D)], 1)
    bin_[...] = mine(hidden, depth * FF // D, me)


def put_shares(me, same, other, start, values, first=0):
    core, chip = me & 1, me >> 1
    rows = values.shape[1]
    for c in range(values.shape[0] // 2):
        one, two = values[2 * c], values[2 * c + 1]
        q = (first // 2 + c) ^ chip
        same[q, start : start + rows, :] = jnp.where(core == 0, one, two).astype(BF)
        other[q, start : start + rows, :] = jnp.where(core == 0, two, one).astype(BF)


def put_smalls(same, other, start, rows):
    block = padded(rows, SMALL)
    for q in range(same.shape[0]):
        same[q, start:, :] = block
        other[q, start:, :] = block


def exchange(value, axis, mask):
    peers = lax.axis_size(axis)
    return lax.ppermute(value, axis, [(i, i ^ mask) for i in range(peers)])


def gather_pieces(slab):
    chips = lax.axis_size("shard") // 2
    pieces = [None] * (2 * chips)
    for q in range(chips):
        pieces[2 * q] = exchange(slab, "shard", 2 * q) if q else slab
    for q in range(chips):
        pieces[2 * q + 1] = exchange(pieces[2 * q], "shard", 1)
    return pieces


def add_pair(here, came):
    return (here.astype(F32) + came.astype(F32)).astype(BF)


def add_cores(same, other):
    came = exchange(other, "shard", 1)
    return [add_pair(same[q], came[q]) for q in range(same.shape[0])]


def to_chips(sums):
    return [sums[0]] + [exchange(sums[q], "shard", 2 * q) for q in range(1, len(sums))]


def add_chips(late, parts):
    half = parts[0].shape[0] // 2
    out = []
    for start in (late * half, (1 - late) * half):
        total = 0.0
        for part in parts:
            total += lax.dynamic_slice_in_dim(part, start, half, 0).astype(F32)
        out.append(total.astype(BF))
    return out


def seq_rest(half):
    reach = 4
    while reach < lax.axis_size("seq"):
        half = add_pair(half, exchange(half, "seq", reach))
        reach *= 2
    return half


def tie(first, second):
    first, second = list(first), list(second)
    out = lax.optimization_barrier((*first, *second))
    return list(out[: len(first)]), list(out[len(first) :])


def block_of(slab, c, depth):
    return slab[:, c * depth : (c + 1) * depth, :].reshape(D, D)


def smalls_of(slab, start):
    return jnp.sum(slab[:, start:, :].astype(F32), 0)


def project_body(me_ref, tokens, halo, *refs):
    shards = len(refs) - 7
    pieces = refs[:shards]
    normed_win, query, key, value, slab, wide, sems = refs[shards:]
    copies = [
        pltpu.make_async_copy(piece, slab.at[me_ref[0] ^ p], sems.at[p])
        for p, piece in enumerate(pieces)
    ]
    for copy in copies:
        copy.start()
    columns = column_places()
    own = WIN - SHIFT
    for copy in copies:
        copy.wait()
    depth = (slab.shape[1] - SMALL) // 3
    small = smalls_of(slab, 3 * depth)
    gain, offset, bias_q, bias_v = (small[r : r + 1] for r in range(4))
    for r in range(WIN):
        x = (tokens[SHIFT + r] if r < own else halo[r - own]).astype(F32)
        normed, _ = norm_stats(x)
        low = (normed * gain + offset).astype(BF)
        wide[:, r] = dot(columns, low).reshape(WINDOWS, SLOT, D)
    normed_win[...] = wide[...].reshape(PADDED, D).astype(BF)
    query[...] = (dot(normed_win[...], block_of(slab, 0, depth)) + bias_q).astype(BF)
    key[...] = dot(normed_win[...], block_of(slab, 1, depth)).astype(BF)
    value[...] = (dot(normed_win[...], block_of(slab, 2, depth)) + bias_v).astype(BF)


def attn_forward_body(slab, reg_rows, reg_lanes, query, key, value, probs, restored, wide, bias):
    n = pl.program_id(0)

    @pl.when(n == 0)
    def _():
        depth = (slab.shape[1] - SMALL) // 3
        small = smalls_of(slab, 3 * depth)
        parts = TAB // D
        empty = (iota((PLACES, LANES), 0) & (SLOT - 1)) == WIN
        turned = []
        for g in range(GROUPS):
            first = 4 + g * parts
            row = jnp.concatenate([small[first + c : first + c + 1] for c in range(parts)], 1)
            row = jnp.broadcast_to(row, (SLOT, TAB))
            row = pltpu.roll(row, 0, 1, stride=GROUP, stride_axis=0)
            rows = [pltpu.roll(row, (2 * WIN - 1) * GROUP * r, 1)[:, :TAB_USED] for r in range(WIN)]
            turned.append(jnp.concatenate(rows, 0).astype(BF))
        for half in range(GROUP // QUAD):
            pick = table_pick(0, half, False)
            for g in range(GROUPS):
                picked = dot(turned[g], pick)
                bias[g * (GROUP // QUAD) + half] = jnp.where(empty, -1e30, picked)

    masks = head_masks()
    penalty = [
        jnp.where(reg_rows[s][:, 0:1] != reg_lanes[s], -100.0, 0.0) for s in range(2)
    ]
    for u in range(QUADS):
        feats = slice(u * FEAT, (u + 1) * FEAT)
        q2 = query[:, feats].astype(F32)
        k2 = key[:, feats].astype(F32)
        v2 = value[:, feats].astype(F32)
        held = []
        for s in range(2):
            part = slice(s * PLACES, (s + 1) * PLACES)
            k, v = k2[part].astype(BF), v2[part].astype(BF)
            logits = dot_nt(k, spread(q2[part], masks)) * SCALE + bias[u] + penalty[s]
            top = jnp.max(logits, 0, keepdims=True)
            powers = jnp.exp(logits - top)
            p = powers * (1.0 / jnp.sum(powers, 0, keepdims=True))
            held.append(p)
            o = own_heads(dot_tn(p.astype(BF), v))
            wide[2 * n + s, :, :, feats] = o.reshape(WIN, SLOT, FEAT)
        probs[0, u] = jnp.concatenate(held, 0).astype(BF)

    @pl.when(n == pl.num_programs(0) - 1)
    def _():
        back = places_column()
        for r in range(WIN):
            here = wide[:, r].reshape(WINDOWS * SLOT, D).astype(BF)
            restored[r * WIDTH : (r + 1) * WIDTH, :] = dot(back, here).astype(BF)


def gelu_parts(h):
    size = jnp.abs(h) * (0.5**0.5)
    t = 1.0 / (1.0 + 0.3275911 * size)
    bell = jnp.exp(-0.5 * h * h)
    poly = t * (
        0.254829592
        + t * (-0.284496736 + t * (1.421413741 + t * (-1.453152027 + t * 1.061405429)))
    )
    tail = 0.5 * poly * bell
    upto = jnp.where(h >= 0, 1.0 - tail, tail)
    return upto, bell * 0.3989422804014327


def mlp_body(
    me_ref,
    tokens,
    token_halo,
    cotangent,
    cot_halo,
    slab,
    restored,
    kept,
    sent,
    grad_mixed,
    grad_win,
    same_a,
    other_a,
    same_b,
    other_b,
    normed_low,
    cot,
    mixed,
    out_sum,
    back_sum,
    wide,
):
    me = me_ref[0]
    shards, height = slab.shape[:2]
    depth = (height - SMALL) // 9
    span = shards * D // FF
    small = smalls_of(slab, 9 * depth)
    gain, offset, bias_o, bias_proj = (small[r : r + 1] for r in range(4))
    own = WIN - SHIFT
    branch = dot(restored[...], block_of(slab, 8, depth)) + bias_proj
    for r in range(WIN):
        part = slice(r * WIDTH, (r + 1) * WIDTH)
        cot[part, :] = cotangent[SHIFT + r] if r < own else cot_halo[r - own]
        x = (tokens[SHIFT + r] if r < own else token_halo[r - own]).astype(F32)
        mixed[part, :] = x + branch[part]
    normed, _ = norm_stats(mixed[...])
    normed_low[...] = (normed * gain + offset).astype(BF)
    vectors = []
    for c in range(FF // D):
        w_in = block_of(slab, c, depth)
        w_out = slab[c * span : (c + 1) * span, 4 * depth : 8 * depth, :].reshape(D, D)
        hidden = dot(normed_low[...], w_in) + small[4 + c : 5 + c]
        upto, density = gelu_parts(hidden)
        active = (hidden * upto).astype(BF)
        slope = upto + hidden * density
        grad = (dot_nt(cot[...], w_out) * slope).astype(BF)
        forward = dot(active, w_out)
        backward = dot_nt(grad, w_in)
        if c == 0:
            out_sum[...] = forward
            back_sum[...] = backward
        else:
            out_sum[...] += forward
            back_sum[...] += backward
        vectors.append(jnp.sum(grad.astype(F32), 0, keepdims=True))
        put_shares(
            me, same_a, other_a, c * depth, dot_tn(normed_low[...], grad).reshape(shards, depth, D)
        )
        put_shares(
            me,
            same_b,
            other_b,
            0,
            dot_tn(active, cot[...]).reshape(span, 4 * depth, D),
            c * span,
        )
    result = mixed[...] + out_sum[...] + bias_o
    kept[...] = result[: own * WIDTH]
    sent[...] = result[own * WIDTH :].astype(BF)
    normed, scale = norm_stats(mixed[...])
    g = back_sum[...]
    gain_sum = jnp.sum(g * normed, 0, keepdims=True)
    offset_sum = jnp.sum(g, 0, keepdims=True)
    cot_sum = jnp.sum(cot[...].astype(F32), 0, keepdims=True)
    grad_mixed[...] = cot[...].astype(F32) + norm_back(g, normed, scale, gain)

    branch = grad_mixed[...].astype(BF)
    branch_sum = jnp.sum(branch.astype(F32), 0, keepdims=True)
    proj = dot_tn(restored[...], branch).reshape(shards, depth, D)
    put_shares(me, same_b, other_b, 4 * depth, proj)
    put_smalls(same_a, other_a, 4 * depth, [gain_sum, offset_sum, cot_sum, branch_sum] + vectors)
    grad_att = dot_nt(branch, block_of(slab, 8, depth)).astype(BF)
    columns = column_places()
    for r in range(WIN):
        wide[:, r] = dot(columns, grad_att[r * WIDTH : (r + 1) * WIDTH]).reshape(WINDOWS, SLOT, D)
    grad_win[...] = wide[...].reshape(PADDED, D).astype(BF)


def attn_backward_body(query, key, value, probs, grad_win, came, out, pairs):
    @pl.when(pl.program_id(0) == 0)
    def _():
        pairs[...] = came[...]

    masks = head_masks()
    for u in range(QUADS):
        feats = slice(u * FEAT, (u + 1) * FEAT)
        q2 = query[:, feats].astype(F32)
        k2 = key[:, feats].astype(F32)
        v2 = value[:, feats].astype(F32)
        go2 = grad_win[:, feats].astype(F32)
        p2 = probs[0, u].astype(F32)
        held = []
        total = pairs[u]
        for s in range(2):
            part = slice(s * PLACES, (s + 1) * PLACES)
            k, v, p_low = (a[part].astype(BF) for a in (k2, v2, p2))
            p = p2[part]
            go_big = spread(go2[part], masks)
            dp = dot_nt(v, go_big)
            dv = dot(p_low, go_big)
            inner = jnp.sum(p * dp, 0, keepdims=True)
            ds = (p * (dp - inner)).astype(BF)
            total += ds.astype(F32)
            dk = dot(ds, spread(q2[part], masks)) * SCALE
            dq = own_heads(dot_tn(ds, k)) * SCALE
            held.append((dq, dk, dv))
        pairs[u] = total
        for c in range(3):
            both = jnp.concatenate([held[0][c], held[1][c]], 0).astype(BF)
            out[:, c * D + u * FEAT : c * D + (u + 1) * FEAT] = both


def attn_last_body(
    me_ref,
    grad_mixed,
    tokens,
    halo,
    slab,
    normed_win,
    pairs,
    *refs,
):
    grads = refs[:-5]
    kept, sent, same, other, wide = refs[-5:]
    me = me_ref[0]
    shards = slab.shape[0]
    depth = (slab.shape[1] - SMALL) // 3
    small = smalls_of(slab, 3 * depth)
    gain = small[0:1]
    own = WIN - SHIFT
    vectors = []
    for c in range(3):
        cols = slice(c * D, (c + 1) * D)
        g = jnp.concatenate([part[:, cols] for part in grads], 0)
        if c != 1:
            vectors.append(jnp.sum(g.astype(F32), 0, keepdims=True))
        put_shares(
            me, same, other, c * depth, dot_tn(normed_win[...], g).reshape(shards, depth, D)
        )
        part = dot_nt(g, block_of(slab, c, depth))
        total = part if c == 0 else total + part
    wide[...] = total.reshape(WINDOWS, WIN, SLOT, D)
    back = places_column()
    gain_sum = jnp.zeros((1, D), F32)
    bias_sum = jnp.zeros((1, D), F32)
    for r in range(WIN):
        here = wide[:, r].reshape(WINDOWS * SLOT, D).astype(BF)
        g = dot(back, here)
        x = (tokens[SHIFT + r] if r < own else halo[r - own]).astype(F32)
        normed, scale = norm_stats(x)
        gain_sum += jnp.sum(g * normed, 0, keepdims=True)
        bias_sum += jnp.sum(g, 0, keepdims=True)
        grad = grad_mixed[r * WIDTH : (r + 1) * WIDTH, :] + norm_back(g, normed, scale, gain)
        if r < own:
            kept[r * WIDTH : (r + 1) * WIDTH, :] = grad
        else:
            sent[(r - own) * WIDTH : (r - own + 1) * WIDTH, :] = grad.astype(BF)

    rows = [gain_sum, bias_sum, vectors[0], vectors[1]]
    halves = GROUP // QUAD
    picks = [table_pick(1, half, True) for half in range(halves)]
    for g in range(GROUPS):
        laid = jnp.zeros((PLACES, TAB_USED), F32)
        for half in range(halves):
            total = pairs[g * halves + half]
            high = total.astype(BF)
            low = (total - high.astype(F32)).astype(BF)
            laid += dot(high, picks[half]) + dot(low, picks[half])
        laid = jnp.concatenate([laid, jnp.zeros((PLACES, TAB - TAB_USED), F32)], 1)
        total = jnp.zeros((SLOT, TAB), F32)
        for r in range(WIN):
            total += pltpu.roll(
                laid[r * SLOT : (r + 1) * SLOT], (2 * WIN - 1) * GROUP * r, 1
            )
        total = pltpu.roll(total, 0, 1, stride=GROUP, stride_axis=0)
        row = jnp.sum(total, 0, keepdims=True)
        rows += [row[:, c * D : (c + 1) * D] for c in range(TAB // D)]
    put_smalls(same, other, 3 * depth, rows)


def region_views(regions, rows, place):
    here = lax.dynamic_slice_in_dim(regions[0], place * rows, rows, 0)
    windows = here.reshape(WIN, WINDOWS, WIN).transpose(1, 0, 2)
    windows = jnp.pad(windows, ((0, 0), (0, 0), (0, SLOT - WIN))).astype(F32)
    windows = windows.reshape(WINDOWS, PLACES)
    by_row = jnp.broadcast_to(windows[:, :, None], (WINDOWS, PLACES, 128))
    by_lane = jnp.tile(windows, (1, QUAD))
    return by_row, by_lane[:, None, :]


def per_device(
    tokens,
    regions,
    cotangent,
    gain_one,
    bias_one,
    w_qkv,
    bias_qv,
    table,
    w_proj,
    bias_proj,
    gain_two,
    bias_two,
    w_in,
    bias_in,
    w_out,
    bias_out,
):
    images, local_rows, columns, _ = tokens.shape
    assert images == 1 and local_rows == WIN and columns == WIDTH
    shards = lax.axis_size("shard")
    me = lax.axis_index("shard").astype(jnp.int32)
    seq = lax.axis_index("seq").astype(jnp.int32)
    where = jnp.stack([me, seq & 1])
    chips = shards // 2
    depth = D // shards
    own = WIN - SHIFT
    attn_params = (gain_one[None], bias_one[None], w_qkv, bias_qv, table.T)
    mlp_params = (
        w_proj,
        bias_proj[None],
        gain_two[None],
        bias_two[None],
        w_in,
        bias_in[None],
        w_out,
        bias_out[None],
    )
    late = seq & 1
    attn_slab, mlp_slab = kernel_call(
        pack_body,
        [like((3 * depth + SMALL, D), BF), like((9 * depth + SMALL, D), BF)],
        (where, *attn_params, *mlp_params),
        smem=1,
    )
    pieces = gather_pieces(attn_slab)
    mlp_all = lax.all_gather(mlp_slab, "shard")
    tokens_here = tokens[0]
    token_halo = shifted_2(tokens_here[:SHIFT], "seq", -1)
    cot_here = cotangent[0]
    cot_halo = shifted_2(cot_here[:SHIFT], "seq", -1)
    by_row, by_lane = region_views(regions, local_rows, seq)

    normed_win, query, key, value, attn_all = kernel_call(
        project_body,
        [like((PADDED, D), BF)] * 4 + [like((shards, *attn_slab.shape), BF)],
        (where, tokens_here, token_halo, *pieces),
        scratch=[
            pltpu.VMEM((WINDOWS, WIN, SLOT, D), F32),
            pltpu.SemaphoreType.DMA((shards,)),
        ],
        smem=1,
        apart=shards,
    )
    pair_rows = 2 * PLACES
    steps = WINDOWS // 2

    def rows_from(first, width=D):
        return pl.BlockSpec((pair_rows, width), lambda i: (first + i, 0))

    def probs_from(first):
        return pl.BlockSpec((1, QUADS, pair_rows, LANES), lambda i: (first + i, 0, 0, 0))

    def fixed(shape):
        return pl.BlockSpec(shape, lambda i: (0,) * len(shape))

    probs, restored = kernel_call(
        attn_forward_body,
        [like((steps, QUADS, pair_rows, LANES), BF), like((TOKENS, D), BF)],
        (attn_all, by_row, by_lane, query, key, value),
        grid=(steps,),
        in_blocks=[
            fixed(attn_all.shape),
            pl.BlockSpec((2, *by_row.shape[1:]), lambda i: (i, 0, 0)),
            pl.BlockSpec((2, *by_lane.shape[1:]), lambda i: (i, 0, 0)),
            rows_from(0),
            rows_from(0),
            rows_from(0),
        ],
        out_blocks=[probs_from(0), fixed((TOKENS, D))],
        scratch=[
            pltpu.VMEM((WINDOWS, WIN, SLOT, D), F32),
            pltpu.VMEM((QUADS, PLACES, LANES), F32),
        ],
    )
    share_a = like((chips, 4 * depth + SMALL, D), BF)
    share_b = like((chips, 5 * depth, D), BF)
    out_kept, out_sent, grad_mixed, grad_win, same_a, other_a, same_b, other_b = kernel_call(
        mlp_body,
        [
            like((own * WIDTH, D), F32),
            like((SHIFT * WIDTH, D), BF),
            like((TOKENS, D), F32),
            like((PADDED, D), BF),
            share_a,
            share_a,
            share_b,
            share_b,
        ],
        (where, tokens_here, token_halo, cot_here, cot_halo, mlp_all, restored),
        scratch=[
            pltpu.VMEM((TOKENS, D), BF),
            pltpu.VMEM((TOKENS, D), BF),
            pltpu.VMEM((TOKENS, D), F32),
            pltpu.VMEM((TOKENS, D), F32),
            pltpu.VMEM((TOKENS, D), F32),
            pltpu.VMEM((WINDOWS, WIN, SLOT, D), F32),
        ],
        smem=1,
    )

    def backward(first, count, grad_win, came):
        sums = like((QUADS, PLACES, LANES), F32)
        return kernel_call(
            attn_backward_body,
            [like((count * pair_rows, 3 * D), BF), sums],
            (query, key, value, probs, grad_win, came),
            grid=(count,),
            in_blocks=[rows_from(first)] * 3
            + [probs_from(first), rows_from(first), fixed(sums.shape)],
            out_blocks=[rows_from(0, 3 * D), fixed(sums.shape)],
            )

    none = jnp.zeros((QUADS, PLACES, LANES), F32)
    count = steps // 2
    early, pairs = backward(0, count, grad_win, none)
    sums, (pairs,) = tie(add_cores(same_a, other_a) + add_cores(same_b, other_b), [pairs])
    parts_a, parts_b = to_chips(sums[:chips]), to_chips(sums[chips:])
    late_part, pairs = backward(count, count, grad_win, pairs)
    (out_halo, *parts_a), (pairs,) = tie([shifted_2(out_sent, "seq", 1), *parts_a], [pairs])
    tok_kept, tok_sent, attn_same, attn_other = kernel_call(
        attn_last_body,
        [
            like((own * WIDTH, D), F32),
            like((SHIFT * WIDTH, D), BF),
            like((chips, 3 * depth + SMALL, D), BF),
            like((chips, 3 * depth + SMALL, D), BF),
        ],
        (where, grad_mixed, tokens_here, token_halo, attn_all, normed_win, pairs, early, late_part),
        scratch=[pltpu.VMEM((WINDOWS, WIN, SLOT, D), F32)],
        smem=1,
    )
    tok_halo = shifted_2(tok_sent, "seq", 1)
    cores = exchange(attn_other, "shard", 1)
    keep, send = add_chips(late, parts_a)
    (send,), (cores,) = tie([send], [cores])
    near_a = exchange(send, "seq", 1)
    sums = [add_pair(attn_same[q], cores[q]) for q in range(chips)]
    sums, (near_a,) = tie(sums, [near_a])
    parts = to_chips(sums)
    half_a = add_pair(keep, near_a)
    (half_a,), parts_b = tie([half_a], parts_b)
    far_a = exchange(half_a, "seq", 2)
    keep_b, send_b = add_chips(late, parts_b)
    (keep_b, send_b), (far_a,) = tie([keep_b, send_b], [far_a])
    near_b = exchange(send_b, "seq", 1)
    half_a = seq_rest(add_pair(half_a, far_a))
    (half_a,), parts = tie([half_a], parts)
    back_a = exchange(half_a, "seq", 1)
    keep, send = add_chips(late, parts)
    (keep, send), (near_b,) = tie([keep, send], [near_b])
    near = exchange(send, "seq", 1)
    half_b = add_pair(keep_b, near_b)
    (half_b,), (near,) = tie([half_b], [near])
    far_b = exchange(half_b, "seq", 2)
    half = add_pair(keep, near)
    (half,), (far_b,) = tie([half], [far_b])
    far = exchange(half, "seq", 2)
    half_b = seq_rest(add_pair(half_b, far_b))
    (half_b,), (far,) = tie([half_b], [far])
    back_b = exchange(half_b, "seq", 1)
    half = seq_rest(add_pair(half, far))
    back = exchange(half, "seq", 1)
    mlp_grads = kernel_call(
        unpack_mlp_body,
        [like(p.shape, F32) for p in mlp_params],
        (where, half_a, back_a, half_b, back_b),
        scratch=[
            pltpu.VMEM((4 * depth + SMALL, D), BF),
            pltpu.VMEM((5 * depth, D), BF),
        ],
        smem=1,
    )
    attn_grads = kernel_call(
        unpack_attn_body,
        [like(p.shape, F32) for p in attn_params],
        (where, half, back),
        scratch=[pltpu.VMEM((3 * depth + SMALL, D), BF)],
        smem=1,
    )
    summed = [*attn_grads[:4], attn_grads[4].T, *mlp_grads]

    def joined(halo, kept):
        return jnp.concatenate([halo.astype(F32), kept], 0).reshape(tokens.shape)

    targets = (
        gain_one,
        bias_one,
        w_qkv,
        bias_qv,
        table,
        w_proj,
        bias_proj,
        gain_two,
        bias_two,
        w_in,
        bias_in,
        w_out,
        bias_out,
    )
    grads = [g.reshape(p.shape) for g, p in zip(summed, targets)]
    return (joined(out_halo, out_kept), joined(tok_halo, tok_kept), *grads)


def solution(mesh):
    return jax.shard_map(
        per_device,
        mesh=mesh,
        in_specs=(
            P("shard", "seq", None, None),
            P("shard", None, None),
            P("shard", "seq", None, None),
            P("shard"),
            P("shard"),
            P("shard", None),
            P(None, "shard"),
            P(None, "shard"),
            P("shard", None),
            P("shard"),
            P("shard"),
            P("shard"),
            P("shard", None),
            P("shard"),
            P("shard", None),
            P("shard"),
        ),
        out_specs=(
            P("shard", "seq", None, None),
            P("shard", "seq", None, None),
            P("shard"),
            P("shard"),
            P("shard", None),
            P(None, "shard"),
            P(None, "shard"),
            P("shard", None),
            P("shard"),
            P("shard"),
            P("shard"),
            P("shard", None),
            P("shard"),
            P("shard", None),
            P("shard"),
        ),
        check_vma=False,
    )
```

```python
import jax
import jax.numpy as jnp
from jax import lax
from jax.experimental import pallas as pl
from jax.experimental.pallas import tpu as pltpu
from jax.sharding import PartitionSpec as P

D = 512
HEADS = 16
HEAD = 32
WIN = 7
SHIFT = 3
FF = 2048
WIDTH = 112
WINDOWS = WIDTH // WIN
SLOT = 8
PLACES = WIN * SLOT
GROUP = 8
GROUPS = HEADS // GROUP
QUAD = 4
QUADS = HEADS // QUAD
FEAT = QUAD * HEAD
HOLD = 64
LANES = QUAD * HOLD
TOKENS = WIN * WIDTH
PADDED = WINDOWS * PLACES
TAB = 1536
TAB_USED = 768
SMALL = 32
EPS = 1e-05
SCALE = HEAD**-0.5
BF = jnp.bfloat16
F32 = jnp.float32
VMEM_LIMIT = 60 * 1024 * 1024


def shifted_2(value, axis, by):
    peers = lax.axis_size(axis)
    return lax.ppermute(value, axis, [(i, (i + by) % peers) for i in range(peers)])


def dot(left, right, dims=((1,), (0,))):
    return lax.dot_general(left, right, (dims, ((), ())), preferred_element_type=F32)


def dot_nt(left, right):
    return dot(left, right, ((1,), (1,)))


def dot_tn(left, right):
    return dot(left, right, ((0,), (0,)))


def iota(shape, axis):
    return lax.broadcasted_iota(jnp.int32, shape, axis)


def one_hot(condition):
    return jnp.where(condition, 1.0, 0.0).astype(BF)


def column_places():
    slot = iota((WINDOWS * SLOT, WIDTH), 0)
    column = iota((WINDOWS * SLOT, WIDTH), 1)
    place = slot & (SLOT - 1)
    wanted = (slot >> 3) * WIN + place + SHIFT
    wanted = jnp.where(wanted >= WIDTH, wanted - WIDTH, wanted)
    return one_hot((wanted == column) & (place < WIN))


def places_column():
    slot = iota((WIDTH, WINDOWS * SLOT), 1)
    column = iota((WIDTH, WINDOWS * SLOT), 0)
    place = slot & (SLOT - 1)
    wanted = (slot >> 3) * WIN + place + SHIFT
    wanted = jnp.where(wanted >= WIDTH, wanted - WIDTH, wanted)
    return one_hot((wanted == column) & (place < WIN))


def head_masks():
    feature = iota((1, FEAT), 1) >> 5
    return [jnp.where(feature == h, 1.0, 0.0).astype(F32) for h in range(QUAD)]


def spread(values, masks):
    empty = jnp.zeros((HOLD - PLACES, FEAT), F32)
    rows = []
    for mask in masks:
        rows += [values * mask, empty]
    return jnp.concatenate(rows, 0).astype(BF)


def own_heads(values):
    feature = iota((PLACES, FEAT), 1) >> 5
    out = values[:PLACES]
    for h in range(1, QUAD):
        out = jnp.where(feature == h, values[h * HOLD : h * HOLD + PLACES], out)
    return out


def table_pick(row_axis, quad, backwards):
    shape = (TAB_USED, LANES) if row_axis == 0 else (LANES, TAB_USED)
    lane = iota(shape, row_axis)
    pair = iota(shape, 1 - row_axis)
    head, place = pair >> 6, pair & (HOLD - 1)
    row, column = place >> 3, place & (SLOT - 1)
    entry = row * (2 * WIN - 1) + column
    if backwards:
        entry = (WIN - 1) * 2 * WIN - entry
    held = head + quad % (GROUP // QUAD) * QUAD
    match = ((lane >> 3) == entry) & ((lane & 7) == held)
    return one_hot(match & (column < WIN) & (row < WIN))


def norm_stats(values):
    average = jnp.mean(values, -1, keepdims=True)
    centered = values - average
    variance = jnp.mean(centered * centered, -1, keepdims=True)
    scale = lax.rsqrt(variance + EPS)
    return centered * scale, scale


def norm_back(grad, normed, scale, gain):
    scaled = grad * gain
    first = jnp.mean(scaled, -1, keepdims=True)
    second = jnp.mean(scaled * normed, -1, keepdims=True)
    return scale * (scaled - first - normed * second)


def whole(memory=pltpu.VMEM):
    return pl.BlockSpec(memory_space=memory)


def kernel_call(
    body, outs, ins, scratch=(), smem=0, apart=0, grid=None, in_blocks=None, out_blocks=None,
    vmem=VMEM_LIMIT,
):
    in_specs = [whole(pltpu.SMEM)] * smem
    in_specs += in_blocks or [whole()] * (len(ins) - smem - apart) + [whole(pl.ANY)] * apart
    options = {"grid": grid} if grid else {}
    return pl.pallas_call(
        body,
        out_shape=tuple(outs),
        in_specs=in_specs,
        out_specs=tuple(out_blocks or [whole()] * len(outs)),
        scratch_shapes=list(scratch),
        cost_estimate=pl.CostEstimate(flops=1024, bytes_accessed=1024, transcendentals=0),
        compiler_params=pltpu.CompilerParams(vmem_limit_bytes=vmem),
        **options,
    )(*ins)


def like(shape, dtype):
    return jax.ShapeDtypeStruct(shape, dtype)


def place(vector, lanes, me):
    w = vector.shape[1]
    pick = one_hot(iota((w, lanes), 1) == iota((w, lanes), 0) + me * w)
    wide = jnp.broadcast_to(vector, (8, w))
    return dot(wide.astype(BF), pick)[0:1]


def mine(row, w, me):
    lanes = row.shape[1]
    pick = one_hot(iota((lanes, w), 0) == iota((lanes, w), 1) + me * w)
    wide = jnp.broadcast_to(row, (8, lanes))
    return dot(wide.astype(BF), pick)[0:1]


def padded(rows, height):
    total = sum(r.shape[0] for r in rows)
    return jnp.concatenate(rows + [jnp.zeros((height - total, D), F32)], 0).astype(BF)


def pack_body(
    me_ref, g1, b1, wqkv, bqv, table, wproj, bproj, g2, b2, win, bin_, wout, bout, attn, mlp
):
    depth = wqkv.shape[0]
    me = me_ref[0]
    for c in range(3):
        attn[c * depth : (c + 1) * depth, :] = wqkv[:, c * D : (c + 1) * D]
    attn[3 * depth : 4 * depth, :] = wproj[...]
    vectors = (g1[...], b1[...], bqv[0:1, :], bqv[1:2, :], bproj[...])
    rows = [place(v, D, me) for v in vectors]
    held, entries = table.shape
    lane = iota((entries, TAB), 1)
    spot = iota((entries, TAB), 0) * GROUP + TAB - (WIN - 1) * 2 * WIN * GROUP
    spot = jnp.where(spot >= TAB, spot - TAB, spot)
    values = table[...].astype(F32).T
    groups = [jnp.zeros((1, TAB), F32) for _ in range(GROUPS)]
    for h in range(held):
        head = me * held + h
        inside = lane == spot + (head & (GROUP - 1))
        row = jnp.sum(jnp.where(inside, values[:, h : h + 1], 0.0), 0, keepdims=True)
        for g in range(GROUPS):
            groups[g] = groups[g] + jnp.where((head >> 3) == g, row, 0.0)
    for g in range(GROUPS):
        rows += [groups[g][:, c * D : (c + 1) * D] for c in range(TAB // D)]
    attn[4 * depth :, :] = padded(rows, SMALL)
    for c in range(FF // D):
        mlp[c * depth : (c + 1) * depth, :] = win[:, c * D : (c + 1) * D]
    mlp[4 * depth : 8 * depth, :] = wout[...]
    hidden_bias = place(bin_[...], FF, me)
    rows = [place(v, D, me) for v in (g2[...], b2[...], bout[...])]
    rows += [hidden_bias[:, c * D : (c + 1) * D] for c in range(FF // D)]
    mlp[8 * depth :, :] = padded(rows, SMALL)


def join_halves(late, half, back, both, sems):
    rows = half.shape[0]
    copies = []
    for n, (part, at) in enumerate(((half, late), (back, 1 - late))):
        to = both.at[pl.ds(pl.multiple_of(at * rows, 16), rows), :]
        copies.append(pltpu.make_async_copy(part, to, sems.at[n]))
    for copy in copies:
        copy.start()
    for copy in copies:
        copy.wait()


def unpack_attn_body(me_ref, half, back, g1, b1, wqkv, bqv, table, attn, sems):
    depth = wqkv.shape[0]
    me = me_ref[0]
    join_halves(me_ref[1], half, back, attn, sems)
    for c in range(3):
        wqkv[:, c * D : (c + 1) * D] = attn[c * depth : (c + 1) * depth, :].astype(F32)
    small = attn[3 * depth :, :].astype(F32)
    g1[...] = mine(small[0:1], depth, me)
    b1[...] = mine(small[1:2], depth, me)
    bqv[0:1, :] = mine(small[2:3], depth, me)
    bqv[1:2, :] = mine(small[3:4], depth, me)
    held, entries = table.shape
    lane = iota((entries, TAB), 1)
    spot = (entries - 1 - iota((entries, TAB), 0)) * GROUP
    parts = TAB // D
    rows = [
        jnp.concatenate([small[4 + g * parts + c : 5 + g * parts + c] for c in range(parts)], 1)
        for g in range(GROUPS)
    ]
    which = iota((entries, held), 1)
    total = jnp.zeros((entries, held), F32)
    for h in range(held):
        head = me * held + h
        row = rows[0]
        for g in range(1, GROUPS):
            row = jnp.where((head >> 3) == g, rows[g], row)
        inside = lane == spot + (head & (GROUP - 1))
        column = jnp.sum(jnp.where(inside, row, 0.0), 1, keepdims=True)
        total = jnp.where(which == h, column, total)
    table[...] = total.T


def unpack_mlp_body(
    me_ref, half, back, wproj, bproj, g2, b2, win, bin_, wout, bout, mlp, sems
):
    depth = win.shape[0]
    me = me_ref[0]
    join_halves(me_ref[1], half, back, mlp, sems)
    for c in range(FF // D):
        win[:, c * D : (c + 1) * D] = mlp[c * depth : (c + 1) * depth, :].astype(F32)
    wout[...] = mlp[4 * depth : 8 * depth, :].astype(F32)
    wproj[...] = mlp[8 * depth : 9 * depth, :].astype(F32)
    small = mlp[9 * depth :, :].astype(F32)
    g2[...] = mine(small[0:1], depth, me)
    b2[...] = mine(small[1:2], depth, me)
    bout[...] = mine(small[2:3], depth, me)
    bproj[...] = mine(small[3:4], depth, me)
    hidden = jnp.concatenate([small[4 + c : 5 + c] for c in range(FF // D)], 1)
    bin_[...] = mine(hidden, depth * FF // D, me)


def put_shares(me, same, other, start, values, first=0):
    core, chip = me & 1, me >> 1
    rows = values.shape[1]
    for c in range(values.shape[0] // 2):
        one, two = values[2 * c], values[2 * c + 1]
        q = (first // 2 + c) ^ chip
        same[q, start : start + rows, :] = jnp.where(core == 0, one, two).astype(BF)
        other[q, start : start + rows, :] = jnp.where(core == 0, two, one).astype(BF)


def put_smalls(same, other, start, rows):
    block = padded(rows, SMALL)
    for q in range(same.shape[0]):
        same[q, start:, :] = block
        other[q, start:, :] = block


def exchange(value, axis, mask):
    peers = lax.axis_size(axis)
    return lax.ppermute(value, axis, [(i, i ^ mask) for i in range(peers)])


def gather_pieces(slab):
    chips = lax.axis_size("shard") // 2
    pieces = [None] * (2 * chips)
    for q in range(chips):
        pieces[2 * q] = exchange(slab, "shard", 2 * q) if q else slab
    for q in range(chips):
        pieces[2 * q + 1] = exchange(pieces[2 * q], "shard", 1)
    return pieces


def add_pair(here, came):
    return (here.astype(F32) + came.astype(F32)).astype(BF)


def add_cores(same, came):
    return [add_pair(same[q], came[q]) for q in range(1, same.shape[0])]


def to_chips(sums):
    return [exchange(s, "shard", 2 * q + 2) for q, s in enumerate(sums)]


def add_chips(late, same, came, parts):
    half = same.shape[1] // 2
    out = []
    for start in (late * half, (1 - late) * half):
        total = 0.0
        for part in (same[0], came[0], *parts):
            total += lax.dynamic_slice_in_dim(part, start, half, 0).astype(F32)
        out.append(total.astype(BF))
    return out


def seq_rest(half):
    reach = 4
    while reach < lax.axis_size("seq"):
        half = add_pair(half, exchange(half, "seq", reach))
        reach *= 2
    return half


def tie(first, second):
    first, second = list(first), list(second)
    out = lax.optimization_barrier((*first, *second))
    return list(out[: len(first)]), list(out[len(first) :])


def block_of(slab, c, depth):
    return slab[:, c * depth : (c + 1) * depth, :].reshape(D, D)


def smalls_of(slab, start):
    return jnp.sum(slab[:, start:, :].astype(F32), 0)


def project_body(me_ref, tokens, halo, *refs):
    shards = len(refs) - 7
    pieces = refs[:shards]
    normed_win, query, key, value, slab, wide, sems = refs[shards:]
    copies = [
        pltpu.make_async_copy(piece, slab.at[me_ref[0] ^ p], sems.at[p])
        for p, piece in enumerate(pieces)
    ]
    for copy in copies:
        copy.start()
    columns = column_places()
    own = WIN - SHIFT
    for copy in copies:
        copy.wait()
    depth = (slab.shape[1] - SMALL) // 4
    small = smalls_of(slab, 4 * depth)
    gain, offset, bias_q, bias_v = (small[r : r + 1] for r in range(4))
    for r in range(WIN):
        x = (tokens[SHIFT + r] if r < own else halo[r - own]).astype(F32)
        normed, _ = norm_stats(x)
        low = (normed * gain + offset).astype(BF)
        wide[:, r] = dot(columns, low).reshape(WINDOWS, SLOT, D)
    normed_win[...] = wide[...].reshape(PADDED, D).astype(BF)
    query[...] = (dot(normed_win[...], block_of(slab, 0, depth)) + bias_q).astype(BF)
    key[...] = dot(normed_win[...], block_of(slab, 1, depth)).astype(BF)
    value[...] = (dot(normed_win[...], block_of(slab, 2, depth)) + bias_v).astype(BF)


def attn_forward_body(
    slab, reg_rows, reg_lanes, tokens, halo, query, key, value, probs, restored, mixed, wide, bias
):
    n = pl.program_id(0)
    depth = (slab.shape[1] - SMALL) // 4

    @pl.when(n == 0)
    def _():
        small = smalls_of(slab, 4 * depth)
        parts = TAB // D
        empty = (iota((PLACES, LANES), 0) & (SLOT - 1)) == WIN
        turned = []
        for g in range(GROUPS):
            first = 5 + g * parts
            row = jnp.concatenate([small[first + c : first + c + 1] for c in range(parts)], 1)
            row = jnp.broadcast_to(row, (SLOT, TAB))
            row = pltpu.roll(row, 0, 1, stride=GROUP, stride_axis=0)
            rows = [pltpu.roll(row, (2 * WIN - 1) * GROUP * r, 1)[:, :TAB_USED] for r in range(WIN)]
            turned.append(jnp.concatenate(rows, 0).astype(BF))
        for half in range(GROUP // QUAD):
            pick = table_pick(0, half, False)
            for g in range(GROUPS):
                picked = dot(turned[g], pick)
                bias[g * (GROUP // QUAD) + half] = jnp.where(empty, -1e30, picked)

    masks = head_masks()
    penalty = [
        jnp.where(reg_rows[s][:, 0:1] != reg_lanes[s], -100.0, 0.0) for s in range(2)
    ]
    parts = [slice(s * PLACES, (s + 1) * PLACES) for s in range(2)]
    units = [(u, s) for u in range(QUADS) for s in range(2)]
    feats = [slice(u * FEAT, (u + 1) * FEAT) for u in range(QUADS)]
    values, scores = [], []
    for u in range(QUADS):
        q2 = query[:, feats[u]].astype(F32)
        k2 = key[:, feats[u]].astype(F32)
        v2 = value[:, feats[u]].astype(F32)
        for s in range(2):
            values.append(v2[parts[s]].astype(BF))
            scores.append(dot_nt(k2[parts[s]].astype(BF), spread(q2[parts[s]], masks)))
    shares = []
    for (u, s), score in zip(units, scores):
        logits = score * SCALE + bias[u] + penalty[s]
        powers = jnp.exp(logits - jnp.max(logits, 0, keepdims=True))
        shares.append(powers * (1.0 / jnp.sum(powers, 0, keepdims=True)))
    wholes = [dot_tn(p.astype(BF), v) for p, v in zip(shares, values)]
    for (u, s), o in zip(units, wholes):
        wide[2 * n + s, :, :, feats[u]] = own_heads(o).reshape(WIN, SLOT, FEAT)
    for u in range(QUADS):
        probs[0, u] = jnp.concatenate(shares[2 * u : 2 * u + 2], 0).astype(BF)

    @pl.when(n == pl.num_programs(0) - 1)
    def _():
        bias_proj = smalls_of(slab, 4 * depth)[4:5]
        back = places_column()
        own = WIN - SHIFT
        for r in range(WIN):
            here = wide[:, r].reshape(WINDOWS * SLOT, D).astype(BF)
            restored[r * WIDTH : (r + 1) * WIDTH, :] = dot(back, here).astype(BF)
        branch = dot(restored[...], block_of(slab, 3, depth)) + bias_proj
        for r in range(WIN):
            x = (tokens[SHIFT + r] if r < own else halo[r - own]).astype(F32)
            mixed[r * WIDTH : (r + 1) * WIDTH, :] = x + branch[r * WIDTH : (r + 1) * WIDTH]


def gelu_parts(h):
    size = jnp.abs(h) * (0.5**0.5)
    t = 1.0 / (1.0 + 0.3275911 * size)
    bell = jnp.exp(-0.5 * h * h)
    poly = t * (
        0.254829592
        + t * (-0.284496736 + t * (1.421413741 + t * (-1.453152027 + t * 1.061405429)))
    )
    tail = 0.5 * poly * bell
    upto = jnp.where(h >= 0, 1.0 - tail, tail)
    return upto, bell * 0.3989422804014327


def mlp_body(
    me_ref,
    mixed,
    cotangent,
    cot_halo,
    slab,
    attn_slab,
    restored,
    kept,
    sent,
    grad_mixed,
    grad_win,
    same,
    other,
    normed_low,
    cot,
    out_sum,
    back_sum,
    wide,
):
    me = me_ref[0]
    shards, height = slab.shape[:2]
    depth = (height - SMALL) // 8
    span = shards * D // FF
    small = smalls_of(slab, 8 * depth)
    gain, offset, bias_o = (small[r : r + 1] for r in range(3))
    own = WIN - SHIFT
    for r in range(WIN):
        part = slice(r * WIDTH, (r + 1) * WIDTH)
        cot[part, :] = cotangent[SHIFT + r] if r < own else cot_halo[r - own]
    normed, _ = norm_stats(mixed[...])
    normed_low[...] = (normed * gain + offset).astype(BF)

    def w_in(c):
        return block_of(slab, c, depth)

    def w_out(c):
        return slab[c * span : (c + 1) * span, 4 * depth : 8 * depth, :].reshape(D, D)

    def ahead(c):
        return dot(normed_low[...], w_in(c)), dot_nt(cot[...], w_out(c))

    vectors = []
    now = ahead(0)
    for c in range(FF // D):
        hidden, grad = now
        if c + 1 < FF // D:
            now = ahead(c + 1)
        hidden = hidden + small[3 + c : 4 + c]
        upto, density = gelu_parts(hidden)
        active = (hidden * upto).astype(BF)
        grad = (grad * (upto + hidden * density)).astype(BF)
        forward = dot(active, w_out(c))
        backward = dot_nt(grad, w_in(c))
        if c == 0:
            out_sum[...] = forward
            back_sum[...] = backward
        else:
            out_sum[...] += forward
            back_sum[...] += backward
        vectors.append(jnp.sum(grad.astype(F32), 0, keepdims=True))
        put_shares(
            me, same, other, c * depth, dot_tn(normed_low[...], grad).reshape(shards, depth, D)
        )
        put_shares(
            me,
            same,
            other,
            4 * depth,
            dot_tn(active, cot[...]).reshape(span, 4 * depth, D),
            c * span,
        )
    result = mixed[...] + out_sum[...] + bias_o
    kept[...] = result[: own * WIDTH]
    sent[...] = result[own * WIDTH :].astype(BF)
    normed, scale = norm_stats(mixed[...])
    g = back_sum[...]
    gain_sum = jnp.sum(g * normed, 0, keepdims=True)
    offset_sum = jnp.sum(g, 0, keepdims=True)
    cot_sum = jnp.sum(cot[...].astype(F32), 0, keepdims=True)
    grad_mixed[...] = cot[...].astype(F32) + norm_back(g, normed, scale, gain)

    branch = grad_mixed[...].astype(BF)
    branch_sum = jnp.sum(branch.astype(F32), 0, keepdims=True)
    proj = dot_tn(restored[...], branch).reshape(shards, depth, D)
    put_shares(me, same, other, 8 * depth, proj)
    put_smalls(same, other, 9 * depth, [gain_sum, offset_sum, cot_sum, branch_sum] + vectors)
    grad_att = dot_nt(branch, block_of(attn_slab, 3, depth)).astype(BF)
    columns = column_places()
    for r in range(WIN):
        wide[:, r] = dot(columns, grad_att[r * WIDTH : (r + 1) * WIDTH]).reshape(WINDOWS, SLOT, D)
    grad_win[...] = wide[...].reshape(PADDED, D).astype(BF)


def attn_backward_body(query, key, value, probs, grad_win, came, out, pairs):
    @pl.when(pl.program_id(0) == 0)
    def _():
        pairs[...] = came[...]

    masks = head_masks()
    parts = [slice(s * PLACES, (s + 1) * PLACES) for s in range(2)]
    feats = [slice(u * FEAT, (u + 1) * FEAT) for u in range(QUADS)]
    keys, shares, grads, queries, slopes = [], [], [], [], []
    for u in range(QUADS):
        q2 = query[:, feats[u]].astype(F32)
        k2 = key[:, feats[u]].astype(F32)
        v2 = value[:, feats[u]].astype(F32)
        go2 = grad_win[:, feats[u]].astype(F32)
        p2 = probs[0, u].astype(F32)
        for part in parts:
            keys.append(k2[part].astype(BF))
            shares.append(p2[part])
            grads.append(spread(go2[part], masks))
            queries.append(spread(q2[part], masks))
            slopes.append(dot_nt(v2[part].astype(BF), grads[-1]))
    lows = []
    for p, dp in zip(shares, slopes):
        inner = jnp.sum(p * dp, 0, keepdims=True)
        lows.append((p * (dp - inner)).astype(BF))
    dvs = [dot(p.astype(BF), go) for p, go in zip(shares, grads)]
    dks = [dot(ds, q) for ds, q in zip(lows, queries)]
    dqs = [dot_tn(ds, k) for ds, k in zip(lows, keys)]
    for u in range(QUADS):
        two = slice(2 * u, 2 * u + 2)
        pairs[u] += lows[2 * u].astype(F32) + lows[2 * u + 1].astype(F32)
        for c, held in enumerate(
            (
                [own_heads(dq) * SCALE for dq in dqs[two]],
                [dk * SCALE for dk in dks[two]],
                dvs[two],
            )
        ):
            both = jnp.concatenate(held, 0).astype(BF)
            out[:, c * D + u * FEAT : c * D + (u + 1) * FEAT] = both


def attn_last_body(
    me_ref,
    grad_mixed,
    tokens,
    halo,
    slab,
    normed_win,
    pairs,
    *refs,
):
    grads = refs[:-7]
    kept, sent, same, other_low, other_high, wide, other = refs[-7:]
    me = me_ref[0]
    shards = slab.shape[0]
    depth = (slab.shape[1] - SMALL) // 4
    small = smalls_of(slab, 4 * depth)
    gain = small[0:1]
    own = WIN - SHIFT
    vectors = []
    for c in range(3):
        cols = slice(c * D, (c + 1) * D)
        g = jnp.concatenate([part[:, cols] for part in grads], 0)
        if c != 1:
            vectors.append(jnp.sum(g.astype(F32), 0, keepdims=True))
        put_shares(
            me, same, other, c * depth, dot_tn(normed_win[...], g).reshape(shards, depth, D)
        )
        part = dot_nt(g, block_of(slab, c, depth))
        total = part if c == 0 else total + part
    wide[...] = total.reshape(WINDOWS, WIN, SLOT, D)
    back = places_column()
    gain_sum = jnp.zeros((1, D), F32)
    bias_sum = jnp.zeros((1, D), F32)
    for r in range(WIN):
        here = wide[:, r].reshape(WINDOWS * SLOT, D).astype(BF)
        g = dot(back, here)
        x = (tokens[SHIFT + r] if r < own else halo[r - own]).astype(F32)
        normed, scale = norm_stats(x)
        gain_sum += jnp.sum(g * normed, 0, keepdims=True)
        bias_sum += jnp.sum(g, 0, keepdims=True)
        grad = grad_mixed[r * WIDTH : (r + 1) * WIDTH, :] + norm_back(g, normed, scale, gain)
        if r < own:
            kept[r * WIDTH : (r + 1) * WIDTH, :] = grad
        else:
            sent[(r - own) * WIDTH : (r - own + 1) * WIDTH, :] = grad.astype(BF)

    rows = [gain_sum, bias_sum, vectors[0], vectors[1]]
    halves = GROUP // QUAD
    picks = [table_pick(1, half, True) for half in range(halves)]
    for g in range(GROUPS):
        laid = jnp.zeros((PLACES, TAB_USED), F32)
        for half in range(halves):
            total = pairs[g * halves + half]
            high = total.astype(BF)
            low = (total - high.astype(F32)).astype(BF)
            laid += dot(high, picks[half]) + dot(low, picks[half])
        laid = jnp.concatenate([laid, jnp.zeros((PLACES, TAB - TAB_USED), F32)], 1)
        total = jnp.zeros((SLOT, TAB), F32)
        for r in range(WIN):
            total += pltpu.roll(
                laid[r * SLOT : (r + 1) * SLOT], (2 * WIN - 1) * GROUP * r, 1
            )
        total = pltpu.roll(total, 0, 1, stride=GROUP, stride_axis=0)
        row = jnp.sum(total, 0, keepdims=True)
        rows += [row[:, c * D : (c + 1) * D] for c in range(TAB // D)]
    put_smalls(same, other, 3 * depth, rows)
    half = other_low.shape[0]
    other_low[...] = other[:half]
    other_high[...] = other[half:]


def region_views(regions, rows, place):
    here = lax.dynamic_slice_in_dim(regions[0], place * rows, rows, 0)
    windows = here.reshape(WIN, WINDOWS, WIN).transpose(1, 0, 2)
    windows = jnp.pad(windows, ((0, 0), (0, 0), (0, SLOT - WIN))).astype(F32)
    windows = windows.reshape(WINDOWS, PLACES)
    by_row = jnp.broadcast_to(windows[:, :, None], (WINDOWS, PLACES, 128))
    by_lane = jnp.tile(jnp.pad(windows, ((0, 0), (0, HOLD - PLACES))), (1, QUAD))
    return by_row, by_lane[:, None, :]


def per_device(
    tokens,
    regions,
    cotangent,
    gain_one,
    bias_one,
    w_qkv,
    bias_qv,
    table,
    w_proj,
    bias_proj,
    gain_two,
    bias_two,
    w_in,
    bias_in,
    w_out,
    bias_out,
):
    images, local_rows, columns, _ = tokens.shape
    assert images == 1 and local_rows == WIN and columns == WIDTH
    shards = lax.axis_size("shard")
    me = lax.axis_index("shard").astype(jnp.int32)
    seq = lax.axis_index("seq").astype(jnp.int32)
    where = jnp.stack([me, seq & 1])
    chips = shards // 2
    depth = D // shards
    own = WIN - SHIFT
    attn_params = (gain_one[None], bias_one[None], w_qkv, bias_qv, table.T)
    mlp_params = (
        w_proj,
        bias_proj[None],
        gain_two[None],
        bias_two[None],
        w_in,
        bias_in[None],
        w_out,
        bias_out[None],
    )
    late = seq & 1
    attn_slab, mlp_slab = kernel_call(
        pack_body,
        [like((4 * depth + SMALL, D), BF), like((8 * depth + SMALL, D), BF)],
        (where, *attn_params, *mlp_params),
        smem=1,
    )
    pieces = gather_pieces(attn_slab)
    mlp_all = lax.all_gather(mlp_slab, "shard")
    tokens_here = tokens[0]
    token_halo = shifted_2(tokens_here[:SHIFT], "seq", -1)
    cot_here = cotangent[0]
    cot_halo = shifted_2(cot_here[:SHIFT], "seq", -1)
    by_row, by_lane = region_views(regions, local_rows, seq)

    normed_win, query, key, value, attn_all = kernel_call(
        project_body,
        [like((PADDED, D), BF)] * 4 + [like((shards, *attn_slab.shape), BF)],
        (where, tokens_here, token_halo, *pieces),
        scratch=[
            pltpu.VMEM((WINDOWS, WIN, SLOT, D), F32),
            pltpu.SemaphoreType.DMA((shards,)),
        ],
        smem=1,
        apart=shards,
    )
    pair_rows = 2 * PLACES
    steps = WINDOWS // 2

    def rows_from(first, width=D):
        return pl.BlockSpec((pair_rows, width), lambda i: (first + i, 0))

    def probs_from(first):
        return pl.BlockSpec((1, QUADS, pair_rows, LANES), lambda i: (first + i, 0, 0, 0))

    def fixed(shape):
        return pl.BlockSpec(shape, lambda i: (0,) * len(shape))

    probs, restored, mixed = kernel_call(
        attn_forward_body,
        [
            like((steps, QUADS, pair_rows, LANES), BF),
            like((TOKENS, D), BF),
            like((TOKENS, D), F32),
        ],
        (attn_all, by_row, by_lane, tokens_here, token_halo, query, key, value),
        grid=(steps,),
        in_blocks=[
            fixed(attn_all.shape),
            pl.BlockSpec((2, *by_row.shape[1:]), lambda i: (i, 0, 0)),
            pl.BlockSpec((2, *by_lane.shape[1:]), lambda i: (i, 0, 0)),
            fixed(tokens_here.shape),
            fixed(token_halo.shape),
            rows_from(0),
            rows_from(0),
            rows_from(0),
        ],
        out_blocks=[probs_from(0), fixed((TOKENS, D)), fixed((TOKENS, D))],
        scratch=[
            pltpu.VMEM((WINDOWS, WIN, SLOT, D), F32),
            pltpu.VMEM((QUADS, PLACES, LANES), F32),
        ],
    )
    share = like((chips, 9 * depth + SMALL, D), BF)
    out_kept, out_sent, grad_mixed, grad_win, mlp_same, mlp_other = kernel_call(
        mlp_body,
        [
            like((own * WIDTH, D), F32),
            like((SHIFT * WIDTH, D), BF),
            like((TOKENS, D), F32),
            like((PADDED, D), BF),
            share,
            share,
        ],
        (where, mixed, cot_here, cot_halo, mlp_all, attn_all, restored),
        scratch=[
            pltpu.VMEM((TOKENS, D), BF),
            pltpu.VMEM((TOKENS, D), BF),
            pltpu.VMEM((TOKENS, D), F32),
            pltpu.VMEM((TOKENS, D), F32),
            pltpu.VMEM((WINDOWS, WIN, SLOT, D), F32),
        ],
        smem=1,
    )

    def backward(first, count, grad_win, came):
        sums = like((QUADS, PLACES, LANES), F32)
        return kernel_call(
            attn_backward_body,
            [like((count * pair_rows, 3 * D), BF), sums],
            (query, key, value, probs, grad_win, came),
            grid=(count,),
            in_blocks=[rows_from(first)] * 3
            + [probs_from(first), rows_from(first), fixed(sums.shape)],
            out_blocks=[rows_from(0, 3 * D), fixed(sums.shape)],
            )

    none = jnp.zeros((QUADS, PLACES, LANES), F32)
    count = steps // 2
    mlp_came = exchange(mlp_other, "shard", 1)
    early, pairs = backward(0, count, grad_win, none)
    sums, (pairs,) = tie(add_cores(mlp_same, mlp_came), [pairs])
    mlp_parts = to_chips(sums)
    late_part, pairs = backward(count, count, grad_win, pairs)
    (out_halo,), (pairs,) = tie([shifted_2(out_sent, "seq", 1)], [pairs])
    tok_kept, tok_sent, attn_same, *attn_others = kernel_call(
        attn_last_body,
        [
            like((own * WIDTH, D), F32),
            like((SHIFT * WIDTH, D), BF),
            like((chips, 3 * depth + SMALL, D), BF),
            like((chips // 2, 3 * depth + SMALL, D), BF),
            like((chips // 2, 3 * depth + SMALL, D), BF),
        ],
        (where, grad_mixed, tokens_here, token_halo, attn_all, normed_win, pairs, early, late_part),
        scratch=[
            pltpu.VMEM((WINDOWS, WIN, SLOT, D), F32),
            pltpu.VMEM((chips, 3 * depth + SMALL, D), BF),
        ],
        smem=1,
    )
    attn_came = [exchange(other, "shard", 1) for other in attn_others]
    mlp_parts, attn_came = tie(mlp_parts, attn_came)
    keep_m, send = add_chips(late, mlp_same, mlp_came, mlp_parts)
    (send,), attn_came = tie([send], attn_came)
    attn_came = [came[q] for came in attn_came for q in range(chips // 2)]
    near_m = exchange(send, "seq", 1)
    attn_parts = to_chips(add_cores(attn_same, attn_came))
    half_m = add_pair(keep_m, near_m)
    (half_m,), attn_parts = tie([half_m], attn_parts)
    far_m = exchange(half_m, "seq", 2)
    keep, send = add_chips(late, attn_same, attn_came, attn_parts)
    near = exchange(send, "seq", 1)
    tok_halo = shifted_2(tok_sent, "seq", 1)
    (near, tok_halo), (far_m,) = tie([near, tok_halo], [far_m])
    half = add_pair(keep, near)
    (half,), (far_m,) = tie([half], [far_m])
    far = exchange(half, "seq", 2)
    half_m = seq_rest(add_pair(half_m, far_m))
    (half_m,), (far,) = tie([half_m], [far])
    back_m = exchange(half_m, "seq", 1)
    half = seq_rest(add_pair(half, far))
    (half,), (back_m,) = tie([half], [back_m])
    back = exchange(half, "seq", 1)
    def unpack(body, params, half, back):
        return kernel_call(
            body,
            [like(p.shape, F32) for p in params],
            (where, half, back),
            scratch=[
                pltpu.VMEM((2 * half.shape[0], D), BF),
                pltpu.SemaphoreType.DMA((2,)),
            ],
            smem=1,
            apart=2,
            vmem=16 * 1024 * 1024,
        )

    mlp_grads = unpack(unpack_mlp_body, mlp_params, half_m, back_m)
    mlp_grads, (back,) = tie(mlp_grads, [back])
    attn_grads = unpack(unpack_attn_body, attn_params, half, back)
    summed = [*attn_grads[:4], attn_grads[4].T, *mlp_grads]

    def joined(halo, kept):
        return jnp.concatenate([halo.astype(F32), kept], 0).reshape(tokens.shape)

    targets = (
        gain_one,
        bias_one,
        w_qkv,
        bias_qv,
        table,
        w_proj,
        bias_proj,
        gain_two,
        bias_two,
        w_in,
        bias_in,
        w_out,
        bias_out,
    )
    grads = [g.reshape(p.shape) for g, p in zip(summed, targets)]
    return (joined(out_halo, out_kept), joined(tok_halo, tok_kept), *grads)


def solution(mesh):
    return jax.shard_map(
        per_device,
        mesh=mesh,
        in_specs=(
            P("shard", "seq", None, None),
            P("shard", None, None),
            P("shard", "seq", None, None),
            P("shard"),
            P("shard"),
            P("shard", None),
            P(None, "shard"),
            P(None, "shard"),
            P("shard", None),
            P("shard"),
            P("shard"),
            P("shard"),
            P("shard", None),
            P("shard"),
            P("shard", None),
            P("shard"),
        ),
        out_specs=(
            P("shard", "seq", None, None),
            P("shard", "seq", None, None),
            P("shard"),
            P("shard"),
            P("shard", None),
            P(None, "shard"),
            P(None, "shard"),
            P("shard", None),
            P("shard"),
            P("shard"),
            P("shard"),
            P("shard", None),
            P("shard"),
            P("shard", None),
            P("shard"),
        ),
        check_vma=False,
    )
```

```python
import math

import jax
import jax.numpy as jnp
from jax import lax
from jax.experimental import pallas as pl
from jax.experimental.pallas import tpu as pltpu
from jax.sharding import PartitionSpec as P

D = 512
HEADS = 16
HEAD = 32
WIN = 7
SHIFT = 3
FF = 2048
WIDTH = 112
WINDOWS = WIDTH // WIN
SLOT = 8
PLACES = WIN * SLOT
GROUP = 8
GROUPS = HEADS // GROUP
QUAD = 4
QUADS = HEADS // QUAD
FEAT = QUAD * HEAD
HOLD = 64
LANES = QUAD * HOLD
TOKENS = WIN * WIDTH
PADDED = WINDOWS * PLACES
TAB = 1536
TAB_USED = 768
SMALL = 32
EPS = 1e-05
SCALE = HEAD**-0.5
BF = jnp.bfloat16
F32 = jnp.float32
VMEM_LIMIT = 36 * 1024 * 1024


def shifted_2(value, axis, by):
    peers = lax.axis_size(axis)
    return lax.ppermute(value, axis, [(i, (i + by) % peers) for i in range(peers)])


def dot(left, right, dims=((1,), (0,))):
    return lax.dot_general(left, right, (dims, ((), ())), preferred_element_type=F32)


def dot_nt(left, right):
    return dot(left, right, ((1,), (1,)))


def dot_tn(left, right):
    return dot(left, right, ((0,), (0,)))


def iota(shape, axis):
    return lax.broadcasted_iota(jnp.int32, shape, axis)


def shard_place():
    return lax.axis_index("shard").astype(jnp.int32)


def late_place():
    return lax.axis_index("seq").astype(jnp.int32) & 1


def one_hot(condition):
    return jnp.where(condition, 1.0, 0.0).astype(BF)


def column_places():
    slot = iota((WINDOWS * SLOT, WIDTH), 0)
    column = iota((WINDOWS * SLOT, WIDTH), 1)
    place = slot & (SLOT - 1)
    wanted = (slot >> 3) * WIN + place + SHIFT
    wanted = jnp.where(wanted >= WIDTH, wanted - WIDTH, wanted)
    return one_hot((wanted == column) & (place < WIN))


def places_column():
    slot = iota((WIDTH, WINDOWS * SLOT), 1)
    column = iota((WIDTH, WINDOWS * SLOT), 0)
    place = slot & (SLOT - 1)
    wanted = (slot >> 3) * WIN + place + SHIFT
    wanted = jnp.where(wanted >= WIDTH, wanted - WIDTH, wanted)
    return one_hot((wanted == column) & (place < WIN))


def head_masks():
    feature = iota((1, FEAT), 1) >> 5
    return [jnp.where(feature == h, 1.0, 0.0).astype(F32) for h in range(QUAD)]


def spread(values, masks):
    empty = jnp.zeros((HOLD - PLACES, FEAT), F32)
    rows = []
    for mask in masks:
        rows += [values * mask, empty]
    return jnp.concatenate(rows, 0).astype(BF)


def own_heads(values):
    feature = iota((PLACES, FEAT), 1) >> 5
    out = values[:PLACES]
    for h in range(1, QUAD):
        out = jnp.where(feature == h, values[h * HOLD : h * HOLD + PLACES], out)
    return out


def table_pick(row_axis, quad, backwards):
    shape = (TAB_USED, LANES) if row_axis == 0 else (LANES, TAB_USED)
    lane = iota(shape, row_axis)
    pair = iota(shape, 1 - row_axis)
    head, place = pair >> 6, pair & (HOLD - 1)
    row, column = place >> 3, place & (SLOT - 1)
    entry = row * (2 * WIN - 1) + column
    if backwards:
        entry = (WIN - 1) * 2 * WIN - entry
    held = head + quad % (GROUP // QUAD) * QUAD
    match = ((lane >> 3) == entry) & ((lane & 7) == held)
    return one_hot(match & (column < WIN) & (row < WIN))


def norm_stats(values):
    average = jnp.mean(values, -1, keepdims=True)
    centered = values - average
    variance = jnp.mean(centered * centered, -1, keepdims=True)
    scale = lax.rsqrt(variance + EPS)
    return centered * scale, scale


def norm_back(grad, normed, scale, gain):
    scaled = grad * gain
    first = jnp.mean(scaled, -1, keepdims=True)
    second = jnp.mean(scaled * normed, -1, keepdims=True)
    return scale * (scaled - first - normed * second)


def whole(memory=pltpu.VMEM):
    return pl.BlockSpec(memory_space=memory)


def kernel_call(
    body, outs, ins, scratch=(), apart=0, grid=None, in_blocks=None, out_blocks=None,
    vmem=VMEM_LIMIT,
):
    in_specs = in_blocks or [whole()] * (len(ins) - apart) + [whole(pl.ANY)] * apart
    options = {"grid": grid} if grid else {}
    return pl.pallas_call(
        body,
        out_shape=tuple(outs),
        in_specs=in_specs,
        out_specs=tuple(out_blocks or [whole()] * len(outs)),
        scratch_shapes=list(scratch),
        cost_estimate=pl.CostEstimate(flops=1024, bytes_accessed=1024, transcendentals=0),
        compiler_params=pltpu.CompilerParams(vmem_limit_bytes=vmem),
        **options,
    )(*ins)


def like(shape, dtype):
    return jax.ShapeDtypeStruct(shape, dtype)


def place(vector, lanes, me):
    w = vector.shape[1]
    pick = one_hot(iota((w, lanes), 1) == iota((w, lanes), 0) + me * w)
    wide = jnp.broadcast_to(vector, (8, w))
    return dot(wide.astype(BF), pick)[0:1]


def mine(row, w, me):
    lanes = row.shape[1]
    pick = one_hot(iota((lanes, w), 0) == iota((lanes, w), 1) + me * w)
    wide = jnp.broadcast_to(row, (8, lanes))
    return dot(wide.astype(BF), pick)[0:1]


def padded(rows, height):
    total = sum(r.shape[0] for r in rows)
    return jnp.concatenate(rows + [jnp.zeros((height - total, D), F32)], 0).astype(BF)


def pack_body(
    g1, b1, wqkv, bqv, table, wproj, bproj, g2, b2, win, bin_, wout, bout, attn, mlp
):
    depth = wqkv.shape[0]
    me = shard_place()
    for c in range(3):
        attn[c * depth : (c + 1) * depth, :] = wqkv[:, c * D : (c + 1) * D]
    attn[3 * depth : 4 * depth, :] = wproj[...]
    vectors = (g1[...], b1[...], bqv[0:1, :], bqv[1:2, :], bproj[...])
    rows = [place(v, D, me) for v in vectors]
    held, entries = table.shape
    lane = iota((entries, TAB), 1)
    spot = iota((entries, TAB), 0) * GROUP + TAB - (WIN - 1) * 2 * WIN * GROUP
    spot = jnp.where(spot >= TAB, spot - TAB, spot)
    values = table[...].astype(F32).T
    groups = [jnp.zeros((1, TAB), F32) for _ in range(GROUPS)]
    for h in range(held):
        head = me * held + h
        inside = lane == spot + (head & (GROUP - 1))
        row = jnp.sum(jnp.where(inside, values[:, h : h + 1], 0.0), 0, keepdims=True)
        for g in range(GROUPS):
            groups[g] = groups[g] + jnp.where((head >> 3) == g, row, 0.0)
    for g in range(GROUPS):
        rows += [groups[g][:, c * D : (c + 1) * D] for c in range(TAB // D)]
    attn[4 * depth :, :] = padded(rows, SMALL)
    for c in range(FF // D):
        mlp[c * depth : (c + 1) * depth, :] = win[:, c * D : (c + 1) * D]
    mlp[4 * depth : 8 * depth, :] = wout[...]
    held = jnp.concatenate([bin_[r : r + 1] for r in range(bin_.shape[0])], 1)
    hidden_bias = place(held, FF, me)
    rows = [place(v, D, me) for v in (g2[...], b2[...], bout[...])]
    rows += [hidden_bias[:, c * D : (c + 1) * D] for c in range(FF // D)]
    mlp[8 * depth :, :] = padded(rows, SMALL)


def join_halves(late, half, back, both, sems):
    rows = half.shape[0]
    copies = []
    for n, (part, at) in enumerate(((half, late), (back, 1 - late))):
        to = both.at[pl.ds(pl.multiple_of(at * rows, 16), rows), :]
        copies.append(pltpu.make_async_copy(part, to, sems.at[n]))
    for copy in copies:
        copy.start()
    for copy in copies:
        copy.wait()


def unpack_attn_body(half, back, g1, b1, wqkv, bqv, table, attn, sems):
    depth = wqkv.shape[0]
    me = shard_place()
    join_halves(late_place(), half, back, attn, sems)
    for c in range(3):
        wqkv[:, c * D : (c + 1) * D] = attn[c * depth : (c + 1) * depth, :].astype(F32)
    small = attn[3 * depth :, :].astype(F32)
    g1[...] = mine(small[0:1], depth, me)
    b1[...] = mine(small[1:2], depth, me)
    bqv[0:1, :] = mine(small[2:3], depth, me)
    bqv[1:2, :] = mine(small[3:4], depth, me)
    held, entries = table.shape
    lane = iota((entries, TAB), 1)
    spot = (entries - 1 - iota((entries, TAB), 0)) * GROUP
    parts = TAB // D
    rows = [
        jnp.concatenate([small[4 + g * parts + c : 5 + g * parts + c] for c in range(parts)], 1)
        for g in range(GROUPS)
    ]
    which = iota((entries, held), 1)
    total = jnp.zeros((entries, held), F32)
    for h in range(held):
        head = me * held + h
        row = rows[0]
        for g in range(1, GROUPS):
            row = jnp.where((head >> 3) == g, rows[g], row)
        inside = lane == spot + (head & (GROUP - 1))
        column = jnp.sum(jnp.where(inside, row, 0.0), 1, keepdims=True)
        total = jnp.where(which == h, column, total)
    table[...] = total.T


def unpack_mlp_body(
    half, back, wproj, bproj, g2, b2, win, bin_, wout, bout, mlp, sems
):
    depth = win.shape[0]
    me = shard_place()
    join_halves(late_place(), half, back, mlp, sems)
    for c in range(FF // D):
        win[:, c * D : (c + 1) * D] = mlp[c * depth : (c + 1) * depth, :].astype(F32)
    wout[...] = mlp[4 * depth : 8 * depth, :].astype(F32)
    wproj[...] = mlp[8 * depth : 9 * depth, :].astype(F32)
    small = mlp[9 * depth :, :].astype(F32)
    g2[...] = mine(small[0:1], depth, me)
    b2[...] = mine(small[1:2], depth, me)
    bout[...] = mine(small[2:3], depth, me)
    bproj[...] = mine(small[3:4], depth, me)
    hidden = jnp.concatenate([small[4 + c : 5 + c] for c in range(FF // D)], 1)
    hidden = mine(hidden, depth * FF // D, me)
    for r in range(bin_.shape[0]):
        bin_[r : r + 1] = hidden[:, r * 128 : (r + 1) * 128]


def put_shares(me, same, other, start, values, first=0):
    core, chip = me & 1, me >> 1
    rows = values.shape[1]
    for c in range(values.shape[0] // 2):
        one, two = values[2 * c], values[2 * c + 1]
        q = (first // 2 + c) ^ chip
        same[q, start : start + rows, :] = jnp.where(core == 0, one, two).astype(BF)
        other[q, start : start + rows, :] = jnp.where(core == 0, two, one).astype(BF)


def put_smalls(same, other, start, rows):
    block = padded(rows, SMALL)
    for q in range(same.shape[0]):
        same[q, start:, :] = block
        other[q, start:, :] = block


def exchange(value, axis, mask):
    peers = lax.axis_size(axis)
    return lax.ppermute(value, axis, [(i, i ^ mask) for i in range(peers)])


def gather_pieces(slab):
    chips = lax.axis_size("shard") // 2
    pieces = [None] * (2 * chips)
    for q in range(chips):
        pieces[2 * q] = exchange(slab, "shard", 2 * q) if q else slab
    for q in range(chips):
        pieces[2 * q + 1] = exchange(pieces[2 * q], "shard", 1)
    return pieces


def add_pair(here, came):
    return (here.astype(F32) + came.astype(F32)).astype(BF)


def add_cores(same, came):
    return [add_pair(same[q], came[q]) for q in range(1, same.shape[0])]


def to_chips(sums):
    return [exchange(s, "shard", 2 * q + 2) for q, s in enumerate(sums)]


def add_chips(late, same, came, parts):
    half = same.shape[1] // 2
    out = []
    for start in (late * half, (1 - late) * half):
        total = 0.0
        for whole_part in (same, came):
            part = lax.dynamic_slice(whole_part, (0, start, 0), (1, half, D))
            total += part.reshape(half, D).astype(F32)
        for part in parts:
            total += lax.dynamic_slice_in_dim(part, start, half, 0).astype(F32)
        out.append(total.astype(BF))
    return out


def seq_rest(half):
    reach = 4
    while reach < lax.axis_size("seq"):
        half = add_pair(half, exchange(half, "seq", reach))
        reach *= 2
    return half


def tie(first, second):
    first, second = list(first), list(second)
    out = lax.optimization_barrier((*first, *second))
    return list(out[: len(first)]), list(out[len(first) :])


def block_of(slab, c, depth):
    return slab[:, c * depth : (c + 1) * depth, :].reshape(D, D)


def smalls_of(slab, start):
    return jnp.sum(slab[:, start:, :].astype(F32), 0)


def project_body(tokens, halo, *refs):
    shards = len(refs) - 7
    pieces = refs[:shards]
    normed_win, query, key, value, slab, wide, sems = refs[shards:]
    copies = [
        pltpu.make_async_copy(piece, slab.at[shard_place() ^ p], sems.at[p])
        for p, piece in enumerate(pieces)
    ]
    for copy in copies:
        copy.start()
    columns = column_places()
    own = WIN - SHIFT
    for copy in copies:
        copy.wait()
    depth = (slab.shape[1] - SMALL) // 4
    small = smalls_of(slab, 4 * depth)
    gain, offset, bias_q, bias_v = (small[r : r + 1] for r in range(4))
    for r in range(WIN):
        x = (tokens[SHIFT + r] if r < own else halo[r - own]).astype(F32)
        normed, _ = norm_stats(x)
        low = (normed * gain + offset).astype(BF)
        wide[:, r] = dot(columns, low).reshape(WINDOWS, SLOT, D)
    normed_win[...] = wide[...].reshape(PADDED, D).astype(BF)
    query[...] = (dot(normed_win[...], block_of(slab, 0, depth)) + bias_q).astype(BF)
    key[...] = dot(normed_win[...], block_of(slab, 1, depth)).astype(BF)
    value[...] = (dot(normed_win[...], block_of(slab, 2, depth)) + bias_v).astype(BF)


def attn_forward_body(
    slab, reg_rows, reg_lanes, tokens, halo, query, key, value, probs, restored, mixed, wide, bias
):
    n = pl.program_id(0)
    depth = (slab.shape[1] - SMALL) // 4

    @pl.when(n == 0)
    def _():
        small = smalls_of(slab, 4 * depth)
        parts = TAB // D
        empty = (iota((PLACES, LANES), 0) & (SLOT - 1)) == WIN
        turned = []
        for g in range(GROUPS):
            first = 5 + g * parts
            row = jnp.concatenate([small[first + c : first + c + 1] for c in range(parts)], 1)
            row = jnp.broadcast_to(row, (SLOT, TAB))
            row = pltpu.roll(row, 0, 1, stride=GROUP, stride_axis=0)
            rows = [pltpu.roll(row, (2 * WIN - 1) * GROUP * r, 1)[:, :TAB_USED] for r in range(WIN)]
            turned.append(jnp.concatenate(rows, 0).astype(BF))
        for half in range(GROUP // QUAD):
            pick = table_pick(0, half, False)
            for g in range(GROUPS):
                picked = dot(turned[g], pick)
                bias[g * (GROUP // QUAD) + half] = jnp.where(empty, -1e30, picked)

    masks = head_masks()
    penalty = [
        jnp.where(reg_rows[s][:, 0:1] != reg_lanes[s], -100.0, 0.0) for s in range(2)
    ]
    parts = [slice(s * PLACES, (s + 1) * PLACES) for s in range(2)]
    units = [(u, s) for u in range(QUADS) for s in range(2)]
    feats = [slice(u * FEAT, (u + 1) * FEAT) for u in range(QUADS)]
    values, scores = [], []
    for u in range(QUADS):
        q2 = query[:, feats[u]].astype(F32)
        k2 = key[:, feats[u]].astype(F32)
        v2 = value[:, feats[u]].astype(F32)
        for s in range(2):
            values.append(v2[parts[s]].astype(BF))
            scores.append(dot_nt(k2[parts[s]].astype(BF), spread(q2[parts[s]], masks)))
    shares = []
    for (u, s), score in zip(units, scores):
        logits = score * SCALE + bias[u] + penalty[s]
        powers = jnp.exp(logits - jnp.max(logits, 0, keepdims=True))
        shares.append(powers * (1.0 / jnp.sum(powers, 0, keepdims=True)))
    wholes = [dot_tn(p.astype(BF), v) for p, v in zip(shares, values)]
    for (u, s), o in zip(units, wholes):
        wide[2 * n + s, :, :, feats[u]] = own_heads(o).reshape(WIN, SLOT, FEAT)
    for u in range(QUADS):
        probs[0, u] = jnp.concatenate(shares[2 * u : 2 * u + 2], 0).astype(BF)

    @pl.when(n == pl.num_programs(0) - 1)
    def _():
        bias_proj = smalls_of(slab, 4 * depth)[4:5]
        back = places_column()
        own = WIN - SHIFT
        for r in range(WIN):
            here = wide[:, r].reshape(WINDOWS * SLOT, D).astype(BF)
            restored[r * WIDTH : (r + 1) * WIDTH, :] = dot(back, here).astype(BF)
        branch = dot(restored[...], block_of(slab, 3, depth)) + bias_proj
        for r in range(WIN):
            x = (tokens[SHIFT + r] if r < own else halo[r - own]).astype(F32)
            mixed[r * WIDTH : (r + 1) * WIDTH, :] = x + branch[r * WIDTH : (r + 1) * WIDTH]


def gelu_parts(h):
    under = 1.0 + (0.3275911 * 0.5**0.5) * jnp.abs(h)
    t = pl.reciprocal(under, approx=True)
    t = t * (2.0 - under * t)
    bell = jnp.exp2(h * h * (-0.5 / math.log(2.0)))
    poly = t * (
        0.127414796
        + t * (-0.142248368 + t * (0.7107068705 + t * (-0.7265760135 + t * 0.5307027145)))
    )
    tail = poly * bell
    upto = jnp.where(h >= 0, 1.0 - tail, tail)
    return upto, bell * 0.3989422804014327


def mlp_body(
    mixed,
    cotangent,
    cot_halo,
    slab,
    attn_slab,
    restored,
    kept,
    sent,
    grad_mixed,
    grad_win,
    same,
    other,
    normed_low,
    cot,
    out_sum,
    back_sum,
    wide,
):
    me = shard_place()
    shards, height = slab.shape[:2]
    depth = (height - SMALL) // 8
    span = shards * D // FF
    small = smalls_of(slab, 8 * depth)
    gain, offset, bias_o = (small[r : r + 1] for r in range(3))
    own = WIN - SHIFT
    for r in range(WIN):
        part = slice(r * WIDTH, (r + 1) * WIDTH)
        cot[part, :] = cotangent[SHIFT + r] if r < own else cot_halo[r - own]
    normed, _ = norm_stats(mixed[...])
    normed_low[...] = (normed * gain + offset).astype(BF)

    def w_in(c):
        return block_of(slab, c, depth)

    def w_out(c):
        return slab[c * span : (c + 1) * span, 4 * depth : 8 * depth, :].reshape(D, D)

    def ahead(c):
        return dot(normed_low[...], w_in(c)), dot_nt(cot[...], w_out(c))

    vectors = []
    now = ahead(0)
    for c in range(FF // D):
        hidden, grad = now
        if c + 1 < FF // D:
            now = ahead(c + 1)
        hidden = hidden + small[3 + c : 4 + c]
        upto, density = gelu_parts(hidden)
        active = (hidden * upto).astype(BF)
        grad = (grad * (upto + hidden * density)).astype(BF)
        forward = dot(active, w_out(c))
        backward = dot_nt(grad, w_in(c))
        if c == 0:
            out_sum[...] = forward
            back_sum[...] = backward
        else:
            out_sum[...] += forward
            back_sum[...] += backward
        vectors.append(jnp.sum(grad.astype(F32), 0, keepdims=True))
        put_shares(
            me, same, other, c * depth, dot_tn(normed_low[...], grad).reshape(shards, depth, D)
        )
        put_shares(
            me,
            same,
            other,
            4 * depth,
            dot_tn(active, cot[...]).reshape(span, 4 * depth, D),
            c * span,
        )
    result = mixed[...] + out_sum[...] + bias_o
    kept[...] = result[: own * WIDTH]
    sent[...] = result[own * WIDTH :].astype(BF)
    normed, scale = norm_stats(mixed[...])
    g = back_sum[...]
    gain_sum = jnp.sum(g * normed, 0, keepdims=True)
    offset_sum = jnp.sum(g, 0, keepdims=True)
    cot_sum = jnp.sum(cot[...].astype(F32), 0, keepdims=True)
    grad_mixed[...] = cot[...].astype(F32) + norm_back(g, normed, scale, gain)

    branch = grad_mixed[...].astype(BF)
    branch_sum = jnp.sum(branch.astype(F32), 0, keepdims=True)
    proj = dot_tn(restored[...], branch).reshape(shards, depth, D)
    put_shares(me, same, other, 8 * depth, proj)
    put_smalls(same, other, 9 * depth, [gain_sum, offset_sum, cot_sum, branch_sum] + vectors)
    grad_att = dot_nt(branch, block_of(attn_slab, 3, depth)).astype(BF)
    columns = column_places()
    for r in range(WIN):
        wide[:, r] = dot(columns, grad_att[r * WIDTH : (r + 1) * WIDTH]).reshape(WINDOWS, SLOT, D)
    grad_win[...] = wide[...].reshape(PADDED, D).astype(BF)


def attn_backward_body(query, key, value, probs, grad_win, came, out, pairs):
    @pl.when(pl.program_id(0) == 0)
    def _():
        pairs[...] = came[...]

    masks = head_masks()
    parts = [slice(s * PLACES, (s + 1) * PLACES) for s in range(2)]
    feats = [slice(u * FEAT, (u + 1) * FEAT) for u in range(QUADS)]
    keys, shares, grads, queries, slopes = [], [], [], [], []
    for u in range(QUADS):
        q2 = query[:, feats[u]].astype(F32)
        k2 = key[:, feats[u]].astype(F32)
        v2 = value[:, feats[u]].astype(F32)
        go2 = grad_win[:, feats[u]].astype(F32)
        p2 = probs[0, u].astype(F32)
        for part in parts:
            keys.append(k2[part].astype(BF))
            shares.append(p2[part])
            grads.append(spread(go2[part], masks))
            queries.append(spread(q2[part], masks))
            slopes.append(dot_nt(v2[part].astype(BF), grads[-1]))
    lows = []
    for p, dp in zip(shares, slopes):
        inner = jnp.sum(p * dp, 0, keepdims=True)
        lows.append((p * (dp - inner)).astype(BF))
    dvs = [dot(p.astype(BF), go) for p, go in zip(shares, grads)]
    dks = [dot(ds, q) for ds, q in zip(lows, queries)]
    dqs = [dot_tn(ds, k) for ds, k in zip(lows, keys)]
    for u in range(QUADS):
        two = slice(2 * u, 2 * u + 2)
        pairs[u] += lows[2 * u].astype(F32) + lows[2 * u + 1].astype(F32)
        for c, held in enumerate(
            (
                [own_heads(dq) * SCALE for dq in dqs[two]],
                [dk * SCALE for dk in dks[two]],
                dvs[two],
            )
        ):
            both = jnp.concatenate(held, 0).astype(BF)
            out[:, c * D + u * FEAT : c * D + (u + 1) * FEAT] = both


def attn_last_body(
    grad_mixed,
    tokens,
    halo,
    slab,
    normed_win,
    pairs,
    *refs,
):
    grads = refs[:-7]
    kept, sent, same, other_low, other_high, wide, other = refs[-7:]
    me = shard_place()
    shards = slab.shape[0]
    depth = (slab.shape[1] - SMALL) // 4
    small = smalls_of(slab, 4 * depth)
    gain = small[0:1]
    own = WIN - SHIFT
    vectors = []
    for c in range(3):
        cols = slice(c * D, (c + 1) * D)
        g = jnp.concatenate([part[:, cols] for part in grads], 0)
        if c != 1:
            vectors.append(jnp.sum(g.astype(F32), 0, keepdims=True))
        put_shares(
            me, same, other, c * depth, dot_tn(normed_win[...], g).reshape(shards, depth, D)
        )
        part = dot_nt(g, block_of(slab, c, depth))
        total = part if c == 0 else total + part
    wide[...] = total.reshape(WINDOWS, WIN, SLOT, D)
    back = places_column()
    gain_sum = jnp.zeros((1, D), F32)
    bias_sum = jnp.zeros((1, D), F32)
    for r in range(WIN):
        here = wide[:, r].reshape(WINDOWS * SLOT, D).astype(BF)
        g = dot(back, here)
        x = (tokens[SHIFT + r] if r < own else halo[r - own]).astype(F32)
        normed, scale = norm_stats(x)
        gain_sum += jnp.sum(g * normed, 0, keepdims=True)
        bias_sum += jnp.sum(g, 0, keepdims=True)
        grad = grad_mixed[r * WIDTH : (r + 1) * WIDTH, :] + norm_back(g, normed, scale, gain)
        if r < own:
            kept[r * WIDTH : (r + 1) * WIDTH, :] = grad
        else:
            sent[(r - own) * WIDTH : (r - own + 1) * WIDTH, :] = grad.astype(BF)

    rows = [gain_sum, bias_sum, vectors[0], vectors[1]]
    halves = GROUP // QUAD
    picks = [table_pick(1, half, True) for half in range(halves)]
    for g in range(GROUPS):
        laid = jnp.zeros((PLACES, TAB_USED), F32)
        for half in range(halves):
            total = pairs[g * halves + half]
            high = total.astype(BF)
            low = (total - high.astype(F32)).astype(BF)
            laid += dot(high, picks[half]) + dot(low, picks[half])
        laid = jnp.concatenate([laid, jnp.zeros((PLACES, TAB - TAB_USED), F32)], 1)
        total = jnp.zeros((SLOT, TAB), F32)
        for r in range(WIN):
            total += pltpu.roll(
                laid[r * SLOT : (r + 1) * SLOT], (2 * WIN - 1) * GROUP * r, 1
            )
        total = pltpu.roll(total, 0, 1, stride=GROUP, stride_axis=0)
        row = jnp.sum(total, 0, keepdims=True)
        rows += [row[:, c * D : (c + 1) * D] for c in range(TAB // D)]
    put_smalls(same, other, 3 * depth, rows)
    half = other_low.shape[0]
    other_low[...] = other[:half]
    other_high[...] = other[half:]


def region_views(regions, rows, place):
    here = lax.dynamic_slice_in_dim(regions[0], place * rows, rows, 0)
    windows = here.reshape(WIN, WINDOWS, WIN).transpose(1, 0, 2)
    windows = jnp.pad(windows, ((0, 0), (0, 0), (0, SLOT - WIN))).astype(F32)
    windows = windows.reshape(WINDOWS, PLACES)
    by_row = jnp.broadcast_to(windows[:, :, None], (WINDOWS, PLACES, 128))
    by_lane = jnp.tile(jnp.pad(windows, ((0, 0), (0, HOLD - PLACES))), (1, QUAD))
    return by_row, by_lane[:, None, :]


def per_device(
    tokens,
    regions,
    cotangent,
    gain_one,
    bias_one,
    w_qkv,
    bias_qv,
    table,
    w_proj,
    bias_proj,
    gain_two,
    bias_two,
    w_in,
    bias_in,
    w_out,
    bias_out,
):
    images, local_rows, columns, _ = tokens.shape
    assert images == 1 and local_rows == WIN and columns == WIDTH
    shards = lax.axis_size("shard")
    seq = lax.axis_index("seq").astype(jnp.int32)
    chips = shards // 2
    depth = D // shards
    own = WIN - SHIFT
    attn_params = (gain_one[None], bias_one[None], w_qkv, bias_qv, table.T)
    mlp_params = (
        w_proj,
        bias_proj[None],
        gain_two[None],
        bias_two[None],
        w_in,
        bias_in.reshape(-1, 128),
        w_out,
        bias_out[None],
    )
    late = seq & 1
    attn_slab, mlp_slab = kernel_call(
        pack_body,
        [like((4 * depth + SMALL, D), BF), like((8 * depth + SMALL, D), BF)],
        (*attn_params, *mlp_params),
        vmem=60 * 1024 * 1024,
    )
    pieces = gather_pieces(attn_slab)
    mlp_all = lax.all_gather(mlp_slab, "shard")
    tokens_here = tokens[0]
    token_halo = shifted_2(tokens_here[:SHIFT], "seq", -1)
    cot_here = cotangent[0]
    cot_halo = shifted_2(cot_here[:SHIFT], "seq", -1)
    by_row, by_lane = region_views(regions, local_rows, seq)

    normed_win, query, key, value, attn_all = kernel_call(
        project_body,
        [like((PADDED, D), BF)] * 4 + [like((shards, *attn_slab.shape), BF)],
        (tokens_here, token_halo, *pieces),
        scratch=[
            pltpu.VMEM((WINDOWS, WIN, SLOT, D), F32),
            pltpu.SemaphoreType.DMA((shards,)),
        ],
        apart=shards,
    )
    pair_rows = 2 * PLACES
    steps = WINDOWS // 2

    def rows_from(first, width=D):
        return pl.BlockSpec((pair_rows, width), lambda i: (first + i, 0))

    def probs_from(first):
        return pl.BlockSpec((1, QUADS, pair_rows, LANES), lambda i: (first + i, 0, 0, 0))

    def fixed(shape):
        return pl.BlockSpec(shape, lambda i: (0,) * len(shape))

    probs, restored, mixed = kernel_call(
        attn_forward_body,
        [
            like((steps, QUADS, pair_rows, LANES), BF),
            like((TOKENS, D), BF),
            like((TOKENS, D), F32),
        ],
        (attn_all, by_row, by_lane, tokens_here, token_halo, query, key, value),
        grid=(steps,),
        in_blocks=[
            fixed(attn_all.shape),
            pl.BlockSpec((2, *by_row.shape[1:]), lambda i: (i, 0, 0)),
            pl.BlockSpec((2, *by_lane.shape[1:]), lambda i: (i, 0, 0)),
            fixed(tokens_here.shape),
            fixed(token_halo.shape),
            rows_from(0),
            rows_from(0),
            rows_from(0),
        ],
        out_blocks=[probs_from(0), fixed((TOKENS, D)), fixed((TOKENS, D))],
        scratch=[
            pltpu.VMEM((WINDOWS, WIN, SLOT, D), F32),
            pltpu.VMEM((QUADS, PLACES, LANES), F32),
        ],
    )
    share = like((chips, 9 * depth + SMALL, D), BF)
    out_kept, out_sent, grad_mixed, grad_win, mlp_same, mlp_other = kernel_call(
        mlp_body,
        [
            like((own * WIDTH, D), F32),
            like((SHIFT * WIDTH, D), BF),
            like((TOKENS, D), F32),
            like((PADDED, D), BF),
            share,
            share,
        ],
        (mixed, cot_here, cot_halo, mlp_all, attn_all, restored),
        scratch=[
            pltpu.VMEM((TOKENS, D), BF),
            pltpu.VMEM((TOKENS, D), BF),
            pltpu.VMEM((TOKENS, D), F32),
            pltpu.VMEM((TOKENS, D), F32),
            pltpu.VMEM((WINDOWS, WIN, SLOT, D), F32),
        ],
    )

    def backward(first, count, grad_win, came):
        sums = like((QUADS, PLACES, LANES), F32)
        return kernel_call(
            attn_backward_body,
            [like((count * pair_rows, 3 * D), BF), sums],
            (query, key, value, probs, grad_win, came),
            grid=(count,),
            in_blocks=[rows_from(first)] * 3
            + [probs_from(first), rows_from(first), fixed(sums.shape)],
            out_blocks=[rows_from(0, 3 * D), fixed(sums.shape)],
            )

    none = jnp.zeros((QUADS, PLACES, LANES), F32)
    count = steps // 2
    mlp_came = exchange(mlp_other, "shard", 1)
    early, pairs = backward(0, count, grad_win, none)
    sums, (pairs,) = tie(add_cores(mlp_same, mlp_came), [pairs])
    mlp_parts = to_chips(sums)
    late_part, pairs = backward(count, count, grad_win, pairs)
    (out_halo,), (pairs,) = tie([shifted_2(out_sent, "seq", 1)], [pairs])
    tok_kept, tok_sent, attn_same, *attn_others = kernel_call(
        attn_last_body,
        [
            like((own * WIDTH, D), F32),
            like((SHIFT * WIDTH, D), BF),
            like((chips, 3 * depth + SMALL, D), BF),
            like((chips // 2, 3 * depth + SMALL, D), BF),
            like((chips // 2, 3 * depth + SMALL, D), BF),
        ],
        (grad_mixed, tokens_here, token_halo, attn_all, normed_win, pairs, early, late_part),
        scratch=[
            pltpu.VMEM((WINDOWS, WIN, SLOT, D), F32),
            pltpu.VMEM((chips, 3 * depth + SMALL, D), BF),
        ],
    )
    attn_came = [exchange(other, "shard", 1) for other in attn_others]
    mlp_parts, attn_came = tie(mlp_parts, attn_came)
    keep_m, send = add_chips(late, mlp_same, mlp_came, mlp_parts)
    near_m = exchange(send, "seq", 1)
    came = [c[q] for c in attn_came for q in range(chips // 2)]
    attn_parts = to_chips([add_pair(attn_same[q], came[q]) for q in range(1, chips)])
    half_m = add_pair(keep_m, near_m)
    (half_m,), attn_parts = tie([half_m], attn_parts)
    far_m = exchange(half_m, "seq", 2)
    keep, send = add_chips(late, attn_same, attn_came[0], attn_parts)
    near = exchange(send, "seq", 1)
    tok_halo = shifted_2(tok_sent, "seq", 1)
    (near, tok_halo), (far_m,) = tie([near, tok_halo], [far_m])
    half = add_pair(keep, near)
    (half,), (far_m,) = tie([half], [far_m])
    far = exchange(half, "seq", 2)
    half_m = seq_rest(add_pair(half_m, far_m))
    (half_m,), (far,) = tie([half_m], [far])
    back_m = exchange(half_m, "seq", 1)
    half = seq_rest(add_pair(half, far))
    (half,), (back_m,) = tie([half], [back_m])
    back = exchange(half, "seq", 1)
    def unpack(body, params, half, back):
        return kernel_call(
            body,
            [like(p.shape, F32) for p in params],
            (half, back),
            scratch=[
                pltpu.VMEM((2 * half.shape[0], D), BF),
                pltpu.SemaphoreType.DMA((2,)),
            ],
                apart=2,
            vmem=16 * 1024 * 1024,
        )

    mlp_grads = unpack(unpack_mlp_body, mlp_params, half_m, back_m)
    mlp_grads, (back,) = tie(mlp_grads, [back])
    attn_grads = unpack(unpack_attn_body, attn_params, half, back)
    summed = [*attn_grads[:4], attn_grads[4].T, *mlp_grads]

    def joined(halo, kept):
        return jnp.concatenate([halo.astype(F32), kept], 0).reshape(tokens.shape)

    targets = (
        gain_one,
        bias_one,
        w_qkv,
        bias_qv,
        table,
        w_proj,
        bias_proj,
        gain_two,
        bias_two,
        w_in,
        bias_in,
        w_out,
        bias_out,
    )
    grads = [g.reshape(p.shape) for g, p in zip(summed, targets)]
    return (joined(out_halo, out_kept), joined(tok_halo, tok_kept), *grads)


def solution(mesh):
    return jax.shard_map(
        per_device,
        mesh=mesh,
        in_specs=(
            P("shard", "seq", None, None),
            P("shard", None, None),
            P("shard", "seq", None, None),
            P("shard"),
            P("shard"),
            P("shard", None),
            P(None, "shard"),
            P(None, "shard"),
            P("shard", None),
            P("shard"),
            P("shard"),
            P("shard"),
            P("shard", None),
            P("shard"),
            P("shard", None),
            P("shard"),
        ),
        out_specs=(
            P("shard", "seq", None, None),
            P("shard", "seq", None, None),
            P("shard"),
            P("shard"),
            P("shard", None),
            P(None, "shard"),
            P(None, "shard"),
            P("shard", None),
            P("shard"),
            P("shard"),
            P("shard"),
            P("shard", None),
            P("shard"),
            P("shard", None),
            P("shard"),
        ),
        check_vma=False,
    )
```

```python
import math

import jax
import jax.numpy as jnp
from jax import lax
from jax.experimental import pallas as pl
from jax.experimental.pallas import tpu as pltpu
from jax.sharding import PartitionSpec as P

D = 512
HEADS = 16
HEAD = 32
WIN = 7
SHIFT = 3
FF = 2048
WIDTH = 112
WINDOWS = WIDTH // WIN
SLOT = 8
PLACES = WIN * SLOT
GROUP = 8
GROUPS = HEADS // GROUP
QUAD = 4
QUADS = HEADS // QUAD
FEAT = QUAD * HEAD
HOLD = 64
LANES = QUAD * HOLD
TOKENS = WIN * WIDTH
PADDED = WINDOWS * PLACES
TAB = 1536
TAB_USED = 768
SMALL = 32
EPS = 1e-05
SCALE = HEAD**-0.5
BF = jnp.bfloat16
F32 = jnp.float32


def shifted_2(value, axis, by):
    peers = lax.axis_size(axis)
    return lax.ppermute(value, axis, [(i, (i + by) % peers) for i in range(peers)])


def dot(left, right, dims=((1,), (0,))):
    return lax.dot_general(left, right, (dims, ((), ())), preferred_element_type=F32)


def dot_nt(left, right):
    return dot(left, right, ((1,), (1,)))


def dot_tn(left, right):
    return dot(left, right, ((0,), (0,)))


def iota(shape, axis):
    return lax.broadcasted_iota(jnp.int32, shape, axis)


def shard_place():
    return lax.axis_index("shard").astype(jnp.int32)


def late_place():
    return lax.axis_index("seq").astype(jnp.int32) & 1


def one_hot(condition):
    return jnp.where(condition, 1.0, 0.0).astype(BF)


def column_places():
    slot = iota((WINDOWS * SLOT, WIDTH), 0)
    column = iota((WINDOWS * SLOT, WIDTH), 1)
    place = slot & (SLOT - 1)
    wanted = (slot >> 3) * WIN + place + SHIFT
    wanted = jnp.where(wanted >= WIDTH, wanted - WIDTH, wanted)
    return one_hot((wanted == column) & (place < WIN))


def places_column():
    slot = iota((WIDTH, WINDOWS * SLOT), 1)
    column = iota((WIDTH, WINDOWS * SLOT), 0)
    place = slot & (SLOT - 1)
    wanted = (slot >> 3) * WIN + place + SHIFT
    wanted = jnp.where(wanted >= WIDTH, wanted - WIDTH, wanted)
    return one_hot((wanted == column) & (place < WIN))


def head_masks():
    feature = iota((1, FEAT), 1) >> 5
    return [jnp.where(feature == h, 1.0, 0.0).astype(F32) for h in range(QUAD)]


def spread(values, masks):
    empty = jnp.zeros((HOLD - PLACES, FEAT), F32)
    rows = []
    for mask in masks:
        rows += [values * mask, empty]
    return jnp.concatenate(rows, 0).astype(BF)


def own_heads(values):
    feature = iota((PLACES, FEAT), 1) >> 5
    out = values[:PLACES]
    for h in range(1, QUAD):
        out = jnp.where(feature == h, values[h * HOLD : h * HOLD + PLACES], out)
    return out


def table_pick(row_axis, quad, backwards):
    shape = (TAB_USED, LANES) if row_axis == 0 else (LANES, TAB_USED)
    lane = iota(shape, row_axis)
    pair = iota(shape, 1 - row_axis)
    head, place = pair >> 6, pair & (HOLD - 1)
    row, column = place >> 3, place & (SLOT - 1)
    entry = row * (2 * WIN - 1) + column
    if backwards:
        entry = (WIN - 1) * 2 * WIN - entry
    held = head + quad % (GROUP // QUAD) * QUAD
    match = ((lane >> 3) == entry) & ((lane & 7) == held)
    return one_hot(match & (column < WIN) & (row < WIN))


def norm_stats(values):
    average = jnp.mean(values, -1, keepdims=True)
    centered = values - average
    variance = jnp.mean(centered * centered, -1, keepdims=True)
    scale = lax.rsqrt(variance + EPS)
    return centered * scale, scale


def norm_back(grad, normed, scale, gain):
    scaled = grad * gain
    first = jnp.mean(scaled, -1, keepdims=True)
    second = jnp.mean(scaled * normed, -1, keepdims=True)
    return scale * (scaled - first - normed * second)


def whole(memory=pltpu.VMEM):
    return pl.BlockSpec(memory_space=memory)


def kernel_call(
    body, outs, ins, scratch=(), apart=0, grid=None, in_blocks=None, out_blocks=None,
    vmem=16,
    flops=1024,
):
    in_specs = in_blocks or [whole()] * (len(ins) - apart) + [whole(pl.ANY)] * apart
    options = {"grid": grid} if grid else {}
    return pl.pallas_call(
        body,
        out_shape=tuple(outs),
        in_specs=in_specs,
        out_specs=tuple(out_blocks or [whole()] * len(outs)),
        scratch_shapes=list(scratch),
        cost_estimate=pl.CostEstimate(flops=flops, bytes_accessed=1024, transcendentals=0),
        compiler_params=pltpu.CompilerParams(vmem_limit_bytes=vmem * 1024 * 1024),
        **options,
    )(*ins)


def like(shape, dtype):
    return jax.ShapeDtypeStruct(shape, dtype)


def place(vector, lanes, me):
    w = vector.shape[1]
    pick = one_hot(iota((w, lanes), 1) == iota((w, lanes), 0) + me * w)
    wide = jnp.broadcast_to(vector, (8, w))
    return dot(wide.astype(BF), pick)[0:1]


def mine(row, w, me):
    lanes = row.shape[1]
    pick = one_hot(iota((lanes, w), 0) == iota((lanes, w), 1) + me * w)
    wide = jnp.broadcast_to(row, (8, lanes))
    return dot(wide.astype(BF), pick)[0:1]


def padded(rows, height):
    total = sum(r.shape[0] for r in rows)
    return jnp.concatenate(rows + [jnp.zeros((height - total, D), F32)], 0).astype(BF)


def pack_body(
    g1, b1, wqkv, bqv, table, wproj, bproj, g2, b2, win, bin_, wout, bout, attn, mlp
):
    depth = wqkv.shape[0]
    me = shard_place()
    for c in range(3):
        attn[c * depth : (c + 1) * depth, :] = wqkv[:, c * D : (c + 1) * D]
    attn[3 * depth : 4 * depth, :] = wproj[...]
    vectors = (g1[...], b1[...], bqv[0:1, :], bqv[1:2, :], bproj[...])
    rows = [place(v, D, me) for v in vectors]
    held, entries = table.shape
    lane = iota((entries, TAB), 1)
    spot = iota((entries, TAB), 0) * GROUP + TAB - (WIN - 1) * 2 * WIN * GROUP
    spot = jnp.where(spot >= TAB, spot - TAB, spot)
    values = table[...].astype(F32).T
    groups = [jnp.zeros((1, TAB), F32) for _ in range(GROUPS)]
    for h in range(held):
        head = me * held + h
        inside = lane == spot + (head & (GROUP - 1))
        row = jnp.sum(jnp.where(inside, values[:, h : h + 1], 0.0), 0, keepdims=True)
        for g in range(GROUPS):
            groups[g] = groups[g] + jnp.where((head >> 3) == g, row, 0.0)
    for g in range(GROUPS):
        rows += [groups[g][:, c * D : (c + 1) * D] for c in range(TAB // D)]
    attn[4 * depth :, :] = padded(rows, SMALL)
    for c in range(FF // D):
        mlp[c * depth : (c + 1) * depth, :] = win[:, c * D : (c + 1) * D]
    mlp[4 * depth : 8 * depth, :] = wout[...]
    held = jnp.concatenate([bin_[r : r + 1] for r in range(bin_.shape[0])], 1)
    hidden_bias = place(held, FF, me)
    rows = [place(v, D, me) for v in (g2[...], b2[...], bout[...])]
    rows += [hidden_bias[:, c * D : (c + 1) * D] for c in range(FF // D)]
    mlp[8 * depth :, :] = padded(rows, SMALL)


def join_halves(late, half, back, both, sems):
    rows = half.shape[0]
    copies = []
    for n, (part, at) in enumerate(((half, late), (back, 1 - late))):
        to = both.at[pl.ds(pl.multiple_of(at * rows, 16), rows), :]
        copies.append(pltpu.make_async_copy(part, to, sems.at[n]))
    for copy in copies:
        copy.start()
    for copy in copies:
        copy.wait()


def unpack_attn_body(half, back, g1, b1, wqkv, bqv, table, attn, sems):
    depth = wqkv.shape[0]
    me = shard_place()
    join_halves(late_place(), half, back, attn, sems)
    for c in range(3):
        wqkv[:, c * D : (c + 1) * D] = attn[c * depth : (c + 1) * depth, :].astype(F32)
    small = attn[3 * depth :, :].astype(F32)
    g1[...] = mine(small[0:1], depth, me)
    b1[...] = mine(small[1:2], depth, me)
    bqv[0:1, :] = mine(small[2:3], depth, me)
    bqv[1:2, :] = mine(small[3:4], depth, me)
    held, entries = table.shape
    lane = iota((entries, TAB), 1)
    spot = (entries - 1 - iota((entries, TAB), 0)) * GROUP
    parts = TAB // D
    rows = [
        jnp.concatenate([small[4 + g * parts + c : 5 + g * parts + c] for c in range(parts)], 1)
        for g in range(GROUPS)
    ]
    which = iota((entries, held), 1)
    total = jnp.zeros((entries, held), F32)
    for h in range(held):
        head = me * held + h
        row = rows[0]
        for g in range(1, GROUPS):
            row = jnp.where((head >> 3) == g, rows[g], row)
        inside = lane == spot + (head & (GROUP - 1))
        column = jnp.sum(jnp.where(inside, row, 0.0), 1, keepdims=True)
        total = jnp.where(which == h, column, total)
    table[...] = total.T


def unpack_in_body(half, back, win, bin_, both, sems):
    depth = win.shape[0]
    join_halves(late_place(), half, back, both, sems)
    for c in range(FF // D):
        win[:, c * D : (c + 1) * D] = both[c * depth : (c + 1) * depth, :].astype(F32)
    small = both[4 * depth :, :].astype(F32)
    hidden = jnp.concatenate([small[c : c + 1] for c in range(FF // D)], 1)
    hidden = mine(hidden, depth * FF // D, shard_place())
    for r in range(bin_.shape[0]):
        bin_[r : r + 1] = hidden[:, r * 128 : (r + 1) * 128]


def unpack_out_body(half, back, wout, wproj, g2, b2, bout, bproj, both, sems):
    depth = wproj.shape[0]
    me = shard_place()
    join_halves(late_place(), half, back, both, sems)
    wout[...] = both[: 4 * depth, :].astype(F32)
    wproj[...] = both[4 * depth : 5 * depth, :].astype(F32)
    small = both[5 * depth :, :].astype(F32)
    g2[...] = mine(small[0:1], depth, me)
    b2[...] = mine(small[1:2], depth, me)
    bout[...] = mine(small[2:3], depth, me)
    bproj[...] = mine(small[3:4], depth, me)


def put_shares(me, same, other, start, values, first=0):
    core, chip = me & 1, me >> 1
    rows = values.shape[1]
    for c in range(values.shape[0] // 2):
        one, two = values[2 * c], values[2 * c + 1]
        q = (first // 2 + c) ^ chip
        same[q, start : start + rows, :] = jnp.where(core == 0, one, two).astype(BF)
        other[q, start : start + rows, :] = jnp.where(core == 0, two, one).astype(BF)


def put_smalls(same, other, start, rows):
    block = padded(rows, SMALL)
    for q in range(same.shape[0]):
        same[q, start:, :] = block
        other[q, start:, :] = block


def exchange(value, axis, mask):
    peers = lax.axis_size(axis)
    return lax.ppermute(value, axis, [(i, i ^ mask) for i in range(peers)])


def gather_pieces(slab):
    chips = lax.axis_size("shard") // 2
    pieces = [None] * (2 * chips)
    for q in range(chips):
        pieces[2 * q] = exchange(slab, "shard", 2 * q) if q else slab
    for q in range(chips):
        pieces[2 * q + 1] = exchange(pieces[2 * q], "shard", 1)
    return pieces


def add_pair(here, came):
    return (here.astype(F32) + came.astype(F32)).astype(BF)


def add_cores(same, came):
    return [add_pair(same[q], came[q]) for q in range(1, same.shape[0])]


def to_chips(sums):
    return [exchange(s, "shard", 2 * q + 2) for q, s in enumerate(sums)]


def add_chips_body(same, came, *refs):
    parts, (keep, send) = refs[:-2], refs[-2:]
    half = keep.shape[0]
    for at, target in ((late_place(), keep), (1 - late_place(), send)):
        rows = pl.ds(pl.multiple_of(at * half, 16), half)
        total = same[0, rows, :].astype(F32) + came[0, rows, :].astype(F32)
        for part in parts:
            total += part[rows, :].astype(F32)
        target[...] = total.astype(BF)


def add_chips(same, came, parts, flops=1024):
    half = like((same.shape[1] // 2, D), BF)
    return kernel_call(add_chips_body, [half, half], (same, came, *parts), flops=flops)


def seq_rest(half):
    reach = 4
    while reach < lax.axis_size("seq"):
        half = add_pair(half, exchange(half, "seq", reach))
        reach *= 2
    return half


def tie(first, second):
    first, second = list(first), list(second)
    out = lax.optimization_barrier((*first, *second))
    return list(out[: len(first)]), list(out[len(first) :])


def block_of(slab, c, depth):
    return slab[:, c * depth : (c + 1) * depth, :].reshape(D, D)


def smalls_of(slab, start):
    return jnp.sum(slab[:, start:, :].astype(F32), 0)


def project_body(tokens, halo, *refs):
    shards = len(refs) - 7
    pieces = refs[:shards]
    normed_win, query, key, value, slab, wide, sems = refs[shards:]
    copies = [
        pltpu.make_async_copy(piece, slab.at[shard_place() ^ p], sems.at[p])
        for p, piece in enumerate(pieces)
    ]
    for copy in copies:
        copy.start()
    columns = column_places()
    own = WIN - SHIFT
    for copy in copies:
        copy.wait()
    depth = (slab.shape[1] - SMALL) // 4
    small = smalls_of(slab, 4 * depth)
    gain, offset, bias_q, bias_v = (small[r : r + 1] for r in range(4))
    for r in range(WIN):
        x = (tokens[SHIFT + r] if r < own else halo[r - own]).astype(F32)
        normed, _ = norm_stats(x)
        low = (normed * gain + offset).astype(BF)
        wide[:, r] = dot(columns, low).reshape(WINDOWS, SLOT, D)
    normed_win[...] = wide[...].reshape(PADDED, D).astype(BF)
    query[...] = (dot(normed_win[...], block_of(slab, 0, depth)) + bias_q).astype(BF)
    key[...] = dot(normed_win[...], block_of(slab, 1, depth)).astype(BF)
    value[...] = (dot(normed_win[...], block_of(slab, 2, depth)) + bias_v).astype(BF)


def attn_forward_body(
    slab, reg_rows, reg_lanes, tokens, halo, query, key, value, probs, restored, mixed, wide, bias
):
    n = pl.program_id(0)
    depth = (slab.shape[1] - SMALL) // 4

    @pl.when(n == 0)
    def _():
        small = smalls_of(slab, 4 * depth)
        parts = TAB // D
        empty = (iota((PLACES, LANES), 0) & (SLOT - 1)) == WIN
        turned = []
        for g in range(GROUPS):
            first = 5 + g * parts
            row = jnp.concatenate([small[first + c : first + c + 1] for c in range(parts)], 1)
            row = jnp.broadcast_to(row, (SLOT, TAB))
            row = pltpu.roll(row, 0, 1, stride=GROUP, stride_axis=0)
            rows = [pltpu.roll(row, (2 * WIN - 1) * GROUP * r, 1)[:, :TAB_USED] for r in range(WIN)]
            turned.append(jnp.concatenate(rows, 0).astype(BF))
        for half in range(GROUP // QUAD):
            pick = table_pick(0, half, False)
            for g in range(GROUPS):
                picked = dot(turned[g], pick)
                bias[g * (GROUP // QUAD) + half] = jnp.where(empty, -1e30, picked)

    masks = head_masks()
    penalty = [
        jnp.where(reg_rows[s][:, 0:1] != reg_lanes[s], -100.0, 0.0) for s in range(2)
    ]
    parts = [slice(s * PLACES, (s + 1) * PLACES) for s in range(2)]
    units = [(u, s) for u in range(QUADS) for s in range(2)]
    feats = [slice(u * FEAT, (u + 1) * FEAT) for u in range(QUADS)]
    values, scores = [], []
    for u in range(QUADS):
        q2 = query[:, feats[u]].astype(F32)
        k2 = key[:, feats[u]].astype(F32)
        v2 = value[:, feats[u]].astype(F32)
        for s in range(2):
            values.append(v2[parts[s]].astype(BF))
            scores.append(dot_nt(k2[parts[s]].astype(BF), spread(q2[parts[s]], masks)))
    shares = []
    for (u, s), score in zip(units, scores):
        logits = score * SCALE + bias[u] + penalty[s]
        powers = jnp.exp(logits - jnp.max(logits, 0, keepdims=True))
        shares.append(powers * (1.0 / jnp.sum(powers, 0, keepdims=True)))
    wholes = [dot_tn(p.astype(BF), v) for p, v in zip(shares, values)]
    for (u, s), o in zip(units, wholes):
        wide[2 * n + s, :, :, feats[u]] = own_heads(o).reshape(WIN, SLOT, FEAT)
    for u in range(QUADS):
        probs[0, u] = jnp.concatenate(shares[2 * u : 2 * u + 2], 0).astype(BF)

    @pl.when(n == pl.num_programs(0) - 1)
    def _():
        bias_proj = smalls_of(slab, 4 * depth)[4:5]
        back = places_column()
        own = WIN - SHIFT
        for r in range(WIN):
            here = wide[:, r].reshape(WINDOWS * SLOT, D).astype(BF)
            restored[r * WIDTH : (r + 1) * WIDTH, :] = dot(back, here).astype(BF)
        branch = dot(restored[...], block_of(slab, 3, depth)) + bias_proj
        for r in range(WIN):
            x = (tokens[SHIFT + r] if r < own else halo[r - own]).astype(F32)
            mixed[r * WIDTH : (r + 1) * WIDTH, :] = x + branch[r * WIDTH : (r + 1) * WIDTH]


def gelu_parts(h):
    under = 1.0 + (0.3275911 * 0.5**0.5) * jnp.abs(h)
    t = pl.reciprocal(under, approx=True)
    t = t * (2.0 - under * t)
    bell = jnp.exp2(h * h * (-0.5 / math.log(2.0)))
    poly = t * (
        0.127414796
        + t * (-0.142248368 + t * (0.7107068705 + t * (-0.7265760135 + t * 0.5307027145)))
    )
    tail = poly * bell
    upto = jnp.where(h >= 0, 1.0 - tail, tail)
    return upto, bell * 0.3989422804014327


def mlp_forward_body(
    mixed, cotangent, cot_halo, slab, kept, sent, cot, actives, back_sum, vectors, same, other
):
    me = shard_place()
    shards, height = slab.shape[:2]
    depth = (height - SMALL) // 8
    span = shards * D // FF
    chunks = FF // D
    small = smalls_of(slab, 8 * depth)
    vectors[...] = small
    gain, offset, bias_o = (small[r : r + 1] for r in range(3))
    own = WIN - SHIFT
    parts = [slice(r * WIDTH, (r + 1) * WIDTH) for r in range(WIN)]
    lows = []
    for r, part in enumerate(parts):
        cot[part, :] = cotangent[SHIFT + r] if r < own else cot_halo[r - own]
        normed, _ = norm_stats(mixed[part, :])
        lows.append((normed * gain + offset).astype(BF))
    normed_low = jnp.concatenate(lows, 0)

    def w_in(c):
        return block_of(slab, c, depth)

    def w_out(c):
        return slab[c * span : (c + 1) * span, 4 * depth : 8 * depth, :].reshape(D, D)

    hiddens, slopes, grads, forward, backward, bias_sums = {}, {}, {}, None, None, []
    for step in range(-1, chunks + 1):
        ahead, behind = step + 1, step - 1
        products = []
        if ahead < chunks:
            products.append(lambda: hiddens.update({ahead: dot(normed_low, w_in(ahead))}))
            products.append(lambda: slopes.update({ahead: dot_nt(cot[...], w_out(ahead))}))
        if behind >= 0:
            active = actives[:, behind * D : (behind + 1) * D]
            grad = grads.pop(behind)

            def add_forward():
                nonlocal forward
                one = dot(active, w_out(behind))
                forward = one if forward is None else forward + one

            def add_backward():
                nonlocal backward
                one = dot_nt(grad, w_in(behind))
                backward = one if backward is None else backward + one

            def weight():
                one = dot_tn(normed_low, grad).reshape(shards, depth, D)
                put_shares(me, same, other, behind * depth, one)

            products += [add_forward, add_backward, weight]
        rows = []
        if 0 <= step < chunks:
            hidden, slope = hiddens.pop(step), slopes.pop(step)
            bias_sum = 0.0
            for r, part in enumerate(parts):
                h = hidden[part] + small[3 + step : 4 + step]
                upto, density = gelu_parts(h)
                actives[part, step * D : (step + 1) * D] = (h * upto).astype(BF)
                rows.append((slope[part] * (upto + h * density)).astype(BF))
                bias_sum += jnp.sum(rows[-1].astype(F32), 0, keepdims=True)
                if r < len(products):
                    products[r]()
            bias_sums.append(bias_sum)
            grads[step] = jnp.concatenate(rows, 0)
        else:
            for product in products:
                product()
    back_sum[...] = backward
    result = mixed[...] + forward + bias_o
    kept[...] = result[: own * WIDTH]
    sent[...] = result[own * WIDTH :].astype(BF)
    put_smalls(same, other, 4 * depth, bias_sums)


def mlp_backward_body(
    mixed,
    cot,
    actives,
    back_sum,
    vectors,
    attn_slab,
    restored,
    grad_mixed,
    grad_win,
    same,
    other,
    wide,
):
    me = shard_place()
    shards, height = attn_slab.shape[:2]
    depth = (height - SMALL) // 4
    span = shards * D // FF
    gain = vectors[0:1]
    parts = [slice(r * WIDTH, (r + 1) * WIDTH) for r in range(WIN)]
    columns = column_places()
    w_proj = block_of(attn_slab, 3, depth)
    sums = [0.0] * 4
    branches = []
    for r, part in enumerate(parts):
        if r < FF // D:
            one = dot_tn(actives[:, r * D : (r + 1) * D], cot[...])
            put_shares(me, same, other, 0, one.reshape(span, 4 * depth, D), r * span)
        normed, scale = norm_stats(mixed[part, :])
        g = back_sum[part, :]
        c = cot[part, :].astype(F32)
        grad = c + norm_back(g, normed, scale, gain)
        grad_mixed[part, :] = grad
        branch = grad.astype(BF)
        branches.append(branch)
        for n, one in enumerate((g * normed, g, c, branch.astype(F32))):
            sums[n] += jnp.sum(one, 0, keepdims=True)
        grad_att = dot_nt(branch, w_proj).astype(BF)
        wide[:, r] = dot(columns, grad_att).reshape(WINDOWS, SLOT, D)
    proj = dot_tn(restored[...], jnp.concatenate(branches, 0)).reshape(shards, depth, D)
    put_shares(me, same, other, 4 * depth, proj)
    put_smalls(same, other, 5 * depth, sums)
    grad_win[...] = wide[...].reshape(PADDED, D).astype(BF)


def attn_backward_body(query, key, value, probs, grad_win, came, out, pairs):
    @pl.when(pl.program_id(0) == 0)
    def _():
        pairs[...] = came[...]

    masks = head_masks()
    parts = [slice(s * PLACES, (s + 1) * PLACES) for s in range(2)]
    feats = [slice(u * FEAT, (u + 1) * FEAT) for u in range(QUADS)]
    keys, shares, grads, queries, slopes = [], [], [], [], []
    for u in range(QUADS):
        q2 = query[:, feats[u]].astype(F32)
        k2 = key[:, feats[u]].astype(F32)
        v2 = value[:, feats[u]].astype(F32)
        go2 = grad_win[:, feats[u]].astype(F32)
        p2 = probs[0, u].astype(F32)
        for part in parts:
            keys.append(k2[part].astype(BF))
            shares.append(p2[part])
            grads.append(spread(go2[part], masks))
            queries.append(spread(q2[part], masks))
            slopes.append(dot_nt(v2[part].astype(BF), grads[-1]))
    lows = []
    for p, dp in zip(shares, slopes):
        inner = jnp.sum(p * dp, 0, keepdims=True)
        lows.append((p * (dp - inner)).astype(BF))
    dvs = [dot(p.astype(BF), go) for p, go in zip(shares, grads)]
    dks = [dot(ds, q) for ds, q in zip(lows, queries)]
    dqs = [dot_tn(ds, k) for ds, k in zip(lows, keys)]
    for u in range(QUADS):
        two = slice(2 * u, 2 * u + 2)
        pairs[u] += lows[2 * u].astype(F32) + lows[2 * u + 1].astype(F32)
        for c, held in enumerate(
            (
                [own_heads(dq) * SCALE for dq in dqs[two]],
                [dk * SCALE for dk in dks[two]],
                dvs[two],
            )
        ):
            both = jnp.concatenate(held, 0).astype(BF)
            out[:, c * D + u * FEAT : c * D + (u + 1) * FEAT] = both


def attn_last_body(
    grad_mixed,
    tokens,
    halo,
    slab,
    normed_win,
    pairs,
    *refs,
):
    grads = refs[:-7]
    kept, sent, same, other_low, other_high, wide, other = refs[-7:]
    me = shard_place()
    shards = slab.shape[0]
    depth = (slab.shape[1] - SMALL) // 4
    small = smalls_of(slab, 4 * depth)
    gain = small[0:1]
    own = WIN - SHIFT
    vectors = []
    for c in range(3):
        cols = slice(c * D, (c + 1) * D)
        g = jnp.concatenate([part[:, cols] for part in grads], 0)
        if c != 1:
            vectors.append(jnp.sum(g.astype(F32), 0, keepdims=True))
        put_shares(
            me, same, other, c * depth, dot_tn(normed_win[...], g).reshape(shards, depth, D)
        )
        part = dot_nt(g, block_of(slab, c, depth))
        total = part if c == 0 else total + part
    wide[...] = total.reshape(WINDOWS, WIN, SLOT, D)
    back = places_column()
    gain_sum = jnp.zeros((1, D), F32)
    bias_sum = jnp.zeros((1, D), F32)
    for r in range(WIN):
        here = wide[:, r].reshape(WINDOWS * SLOT, D).astype(BF)
        g = dot(back, here)
        x = (tokens[SHIFT + r] if r < own else halo[r - own]).astype(F32)
        normed, scale = norm_stats(x)
        gain_sum += jnp.sum(g * normed, 0, keepdims=True)
        bias_sum += jnp.sum(g, 0, keepdims=True)
        grad = grad_mixed[r * WIDTH : (r + 1) * WIDTH, :] + norm_back(g, normed, scale, gain)
        if r < own:
            kept[r * WIDTH : (r + 1) * WIDTH, :] = grad
        else:
            sent[(r - own) * WIDTH : (r - own + 1) * WIDTH, :] = grad.astype(BF)

    rows = [gain_sum, bias_sum, vectors[0], vectors[1]]
    halves = GROUP // QUAD
    picks = [table_pick(1, half, True) for half in range(halves)]
    for g in range(GROUPS):
        laid = jnp.zeros((PLACES, TAB_USED), F32)
        for half in range(halves):
            total = pairs[g * halves + half]
            high = total.astype(BF)
            low = (total - high.astype(F32)).astype(BF)
            laid += dot(high, picks[half]) + dot(low, picks[half])
        laid = jnp.concatenate([laid, jnp.zeros((PLACES, TAB - TAB_USED), F32)], 1)
        total = jnp.zeros((SLOT, TAB), F32)
        for r in range(WIN):
            total += pltpu.roll(
                laid[r * SLOT : (r + 1) * SLOT], (2 * WIN - 1) * GROUP * r, 1
            )
        total = pltpu.roll(total, 0, 1, stride=GROUP, stride_axis=0)
        row = jnp.sum(total, 0, keepdims=True)
        rows += [row[:, c * D : (c + 1) * D] for c in range(TAB // D)]
    put_smalls(same, other, 3 * depth, rows)
    half = other_low.shape[0]
    other_low[...] = other[:half]
    other_high[...] = other[half:]


def region_views(regions, rows, place):
    here = lax.dynamic_slice_in_dim(regions[0], place * rows, rows, 0)
    windows = here.reshape(WIN, WINDOWS, WIN).transpose(1, 0, 2)
    windows = jnp.pad(windows, ((0, 0), (0, 0), (0, SLOT - WIN))).astype(F32)
    windows = windows.reshape(WINDOWS, PLACES)
    by_row = jnp.broadcast_to(windows[:, :, None], (WINDOWS, PLACES, 128))
    by_lane = jnp.tile(jnp.pad(windows, ((0, 0), (0, HOLD - PLACES))), (1, QUAD))
    return by_row, by_lane[:, None, :]


def per_device(
    tokens,
    regions,
    cotangent,
    gain_one,
    bias_one,
    w_qkv,
    bias_qv,
    table,
    w_proj,
    bias_proj,
    gain_two,
    bias_two,
    w_in,
    bias_in,
    w_out,
    bias_out,
):
    images, local_rows, columns, _ = tokens.shape
    assert images == 1 and local_rows == WIN and columns == WIDTH
    shards = lax.axis_size("shard")
    seq = lax.axis_index("seq").astype(jnp.int32)
    chips = shards // 2
    depth = D // shards
    own = WIN - SHIFT
    attn_params = (gain_one[None], bias_one[None], w_qkv, bias_qv, table.T)
    bin_rows = bias_in.reshape(-1, 128)
    mlp_params = (
        w_proj,
        bias_proj[None],
        gain_two[None],
        bias_two[None],
        w_in,
        bin_rows,
        w_out,
        bias_out[None],
    )
    attn_slab, mlp_slab = kernel_call(
        pack_body,
        [like((4 * depth + SMALL, D), BF), like((8 * depth + SMALL, D), BF)],
        (*attn_params, *mlp_params),
        vmem=60,
    )
    pieces = gather_pieces(attn_slab)
    mlp_all = lax.all_gather(mlp_slab, "shard")
    tokens_here = tokens[0]
    token_halo = shifted_2(tokens_here[:SHIFT], "seq", -1)
    cot_here = cotangent[0]
    cot_halo = shifted_2(cot_here[:SHIFT], "seq", -1)
    by_row, by_lane = region_views(regions, local_rows, seq)

    normed_win, query, key, value, attn_all = kernel_call(
        project_body,
        [like((PADDED, D), BF)] * 4 + [like((shards, *attn_slab.shape), BF)],
        (tokens_here, token_halo, *pieces),
        scratch=[
            pltpu.VMEM((WINDOWS, WIN, SLOT, D), F32),
            pltpu.SemaphoreType.DMA((shards,)),
        ],
        apart=shards,
    )
    pair_rows = 2 * PLACES
    steps = WINDOWS // 2

    def rows_from(first, width=D):
        return pl.BlockSpec((pair_rows, width), lambda i: (first + i, 0))

    def probs_from(first):
        return pl.BlockSpec((1, QUADS, pair_rows, LANES), lambda i: (first + i, 0, 0, 0))

    def fixed(shape):
        return pl.BlockSpec(shape, lambda i: (0,) * len(shape))

    probs, restored, mixed = kernel_call(
        attn_forward_body,
        [
            like((steps, QUADS, pair_rows, LANES), BF),
            like((TOKENS, D), BF),
            like((TOKENS, D), F32),
        ],
        (attn_all, by_row, by_lane, tokens_here, token_halo, query, key, value),
        grid=(steps,),
        in_blocks=[
            fixed(attn_all.shape),
            pl.BlockSpec((2, *by_row.shape[1:]), lambda i: (i, 0, 0)),
            pl.BlockSpec((2, *by_lane.shape[1:]), lambda i: (i, 0, 0)),
            fixed(tokens_here.shape),
            fixed(token_halo.shape),
            rows_from(0),
            rows_from(0),
            rows_from(0),
        ],
        out_blocks=[probs_from(0), fixed((TOKENS, D)), fixed((TOKENS, D))],
        scratch=[
            pltpu.VMEM((WINDOWS, WIN, SLOT, D), F32),
            pltpu.VMEM((QUADS, PLACES, LANES), F32),
        ],
    )
    share_a = like((chips, 4 * depth + SMALL, D), BF)
    share_b = like((chips, 5 * depth + SMALL, D), BF)
    out_kept, out_sent, cot, actives, back_sum, vectors, same_a, other_a = kernel_call(
        mlp_forward_body,
        [
            like((own * WIDTH, D), F32),
            like((SHIFT * WIDTH, D), BF),
            like((TOKENS, D), BF),
            like((TOKENS, FF), BF),
            like((TOKENS, D), F32),
            like((SMALL, D), F32),
            share_a,
            share_a,
        ],
        (mixed, cot_here, cot_halo, mlp_all),
        vmem=24,
    )
    grad_mixed, grad_win, same_b, other_b = kernel_call(
        mlp_backward_body,
        [like((TOKENS, D), F32), like((PADDED, D), BF), share_b, share_b],
        (mixed, cot, actives, back_sum, vectors, attn_all, restored),
        scratch=[pltpu.VMEM((WINDOWS, WIN, SLOT, D), F32)],
    )

    def backward(first, count, grad_win, came):
        sums = like((QUADS, PLACES, LANES), F32)
        return kernel_call(
            attn_backward_body,
            [like((count * pair_rows, 3 * D), BF), sums],
            (query, key, value, probs, grad_win, came),
            grid=(count,),
            in_blocks=[rows_from(first)] * 3
            + [probs_from(first), rows_from(first), fixed(sums.shape)],
            out_blocks=[rows_from(0, 3 * D), fixed(sums.shape)],
            )

    none = jnp.zeros((QUADS, PLACES, LANES), F32)
    count = steps // 2
    came_a = exchange(other_a, "shard", 1)
    sums, (grad_win,) = tie(add_cores(same_a, came_a), [grad_win])
    parts_a = to_chips(sums)
    came_b = exchange(other_b, "shard", 1)
    early, pairs = backward(0, count, grad_win, none)
    sums, (pairs,) = tie(add_cores(same_b, came_b), [pairs])
    parts_b = to_chips(sums)
    late_part, pairs = backward(count, count, grad_win, pairs)
    parts_a, (pairs,) = tie(parts_a, [pairs])
    (out_halo,), (pairs,) = tie([shifted_2(out_sent, "seq", 1)], [pairs])
    tok_kept, tok_sent, attn_same, *attn_others = kernel_call(
        attn_last_body,
        [
            like((own * WIDTH, D), F32),
            like((SHIFT * WIDTH, D), BF),
            like((chips, 3 * depth + SMALL, D), BF),
            like((chips // 2, 3 * depth + SMALL, D), BF),
            like((chips // 2, 3 * depth + SMALL, D), BF),
        ],
        (grad_mixed, tokens_here, token_halo, attn_all, normed_win, pairs, early, late_part),
        scratch=[
            pltpu.VMEM((WINDOWS, WIN, SLOT, D), F32),
            pltpu.VMEM((chips, 3 * depth + SMALL, D), BF),
        ],
    )
    attn_came = [exchange(other, "shard", 1) for other in attn_others]
    keep_a, send = add_chips(same_a, came_a, parts_a)
    (send,), parts_b = tie([send], parts_b)
    near_a = exchange(send, "seq", 1)
    keep_b, send = add_chips(same_b, came_b, parts_b, 10_000_000_000)
    (send,), attn_came = tie([send], attn_came)
    near_b = exchange(send, "seq", 1)
    came = [c[q] for c in attn_came for q in range(chips // 2)]
    sums = [add_pair(attn_same[q], came[q]) for q in range(1, chips)]
    sums, (near_a,) = tie(sums, [near_a])
    attn_parts = to_chips(sums)
    half_a = add_pair(keep_a, near_a)
    (half_a,), (near_b,) = tie([half_a], [near_b])
    far_a = exchange(half_a, "seq", 2)
    half_b = add_pair(keep_b, near_b)
    (half_b,), attn_parts = tie([half_b], attn_parts)
    far_b = exchange(half_b, "seq", 2)
    keep, send = add_chips(attn_same, attn_came[0], attn_parts)
    tok_halo = shifted_2(tok_sent, "seq", 1)
    (keep, send, tok_halo), (far_a,) = tie([keep, send, tok_halo], [far_a])
    near = exchange(send, "seq", 1)
    half_a = seq_rest(add_pair(half_a, far_a))
    (half_a,), (near,) = tie([half_a], [near])
    back_a = exchange(half_a, "seq", 1)
    half = add_pair(keep, near)
    (half,), (far_b,) = tie([half], [far_b])
    far = exchange(half, "seq", 2)
    half_b = seq_rest(add_pair(half_b, far_b))
    (half_b,), (far,) = tie([half_b], [far])
    back_b = exchange(half_b, "seq", 1)
    half = seq_rest(add_pair(half, far))
    (half,), (back_a,) = tie([half], [back_a])
    back = exchange(half, "seq", 1)
    def unpack(body, params, half, back):
        return kernel_call(
            body,
            [like(p.shape, F32) for p in params],
            (half, back),
            scratch=[
                pltpu.VMEM((2 * half.shape[0], D), BF),
                pltpu.SemaphoreType.DMA((2,)),
            ],
                apart=2,
        )

    in_grads = unpack(unpack_in_body, (w_in, bin_rows), half_a, back_a)
    in_grads, (back_b,) = tie(in_grads, [back_b])
    column = gain_two[None]
    out_grads = unpack(unpack_out_body, (w_out, w_proj, *[column] * 4), half_b, back_b)
    out_grads, (back,) = tie(out_grads, [back])
    attn_grads = unpack(unpack_attn_body, attn_params, half, back)
    g_wout, g_wproj, g_gain, g_offset, g_bout, g_bproj = out_grads
    summed = [*attn_grads[:4], attn_grads[4].T, g_wproj, g_bproj, g_gain, g_offset]
    summed += [*in_grads, g_wout, g_bout]

    def joined(halo, kept):
        return jnp.concatenate([halo.astype(F32), kept], 0).reshape(tokens.shape)

    targets = (
        gain_one,
        bias_one,
        w_qkv,
        bias_qv,
        table,
        w_proj,
        bias_proj,
        gain_two,
        bias_two,
        w_in,
        bias_in,
        w_out,
        bias_out,
    )
    grads = [g.reshape(p.shape) for g, p in zip(summed, targets)]
    return (joined(out_halo, out_kept), joined(tok_halo, tok_kept), *grads)


def solution(mesh):
    return jax.shard_map(
        per_device,
        mesh=mesh,
        in_specs=(
            P("shard", "seq", None, None),
            P("shard", None, None),
            P("shard", "seq", None, None),
            P("shard"),
            P("shard"),
            P("shard", None),
            P(None, "shard"),
            P(None, "shard"),
            P("shard", None),
            P("shard"),
            P("shard"),
            P("shard"),
            P("shard", None),
            P("shard"),
            P("shard", None),
            P("shard"),
        ),
        out_specs=(
            P("shard", "seq", None, None),
            P("shard", "seq", None, None),
            P("shard"),
            P("shard"),
            P("shard", None),
            P(None, "shard"),
            P(None, "shard"),
            P("shard", None),
            P("shard"),
            P("shard"),
            P("shard"),
            P("shard", None),
            P("shard"),
            P("shard", None),
            P("shard"),
        ),
        check_vma=False,
    )
```

```python
import math

import jax
import jax.numpy as jnp
from jax import lax
from jax.experimental import pallas as pl
from jax.experimental.pallas import tpu as pltpu
from jax.sharding import PartitionSpec as P

D = 512
HEADS = 16
HEAD = 32
WIN = 7
SHIFT = 3
FF = 2048
WIDTH = 112
WINDOWS = WIDTH // WIN
SLOT = 8
PLACES = WIN * SLOT
GROUP = 8
GROUPS = HEADS // GROUP
QUAD = 4
QUADS = HEADS // QUAD
FEAT = QUAD * HEAD
HOLD = 64
LANES = QUAD * HOLD
TOKENS = WIN * WIDTH
PADDED = WINDOWS * PLACES
TAB = 1536
TAB_USED = 768
SMALL = 32
EPS = 1e-05
SCALE = HEAD**-0.5
BF = jnp.bfloat16
F32 = jnp.float32


def shifted_2(value, axis, by):
    peers = lax.axis_size(axis)
    return lax.ppermute(value, axis, [(i, (i + by) % peers) for i in range(peers)])


def dot(left, right, dims=((1,), (0,))):
    return lax.dot_general(left, right, (dims, ((), ())), preferred_element_type=F32)


def dot_nt(left, right):
    return dot(left, right, ((1,), (1,)))


def dot_tn(left, right):
    return dot(left, right, ((0,), (0,)))


def iota(shape, axis):
    return lax.broadcasted_iota(jnp.int32, shape, axis)


def shard_place():
    return lax.axis_index("shard").astype(jnp.int32)


def late_place():
    return lax.axis_index("seq").astype(jnp.int32) & 1


def one_hot(condition):
    return jnp.where(condition, 1.0, 0.0).astype(BF)


def column_places():
    slot = iota((WINDOWS * SLOT, WIDTH), 0)
    column = iota((WINDOWS * SLOT, WIDTH), 1)
    place = slot & (SLOT - 1)
    wanted = (slot >> 3) * WIN + place + SHIFT
    wanted = jnp.where(wanted >= WIDTH, wanted - WIDTH, wanted)
    return one_hot((wanted == column) & (place < WIN))


def places_column():
    slot = iota((WIDTH, WINDOWS * SLOT), 1)
    column = iota((WIDTH, WINDOWS * SLOT), 0)
    place = slot & (SLOT - 1)
    wanted = (slot >> 3) * WIN + place + SHIFT
    wanted = jnp.where(wanted >= WIDTH, wanted - WIDTH, wanted)
    return one_hot((wanted == column) & (place < WIN))


def head_masks():
    feature = iota((1, FEAT), 1) >> 5
    return [jnp.where(feature == h, 1.0, 0.0).astype(F32) for h in range(QUAD)]


def spread(values, masks):
    empty = jnp.zeros((HOLD - PLACES, FEAT), F32)
    rows = []
    for mask in masks:
        rows += [values * mask, empty]
    return jnp.concatenate(rows, 0).astype(BF)


def own_heads(values):
    feature = iota((PLACES, FEAT), 1) >> 5
    out = values[:PLACES]
    for h in range(1, QUAD):
        out = jnp.where(feature == h, values[h * HOLD : h * HOLD + PLACES], out)
    return out


def table_pick(row_axis, quad, backwards):
    shape = (TAB_USED, LANES) if row_axis == 0 else (LANES, TAB_USED)
    lane = iota(shape, row_axis)
    pair = iota(shape, 1 - row_axis)
    head, place = pair >> 6, pair & (HOLD - 1)
    row, column = place >> 3, place & (SLOT - 1)
    entry = row * (2 * WIN - 1) + column
    if backwards:
        entry = (WIN - 1) * 2 * WIN - entry
    held = head + quad % (GROUP // QUAD) * QUAD
    match = ((lane >> 3) == entry) & ((lane & 7) == held)
    return one_hot(match & (column < WIN) & (row < WIN))


def norm_stats(values):
    average = jnp.mean(values, -1, keepdims=True)
    centered = values - average
    variance = jnp.mean(centered * centered, -1, keepdims=True)
    scale = lax.rsqrt(variance + EPS)
    return centered * scale, scale


def norm_back(grad, normed, scale, gain):
    scaled = grad * gain
    first = jnp.mean(scaled, -1, keepdims=True)
    second = jnp.mean(scaled * normed, -1, keepdims=True)
    return scale * (scaled - first - normed * second)


def whole(memory=pltpu.VMEM):
    return pl.BlockSpec(memory_space=memory)


def kernel_call(
    body, outs, ins, scratch=(), apart=0, grid=None, in_blocks=None, out_blocks=None,
    vmem=16,
    flops=1024,
):
    in_specs = in_blocks or [whole()] * (len(ins) - apart) + [whole(pl.ANY)] * apart
    options = {"grid": grid} if grid else {}
    return pl.pallas_call(
        body,
        out_shape=tuple(outs),
        in_specs=in_specs,
        out_specs=tuple(out_blocks or [whole()] * len(outs)),
        scratch_shapes=list(scratch),
        cost_estimate=pl.CostEstimate(flops=flops, bytes_accessed=1024, transcendentals=0),
        compiler_params=pltpu.CompilerParams(vmem_limit_bytes=vmem * 1024 * 1024),
        **options,
    )(*ins)


def like(shape, dtype):
    return jax.ShapeDtypeStruct(shape, dtype)


def place(vector, lanes, me):
    w = vector.shape[1]
    pick = one_hot(iota((w, lanes), 1) == iota((w, lanes), 0) + me * w)
    wide = jnp.broadcast_to(vector, (8, w))
    return dot(wide.astype(BF), pick)[0:1]


def mine(row, w, me):
    lanes = row.shape[1]
    pick = one_hot(iota((lanes, w), 0) == iota((lanes, w), 1) + me * w)
    wide = jnp.broadcast_to(row, (8, lanes))
    return dot(wide.astype(BF), pick)[0:1]


def padded(rows, height):
    total = sum(r.shape[0] for r in rows)
    return jnp.concatenate(rows + [jnp.zeros((height - total, D), F32)], 0).astype(BF)


def pack_body(
    g1, b1, wqkv, bqv, table, wproj, bproj, g2, b2, win, bin_, wout, bout, attn, mlp, out
):
    depth = wqkv.shape[0]
    me = shard_place()
    for c in range(3):
        attn[c * depth : (c + 1) * depth, :] = wqkv[:, c * D : (c + 1) * D]
    attn[3 * depth : 4 * depth, :] = wproj[...]
    vectors = (g1[...], b1[...], bqv[0:1, :], bqv[1:2, :], bproj[...])
    rows = [place(v, D, me) for v in vectors]
    held, entries = table.shape
    lane = iota((entries, TAB), 1)
    spot = iota((entries, TAB), 0) * GROUP + TAB - (WIN - 1) * 2 * WIN * GROUP
    spot = jnp.where(spot >= TAB, spot - TAB, spot)
    values = table[...].astype(F32).T
    groups = [jnp.zeros((1, TAB), F32) for _ in range(GROUPS)]
    for h in range(held):
        head = me * held + h
        inside = lane == spot + (head & (GROUP - 1))
        row = jnp.sum(jnp.where(inside, values[:, h : h + 1], 0.0), 0, keepdims=True)
        for g in range(GROUPS):
            groups[g] = groups[g] + jnp.where((head >> 3) == g, row, 0.0)
    for g in range(GROUPS):
        rows += [groups[g][:, c * D : (c + 1) * D] for c in range(TAB // D)]
    attn[4 * depth :, :] = padded(rows, SMALL)
    for c in range(FF // D):
        mlp[c * depth : (c + 1) * depth, :] = win[:, c * D : (c + 1) * D]
    out[...] = wout[...]
    held = jnp.concatenate([bin_[r : r + 1] for r in range(bin_.shape[0])], 1)
    hidden_bias = place(held, FF, me)
    rows = [place(v, D, me) for v in (g2[...], b2[...], bout[...])]
    rows += [hidden_bias[:, c * D : (c + 1) * D] for c in range(FF // D)]
    mlp[4 * depth :, :] = padded(rows, SMALL)


def join_halves(late, half, back, both, sems):
    rows = half.shape[0]
    copies = []
    for n, (part, at) in enumerate(((half, late), (back, 1 - late))):
        to = both.at[pl.ds(pl.multiple_of(at * rows, 16), rows), :]
        copies.append(pltpu.make_async_copy(part, to, sems.at[n]))
    for copy in copies:
        copy.start()
    for copy in copies:
        copy.wait()


def unpack_attn_body(half, back, g1, b1, wqkv, bqv, table, attn, sems):
    depth = wqkv.shape[0]
    me = shard_place()
    join_halves(late_place(), half, back, attn, sems)
    for c in range(3):
        wqkv[:, c * D : (c + 1) * D] = attn[c * depth : (c + 1) * depth, :].astype(F32)
    small = attn[3 * depth :, :].astype(F32)
    g1[...] = mine(small[0:1], depth, me)
    b1[...] = mine(small[1:2], depth, me)
    bqv[0:1, :] = mine(small[2:3], depth, me)
    bqv[1:2, :] = mine(small[3:4], depth, me)
    held, entries = table.shape
    lane = iota((entries, TAB), 1)
    spot = (entries - 1 - iota((entries, TAB), 0)) * GROUP
    parts = TAB // D
    rows = [
        jnp.concatenate([small[4 + g * parts + c : 5 + g * parts + c] for c in range(parts)], 1)
        for g in range(GROUPS)
    ]
    which = iota((entries, held), 1)
    total = jnp.zeros((entries, held), F32)
    for h in range(held):
        head = me * held + h
        row = rows[0]
        for g in range(1, GROUPS):
            row = jnp.where((head >> 3) == g, rows[g], row)
        inside = lane == spot + (head & (GROUP - 1))
        column = jnp.sum(jnp.where(inside, row, 0.0), 1, keepdims=True)
        total = jnp.where(which == h, column, total)
    table[...] = total.T


def unpack_in_body(half, back, win, bin_, both, sems):
    depth = win.shape[0]
    join_halves(late_place(), half, back, both, sems)
    for c in range(FF // D):
        win[:, c * D : (c + 1) * D] = both[c * depth : (c + 1) * depth, :].astype(F32)
    small = both[4 * depth :, :].astype(F32)
    hidden = jnp.concatenate([small[c : c + 1] for c in range(FF // D)], 1)
    hidden = mine(hidden, depth * FF // D, shard_place())
    for r in range(bin_.shape[0]):
        bin_[r : r + 1] = hidden[:, r * 128 : (r + 1) * 128]


def unpack_out_body(half, back, wout, wproj, g2, b2, bout, bproj, both, sems):
    depth = wproj.shape[0]
    me = shard_place()
    join_halves(late_place(), half, back, both, sems)
    wout[...] = both[: 4 * depth, :].astype(F32)
    wproj[...] = both[4 * depth : 5 * depth, :].astype(F32)
    small = both[5 * depth :, :].astype(F32)
    g2[...] = mine(small[0:1], depth, me)
    b2[...] = mine(small[1:2], depth, me)
    bout[...] = mine(small[2:3], depth, me)
    bproj[...] = mine(small[3:4], depth, me)


def put_shares(me, same, other, start, values, first=0):
    core, chip = me & 1, me >> 1
    rows = values.shape[1]
    for c in range(values.shape[0] // 2):
        one, two = values[2 * c], values[2 * c + 1]
        q = (first // 2 + c) ^ chip
        same[q, start : start + rows, :] = jnp.where(core == 0, one, two).astype(BF)
        other[q, start : start + rows, :] = jnp.where(core == 0, two, one).astype(BF)


def put_smalls(same, other, start, rows):
    block = padded(rows, SMALL)
    for q in range(same.shape[0]):
        same[q, start:, :] = block
        other[q, start:, :] = block


def exchange(value, axis, mask):
    peers = lax.axis_size(axis)
    return lax.ppermute(value, axis, [(i, i ^ mask) for i in range(peers)])


def gather_pieces(slab):
    chips = lax.axis_size("shard") // 2
    pieces = [None] * (2 * chips)
    for q in range(chips):
        pieces[2 * q] = exchange(slab, "shard", 2 * q) if q else slab
    for q in range(chips):
        pieces[2 * q + 1] = exchange(pieces[2 * q], "shard", 1)
    return pieces


def add_pair(here, came):
    return (here.astype(F32) + came.astype(F32)).astype(BF)


def add_cores(same, came):
    return [add_pair(same[q], came[q]) for q in range(1, same.shape[0])]


def to_chips(sums):
    return [exchange(s, "shard", 2 * q + 2) for q, s in enumerate(sums)]


def add_chips_body(same, came, *refs):
    parts, (keep, send) = refs[:-2], refs[-2:]
    half = keep.shape[0]
    for at, target in ((late_place(), keep), (1 - late_place(), send)):
        rows = pl.ds(pl.multiple_of(at * half, 16), half)
        total = same[0, rows, :].astype(F32) + came[0, rows, :].astype(F32)
        for part in parts:
            total += part[rows, :].astype(F32)
        target[...] = total.astype(BF)


def add_chips(same, came, parts, flops=1024):
    half = like((same.shape[1] // 2, D), BF)
    return kernel_call(add_chips_body, [half, half], (same, came, *parts), flops=flops)


def seq_rest(half):
    reach = 4
    while reach < lax.axis_size("seq"):
        half = add_pair(half, exchange(half, "seq", reach))
        reach *= 2
    return half


def tie(first, second):
    first, second = list(first), list(second)
    out = lax.optimization_barrier((*first, *second))
    return list(out[: len(first)]), list(out[len(first) :])


def block_of(slab, c, depth):
    me = shard_place()
    rows = [slab[k ^ me, c * depth : (c + 1) * depth, :] for k in range(slab.shape[0])]
    return jnp.concatenate(rows, 0)


def smalls_of(slab, start):
    return jnp.sum(slab[:, start:, :].astype(F32), 0)


def project_body(tokens, halo, slab, normed_win, query, key, value, wide):
    columns = column_places()
    own = WIN - SHIFT
    depth = (slab.shape[1] - SMALL) // 4
    small = smalls_of(slab, 4 * depth)
    gain, offset, bias_q, bias_v = (small[r : r + 1] for r in range(4))
    for r in range(WIN):
        x = (tokens[SHIFT + r] if r < own else halo[r - own]).astype(F32)
        normed, _ = norm_stats(x)
        low = (normed * gain + offset).astype(BF)
        wide[:, r] = dot(columns, low).reshape(WINDOWS, SLOT, D)
    normed_win[...] = wide[...].reshape(PADDED, D).astype(BF)
    query[...] = (dot(normed_win[...], block_of(slab, 0, depth)) + bias_q).astype(BF)
    key[...] = dot(normed_win[...], block_of(slab, 1, depth)).astype(BF)
    value[...] = (dot(normed_win[...], block_of(slab, 2, depth)) + bias_v).astype(BF)


def attn_forward_body(
    slab, reg_rows, reg_lanes, tokens, halo, query, key, value, probs, restored, mixed, wide, bias
):
    n = pl.program_id(0)
    depth = (slab.shape[1] - SMALL) // 4

    @pl.when(n == 0)
    def _():
        small = smalls_of(slab, 4 * depth)
        parts = TAB // D
        empty = (iota((PLACES, LANES), 0) & (SLOT - 1)) == WIN
        turned = []
        for g in range(GROUPS):
            first = 5 + g * parts
            row = jnp.concatenate([small[first + c : first + c + 1] for c in range(parts)], 1)
            row = jnp.broadcast_to(row, (SLOT, TAB))
            row = pltpu.roll(row, 0, 1, stride=GROUP, stride_axis=0)
            rows = [pltpu.roll(row, (2 * WIN - 1) * GROUP * r, 1)[:, :TAB_USED] for r in range(WIN)]
            turned.append(jnp.concatenate(rows, 0).astype(BF))
        for half in range(GROUP // QUAD):
            pick = table_pick(0, half, False)
            for g in range(GROUPS):
                picked = dot(turned[g], pick)
                bias[g * (GROUP // QUAD) + half] = jnp.where(empty, -1e30, picked)

    masks = head_masks()
    penalty = [
        jnp.where(reg_rows[s][:, 0:1] != reg_lanes[s], -100.0, 0.0) for s in range(2)
    ]
    parts = [slice(s * PLACES, (s + 1) * PLACES) for s in range(2)]
    units = [(u, s) for u in range(QUADS) for s in range(2)]
    feats = [slice(u * FEAT, (u + 1) * FEAT) for u in range(QUADS)]
    values, scores = [], []
    for u in range(QUADS):
        q2 = query[:, feats[u]].astype(F32)
        k2 = key[:, feats[u]].astype(F32)
        v2 = value[:, feats[u]].astype(F32)
        for s in range(2):
            values.append(v2[parts[s]].astype(BF))
            scores.append(dot_nt(k2[parts[s]].astype(BF), spread(q2[parts[s]], masks)))
    shares = []
    for (u, s), score in zip(units, scores):
        logits = score * SCALE + bias[u] + penalty[s]
        powers = jnp.exp(logits - jnp.max(logits, 0, keepdims=True))
        shares.append(powers * (1.0 / jnp.sum(powers, 0, keepdims=True)))
    wholes = [dot_tn(p.astype(BF), v) for p, v in zip(shares, values)]
    for (u, s), o in zip(units, wholes):
        wide[2 * n + s, :, :, feats[u]] = own_heads(o).reshape(WIN, SLOT, FEAT)
    for u in range(QUADS):
        probs[0, u] = jnp.concatenate(shares[2 * u : 2 * u + 2], 0).astype(BF)

    @pl.when(n == pl.num_programs(0) - 1)
    def _():
        bias_proj = smalls_of(slab, 4 * depth)[4:5]
        back = places_column()
        own = WIN - SHIFT
        for r in range(WIN):
            here = wide[:, r].reshape(WINDOWS * SLOT, D).astype(BF)
            restored[r * WIDTH : (r + 1) * WIDTH, :] = dot(back, here).astype(BF)
        branch = dot(restored[...], block_of(slab, 3, depth)) + bias_proj
        for r in range(WIN):
            x = (tokens[SHIFT + r] if r < own else halo[r - own]).astype(F32)
            mixed[r * WIDTH : (r + 1) * WIDTH, :] = x + branch[r * WIDTH : (r + 1) * WIDTH]


def gelu_parts(h):
    under = 1.0 + (0.3275911 * 0.5**0.5) * jnp.abs(h)
    t = pl.reciprocal(under, approx=True)
    t = t * (2.0 - under * t)
    bell = jnp.exp2(h * h * (-0.5 / math.log(2.0)))
    poly = t * (
        0.127414796
        + t * (-0.142248368 + t * (0.7107068705 + t * (-0.7265760135 + t * 0.5307027145)))
    )
    tail = poly * bell
    upto = jnp.where(h >= 0, 1.0 - tail, tail)
    return upto, bell * 0.3989422804014327


def mlp_forward_body(
    mixed,
    cotangent,
    cot_halo,
    slab,
    out_slab,
    kept,
    sent,
    cot,
    actives,
    back_sum,
    vectors,
    same,
    other,
):
    me = shard_place()
    shards, height = slab.shape[:2]
    depth = (height - SMALL) // 4
    span = shards * D // FF
    chunks = FF // D
    small = smalls_of(slab, 4 * depth)
    vectors[...] = small
    gain, offset, bias_o = (small[r : r + 1] for r in range(3))
    own = WIN - SHIFT
    parts = [slice(r * WIDTH, (r + 1) * WIDTH) for r in range(WIN)]
    lows = []
    for r, part in enumerate(parts):
        cot[part, :] = cotangent[SHIFT + r] if r < own else cot_halo[r - own]
        normed, _ = norm_stats(mixed[part, :])
        lows.append((normed * gain + offset).astype(BF))
    normed_low = jnp.concatenate(lows, 0)

    def w_in(c):
        return slab[:, c * depth : (c + 1) * depth, :].reshape(D, D)

    def w_out(c):
        rows = [out_slab[k ^ me] for k in range(c * span, (c + 1) * span)]
        return jnp.concatenate(rows, 0)

    hiddens, slopes, grads, forward, backward, bias_sums = {}, {}, {}, None, None, []
    for step in range(-1, chunks + 1):
        ahead, behind = step + 1, step - 1
        products = []
        if ahead < chunks:
            products.append(lambda: hiddens.update({ahead: dot(normed_low, w_in(ahead))}))
            products.append(lambda: slopes.update({ahead: dot_nt(cot[...], w_out(ahead))}))
        if behind >= 0:
            active = actives[:, behind * D : (behind + 1) * D]
            grad = grads.pop(behind)

            def add_forward():
                nonlocal forward
                one = dot(active, w_out(behind))
                forward = one if forward is None else forward + one

            def add_backward():
                nonlocal backward
                one = dot_nt(grad, w_in(behind))
                backward = one if backward is None else backward + one

            def weight():
                one = dot_tn(normed_low, grad).reshape(shards, depth, D)
                put_shares(me, same, other, behind * depth, one)

            products += [add_forward, add_backward, weight]
        rows = []
        if 0 <= step < chunks:
            hidden, slope = hiddens.pop(step), slopes.pop(step)
            bias_sum = 0.0
            for r, part in enumerate(parts):
                h = hidden[part] + small[3 + step : 4 + step]
                upto, density = gelu_parts(h)
                actives[part, step * D : (step + 1) * D] = (h * upto).astype(BF)
                rows.append((slope[part] * (upto + h * density)).astype(BF))
                bias_sum += jnp.sum(rows[-1].astype(F32), 0, keepdims=True)
                if r < len(products):
                    products[r]()
            bias_sums.append(bias_sum)
            grads[step] = jnp.concatenate(rows, 0)
        else:
            for product in products:
                product()
    back_sum[...] = backward
    result = mixed[...] + forward + bias_o
    kept[...] = result[: own * WIDTH]
    sent[...] = result[own * WIDTH :].astype(BF)
    put_smalls(same, other, 4 * depth, bias_sums)


def mlp_backward_body(
    mixed,
    cot,
    actives,
    back_sum,
    vectors,
    attn_slab,
    restored,
    grad_mixed,
    grad_win,
    same,
    other,
    wide,
):
    me = shard_place()
    shards, height = attn_slab.shape[:2]
    depth = (height - SMALL) // 4
    span = shards * D // FF
    gain = vectors[0:1]
    parts = [slice(r * WIDTH, (r + 1) * WIDTH) for r in range(WIN)]
    columns = column_places()
    w_proj = block_of(attn_slab, 3, depth)
    sums = [0.0] * 4
    branches = []
    for r, part in enumerate(parts):
        if r < FF // D:
            one = dot_tn(actives[:, r * D : (r + 1) * D], cot[...])
            put_shares(me, same, other, 0, one.reshape(span, 4 * depth, D), r * span)
        normed, scale = norm_stats(mixed[part, :])
        g = back_sum[part, :]
        c = cot[part, :].astype(F32)
        grad = c + norm_back(g, normed, scale, gain)
        grad_mixed[part, :] = grad
        branch = grad.astype(BF)
        branches.append(branch)
        for n, one in enumerate((g * normed, g, c, branch.astype(F32))):
            sums[n] += jnp.sum(one, 0, keepdims=True)
        grad_att = dot_nt(branch, w_proj).astype(BF)
        wide[:, r] = dot(columns, grad_att).reshape(WINDOWS, SLOT, D)
    proj = dot_tn(restored[...], jnp.concatenate(branches, 0)).reshape(shards, depth, D)
    put_shares(me, same, other, 4 * depth, proj)
    put_smalls(same, other, 5 * depth, sums)
    grad_win[...] = wide[...].reshape(PADDED, D).astype(BF)


def attn_backward_body(query, key, value, probs, grad_win, came, out, pairs):
    @pl.when(pl.program_id(0) == 0)
    def _():
        pairs[...] = came[...]

    masks = head_masks()
    parts = [slice(s * PLACES, (s + 1) * PLACES) for s in range(2)]
    feats = [slice(u * FEAT, (u + 1) * FEAT) for u in range(QUADS)]
    keys, shares, grads, queries, slopes = [], [], [], [], []
    for u in range(QUADS):
        q2 = query[:, feats[u]].astype(F32)
        k2 = key[:, feats[u]].astype(F32)
        v2 = value[:, feats[u]].astype(F32)
        go2 = grad_win[:, feats[u]].astype(F32)
        p2 = probs[0, u].astype(F32)
        for part in parts:
            keys.append(k2[part].astype(BF))
            shares.append(p2[part])
            grads.append(spread(go2[part], masks))
            queries.append(spread(q2[part], masks))
            slopes.append(dot_nt(v2[part].astype(BF), grads[-1]))
    lows = []
    for p, dp in zip(shares, slopes):
        inner = jnp.sum(p * dp, 0, keepdims=True)
        lows.append((p * (dp - inner)).astype(BF))
    dvs = [dot(p.astype(BF), go) for p, go in zip(shares, grads)]
    dks = [dot(ds, q) for ds, q in zip(lows, queries)]
    dqs = [dot_tn(ds, k) for ds, k in zip(lows, keys)]
    for u in range(QUADS):
        two = slice(2 * u, 2 * u + 2)
        pairs[u] += lows[2 * u].astype(F32) + lows[2 * u + 1].astype(F32)
        for c, held in enumerate(
            (
                [own_heads(dq) * SCALE for dq in dqs[two]],
                [dk * SCALE for dk in dks[two]],
                dvs[two],
            )
        ):
            both = jnp.concatenate(held, 0).astype(BF)
            out[:, c * D + u * FEAT : c * D + (u + 1) * FEAT] = both


def attn_last_body(
    grad_mixed,
    tokens,
    halo,
    slab,
    normed_win,
    pairs,
    *refs,
):
    grads = refs[:-5]
    kept, sent, same, other, wide = refs[-5:]
    me = shard_place()
    shards = slab.shape[0]
    depth = (slab.shape[1] - SMALL) // 4
    small = smalls_of(slab, 4 * depth)
    gain = small[0:1]
    own = WIN - SHIFT
    vectors = []
    for c in range(3):
        cols = slice(c * D, (c + 1) * D)
        g = jnp.concatenate([part[:, cols] for part in grads], 0)
        if c != 1:
            vectors.append(jnp.sum(g.astype(F32), 0, keepdims=True))
        put_shares(
            me, same, other, c * depth, dot_tn(normed_win[...], g).reshape(shards, depth, D)
        )
        part = dot_nt(g, block_of(slab, c, depth))
        total = part if c == 0 else total + part
    wide[...] = total.reshape(WINDOWS, WIN, SLOT, D)
    back = places_column()
    gain_sum = jnp.zeros((1, D), F32)
    bias_sum = jnp.zeros((1, D), F32)
    for r in range(WIN):
        here = wide[:, r].reshape(WINDOWS * SLOT, D).astype(BF)
        g = dot(back, here)
        x = (tokens[SHIFT + r] if r < own else halo[r - own]).astype(F32)
        normed, scale = norm_stats(x)
        gain_sum += jnp.sum(g * normed, 0, keepdims=True)
        bias_sum += jnp.sum(g, 0, keepdims=True)
        grad = grad_mixed[r * WIDTH : (r + 1) * WIDTH, :] + norm_back(g, normed, scale, gain)
        if r < own:
            kept[r * WIDTH : (r + 1) * WIDTH, :] = grad
        else:
            sent[(r - own) * WIDTH : (r - own + 1) * WIDTH, :] = grad.astype(BF)

    rows = [gain_sum, bias_sum, vectors[0], vectors[1]]
    halves = GROUP // QUAD
    picks = [table_pick(1, half, True) for half in range(halves)]
    for g in range(GROUPS):
        laid = jnp.zeros((PLACES, TAB_USED), F32)
        for half in range(halves):
            total = pairs[g * halves + half]
            high = total.astype(BF)
            low = (total - high.astype(F32)).astype(BF)
            laid += dot(high, picks[half]) + dot(low, picks[half])
        laid = jnp.concatenate([laid, jnp.zeros((PLACES, TAB - TAB_USED), F32)], 1)
        total = jnp.zeros((SLOT, TAB), F32)
        for r in range(WIN):
            total += pltpu.roll(
                laid[r * SLOT : (r + 1) * SLOT], (2 * WIN - 1) * GROUP * r, 1
            )
        total = pltpu.roll(total, 0, 1, stride=GROUP, stride_axis=0)
        row = jnp.sum(total, 0, keepdims=True)
        rows += [row[:, c * D : (c + 1) * D] for c in range(TAB // D)]
    put_smalls(same, other, 3 * depth, rows)


def region_views(regions, rows, place):
    here = lax.dynamic_slice_in_dim(regions[0], place * rows, rows, 0)
    windows = here.reshape(WIN, WINDOWS, WIN).transpose(1, 0, 2)
    windows = jnp.pad(windows, ((0, 0), (0, 0), (0, SLOT - WIN))).astype(F32)
    windows = windows.reshape(WINDOWS, PLACES)
    by_row = jnp.broadcast_to(windows[:, :, None], (WINDOWS, PLACES, 128))
    by_lane = jnp.tile(jnp.pad(windows, ((0, 0), (0, HOLD - PLACES))), (1, QUAD))
    return by_row, by_lane[:, None, :]


def per_device(
    tokens,
    regions,
    cotangent,
    gain_one,
    bias_one,
    w_qkv,
    bias_qv,
    table,
    w_proj,
    bias_proj,
    gain_two,
    bias_two,
    w_in,
    bias_in,
    w_out,
    bias_out,
):
    images, local_rows, columns, _ = tokens.shape
    assert images == 1 and local_rows == WIN and columns == WIDTH
    shards = lax.axis_size("shard")
    seq = lax.axis_index("seq").astype(jnp.int32)
    chips = shards // 2
    depth = D // shards
    own = WIN - SHIFT
    attn_params = (gain_one[None], bias_one[None], w_qkv, bias_qv, table.T)
    bin_rows = bias_in.reshape(-1, 128)
    mlp_params = (
        w_proj,
        bias_proj[None],
        gain_two[None],
        bias_two[None],
        w_in,
        bin_rows,
        w_out,
        bias_out[None],
    )
    attn_slab, mlp_slab, out_slab = kernel_call(
        pack_body,
        [like((4 * depth + SMALL, D), BF)] * 2 + [like((4 * depth, D), BF)],
        (*attn_params, *mlp_params),
        vmem=60,
    )
    pieces = gather_pieces(attn_slab)
    pieces, (out_slab,) = tie(pieces, [out_slab])
    attn_all = jnp.stack(pieces)
    out_pieces = gather_pieces(out_slab)
    mlp_all = lax.all_gather(mlp_slab, "shard")
    tokens_here = tokens[0]
    token_halo = shifted_2(tokens_here[:SHIFT], "seq", -1)
    cot_here = cotangent[0]
    cot_halo = shifted_2(cot_here[:SHIFT], "seq", -1)
    by_row, by_lane = region_views(regions, local_rows, seq)

    normed_win, query, key, value = kernel_call(
        project_body,
        [like((PADDED, D), BF)] * 4,
        (tokens_here, token_halo, attn_all),
        scratch=[pltpu.VMEM((WINDOWS, WIN, SLOT, D), F32)],
    )
    pair_rows = 2 * PLACES
    steps = WINDOWS // 2

    def rows_from(first, width=D):
        return pl.BlockSpec((pair_rows, width), lambda i: (first + i, 0))

    def probs_from(first):
        return pl.BlockSpec((1, QUADS, pair_rows, LANES), lambda i: (first + i, 0, 0, 0))

    def fixed(shape):
        return pl.BlockSpec(shape, lambda i: (0,) * len(shape))

    probs, restored, mixed = kernel_call(
        attn_forward_body,
        [
            like((steps, QUADS, pair_rows, LANES), BF),
            like((TOKENS, D), BF),
            like((TOKENS, D), F32),
        ],
        (attn_all, by_row, by_lane, tokens_here, token_halo, query, key, value),
        grid=(steps,),
        in_blocks=[
            fixed(attn_all.shape),
            pl.BlockSpec((2, *by_row.shape[1:]), lambda i: (i, 0, 0)),
            pl.BlockSpec((2, *by_lane.shape[1:]), lambda i: (i, 0, 0)),
            fixed(tokens_here.shape),
            fixed(token_halo.shape),
            rows_from(0),
            rows_from(0),
            rows_from(0),
        ],
        out_blocks=[probs_from(0), fixed((TOKENS, D)), fixed((TOKENS, D))],
        scratch=[
            pltpu.VMEM((WINDOWS, WIN, SLOT, D), F32),
            pltpu.VMEM((QUADS, PLACES, LANES), F32),
        ],
    )
    share_a = like((chips, 4 * depth + SMALL, D), BF)
    share_b = like((chips, 5 * depth + SMALL, D), BF)
    out_kept, out_sent, cot, actives, back_sum, vectors, same_a, other_a = kernel_call(
        mlp_forward_body,
        [
            like((own * WIDTH, D), F32),
            like((SHIFT * WIDTH, D), BF),
            like((TOKENS, D), BF),
            like((TOKENS, FF), BF),
            like((TOKENS, D), F32),
            like((SMALL, D), F32),
            share_a,
            share_a,
        ],
        (mixed, cot_here, cot_halo, mlp_all, jnp.stack(out_pieces)),
    )
    grad_mixed, grad_win, same_b, other_b = kernel_call(
        mlp_backward_body,
        [like((TOKENS, D), F32), like((PADDED, D), BF), share_b, share_b],
        (mixed, cot, actives, back_sum, vectors, attn_all, restored),
        scratch=[pltpu.VMEM((WINDOWS, WIN, SLOT, D), F32)],
    )

    def backward(first, count, grad_win, came):
        sums = like((QUADS, PLACES, LANES), F32)
        return kernel_call(
            attn_backward_body,
            [like((count * pair_rows, 3 * D), BF), sums],
            (query, key, value, probs, grad_win, came),
            grid=(count,),
            in_blocks=[rows_from(first)] * 3
            + [probs_from(first), rows_from(first), fixed(sums.shape)],
            out_blocks=[rows_from(0, 3 * D), fixed(sums.shape)],
            )

    none = jnp.zeros((QUADS, PLACES, LANES), F32)
    count = steps // 2
    came_a = exchange(other_a, "shard", 1)
    sums, (grad_win,) = tie(add_cores(same_a, came_a), [grad_win])
    parts_a = to_chips(sums)
    came_b = exchange(other_b, "shard", 1)
    early, pairs = backward(0, count, grad_win, none)
    sums, (pairs,) = tie(add_cores(same_b, came_b), [pairs])
    parts_b = to_chips(sums)
    late_part, pairs = backward(count, count, grad_win, pairs)
    keep_a, send = add_chips(same_a, came_a, parts_a)
    (send,), (pairs,) = tie([send], [pairs])
    near_a = exchange(send, "seq", 1)
    (out_halo,), (pairs,) = tie([shifted_2(out_sent, "seq", 1)], [pairs])
    tok_kept, tok_sent, attn_same, attn_other = kernel_call(
        attn_last_body,
        [
            like((own * WIDTH, D), F32),
            like((SHIFT * WIDTH, D), BF),
            like((chips, 3 * depth + SMALL, D), BF),
            like((chips, 3 * depth + SMALL, D), BF),
        ],
        (grad_mixed, tokens_here, token_halo, attn_all, normed_win, pairs, early, late_part),
        scratch=[pltpu.VMEM((WINDOWS, WIN, SLOT, D), F32)],
    )
    half_a = add_pair(keep_a, near_a)
    (half_a,), (attn_other, tok_sent) = tie([half_a], [attn_other, tok_sent])
    far_a = exchange(half_a, "seq", 2)
    attn_came = exchange(attn_other, "shard", 1)
    keep_b, send = add_chips(same_b, came_b, parts_b, 10_000_000_000)
    (send,), (attn_came,) = tie([send], [attn_came])
    near_b = exchange(send, "seq", 1)
    sums, (far_a,) = tie(add_cores(attn_same, attn_came), [far_a])
    attn_parts = to_chips(sums)
    half_a = seq_rest(add_pair(half_a, far_a))
    (half_a,), (near_b, tok_sent) = tie([half_a], [near_b, tok_sent])
    tok_halo = shifted_2(tok_sent, "seq", 1)
    half_b = add_pair(keep_b, near_b)
    (half_b,), attn_parts = tie([half_b], attn_parts)
    far_b = exchange(half_b, "seq", 2)
    keep, send = add_chips(attn_same, attn_came, attn_parts)
    near = exchange(send, "seq", 1)
    back_a = exchange(half_a, "seq", 1)
    half = add_pair(keep, near)
    (half, tok_halo), (far_b,) = tie([half, tok_halo], [far_b])
    far = exchange(half, "seq", 2)
    half_b = seq_rest(add_pair(half_b, far_b))
    (half_b,), (far,) = tie([half_b], [far])
    back_b = exchange(half_b, "seq", 1)
    half = seq_rest(add_pair(half, far))
    (half,), (back_a,) = tie([half], [back_a])
    back = exchange(half, "seq", 1)
    def unpack(body, params, half, back):
        return kernel_call(
            body,
            [like(p.shape, F32) for p in params],
            (half, back),
            scratch=[
                pltpu.VMEM((2 * half.shape[0], D), BF),
                pltpu.SemaphoreType.DMA((2,)),
            ],
                apart=2,
        )

    in_grads = unpack(unpack_in_body, (w_in, bin_rows), half_a, back_a)
    in_grads, (back_b,) = tie(in_grads, [back_b])
    column = gain_two[None]
    out_grads = unpack(unpack_out_body, (w_out, w_proj, *[column] * 4), half_b, back_b)
    out_grads, (back,) = tie(out_grads, [back])
    attn_grads = unpack(unpack_attn_body, attn_params, half, back)
    g_wout, g_wproj, g_gain, g_offset, g_bout, g_bproj = out_grads
    summed = [*attn_grads[:4], attn_grads[4].T, g_wproj, g_bproj, g_gain, g_offset]
    summed += [*in_grads, g_wout, g_bout]

    def joined(halo, kept):
        return jnp.concatenate([halo.astype(F32), kept], 0).reshape(tokens.shape)

    targets = (
        gain_one,
        bias_one,
        w_qkv,
        bias_qv,
        table,
        w_proj,
        bias_proj,
        gain_two,
        bias_two,
        w_in,
        bias_in,
        w_out,
        bias_out,
    )
    grads = [g.reshape(p.shape) for g, p in zip(summed, targets)]
    return (joined(out_halo, out_kept), joined(tok_halo, tok_kept), *grads)


def solution(mesh):
    return jax.shard_map(
        per_device,
        mesh=mesh,
        in_specs=(
            P("shard", "seq", None, None),
            P("shard", None, None),
            P("shard", "seq", None, None),
            P("shard"),
            P("shard"),
            P("shard", None),
            P(None, "shard"),
            P(None, "shard"),
            P("shard", None),
            P("shard"),
            P("shard"),
            P("shard"),
            P("shard", None),
            P("shard"),
            P("shard", None),
            P("shard"),
        ),
        out_specs=(
            P("shard", "seq", None, None),
            P("shard", "seq", None, None),
            P("shard"),
            P("shard"),
            P("shard", None),
            P(None, "shard"),
            P(None, "shard"),
            P("shard", None),
            P("shard"),
            P("shard"),
            P("shard"),
            P("shard", None),
            P("shard"),
            P("shard", None),
            P("shard"),
        ),
        check_vma=False,
    )
```

```python
import math

import jax
import jax.numpy as jnp
from jax import lax
from jax.experimental import pallas as pl
from jax.experimental.pallas import tpu as pltpu
from jax.sharding import PartitionSpec as P

D = 512
HEADS = 16
HEAD = 32
WIN = 7
SHIFT = 3
FF = 2048
WIDTH = 112
WINDOWS = WIDTH // WIN
SLOT = 8
PLACES = WIN * SLOT
GROUP = 8
GROUPS = HEADS // GROUP
QUAD = 4
QUADS = HEADS // QUAD
FEAT = QUAD * HEAD
HOLD = 64
LANES = QUAD * HOLD
TOKENS = WIN * WIDTH
PADDED = WINDOWS * PLACES
TAB = 1536
TAB_USED = 768
SMALL = 32
EPS = 1e-05
SCALE = HEAD**-0.5
BF = jnp.bfloat16
F32 = jnp.float32


def shifted_2(value, axis, by):
    peers = lax.axis_size(axis)
    return lax.ppermute(value, axis, [(i, (i + by) % peers) for i in range(peers)])


def dot(left, right, dims=((1,), (0,))):
    return lax.dot_general(left, right, (dims, ((), ())), preferred_element_type=F32)


def dot_nt(left, right):
    return dot(left, right, ((1,), (1,)))


def dot_tn(left, right):
    return dot(left, right, ((0,), (0,)))


def iota(shape, axis):
    return lax.broadcasted_iota(jnp.int32, shape, axis)


def shard_place():
    return lax.axis_index("shard").astype(jnp.int32)


def late_place():
    return lax.axis_index("seq").astype(jnp.int32) & 1


def one_hot(condition):
    return jnp.where(condition, 1.0, 0.0).astype(BF)


def column_places():
    slot = iota((WINDOWS * SLOT, WIDTH), 0)
    column = iota((WINDOWS * SLOT, WIDTH), 1)
    place = slot & (SLOT - 1)
    wanted = (slot >> 3) * WIN + place + SHIFT
    wanted = jnp.where(wanted >= WIDTH, wanted - WIDTH, wanted)
    return one_hot((wanted == column) & (place < WIN))


def places_column():
    slot = iota((WIDTH, WINDOWS * SLOT), 1)
    column = iota((WIDTH, WINDOWS * SLOT), 0)
    place = slot & (SLOT - 1)
    wanted = (slot >> 3) * WIN + place + SHIFT
    wanted = jnp.where(wanted >= WIDTH, wanted - WIDTH, wanted)
    return one_hot((wanted == column) & (place < WIN))


def head_masks():
    feature = iota((1, FEAT), 1) >> 5
    return [jnp.where(feature == h, 1.0, 0.0).astype(F32) for h in range(QUAD)]


def spread(values, masks):
    empty = jnp.zeros((HOLD - PLACES, FEAT), F32)
    rows = []
    for mask in masks:
        rows += [values * mask, empty]
    return jnp.concatenate(rows, 0).astype(BF)


def own_heads(values):
    feature = iota((PLACES, FEAT), 1) >> 5
    out = values[:PLACES]
    for h in range(1, QUAD):
        out = jnp.where(feature == h, values[h * HOLD : h * HOLD + PLACES], out)
    return out


def table_pick(row_axis, quad, backwards):
    shape = (TAB_USED, LANES) if row_axis == 0 else (LANES, TAB_USED)
    lane = iota(shape, row_axis)
    pair = iota(shape, 1 - row_axis)
    head, place = pair >> 6, pair & (HOLD - 1)
    row, column = place >> 3, place & (SLOT - 1)
    entry = row * (2 * WIN - 1) + column
    if backwards:
        entry = (WIN - 1) * 2 * WIN - entry
    held = head + quad % (GROUP // QUAD) * QUAD
    match = ((lane >> 3) == entry) & ((lane & 7) == held)
    return one_hot(match & (column < WIN) & (row < WIN))


def norm_stats(values):
    average = jnp.mean(values, -1, keepdims=True)
    centered = values - average
    variance = jnp.mean(centered * centered, -1, keepdims=True)
    scale = lax.rsqrt(variance + EPS)
    return centered * scale, scale


def norm_back(grad, normed, scale, gain):
    scaled = grad * gain
    first = jnp.mean(scaled, -1, keepdims=True)
    second = jnp.mean(scaled * normed, -1, keepdims=True)
    return scale * (scaled - first - normed * second)


def whole(memory=pltpu.VMEM):
    return pl.BlockSpec(memory_space=memory)


def kernel_call(
    body, outs, ins, scratch=(), apart=0, grid=None, in_blocks=None, out_blocks=None,
    vmem=16,
    flops=1024,
):
    in_specs = in_blocks or [whole()] * (len(ins) - apart) + [whole(pl.ANY)] * apart
    options = {"grid": grid} if grid else {}
    return pl.pallas_call(
        body,
        out_shape=tuple(outs),
        in_specs=in_specs,
        out_specs=tuple(out_blocks or [whole()] * len(outs)),
        scratch_shapes=list(scratch),
        cost_estimate=pl.CostEstimate(flops=flops, bytes_accessed=1024, transcendentals=0),
        compiler_params=pltpu.CompilerParams(vmem_limit_bytes=vmem * 1024 * 1024),
        **options,
    )(*ins)


def like(shape, dtype):
    return jax.ShapeDtypeStruct(shape, dtype)


def place(vector, lanes, me):
    w = vector.shape[1]
    pick = one_hot(iota((w, lanes), 1) == iota((w, lanes), 0) + me * w)
    wide = jnp.broadcast_to(vector, (8, w))
    return dot(wide.astype(BF), pick)[0:1]


def mine(row, w, me):
    lanes = row.shape[1]
    pick = one_hot(iota((lanes, w), 0) == iota((lanes, w), 1) + me * w)
    wide = jnp.broadcast_to(row, (8, lanes))
    return dot(wide.astype(BF), pick)[0:1]


def padded(rows, height):
    total = sum(r.shape[0] for r in rows)
    return jnp.concatenate(rows + [jnp.zeros((height - total, D), F32)], 0).astype(BF)


def pack_body(
    g1, b1, wqkv, bqv, table, wproj, bproj, g2, b2, win, bin_, wout, bout, attn, mlp, out
):
    depth = wqkv.shape[0]
    me = shard_place()
    for c in range(3):
        attn[c * depth : (c + 1) * depth, :] = wqkv[:, c * D : (c + 1) * D]
    attn[3 * depth : 4 * depth, :] = wproj[...]
    vectors = (g1[...], b1[...], bqv[0:1, :], bqv[1:2, :], bproj[...])
    rows = [place(v, D, me) for v in vectors]
    held, entries = table.shape
    lane = iota((entries, TAB), 1)
    spot = iota((entries, TAB), 0) * GROUP + TAB - (WIN - 1) * 2 * WIN * GROUP
    spot = jnp.where(spot >= TAB, spot - TAB, spot)
    values = table[...].astype(F32).T
    groups = [jnp.zeros((1, TAB), F32) for _ in range(GROUPS)]
    for h in range(held):
        head = me * held + h
        inside = lane == spot + (head & (GROUP - 1))
        row = jnp.sum(jnp.where(inside, values[:, h : h + 1], 0.0), 0, keepdims=True)
        for g in range(GROUPS):
            groups[g] = groups[g] + jnp.where((head >> 3) == g, row, 0.0)
    for g in range(GROUPS):
        rows += [groups[g][:, c * D : (c + 1) * D] for c in range(TAB // D)]
    attn[4 * depth :, :] = padded(rows, SMALL)
    for c in range(FF // D):
        mlp[c * depth : (c + 1) * depth, :] = win[:, c * D : (c + 1) * D]
    out[...] = wout[...]
    held = jnp.concatenate([bin_[r : r + 1] for r in range(bin_.shape[0])], 1)
    hidden_bias = place(held, FF, me)
    rows = [place(v, D, me) for v in (g2[...], b2[...], bout[...])]
    rows += [hidden_bias[:, c * D : (c + 1) * D] for c in range(FF // D)]
    mlp[4 * depth :, :] = padded(rows, SMALL)


def join_halves(late, half, back, both, sems):
    rows = half.shape[0]
    copies = []
    for n, (part, at) in enumerate(((half, late), (back, 1 - late))):
        to = both.at[pl.ds(pl.multiple_of(at * rows, 16), rows), :]
        copies.append(pltpu.make_async_copy(part, to, sems.at[n]))
    for copy in copies:
        copy.start()
    for copy in copies:
        copy.wait()


def unpack_attn_body(half, back, g1, b1, wqkv, bqv, table, attn, sems):
    depth = wqkv.shape[0]
    me = shard_place()
    join_halves(late_place(), half, back, attn, sems)
    for c in range(3):
        wqkv[:, c * D : (c + 1) * D] = attn[c * depth : (c + 1) * depth, :].astype(F32)
    small = attn[3 * depth :, :].astype(F32)
    g1[...] = mine(small[0:1], depth, me)
    b1[...] = mine(small[1:2], depth, me)
    bqv[0:1, :] = mine(small[2:3], depth, me)
    bqv[1:2, :] = mine(small[3:4], depth, me)
    held, entries = table.shape
    lane = iota((entries, TAB), 1)
    spot = (entries - 1 - iota((entries, TAB), 0)) * GROUP
    parts = TAB // D
    rows = [
        jnp.concatenate([small[4 + g * parts + c : 5 + g * parts + c] for c in range(parts)], 1)
        for g in range(GROUPS)
    ]
    which = iota((entries, held), 1)
    total = jnp.zeros((entries, held), F32)
    for h in range(held):
        head = me * held + h
        row = rows[0]
        for g in range(1, GROUPS):
            row = jnp.where((head >> 3) == g, rows[g], row)
        inside = lane == spot + (head & (GROUP - 1))
        column = jnp.sum(jnp.where(inside, row, 0.0), 1, keepdims=True)
        total = jnp.where(which == h, column, total)
    table[...] = total.T


def unpack_in_body(half, back, win, bin_, both, sems):
    depth = win.shape[0]
    join_halves(late_place(), half, back, both, sems)
    for c in range(FF // D):
        win[:, c * D : (c + 1) * D] = both[c * depth : (c + 1) * depth, :].astype(F32)
    small = both[4 * depth :, :].astype(F32)
    hidden = jnp.concatenate([small[c : c + 1] for c in range(FF // D)], 1)
    hidden = mine(hidden, depth * FF // D, shard_place())
    for r in range(bin_.shape[0]):
        bin_[r : r + 1] = hidden[:, r * 128 : (r + 1) * 128]


def unpack_out_body(half, back, wout, wproj, g2, b2, bout, bproj, both, sems):
    depth = wproj.shape[0]
    me = shard_place()
    join_halves(late_place(), half, back, both, sems)
    wout[...] = both[: 4 * depth, :].astype(F32)
    wproj[...] = both[4 * depth : 5 * depth, :].astype(F32)
    small = both[5 * depth :, :].astype(F32)
    g2[...] = mine(small[0:1], depth, me)
    b2[...] = mine(small[1:2], depth, me)
    bout[...] = mine(small[2:3], depth, me)
    bproj[...] = mine(small[3:4], depth, me)


def put_shares(me, same, other, start, values, first=0):
    core, chip = me & 1, me >> 1
    rows = values.shape[1]
    for c in range(values.shape[0] // 2):
        one, two = values[2 * c], values[2 * c + 1]
        q = (first // 2 + c) ^ chip
        same[q, start : start + rows, :] = jnp.where(core == 0, one, two).astype(BF)
        other[q, start : start + rows, :] = jnp.where(core == 0, two, one).astype(BF)


def put_smalls(same, other, start, rows):
    block = padded(rows, SMALL)
    for q in range(same.shape[0]):
        same[q, start:, :] = block
        other[q, start:, :] = block


def exchange(value, axis, mask):
    peers = lax.axis_size(axis)
    return lax.ppermute(value, axis, [(i, i ^ mask) for i in range(peers)])


def gather_pieces(slab):
    chips = lax.axis_size("shard") // 2
    pieces = [None] * (2 * chips)
    for q in range(chips):
        pieces[2 * q] = exchange(slab, "shard", 2 * q) if q else slab
    for q in range(chips):
        pieces[2 * q + 1] = exchange(pieces[2 * q], "shard", 1)
    return pieces


def add_pair(here, came):
    return (here.astype(F32) + came.astype(F32)).astype(BF)


def add_cores(same, came):
    return [add_pair(same[q], came[q]) for q in range(1, same.shape[0])]


def to_chips(sums):
    return [exchange(s, "shard", 2 * q + 2) for q, s in enumerate(sums)]


def add_chips_body(same, came, *refs):
    parts, (keep, send) = refs[:-2], refs[-2:]
    half = keep.shape[0]
    for at, target in ((late_place(), keep), (1 - late_place(), send)):
        rows = pl.ds(pl.multiple_of(at * half, 16), half)
        total = same[0, rows, :].astype(F32) + came[0, rows, :].astype(F32)
        for part in parts:
            total += part[rows, :].astype(F32)
        target[...] = total.astype(BF)


def add_chips(same, came, parts, flops=1024):
    half = like((same.shape[1] // 2, D), BF)
    return kernel_call(add_chips_body, [half, half], (same, came, *parts), flops=flops)


def seq_rest(half):
    reach = 4
    while reach < lax.axis_size("seq"):
        half = add_pair(half, exchange(half, "seq", reach))
        reach *= 2
    return half


def tie(first, second):
    first, second = list(first), list(second)
    out = lax.optimization_barrier((*first, *second))
    return list(out[: len(first)]), list(out[len(first) :])


def block_of(slab, c, depth):
    me = shard_place()
    rows = [slab[k ^ me, c * depth : (c + 1) * depth, :] for k in range(slab.shape[0])]
    return jnp.concatenate(rows, 0)


def smalls_of(slab, start):
    return jnp.sum(slab[:, start:, :].astype(F32), 0)


def project_body(tokens, halo, slab, normed_win, query, key, value, wide):
    columns = column_places()
    own = WIN - SHIFT
    depth = (slab.shape[1] - SMALL) // 4
    small = smalls_of(slab, 4 * depth)
    gain, offset, bias_q, bias_v = (small[r : r + 1] for r in range(4))
    for r in range(WIN):
        x = (tokens[SHIFT + r] if r < own else halo[r - own]).astype(F32)
        normed, _ = norm_stats(x)
        low = (normed * gain + offset).astype(BF)
        wide[:, r] = dot(columns, low).reshape(WINDOWS, SLOT, D)
    normed_win[...] = wide[...].reshape(PADDED, D).astype(BF)
    query[...] = (dot(normed_win[...], block_of(slab, 0, depth)) + bias_q).astype(BF)
    key[...] = dot(normed_win[...], block_of(slab, 1, depth)).astype(BF)
    value[...] = (dot(normed_win[...], block_of(slab, 2, depth)) + bias_v).astype(BF)


def attn_forward_body(
    slab, reg_rows, reg_lanes, tokens, halo, query, key, value, probs, restored, mixed, wide, bias
):
    n = pl.program_id(0)
    depth = (slab.shape[1] - SMALL) // 4

    @pl.when(n == 0)
    def _():
        small = smalls_of(slab, 4 * depth)
        parts = TAB // D
        empty = (iota((PLACES, LANES), 0) & (SLOT - 1)) == WIN
        turned = []
        for g in range(GROUPS):
            first = 5 + g * parts
            row = jnp.concatenate([small[first + c : first + c + 1] for c in range(parts)], 1)
            row = jnp.broadcast_to(row, (SLOT, TAB))
            row = pltpu.roll(row, 0, 1, stride=GROUP, stride_axis=0)
            rows = [pltpu.roll(row, (2 * WIN - 1) * GROUP * r, 1)[:, :TAB_USED] for r in range(WIN)]
            turned.append(jnp.concatenate(rows, 0).astype(BF))
        for half in range(GROUP // QUAD):
            pick = table_pick(0, half, False)
            for g in range(GROUPS):
                picked = dot(turned[g], pick)
                bias[g * (GROUP // QUAD) + half] = jnp.where(empty, -1e30, picked)

    masks = head_masks()
    penalty = [
        jnp.where(reg_rows[s][:, 0:1] != reg_lanes[s], -100.0, 0.0) for s in range(2)
    ]
    parts = [slice(s * PLACES, (s + 1) * PLACES) for s in range(2)]
    units = [(u, s) for u in range(QUADS) for s in range(2)]
    feats = [slice(u * FEAT, (u + 1) * FEAT) for u in range(QUADS)]
    values, scores = [], []
    for u in range(QUADS):
        q2 = query[:, feats[u]].astype(F32)
        k2 = key[:, feats[u]].astype(F32)
        v2 = value[:, feats[u]].astype(F32)
        for s in range(2):
            values.append(v2[parts[s]].astype(BF))
            scores.append(dot_nt(k2[parts[s]].astype(BF), spread(q2[parts[s]], masks)))
    shares = []
    for (u, s), score in zip(units, scores):
        logits = score * SCALE + bias[u] + penalty[s]
        powers = jnp.exp(logits - jnp.max(logits, 0, keepdims=True))
        shares.append(powers * (1.0 / jnp.sum(powers, 0, keepdims=True)))
    wholes = [dot_tn(p.astype(BF), v) for p, v in zip(shares, values)]
    for (u, s), o in zip(units, wholes):
        wide[2 * n + s, :, :, feats[u]] = own_heads(o).reshape(WIN, SLOT, FEAT)
    for u in range(QUADS):
        probs[0, u] = jnp.concatenate(shares[2 * u : 2 * u + 2], 0).astype(BF)

    @pl.when(n == pl.num_programs(0) - 1)
    def _():
        bias_proj = smalls_of(slab, 4 * depth)[4:5]
        back = places_column()
        own = WIN - SHIFT
        for r in range(WIN):
            here = wide[:, r].reshape(WINDOWS * SLOT, D).astype(BF)
            restored[r * WIDTH : (r + 1) * WIDTH, :] = dot(back, here).astype(BF)
        branch = dot(restored[...], block_of(slab, 3, depth)) + bias_proj
        for r in range(WIN):
            x = (tokens[SHIFT + r] if r < own else halo[r - own]).astype(F32)
            mixed[r * WIDTH : (r + 1) * WIDTH, :] = x + branch[r * WIDTH : (r + 1) * WIDTH]


def gelu_parts(h):
    under = 1.0 + (0.3275911 * 0.5**0.5) * jnp.abs(h)
    t = pl.reciprocal(under, approx=True)
    t = t * (2.0 - under * t)
    bell = jnp.exp2(h * h * (-0.5 / math.log(2.0)))
    poly = t * (
        0.127414796
        + t * (-0.142248368 + t * (0.7107068705 + t * (-0.7265760135 + t * 0.5307027145)))
    )
    tail = poly * bell
    upto = jnp.where(h >= 0, 1.0 - tail, tail)
    return upto, bell * 0.3989422804014327


def mlp_forward_body(
    mixed,
    cotangent,
    cot_halo,
    slab,
    out_slab,
    kept,
    sent,
    cot,
    actives,
    back_sum,
    vectors,
    same,
    other,
):
    me = shard_place()
    shards, height = slab.shape[:2]
    depth = (height - SMALL) // 4
    span = shards * D // FF
    chunks = FF // D
    small = smalls_of(slab, 4 * depth)
    vectors[...] = small
    gain, offset, bias_o = (small[r : r + 1] for r in range(3))
    own = WIN - SHIFT
    parts = [slice(r * WIDTH, (r + 1) * WIDTH) for r in range(WIN)]
    lows = []
    for r, part in enumerate(parts):
        cot[part, :] = cotangent[SHIFT + r] if r < own else cot_halo[r - own]
        normed, _ = norm_stats(mixed[part, :])
        lows.append((normed * gain + offset).astype(BF))
    normed_low = jnp.concatenate(lows, 0)

    def w_in(c):
        return slab[:, c * depth : (c + 1) * depth, :].reshape(D, D)

    def w_out(c):
        rows = [out_slab[k ^ me] for k in range(c * span, (c + 1) * span)]
        return jnp.concatenate(rows, 0)

    hiddens, slopes, grads, forward, backward, bias_sums = {}, {}, {}, None, None, []
    for step in range(-1, chunks + 1):
        ahead, behind = step + 1, step - 1
        products = []
        if ahead < chunks:
            products.append(lambda: hiddens.update({ahead: dot(normed_low, w_in(ahead))}))
            products.append(lambda: slopes.update({ahead: dot_nt(cot[...], w_out(ahead))}))
        if behind >= 0:
            active = actives[:, behind * D : (behind + 1) * D]
            grad = grads.pop(behind)

            def add_forward():
                nonlocal forward
                one = dot(active, w_out(behind))
                forward = one if forward is None else forward + one

            def add_backward():
                nonlocal backward
                one = dot_nt(grad, w_in(behind))
                backward = one if backward is None else backward + one

            def weight():
                one = dot_tn(normed_low, grad).reshape(shards, depth, D)
                put_shares(me, same, other, behind * depth, one)

            products += [add_forward, add_backward, weight]
        rows = []
        if 0 <= step < chunks:
            hidden, slope = hiddens.pop(step), slopes.pop(step)
            bias_sum = 0.0
            for r, part in enumerate(parts):
                h = hidden[part] + small[3 + step : 4 + step]
                upto, density = gelu_parts(h)
                actives[part, step * D : (step + 1) * D] = (h * upto).astype(BF)
                rows.append((slope[part] * (upto + h * density)).astype(BF))
                bias_sum += jnp.sum(rows[-1].astype(F32), 0, keepdims=True)
                if r < len(products):
                    products[r]()
            bias_sums.append(bias_sum)
            grads[step] = jnp.concatenate(rows, 0)
        else:
            for product in products:
                product()
    back_sum[...] = backward
    result = mixed[...] + forward + bias_o
    kept[...] = result[: own * WIDTH]
    sent[...] = result[own * WIDTH :].astype(BF)
    put_smalls(same, other, 4 * depth, bias_sums)


def mlp_backward_body(
    mixed,
    cot,
    actives,
    back_sum,
    vectors,
    attn_slab,
    restored,
    grad_mixed,
    grad_win,
    same,
    other,
    wide,
):
    me = shard_place()
    shards, height = attn_slab.shape[:2]
    depth = (height - SMALL) // 4
    span = shards * D // FF
    gain = vectors[0:1]
    parts = [slice(r * WIDTH, (r + 1) * WIDTH) for r in range(WIN)]
    columns = column_places()
    w_proj = block_of(attn_slab, 3, depth)
    sums = [0.0] * 4
    branches = []
    for r, part in enumerate(parts):
        if r < FF // D:
            one = dot_tn(actives[:, r * D : (r + 1) * D], cot[...])
            put_shares(me, same, other, 0, one.reshape(span, 4 * depth, D), r * span)
        normed, scale = norm_stats(mixed[part, :])
        g = back_sum[part, :]
        c = cot[part, :].astype(F32)
        grad = c + norm_back(g, normed, scale, gain)
        grad_mixed[part, :] = grad
        branch = grad.astype(BF)
        branches.append(branch)
        for n, one in enumerate((g * normed, g, c, branch.astype(F32))):
            sums[n] += jnp.sum(one, 0, keepdims=True)
        grad_att = dot_nt(branch, w_proj).astype(BF)
        wide[:, r] = dot(columns, grad_att).reshape(WINDOWS, SLOT, D)
    proj = dot_tn(restored[...], jnp.concatenate(branches, 0)).reshape(shards, depth, D)
    put_shares(me, same, other, 4 * depth, proj)
    put_smalls(same, other, 5 * depth, sums)
    grad_win[...] = wide[...].reshape(PADDED, D).astype(BF)


def attn_backward_body(query, key, value, probs, grad_win, came, out, pairs):
    @pl.when(pl.program_id(0) == 0)
    def _():
        pairs[...] = came[...]

    masks = head_masks()
    parts = [slice(s * PLACES, (s + 1) * PLACES) for s in range(2)]
    feats = [slice(u * FEAT, (u + 1) * FEAT) for u in range(QUADS)]
    keys, shares, grads, queries, slopes = [], [], [], [], []
    for u in range(QUADS):
        q2 = query[:, feats[u]].astype(F32)
        k2 = key[:, feats[u]].astype(F32)
        v2 = value[:, feats[u]].astype(F32)
        go2 = grad_win[:, feats[u]].astype(F32)
        p2 = probs[0, u].astype(F32)
        for part in parts:
            keys.append(k2[part].astype(BF))
            shares.append(p2[part])
            grads.append(spread(go2[part], masks))
            queries.append(spread(q2[part], masks))
            slopes.append(dot_nt(v2[part].astype(BF), grads[-1]))
    lows = []
    for p, dp in zip(shares, slopes):
        inner = jnp.sum(p * dp, 0, keepdims=True)
        lows.append((p * (dp - inner)).astype(BF))
    dvs = [dot(p.astype(BF), go) for p, go in zip(shares, grads)]
    dks = [dot(ds, q) for ds, q in zip(lows, queries)]
    dqs = [dot_tn(ds, k) for ds, k in zip(lows, keys)]
    for u in range(QUADS):
        two = slice(2 * u, 2 * u + 2)
        pairs[u] += lows[2 * u].astype(F32) + lows[2 * u + 1].astype(F32)
        for c, held in enumerate(
            (
                [own_heads(dq) * SCALE for dq in dqs[two]],
                [dk * SCALE for dk in dks[two]],
                dvs[two],
            )
        ):
            both = jnp.concatenate(held, 0).astype(BF)
            out[:, c * D + u * FEAT : c * D + (u + 1) * FEAT] = both


def attn_last_body(
    grad_mixed,
    tokens,
    halo,
    slab,
    normed_win,
    pairs,
    *refs,
):
    grads = refs[:-5]
    kept, sent, same, other, wide = refs[-5:]
    me = shard_place()
    shards = slab.shape[0]
    depth = (slab.shape[1] - SMALL) // 4
    small = smalls_of(slab, 4 * depth)
    gain = small[0:1]
    own = WIN - SHIFT
    vectors = []
    for c in range(3):
        cols = slice(c * D, (c + 1) * D)
        g = jnp.concatenate([part[:, cols] for part in grads], 0)
        if c != 1:
            vectors.append(jnp.sum(g.astype(F32), 0, keepdims=True))
        put_shares(
            me, same, other, c * depth, dot_tn(normed_win[...], g).reshape(shards, depth, D)
        )
        part = dot_nt(g, block_of(slab, c, depth))
        total = part if c == 0 else total + part
    wide[...] = total.reshape(WINDOWS, WIN, SLOT, D)
    back = places_column()
    gain_sum = jnp.zeros((1, D), F32)
    bias_sum = jnp.zeros((1, D), F32)
    for r in range(WIN):
        here = wide[:, r].reshape(WINDOWS * SLOT, D).astype(BF)
        g = dot(back, here)
        x = (tokens[SHIFT + r] if r < own else halo[r - own]).astype(F32)
        normed, scale = norm_stats(x)
        gain_sum += jnp.sum(g * normed, 0, keepdims=True)
        bias_sum += jnp.sum(g, 0, keepdims=True)
        grad = grad_mixed[r * WIDTH : (r + 1) * WIDTH, :] + norm_back(g, normed, scale, gain)
        if r < own:
            kept[r * WIDTH : (r + 1) * WIDTH, :] = grad
        else:
            sent[(r - own) * WIDTH : (r - own + 1) * WIDTH, :] = grad.astype(BF)

    rows = [gain_sum, bias_sum, vectors[0], vectors[1]]
    halves = GROUP // QUAD
    picks = [table_pick(1, half, True) for half in range(halves)]
    for g in range(GROUPS):
        laid = jnp.zeros((PLACES, TAB_USED), F32)
        for half in range(halves):
            total = pairs[g * halves + half]
            high = total.astype(BF)
            low = (total - high.astype(F32)).astype(BF)
            laid += dot(high, picks[half]) + dot(low, picks[half])
        laid = jnp.concatenate([laid, jnp.zeros((PLACES, TAB - TAB_USED), F32)], 1)
        total = jnp.zeros((SLOT, TAB), F32)
        for r in range(WIN):
            total += pltpu.roll(
                laid[r * SLOT : (r + 1) * SLOT], (2 * WIN - 1) * GROUP * r, 1
            )
        total = pltpu.roll(total, 0, 1, stride=GROUP, stride_axis=0)
        row = jnp.sum(total, 0, keepdims=True)
        rows += [row[:, c * D : (c + 1) * D] for c in range(TAB // D)]
    put_smalls(same, other, 3 * depth, rows)


def region_views(regions, rows, place):
    here = lax.dynamic_slice_in_dim(regions[0], place * rows, rows, 0)
    windows = here.reshape(WIN, WINDOWS, WIN).transpose(1, 0, 2)
    windows = jnp.pad(windows, ((0, 0), (0, 0), (0, SLOT - WIN))).astype(F32)
    windows = windows.reshape(WINDOWS, PLACES)
    by_row = jnp.broadcast_to(windows[:, :, None], (WINDOWS, PLACES, 128))
    by_lane = jnp.tile(jnp.pad(windows, ((0, 0), (0, HOLD - PLACES))), (1, QUAD))
    return by_row, by_lane[:, None, :]


def per_device(
    tokens,
    regions,
    cotangent,
    gain_one,
    bias_one,
    w_qkv,
    bias_qv,
    table,
    w_proj,
    bias_proj,
    gain_two,
    bias_two,
    w_in,
    bias_in,
    w_out,
    bias_out,
):
    images, local_rows, columns, _ = tokens.shape
    assert images == 1 and local_rows == WIN and columns == WIDTH
    shards = lax.axis_size("shard")
    seq = lax.axis_index("seq").astype(jnp.int32)
    chips = shards // 2
    depth = D // shards
    own = WIN - SHIFT
    attn_params = (gain_one[None], bias_one[None], w_qkv, bias_qv, table.T)
    bin_rows = bias_in.reshape(-1, 128)
    mlp_params = (
        w_proj,
        bias_proj[None],
        gain_two[None],
        bias_two[None],
        w_in,
        bin_rows,
        w_out,
        bias_out[None],
    )
    attn_slab, mlp_slab, out_slab = kernel_call(
        pack_body,
        [like((4 * depth + SMALL, D), BF)] * 2 + [like((4 * depth, D), BF)],
        (*attn_params, *mlp_params),
        vmem=60,
    )
    pieces = gather_pieces(attn_slab)
    pieces, (out_slab,) = tie(pieces, [out_slab])
    attn_all = jnp.stack(pieces)
    out_pieces = gather_pieces(out_slab)
    mlp_all = lax.all_gather(mlp_slab, "shard")
    tokens_here = tokens[0]
    token_halo = shifted_2(tokens_here[:SHIFT], "seq", -1)
    cot_here = cotangent[0]
    cot_halo = shifted_2(cot_here[:SHIFT], "seq", -1)
    by_row, by_lane = region_views(regions, local_rows, seq)

    normed_win, query, key, value = kernel_call(
        project_body,
        [like((PADDED, D), BF)] * 4,
        (tokens_here, token_halo, attn_all),
        scratch=[pltpu.VMEM((WINDOWS, WIN, SLOT, D), F32)],
    )
    pair_rows = 2 * PLACES
    steps = WINDOWS // 2

    def rows_from(first, width=D):
        return pl.BlockSpec((pair_rows, width), lambda i: (first + i, 0))

    def probs_from(first):
        return pl.BlockSpec((1, QUADS, pair_rows, LANES), lambda i: (first + i, 0, 0, 0))

    def fixed(shape):
        return pl.BlockSpec(shape, lambda i: (0,) * len(shape))

    probs, restored, mixed = kernel_call(
        attn_forward_body,
        [
            like((steps, QUADS, pair_rows, LANES), BF),
            like((TOKENS, D), BF),
            like((TOKENS, D), F32),
        ],
        (attn_all, by_row, by_lane, tokens_here, token_halo, query, key, value),
        grid=(steps,),
        in_blocks=[
            fixed(attn_all.shape),
            pl.BlockSpec((2, *by_row.shape[1:]), lambda i: (i, 0, 0)),
            pl.BlockSpec((2, *by_lane.shape[1:]), lambda i: (i, 0, 0)),
            fixed(tokens_here.shape),
            fixed(token_halo.shape),
            rows_from(0),
            rows_from(0),
            rows_from(0),
        ],
        out_blocks=[probs_from(0), fixed((TOKENS, D)), fixed((TOKENS, D))],
        scratch=[
            pltpu.VMEM((WINDOWS, WIN, SLOT, D), F32),
            pltpu.VMEM((QUADS, PLACES, LANES), F32),
        ],
    )
    share_a = like((chips, 4 * depth + SMALL, D), BF)
    share_b = like((chips, 5 * depth + SMALL, D), BF)
    out_kept, out_sent, cot, actives, back_sum, vectors, same_a, other_a = kernel_call(
        mlp_forward_body,
        [
            like((own * WIDTH, D), F32),
            like((SHIFT * WIDTH, D), BF),
            like((TOKENS, D), BF),
            like((TOKENS, FF), BF),
            like((TOKENS, D), F32),
            like((SMALL, D), F32),
            share_a,
            share_a,
        ],
        (mixed, cot_here, cot_halo, mlp_all, jnp.stack(out_pieces)),
    )
    grad_mixed, grad_win, same_b, other_b = kernel_call(
        mlp_backward_body,
        [like((TOKENS, D), F32), like((PADDED, D), BF), share_b, share_b],
        (mixed, cot, actives, back_sum, vectors, attn_all, restored),
        scratch=[pltpu.VMEM((WINDOWS, WIN, SLOT, D), F32)],
    )

    def backward(first, count, grad_win, came):
        sums = like((QUADS, PLACES, LANES), F32)
        return kernel_call(
            attn_backward_body,
            [like((count * pair_rows, 3 * D), BF), sums],
            (query, key, value, probs, grad_win, came),
            grid=(count,),
            in_blocks=[rows_from(first)] * 3
            + [probs_from(first), rows_from(first), fixed(sums.shape)],
            out_blocks=[rows_from(0, 3 * D), fixed(sums.shape)],
            )

    none = jnp.zeros((QUADS, PLACES, LANES), F32)
    count = steps // 2
    came_a = exchange(other_a, "shard", 1)
    sums, (grad_win,) = tie(add_cores(same_a, came_a), [grad_win])
    parts_a = to_chips(sums)
    came_b = exchange(other_b, "shard", 1)
    early, pairs = backward(0, count, grad_win, none)
    sums, (pairs,) = tie(add_cores(same_b, came_b), [pairs])
    parts_b = to_chips(sums)
    late_part, pairs = backward(count, count, grad_win, pairs)
    keep_a, send = add_chips(same_a, came_a, parts_a)
    (send,), (pairs,) = tie([send], [pairs])
    near_a = exchange(send, "seq", 1)
    (out_halo,), (pairs,) = tie([shifted_2(out_sent, "seq", 1)], [pairs])
    tok_kept, tok_sent, attn_same, attn_other = kernel_call(
        attn_last_body,
        [
            like((own * WIDTH, D), F32),
            like((SHIFT * WIDTH, D), BF),
            like((chips, 3 * depth + SMALL, D), BF),
            like((chips, 3 * depth + SMALL, D), BF),
        ],
        (grad_mixed, tokens_here, token_halo, attn_all, normed_win, pairs, early, late_part),
        scratch=[pltpu.VMEM((WINDOWS, WIN, SLOT, D), F32)],
    )
    half_a = add_pair(keep_a, near_a)
    (half_a,), (attn_other, tok_sent) = tie([half_a], [attn_other, tok_sent])
    far_a = exchange(half_a, "seq", 2)
    attn_came = exchange(attn_other, "shard", 1)
    keep_b, send = add_chips(same_b, came_b, parts_b, 10_000_000_000)
    (send,), (attn_came,) = tie([send], [attn_came])
    near_b = exchange(send, "seq", 1)
    sums, (far_a,) = tie(add_cores(attn_same, attn_came), [far_a])
    attn_parts = to_chips(sums)
    half_a = seq_rest(add_pair(half_a, far_a))
    (half_a,), (near_b, tok_sent) = tie([half_a], [near_b, tok_sent])
    tok_halo = shifted_2(tok_sent, "seq", 1)
    half_b = add_pair(keep_b, near_b)
    far_b = exchange(half_b, "seq", 2)
    attn_parts, (far_b,) = tie(attn_parts, [far_b])
    half_b = seq_rest(add_pair(half_b, far_b))
    (half_b,), attn_parts = tie([half_b], attn_parts)
    keep, send = add_chips(attn_same, attn_came, attn_parts)
    def unpack(body, params, half, back):
        return kernel_call(
            body,
            [like(p.shape, F32) for p in params],
            (half, back),
            scratch=[
                pltpu.VMEM((2 * half.shape[0], D), BF),
                pltpu.SemaphoreType.DMA((2,)),
            ],
                apart=2,
        )

    def joined(halo, kept):
        return jnp.concatenate([halo.astype(F32), kept], 0).reshape(tokens.shape)

    near = exchange(send, "seq", 1)
    back_b = exchange(half_b, "seq", 1)
    half = add_pair(keep, near)
    far = exchange(half, "seq", 2)
    back_a = exchange(half_a, "seq", 1)
    half = seq_rest(add_pair(half, far))
    back = exchange(half, "seq", 1)
    in_grads = unpack(unpack_in_body, (w_in, bin_rows), half_a, back_a)
    column = gain_two[None]
    out_grads = unpack(unpack_out_body, (w_out, w_proj, *[column] * 4), half_b, back_b)
    grad_tokens = joined(tok_halo, tok_kept)
    output = joined(out_halo, out_kept)
    early, (back,) = tie([*in_grads, *out_grads, grad_tokens, output], [back])
    in_grads, out_grads, (grad_tokens, output) = early[:2], early[2:8], early[8:]
    attn_grads = unpack(unpack_attn_body, attn_params, half, back)
    g_wout, g_wproj, g_gain, g_offset, g_bout, g_bproj = out_grads
    summed = [*attn_grads[:4], attn_grads[4].T, g_wproj, g_bproj, g_gain, g_offset]
    summed += [*in_grads, g_wout, g_bout]

    targets = (
        gain_one,
        bias_one,
        w_qkv,
        bias_qv,
        table,
        w_proj,
        bias_proj,
        gain_two,
        bias_two,
        w_in,
        bias_in,
        w_out,
        bias_out,
    )
    grads = [g.reshape(p.shape) for g, p in zip(summed, targets)]
    return (output, grad_tokens, *grads)


def solution(mesh):
    return jax.shard_map(
        per_device,
        mesh=mesh,
        in_specs=(
            P("shard", "seq", None, None),
            P("shard", None, None),
            P("shard", "seq", None, None),
            P("shard"),
            P("shard"),
            P("shard", None),
            P(None, "shard"),
            P(None, "shard"),
            P("shard", None),
            P("shard"),
            P("shard"),
            P("shard"),
            P("shard", None),
            P("shard"),
            P("shard", None),
            P("shard"),
        ),
        out_specs=(
            P("shard", "seq", None, None),
            P("shard", "seq", None, None),
            P("shard"),
            P("shard"),
            P("shard", None),
            P(None, "shard"),
            P(None, "shard"),
            P("shard", None),
            P("shard"),
            P("shard"),
            P("shard"),
            P("shard", None),
            P("shard"),
            P("shard", None),
            P("shard"),
        ),
        check_vma=False,
    )
```

```python
import math

import jax
import jax.numpy as jnp
from jax import lax
from jax.experimental import pallas as pl
from jax.experimental.pallas import tpu as pltpu
from jax.sharding import PartitionSpec as P

D = 512
HEADS = 16
HEAD = 32
WIN = 7
SHIFT = 3
FF = 2048
WIDTH = 112
WINDOWS = WIDTH // WIN
SLOT = 8
PLACES = WIN * SLOT
GROUP = 8
GROUPS = HEADS // GROUP
QUAD = 4
QUADS = HEADS // QUAD
FEAT = QUAD * HEAD
HOLD = 64
LANES = QUAD * HOLD
TOKENS = WIN * WIDTH
PADDED = WINDOWS * PLACES
TAB = 1536
TAB_USED = 768
SMALL = 32
EPS = 1e-05
SCALE = HEAD**-0.5
BF = jnp.bfloat16
F32 = jnp.float32


def shifted_2(value, axis, by):
    peers = lax.axis_size(axis)
    return lax.ppermute(value, axis, [(i, (i + by) % peers) for i in range(peers)])


def dot(left, right, dims=((1,), (0,))):
    return lax.dot_general(left, right, (dims, ((), ())), preferred_element_type=F32)


def dot_nt(left, right):
    return dot(left, right, ((1,), (1,)))


def dot_tn(left, right):
    return dot(left, right, ((0,), (0,)))


def iota(shape, axis):
    return lax.broadcasted_iota(jnp.int32, shape, axis)


def shard_place():
    return lax.axis_index("shard").astype(jnp.int32)


def late_place():
    return lax.axis_index("seq").astype(jnp.int32) & 1


def one_hot(condition):
    return jnp.where(condition, 1.0, 0.0).astype(BF)


def column_places():
    slot = iota((WINDOWS * SLOT, WIDTH), 0)
    column = iota((WINDOWS * SLOT, WIDTH), 1)
    place = slot & (SLOT - 1)
    wanted = (slot >> 3) * WIN + place + SHIFT
    wanted = jnp.where(wanted >= WIDTH, wanted - WIDTH, wanted)
    return one_hot((wanted == column) & (place < WIN))


def places_column():
    slot = iota((WIDTH, WINDOWS * SLOT), 1)
    column = iota((WIDTH, WINDOWS * SLOT), 0)
    place = slot & (SLOT - 1)
    wanted = (slot >> 3) * WIN + place + SHIFT
    wanted = jnp.where(wanted >= WIDTH, wanted - WIDTH, wanted)
    return one_hot((wanted == column) & (place < WIN))


def head_masks():
    feature = iota((1, FEAT), 1) >> 5
    return [jnp.where(feature == h, 1.0, 0.0).astype(F32) for h in range(QUAD)]


def spread(values, masks):
    empty = jnp.zeros((HOLD - PLACES, FEAT), F32)
    rows = []
    for mask in masks:
        rows += [values * mask, empty]
    return jnp.concatenate(rows, 0).astype(BF)


def own_heads(values):
    feature = iota((PLACES, FEAT), 1) >> 5
    out = values[:PLACES]
    for h in range(1, QUAD):
        out = jnp.where(feature == h, values[h * HOLD : h * HOLD + PLACES], out)
    return out


def table_pick(row_axis, quad, backwards):
    shape = (TAB_USED, LANES) if row_axis == 0 else (LANES, TAB_USED)
    lane = iota(shape, row_axis)
    pair = iota(shape, 1 - row_axis)
    head, place = pair >> 6, pair & (HOLD - 1)
    row, column = place >> 3, place & (SLOT - 1)
    entry = row * (2 * WIN - 1) + column
    if backwards:
        entry = (WIN - 1) * 2 * WIN - entry
    held = head + quad % (GROUP // QUAD) * QUAD
    match = ((lane >> 3) == entry) & ((lane & 7) == held)
    return one_hot(match & (column < WIN) & (row < WIN))


def norm_stats(values):
    average = jnp.mean(values, -1, keepdims=True)
    centered = values - average
    variance = jnp.mean(centered * centered, -1, keepdims=True)
    scale = lax.rsqrt(variance + EPS)
    return centered * scale, scale


def norm_back(grad, normed, scale, gain):
    scaled = grad * gain
    first = jnp.mean(scaled, -1, keepdims=True)
    second = jnp.mean(scaled * normed, -1, keepdims=True)
    return scale * (scaled - first - normed * second)


def whole(memory=pltpu.VMEM):
    return pl.BlockSpec(memory_space=memory)


def kernel_call(
    body, outs, ins, scratch=(), apart=0, grid=None, in_blocks=None, out_blocks=None,
    vmem=16,
    flops=1024,
):
    in_specs = in_blocks or [whole()] * (len(ins) - apart) + [whole(pl.ANY)] * apart
    options = {"grid": grid} if grid else {}
    return pl.pallas_call(
        body,
        out_shape=tuple(outs),
        in_specs=in_specs,
        out_specs=tuple(out_blocks or [whole()] * len(outs)),
        scratch_shapes=list(scratch),
        cost_estimate=pl.CostEstimate(flops=flops, bytes_accessed=1024, transcendentals=0),
        compiler_params=pltpu.CompilerParams(vmem_limit_bytes=vmem * 1024 * 1024),
        **options,
    )(*ins)


def like(shape, dtype):
    return jax.ShapeDtypeStruct(shape, dtype)


def place(vector, lanes, me):
    w = vector.shape[1]
    pick = one_hot(iota((w, lanes), 1) == iota((w, lanes), 0) + me * w)
    wide = jnp.broadcast_to(vector, (8, w))
    return dot(wide.astype(BF), pick)[0:1]


def mine(row, w, me):
    lanes = row.shape[1]
    pick = one_hot(iota((lanes, w), 0) == iota((lanes, w), 1) + me * w)
    wide = jnp.broadcast_to(row, (8, lanes))
    return dot(wide.astype(BF), pick)[0:1]


def padded(rows, height):
    total = sum(r.shape[0] for r in rows)
    return jnp.concatenate(rows + [jnp.zeros((height - total, D), F32)], 0).astype(BF)


def pack_body(
    g1, b1, wqkv, bqv, table, wproj, bproj, g2, b2, win, bin_, wout, bout, attn, mlp, out
):
    depth = wqkv.shape[0]
    me = shard_place()
    for c in range(3):
        attn[c * depth : (c + 1) * depth, :] = wqkv[:, c * D : (c + 1) * D]
    attn[3 * depth : 4 * depth, :] = wproj[...]
    vectors = (g1[...], b1[...], bqv[0:1, :], bqv[1:2, :], bproj[...])
    rows = [place(v, D, me) for v in vectors]
    held, entries = table.shape
    lane = iota((entries, TAB), 1)
    spot = iota((entries, TAB), 0) * GROUP + TAB - (WIN - 1) * 2 * WIN * GROUP
    spot = jnp.where(spot >= TAB, spot - TAB, spot)
    values = table[...].astype(F32).T
    groups = [jnp.zeros((1, TAB), F32) for _ in range(GROUPS)]
    for h in range(held):
        head = me * held + h
        inside = lane == spot + (head & (GROUP - 1))
        row = jnp.sum(jnp.where(inside, values[:, h : h + 1], 0.0), 0, keepdims=True)
        for g in range(GROUPS):
            groups[g] = groups[g] + jnp.where((head >> 3) == g, row, 0.0)
    for g in range(GROUPS):
        rows += [groups[g][:, c * D : (c + 1) * D] for c in range(TAB // D)]
    attn[4 * depth :, :] = padded(rows, SMALL)
    for c in range(FF // D):
        mlp[c * depth : (c + 1) * depth, :] = win[:, c * D : (c + 1) * D]
    out[...] = wout[...]
    held = jnp.concatenate([bin_[r : r + 1] for r in range(bin_.shape[0])], 1)
    hidden_bias = place(held, FF, me)
    rows = [place(v, D, me) for v in (g2[...], b2[...], bout[...])]
    rows += [hidden_bias[:, c * D : (c + 1) * D] for c in range(FF // D)]
    mlp[4 * depth :, :] = padded(rows, SMALL)


def join_halves(late, half, back, both, sems):
    rows = half.shape[0]
    copies = []
    for n, (part, at) in enumerate(((half, late), (back, 1 - late))):
        to = both.at[pl.ds(pl.multiple_of(at * rows, 16), rows), :]
        copies.append(pltpu.make_async_copy(part, to, sems.at[n]))
    for copy in copies:
        copy.start()
    for copy in copies:
        copy.wait()


def unpack_attn_body(half, back, g1, b1, wqkv, bqv, table, attn, sems):
    depth = wqkv.shape[0]
    me = shard_place()
    join_halves(late_place(), half, back, attn, sems)
    for c in range(3):
        wqkv[:, c * D : (c + 1) * D] = attn[c * depth : (c + 1) * depth, :].astype(F32)
    small = attn[3 * depth :, :].astype(F32)
    g1[...] = mine(small[0:1], depth, me)
    b1[...] = mine(small[1:2], depth, me)
    bqv[0:1, :] = mine(small[2:3], depth, me)
    bqv[1:2, :] = mine(small[3:4], depth, me)
    held, entries = table.shape
    lane = iota((entries, TAB), 1)
    spot = (entries - 1 - iota((entries, TAB), 0)) * GROUP
    parts = TAB // D
    rows = [
        jnp.concatenate([small[4 + g * parts + c : 5 + g * parts + c] for c in range(parts)], 1)
        for g in range(GROUPS)
    ]
    which = iota((entries, held), 1)
    total = jnp.zeros((entries, held), F32)
    for h in range(held):
        head = me * held + h
        row = rows[0]
        for g in range(1, GROUPS):
            row = jnp.where((head >> 3) == g, rows[g], row)
        inside = lane == spot + (head & (GROUP - 1))
        column = jnp.sum(jnp.where(inside, row, 0.0), 1, keepdims=True)
        total = jnp.where(which == h, column, total)
    table[...] = total.T


def unpack_in_body(half, back, win, bin_, both, sems):
    depth = win.shape[0]
    join_halves(late_place(), half, back, both, sems)
    for c in range(FF // D):
        win[:, c * D : (c + 1) * D] = both[c * depth : (c + 1) * depth, :].astype(F32)
    small = both[4 * depth :, :].astype(F32)
    hidden = jnp.concatenate([small[c : c + 1] for c in range(FF // D)], 1)
    hidden = mine(hidden, depth * FF // D, shard_place())
    for r in range(bin_.shape[0]):
        bin_[r : r + 1] = hidden[:, r * 128 : (r + 1) * 128]


def unpack_out_body(half, back, wout, wproj, g2, b2, bout, bproj, both, sems):
    depth = wproj.shape[0]
    me = shard_place()
    join_halves(late_place(), half, back, both, sems)
    wout[...] = both[: 4 * depth, :].astype(F32)
    wproj[...] = both[4 * depth : 5 * depth, :].astype(F32)
    small = both[5 * depth :, :].astype(F32)
    g2[...] = mine(small[0:1], depth, me)
    b2[...] = mine(small[1:2], depth, me)
    bout[...] = mine(small[2:3], depth, me)
    bproj[...] = mine(small[3:4], depth, me)


def put_shares(me, same, other, start, values, first=0):
    core, chip = me & 1, me >> 1
    rows = values.shape[1]
    for c in range(values.shape[0] // 2):
        one, two = values[2 * c], values[2 * c + 1]
        q = (first // 2 + c) ^ chip
        same[q, start : start + rows, :] = jnp.where(core == 0, one, two).astype(BF)
        other[q, start : start + rows, :] = jnp.where(core == 0, two, one).astype(BF)


def put_smalls(same, other, start, rows):
    block = padded(rows, SMALL)
    for q in range(same.shape[0]):
        same[q, start:, :] = block
        other[q, start:, :] = block


def exchange(value, axis, mask):
    peers = lax.axis_size(axis)
    return lax.ppermute(value, axis, [(i, i ^ mask) for i in range(peers)])


def gather_pieces(slab):
    chips = lax.axis_size("shard") // 2
    pieces = [None] * (2 * chips)
    for q in range(chips):
        pieces[2 * q] = exchange(slab, "shard", 2 * q) if q else slab
    for q in range(chips):
        pieces[2 * q + 1] = exchange(pieces[2 * q], "shard", 1)
    return pieces


def add_pair(here, came):
    return (here.astype(F32) + came.astype(F32)).astype(BF)


def add_cores(same, came):
    return [add_pair(same[q], came[q]) for q in range(1, same.shape[0])]


def to_chips(sums):
    return [exchange(s, "shard", 2 * q + 2) for q, s in enumerate(sums)]


def add_chips_body(same, came, *refs):
    parts, (keep, send) = refs[:-2], refs[-2:]
    half = keep.shape[0]
    for at, target in ((late_place(), keep), (1 - late_place(), send)):
        rows = pl.ds(pl.multiple_of(at * half, 16), half)
        total = same[0, rows, :].astype(F32) + came[0, rows, :].astype(F32)
        for part in parts:
            total += part[rows, :].astype(F32)
        target[...] = total.astype(BF)


def add_chips(same, came, parts, flops=1024):
    half = like((same.shape[1] // 2, D), BF)
    return kernel_call(add_chips_body, [half, half], (same, came, *parts), flops=flops)


def seq_rest(half):
    reach = 4
    while reach < lax.axis_size("seq"):
        half = add_pair(half, exchange(half, "seq", reach))
        reach *= 2
    return half


def tie(first, second):
    first, second = list(first), list(second)
    out = lax.optimization_barrier((*first, *second))
    return list(out[: len(first)]), list(out[len(first) :])


def block_of(slab, c, depth):
    me = shard_place()
    rows = [slab[k ^ me, c * depth : (c + 1) * depth, :] for k in range(slab.shape[0])]
    return jnp.concatenate(rows, 0)


def smalls_of(slab, start):
    return jnp.sum(slab[:, start:, :].astype(F32), 0)


def project_body(tokens, halo, slab, normed_win, query, key, value, wide):
    columns = column_places()
    own = WIN - SHIFT
    depth = (slab.shape[1] - SMALL) // 4
    small = smalls_of(slab, 4 * depth)
    gain, offset, bias_q, bias_v = (small[r : r + 1] for r in range(4))
    for r in range(WIN):
        x = (tokens[SHIFT + r] if r < own else halo[r - own]).astype(F32)
        normed, _ = norm_stats(x)
        low = (normed * gain + offset).astype(BF)
        wide[:, r] = dot(columns, low).reshape(WINDOWS, SLOT, D)
    normed_win[...] = wide[...].reshape(PADDED, D).astype(BF)
    query[...] = (dot(normed_win[...], block_of(slab, 0, depth)) + bias_q).astype(BF)
    key[...] = dot(normed_win[...], block_of(slab, 1, depth)).astype(BF)
    value[...] = (dot(normed_win[...], block_of(slab, 2, depth)) + bias_v).astype(BF)


def attn_forward_body(
    slab, reg_rows, reg_lanes, tokens, halo, query, key, value, probs, restored, mixed, wide, bias
):
    n = pl.program_id(0)
    depth = (slab.shape[1] - SMALL) // 4

    @pl.when(n == 0)
    def _():
        small = smalls_of(slab, 4 * depth)
        parts = TAB // D
        empty = (iota((PLACES, LANES), 0) & (SLOT - 1)) == WIN
        turned = []
        for g in range(GROUPS):
            first = 5 + g * parts
            row = jnp.concatenate([small[first + c : first + c + 1] for c in range(parts)], 1)
            row = jnp.broadcast_to(row, (SLOT, TAB))
            row = pltpu.roll(row, 0, 1, stride=GROUP, stride_axis=0)
            rows = [pltpu.roll(row, (2 * WIN - 1) * GROUP * r, 1)[:, :TAB_USED] for r in range(WIN)]
            turned.append(jnp.concatenate(rows, 0).astype(BF))
        for half in range(GROUP // QUAD):
            pick = table_pick(0, half, False)
            for g in range(GROUPS):
                picked = dot(turned[g], pick)
                bias[g * (GROUP // QUAD) + half] = jnp.where(empty, -1e30, picked)

    masks = head_masks()
    penalty = [
        jnp.where(reg_rows[s][:, 0:1] != reg_lanes[s], -100.0, 0.0) for s in range(2)
    ]
    parts = [slice(s * PLACES, (s + 1) * PLACES) for s in range(2)]
    units = [(u, s) for u in range(QUADS) for s in range(2)]
    feats = [slice(u * FEAT, (u + 1) * FEAT) for u in range(QUADS)]
    values, scores = [], []
    for u in range(QUADS):
        q2 = query[:, feats[u]].astype(F32)
        k2 = key[:, feats[u]].astype(F32)
        v2 = value[:, feats[u]].astype(F32)
        for s in range(2):
            values.append(v2[parts[s]].astype(BF))
            scores.append(dot_nt(k2[parts[s]].astype(BF), spread(q2[parts[s]], masks)))
    shares = []
    for (u, s), score in zip(units, scores):
        logits = score * SCALE + bias[u] + penalty[s]
        powers = jnp.exp(logits - jnp.max(logits, 0, keepdims=True))
        shares.append(powers * (1.0 / jnp.sum(powers, 0, keepdims=True)))
    wholes = [dot_tn(p.astype(BF), v) for p, v in zip(shares, values)]
    for (u, s), o in zip(units, wholes):
        wide[2 * n + s, :, :, feats[u]] = own_heads(o).reshape(WIN, SLOT, FEAT)
    for u in range(QUADS):
        probs[0, u] = jnp.concatenate(shares[2 * u : 2 * u + 2], 0).astype(BF)

    @pl.when(n == pl.num_programs(0) - 1)
    def _():
        bias_proj = smalls_of(slab, 4 * depth)[4:5]
        back = places_column()
        own = WIN - SHIFT
        for r in range(WIN):
            here = wide[:, r].reshape(WINDOWS * SLOT, D).astype(BF)
            restored[r * WIDTH : (r + 1) * WIDTH, :] = dot(back, here).astype(BF)
        branch = dot(restored[...], block_of(slab, 3, depth)) + bias_proj
        for r in range(WIN):
            x = (tokens[SHIFT + r] if r < own else halo[r - own]).astype(F32)
            mixed[r * WIDTH : (r + 1) * WIDTH, :] = x + branch[r * WIDTH : (r + 1) * WIDTH]


def gelu_parts(h):
    under = 1.0 + (0.3275911 * 0.5**0.5) * jnp.abs(h)
    t = pl.reciprocal(under, approx=True)
    t = t * (2.0 - under * t)
    bell = jnp.exp2(h * h * (-0.5 / math.log(2.0)))
    poly = t * (
        0.127414796
        + t * (-0.142248368 + t * (0.7107068705 + t * (-0.7265760135 + t * 0.5307027145)))
    )
    tail = poly * bell
    upto = jnp.where(h >= 0, 1.0 - tail, tail)
    return upto, bell * 0.3989422804014327


def mlp_forward_body(
    mixed,
    out_slab,
    cotangent,
    cot_halo,
    slab_far,
    kept,
    sent,
    cot_rows,
    actives,
    back_sum,
    vectors,
    same,
    other,
    slab,
    sems,
):
    own = WIN - SHIFT
    copies = [
        pltpu.make_async_copy(slab_far, slab, sems.at[0]),
        pltpu.make_async_copy(cotangent.at[SHIFT:], cot_rows.at[:own], sems.at[1]),
        pltpu.make_async_copy(cot_halo, cot_rows.at[own:], sems.at[2]),
    ]
    for copy in copies:
        copy.start()
    me = shard_place()
    shards, height = slab.shape[:2]
    depth = (height - SMALL) // 4
    span = shards * D // FF
    chunks = FF // D
    parts = [slice(r * WIDTH, (r + 1) * WIDTH) for r in range(WIN)]
    normeds = [norm_stats(mixed[part, :])[0] for part in parts]
    for copy in copies:
        copy.wait()
    small = smalls_of(slab, 4 * depth)
    vectors[...] = small
    gain, offset, bias_o = (small[r : r + 1] for r in range(3))
    cot = cot_rows[...].reshape(TOKENS, D)
    lows = [(normed * gain + offset).astype(BF) for normed in normeds]
    normed_low = jnp.concatenate(lows, 0)

    def w_in(c):
        return slab[:, c * depth : (c + 1) * depth, :].reshape(D, D)

    def w_out(c):
        rows = [out_slab[k ^ me] for k in range(c * span, (c + 1) * span)]
        return jnp.concatenate(rows, 0)

    hiddens, slopes, grads, forward, backward, bias_sums = {}, {}, {}, None, None, []
    for step in range(-1, chunks + 1):
        ahead, behind = step + 1, step - 1
        products = []
        if ahead < chunks:
            products.append(lambda: hiddens.update({ahead: dot(normed_low, w_in(ahead))}))
            products.append(lambda: slopes.update({ahead: dot_nt(cot, w_out(ahead))}))
        if behind >= 0:
            active = actives[:, behind * D : (behind + 1) * D]
            grad = grads.pop(behind)

            def add_forward():
                nonlocal forward
                one = dot(active, w_out(behind))
                forward = one if forward is None else forward + one

            def add_backward():
                nonlocal backward
                one = dot_nt(grad, w_in(behind))
                backward = one if backward is None else backward + one

            def weight():
                one = dot_tn(normed_low, grad).reshape(shards, depth, D)
                put_shares(me, same, other, behind * depth, one)

            products += [add_forward, add_backward, weight]
        rows = []
        if 0 <= step < chunks:
            hidden, slope = hiddens.pop(step), slopes.pop(step)
            bias_sum = 0.0
            for r, part in enumerate(parts):
                h = hidden[part] + small[3 + step : 4 + step]
                upto, density = gelu_parts(h)
                actives[part, step * D : (step + 1) * D] = (h * upto).astype(BF)
                rows.append((slope[part] * (upto + h * density)).astype(BF))
                bias_sum += jnp.sum(rows[-1].astype(F32), 0, keepdims=True)
                if r < len(products):
                    products[r]()
            bias_sums.append(bias_sum)
            grads[step] = jnp.concatenate(rows, 0)
        else:
            for product in products:
                product()
    back_sum[...] = backward
    result = mixed[...] + forward + bias_o
    kept[...] = result[: own * WIDTH]
    sent[...] = result[own * WIDTH :].astype(BF)
    put_smalls(same, other, 4 * depth, bias_sums)


def mlp_backward_body(
    mixed,
    cot,
    actives,
    back_sum,
    vectors,
    attn_slab,
    restored,
    grad_mixed,
    grad_win,
    same,
    other,
    wide,
):
    me = shard_place()
    shards, height = attn_slab.shape[:2]
    depth = (height - SMALL) // 4
    span = shards * D // FF
    gain = vectors[0:1]
    parts = [slice(r * WIDTH, (r + 1) * WIDTH) for r in range(WIN)]
    columns = column_places()
    w_proj = block_of(attn_slab, 3, depth)
    sums = [0.0] * 4
    branches = []
    for r, part in enumerate(parts):
        if r < FF // D:
            one = dot_tn(actives[:, r * D : (r + 1) * D], cot[...])
            put_shares(me, same, other, 0, one.reshape(span, 4 * depth, D), r * span)
        normed, scale = norm_stats(mixed[part, :])
        g = back_sum[part, :]
        c = cot[part, :].astype(F32)
        grad = c + norm_back(g, normed, scale, gain)
        grad_mixed[part, :] = grad
        branch = grad.astype(BF)
        branches.append(branch)
        for n, one in enumerate((g * normed, g, c, branch.astype(F32))):
            sums[n] += jnp.sum(one, 0, keepdims=True)
        grad_att = dot_nt(branch, w_proj).astype(BF)
        wide[:, r] = dot(columns, grad_att).reshape(WINDOWS, SLOT, D)
    proj = dot_tn(restored[...], jnp.concatenate(branches, 0)).reshape(shards, depth, D)
    put_shares(me, same, other, 4 * depth, proj)
    put_smalls(same, other, 5 * depth, sums)
    grad_win[...] = wide[...].reshape(PADDED, D).astype(BF)


def attn_backward_body(query, key, value, probs, grad_win, came, out, pairs):
    @pl.when(pl.program_id(0) == 0)
    def _():
        pairs[...] = came[...]

    masks = head_masks()
    parts = [slice(s * PLACES, (s + 1) * PLACES) for s in range(2)]
    feats = [slice(u * FEAT, (u + 1) * FEAT) for u in range(QUADS)]
    keys, shares, grads, queries, slopes = [], [], [], [], []
    for u in range(QUADS):
        q2 = query[:, feats[u]].astype(F32)
        k2 = key[:, feats[u]].astype(F32)
        v2 = value[:, feats[u]].astype(F32)
        go2 = grad_win[:, feats[u]].astype(F32)
        p2 = probs[0, u].astype(F32)
        for part in parts:
            keys.append(k2[part].astype(BF))
            shares.append(p2[part])
            grads.append(spread(go2[part], masks))
            queries.append(spread(q2[part], masks))
            slopes.append(dot_nt(v2[part].astype(BF), grads[-1]))
    lows = []
    for p, dp in zip(shares, slopes):
        inner = jnp.sum(p * dp, 0, keepdims=True)
        lows.append((p * (dp - inner)).astype(BF))
    dvs = [dot(p.astype(BF), go) for p, go in zip(shares, grads)]
    dks = [dot(ds, q) for ds, q in zip(lows, queries)]
    dqs = [dot_tn(ds, k) for ds, k in zip(lows, keys)]
    for u in range(QUADS):
        two = slice(2 * u, 2 * u + 2)
        pairs[u] += lows[2 * u].astype(F32) + lows[2 * u + 1].astype(F32)
        for c, held in enumerate(
            (
                [own_heads(dq) * SCALE for dq in dqs[two]],
                [dk * SCALE for dk in dks[two]],
                dvs[two],
            )
        ):
            both = jnp.concatenate(held, 0).astype(BF)
            out[:, c * D + u * FEAT : c * D + (u + 1) * FEAT] = both


def attn_last_body(
    grad_mixed,
    tokens,
    halo,
    slab,
    normed_win,
    pairs,
    *refs,
):
    grads = refs[:-5]
    kept, sent, same, other, wide = refs[-5:]
    me = shard_place()
    shards = slab.shape[0]
    depth = (slab.shape[1] - SMALL) // 4
    small = smalls_of(slab, 4 * depth)
    gain = small[0:1]
    own = WIN - SHIFT
    vectors = []
    for c in range(3):
        cols = slice(c * D, (c + 1) * D)
        g = jnp.concatenate([part[:, cols] for part in grads], 0)
        if c != 1:
            vectors.append(jnp.sum(g.astype(F32), 0, keepdims=True))
        put_shares(
            me, same, other, c * depth, dot_tn(normed_win[...], g).reshape(shards, depth, D)
        )
        part = dot_nt(g, block_of(slab, c, depth))
        total = part if c == 0 else total + part
    wide[...] = total.reshape(WINDOWS, WIN, SLOT, D)
    back = places_column()
    gain_sum = jnp.zeros((1, D), F32)
    bias_sum = jnp.zeros((1, D), F32)
    for r in range(WIN):
        here = wide[:, r].reshape(WINDOWS * SLOT, D).astype(BF)
        g = dot(back, here)
        x = (tokens[SHIFT + r] if r < own else halo[r - own]).astype(F32)
        normed, scale = norm_stats(x)
        gain_sum += jnp.sum(g * normed, 0, keepdims=True)
        bias_sum += jnp.sum(g, 0, keepdims=True)
        grad = grad_mixed[r * WIDTH : (r + 1) * WIDTH, :] + norm_back(g, normed, scale, gain)
        if r < own:
            kept[r * WIDTH : (r + 1) * WIDTH, :] = grad
        else:
            sent[(r - own) * WIDTH : (r - own + 1) * WIDTH, :] = grad.astype(BF)

    rows = [gain_sum, bias_sum, vectors[0], vectors[1]]
    halves = GROUP // QUAD
    picks = [table_pick(1, half, True) for half in range(halves)]
    for g in range(GROUPS):
        laid = jnp.zeros((PLACES, TAB_USED), F32)
        for half in range(halves):
            total = pairs[g * halves + half]
            high = total.astype(BF)
            low = (total - high.astype(F32)).astype(BF)
            laid += dot(high, picks[half]) + dot(low, picks[half])
        laid = jnp.concatenate([laid, jnp.zeros((PLACES, TAB - TAB_USED), F32)], 1)
        total = jnp.zeros((SLOT, TAB), F32)
        for r in range(WIN):
            total += pltpu.roll(
                laid[r * SLOT : (r + 1) * SLOT], (2 * WIN - 1) * GROUP * r, 1
            )
        total = pltpu.roll(total, 0, 1, stride=GROUP, stride_axis=0)
        row = jnp.sum(total, 0, keepdims=True)
        rows += [row[:, c * D : (c + 1) * D] for c in range(TAB // D)]
    put_smalls(same, other, 3 * depth, rows)


def region_views(regions, rows, place):
    here = lax.dynamic_slice_in_dim(regions[0], place * rows, rows, 0)
    windows = here.reshape(WIN, WINDOWS, WIN).transpose(1, 0, 2)
    windows = jnp.pad(windows, ((0, 0), (0, 0), (0, SLOT - WIN))).astype(F32)
    windows = windows.reshape(WINDOWS, PLACES)
    by_row = jnp.broadcast_to(windows[:, :, None], (WINDOWS, PLACES, 128))
    by_lane = jnp.tile(jnp.pad(windows, ((0, 0), (0, HOLD - PLACES))), (1, QUAD))
    return by_row, by_lane[:, None, :]


def per_device(
    tokens,
    regions,
    cotangent,
    gain_one,
    bias_one,
    w_qkv,
    bias_qv,
    table,
    w_proj,
    bias_proj,
    gain_two,
    bias_two,
    w_in,
    bias_in,
    w_out,
    bias_out,
):
    images, local_rows, columns, _ = tokens.shape
    assert images == 1 and local_rows == WIN and columns == WIDTH
    shards = lax.axis_size("shard")
    seq = lax.axis_index("seq").astype(jnp.int32)
    chips = shards // 2
    depth = D // shards
    own = WIN - SHIFT
    attn_params = (gain_one[None], bias_one[None], w_qkv, bias_qv, table.T)
    bin_rows = bias_in.reshape(-1, 128)
    mlp_params = (
        w_proj,
        bias_proj[None],
        gain_two[None],
        bias_two[None],
        w_in,
        bin_rows,
        w_out,
        bias_out[None],
    )
    attn_slab, mlp_slab, out_slab = kernel_call(
        pack_body,
        [like((4 * depth + SMALL, D), BF)] * 2 + [like((4 * depth, D), BF)],
        (*attn_params, *mlp_params),
        vmem=60,
    )
    pieces = gather_pieces(attn_slab)
    pieces, (out_slab,) = tie(pieces, [out_slab])
    attn_all = jnp.stack(pieces)
    out_pieces = gather_pieces(out_slab)
    mlp_all = lax.all_gather(mlp_slab, "shard")
    tokens_here = tokens[0]
    token_halo = shifted_2(tokens_here[:SHIFT], "seq", -1)
    cot_here = cotangent[0]
    cot_halo = shifted_2(cot_here[:SHIFT], "seq", -1)
    by_row, by_lane = region_views(regions, local_rows, seq)

    normed_win, query, key, value = kernel_call(
        project_body,
        [like((PADDED, D), BF)] * 4,
        (tokens_here, token_halo, attn_all),
        scratch=[pltpu.VMEM((WINDOWS, WIN, SLOT, D), F32)],
    )
    pair_rows = 2 * PLACES
    steps = WINDOWS // 2

    def rows_from(first, width=D):
        return pl.BlockSpec((pair_rows, width), lambda i: (first + i, 0))

    def probs_from(first):
        return pl.BlockSpec((1, QUADS, pair_rows, LANES), lambda i: (first + i, 0, 0, 0))

    def fixed(shape):
        return pl.BlockSpec(shape, lambda i: (0,) * len(shape))

    probs, restored, mixed = kernel_call(
        attn_forward_body,
        [
            like((steps, QUADS, pair_rows, LANES), BF),
            like((TOKENS, D), BF),
            like((TOKENS, D), F32),
        ],
        (attn_all, by_row, by_lane, tokens_here, token_halo, query, key, value),
        grid=(steps,),
        in_blocks=[
            fixed(attn_all.shape),
            pl.BlockSpec((2, *by_row.shape[1:]), lambda i: (i, 0, 0)),
            pl.BlockSpec((2, *by_lane.shape[1:]), lambda i: (i, 0, 0)),
            fixed(tokens_here.shape),
            fixed(token_halo.shape),
            rows_from(0),
            rows_from(0),
            rows_from(0),
        ],
        out_blocks=[probs_from(0), fixed((TOKENS, D)), fixed((TOKENS, D))],
        scratch=[
            pltpu.VMEM((WINDOWS, WIN, SLOT, D), F32),
            pltpu.VMEM((QUADS, PLACES, LANES), F32),
        ],
    )
    share_a = like((chips, 4 * depth + SMALL, D), BF)
    share_b = like((chips, 5 * depth + SMALL, D), BF)
    out_kept, out_sent, cot, actives, back_sum, vectors, same_a, other_a = kernel_call(
        mlp_forward_body,
        [
            like((own * WIDTH, D), F32),
            like((SHIFT * WIDTH, D), BF),
            like((WIN, WIDTH, D), BF),
            like((TOKENS, FF), BF),
            like((TOKENS, D), F32),
            like((SMALL, D), F32),
            share_a,
            share_a,
        ],
        (mixed, jnp.stack(out_pieces), cot_here, cot_halo, mlp_all),
        scratch=[pltpu.VMEM(mlp_all.shape, BF), pltpu.SemaphoreType.DMA((3,))],
        apart=3,
    )
    grad_mixed, grad_win, same_b, other_b = kernel_call(
        mlp_backward_body,
        [like((TOKENS, D), F32), like((PADDED, D), BF), share_b, share_b],
        (mixed, cot.reshape(TOKENS, D), actives, back_sum, vectors, attn_all, restored),
        scratch=[pltpu.VMEM((WINDOWS, WIN, SLOT, D), F32)],
    )

    def backward(first, count, grad_win, came):
        sums = like((QUADS, PLACES, LANES), F32)
        return kernel_call(
            attn_backward_body,
            [like((count * pair_rows, 3 * D), BF), sums],
            (query, key, value, probs, grad_win, came),
            grid=(count,),
            in_blocks=[rows_from(first)] * 3
            + [probs_from(first), rows_from(first), fixed(sums.shape)],
            out_blocks=[rows_from(0, 3 * D), fixed(sums.shape)],
            )

    none = jnp.zeros((QUADS, PLACES, LANES), F32)
    count = steps // 2
    came_a = exchange(other_a, "shard", 1)
    sums, (grad_win,) = tie(add_cores(same_a, came_a), [grad_win])
    parts_a = to_chips(sums)
    came_b = exchange(other_b, "shard", 1)
    early, pairs = backward(0, count, grad_win, none)
    sums, (pairs,) = tie(add_cores(same_b, came_b), [pairs])
    parts_b = to_chips(sums)
    late_part, pairs = backward(count, count, grad_win, pairs)
    keep_a, send = add_chips(same_a, came_a, parts_a)
    (send,), (pairs,) = tie([send], [pairs])
    near_a = exchange(send, "seq", 1)
    (out_halo,), (pairs,) = tie([shifted_2(out_sent, "seq", 1)], [pairs])
    tok_kept, tok_sent, attn_same, attn_other = kernel_call(
        attn_last_body,
        [
            like((own * WIDTH, D), F32),
            like((SHIFT * WIDTH, D), BF),
            like((chips, 3 * depth + SMALL, D), BF),
            like((chips, 3 * depth + SMALL, D), BF),
        ],
        (grad_mixed, tokens_here, token_halo, attn_all, normed_win, pairs, early, late_part),
        scratch=[pltpu.VMEM((WINDOWS, WIN, SLOT, D), F32)],
    )
    half_a = add_pair(keep_a, near_a)
    (half_a,), (attn_other, tok_sent) = tie([half_a], [attn_other, tok_sent])
    far_a = exchange(half_a, "seq", 2)
    attn_came = exchange(attn_other, "shard", 1)
    keep_b, send = add_chips(same_b, came_b, parts_b, 10_000_000_000)
    (send,), (attn_came,) = tie([send], [attn_came])
    near_b = exchange(send, "seq", 1)
    sums, (far_a,) = tie(add_cores(attn_same, attn_came), [far_a])
    attn_parts = to_chips(sums)
    half_a = seq_rest(add_pair(half_a, far_a))
    (half_a,), (near_b,) = tie([half_a], [near_b])
    tok_halo = shifted_2(tok_sent, "seq", 1)
    half_b = add_pair(keep_b, near_b)
    far_b = exchange(half_b, "seq", 2)
    (*attn_parts, tok_halo), (far_b,) = tie([*attn_parts, tok_halo], [far_b])
    half_b = seq_rest(add_pair(half_b, far_b))
    (half_b,), attn_parts = tie([half_b], attn_parts)
    keep, send = add_chips(attn_same, attn_came, attn_parts)
    def unpack(body, params, half, back):
        return kernel_call(
            body,
            [like(p.shape, F32) for p in params],
            (half, back),
            scratch=[
                pltpu.VMEM((2 * half.shape[0], D), BF),
                pltpu.SemaphoreType.DMA((2,)),
            ],
                apart=2,
        )

    def joined(halo, kept):
        return jnp.concatenate([halo.astype(F32), kept], 0).reshape(tokens.shape)

    near = exchange(send, "seq", 1)
    back_b = exchange(half_b, "seq", 1)
    half = add_pair(keep, near)
    far = exchange(half, "seq", 2)
    back_a = exchange(half_a, "seq", 1)
    half = seq_rest(add_pair(half, far))
    back = exchange(half, "seq", 1)
    in_grads = unpack(unpack_in_body, (w_in, bin_rows), half_a, back_a)
    column = gain_two[None]
    out_grads = unpack(unpack_out_body, (w_out, w_proj, *[column] * 4), half_b, back_b)
    grad_tokens = joined(tok_halo, tok_kept)
    output = joined(out_halo, out_kept)
    early, (back,) = tie([*in_grads, *out_grads, grad_tokens, output], [back])
    in_grads, out_grads, (grad_tokens, output) = early[:2], early[2:8], early[8:]
    attn_grads = unpack(unpack_attn_body, attn_params, half, back)
    g_wout, g_wproj, g_gain, g_offset, g_bout, g_bproj = out_grads
    summed = [*attn_grads[:4], attn_grads[4].T, g_wproj, g_bproj, g_gain, g_offset]
    summed += [*in_grads, g_wout, g_bout]

    targets = (
        gain_one,
        bias_one,
        w_qkv,
        bias_qv,
        table,
        w_proj,
        bias_proj,
        gain_two,
        bias_two,
        w_in,
        bias_in,
        w_out,
        bias_out,
    )
    grads = [g.reshape(p.shape) for g, p in zip(summed, targets)]
    return (output, grad_tokens, *grads)


def solution(mesh):
    return jax.shard_map(
        per_device,
        mesh=mesh,
        in_specs=(
            P("shard", "seq", None, None),
            P("shard", None, None),
            P("shard", "seq", None, None),
            P("shard"),
            P("shard"),
            P("shard", None),
            P(None, "shard"),
            P(None, "shard"),
            P("shard", None),
            P("shard"),
            P("shard"),
            P("shard"),
            P("shard", None),
            P("shard"),
            P("shard", None),
            P("shard"),
        ),
        out_specs=(
            P("shard", "seq", None, None),
            P("shard", "seq", None, None),
            P("shard"),
            P("shard"),
            P("shard", None),
            P(None, "shard"),
            P(None, "shard"),
            P("shard", None),
            P("shard"),
            P("shard"),
            P("shard"),
            P("shard", None),
            P("shard"),
            P("shard", None),
            P("shard"),
        ),
        check_vma=False,
    )
```

```python
import math

import jax
import jax.numpy as jnp
from jax import lax
from jax.experimental import pallas as pl
from jax.experimental.pallas import tpu as pltpu
from jax.sharding import PartitionSpec as P

D = 512
HEADS = 16
HEAD = 32
WIN = 7
SHIFT = 3
FF = 2048
WIDTH = 112
WINDOWS = WIDTH // WIN
SLOT = 8
PLACES = WIN * SLOT
GROUP = 8
GROUPS = HEADS // GROUP
QUAD = 4
QUADS = HEADS // QUAD
FEAT = QUAD * HEAD
HOLD = 64
LANES = QUAD * HOLD
TOKENS = WIN * WIDTH
PADDED = WINDOWS * PLACES
TAB = 1536
TAB_USED = 768
SMALL = 32
EPS = 1e-05
SCALE = HEAD**-0.5
BF = jnp.bfloat16
F32 = jnp.float32


def shifted_2(value, axis, by):
    peers = lax.axis_size(axis)
    return lax.ppermute(value, axis, [(i, (i + by) % peers) for i in range(peers)])


def dot(left, right, dims=((1,), (0,))):
    return lax.dot_general(left, right, (dims, ((), ())), preferred_element_type=F32)


def dot_nt(left, right):
    return dot(left, right, ((1,), (1,)))


def dot_tn(left, right):
    return dot(left, right, ((0,), (0,)))


def iota(shape, axis):
    return lax.broadcasted_iota(jnp.int32, shape, axis)


def shard_place():
    return lax.axis_index("shard").astype(jnp.int32)


def late_place():
    return lax.axis_index("seq").astype(jnp.int32) & 1


def one_hot(condition):
    return jnp.where(condition, 1.0, 0.0).astype(BF)


def column_places():
    slot = iota((WINDOWS * SLOT, WIDTH), 0)
    column = iota((WINDOWS * SLOT, WIDTH), 1)
    place = slot & (SLOT - 1)
    wanted = (slot >> 3) * WIN + place + SHIFT
    wanted = jnp.where(wanted >= WIDTH, wanted - WIDTH, wanted)
    return one_hot((wanted == column) & (place < WIN))


def places_column():
    slot = iota((WIDTH, WINDOWS * SLOT), 1)
    column = iota((WIDTH, WINDOWS * SLOT), 0)
    place = slot & (SLOT - 1)
    wanted = (slot >> 3) * WIN + place + SHIFT
    wanted = jnp.where(wanted >= WIDTH, wanted - WIDTH, wanted)
    return one_hot((wanted == column) & (place < WIN))


def head_masks():
    feature = iota((1, FEAT), 1) >> 5
    return [jnp.where(feature == h, 1.0, 0.0).astype(F32) for h in range(QUAD)]


def spread(values, masks):
    empty = jnp.zeros((HOLD - PLACES, FEAT), F32)
    rows = []
    for mask in masks:
        rows += [values * mask, empty]
    return jnp.concatenate(rows, 0).astype(BF)


def own_heads(values):
    feature = iota((PLACES, FEAT), 1) >> 5
    out = values[:PLACES]
    for h in range(1, QUAD):
        out = jnp.where(feature == h, values[h * HOLD : h * HOLD + PLACES], out)
    return out


def table_pick(row_axis, quad, backwards):
    shape = (TAB_USED, LANES) if row_axis == 0 else (LANES, TAB_USED)
    lane = iota(shape, row_axis)
    pair = iota(shape, 1 - row_axis)
    head, place = pair >> 6, pair & (HOLD - 1)
    row, column = place >> 3, place & (SLOT - 1)
    entry = row * (2 * WIN - 1) + column
    if backwards:
        entry = (WIN - 1) * 2 * WIN - entry
    held = head + quad % (GROUP // QUAD) * QUAD
    match = ((lane >> 3) == entry) & ((lane & 7) == held)
    return one_hot(match & (column < WIN) & (row < WIN))


def norm_stats(values):
    average = jnp.mean(values, -1, keepdims=True)
    centered = values - average
    variance = jnp.mean(centered * centered, -1, keepdims=True)
    scale = lax.rsqrt(variance + EPS)
    return centered * scale, scale


def norm_back(grad, normed, scale, gain):
    scaled = grad * gain
    first = jnp.mean(scaled, -1, keepdims=True)
    second = jnp.mean(scaled * normed, -1, keepdims=True)
    return scale * (scaled - first - normed * second)


def whole(memory=pltpu.VMEM):
    return pl.BlockSpec(memory_space=memory)


def kernel_call(
    body, outs, ins, scratch=(), apart=0, grid=None, in_blocks=None, out_blocks=None,
    vmem=16,
    flops=1024,
):
    in_specs = in_blocks or [whole()] * (len(ins) - apart) + [whole(pl.ANY)] * apart
    options = {"grid": grid} if grid else {}
    return pl.pallas_call(
        body,
        out_shape=tuple(outs),
        in_specs=in_specs,
        out_specs=tuple(out_blocks or [whole()] * len(outs)),
        scratch_shapes=list(scratch),
        cost_estimate=pl.CostEstimate(flops=flops, bytes_accessed=1024, transcendentals=0),
        compiler_params=pltpu.CompilerParams(vmem_limit_bytes=vmem * 1024 * 1024),
        **options,
    )(*ins)


def like(shape, dtype):
    return jax.ShapeDtypeStruct(shape, dtype)


def place(vector, lanes, me):
    w = vector.shape[1]
    pick = one_hot(iota((w, lanes), 1) == iota((w, lanes), 0) + me * w)
    wide = jnp.broadcast_to(vector, (8, w))
    return dot(wide.astype(BF), pick)[0:1]


def mine(row, w, me):
    lanes = row.shape[1]
    pick = one_hot(iota((lanes, w), 0) == iota((lanes, w), 1) + me * w)
    wide = jnp.broadcast_to(row, (8, lanes))
    return dot(wide.astype(BF), pick)[0:1]


def padded(rows, height):
    total = sum(r.shape[0] for r in rows)
    return jnp.concatenate(rows + [jnp.zeros((height - total, D), F32)], 0).astype(BF)


def pack_body(
    g1, b1, wqkv, bqv, table, wproj, bproj, g2, b2, win, bin_, wout, bout, attn, mlp, out
):
    depth = wqkv.shape[0]
    me = shard_place()
    for c in range(3):
        attn[c * depth : (c + 1) * depth, :] = wqkv[:, c * D : (c + 1) * D]
    attn[3 * depth : 4 * depth, :] = wproj[...]
    vectors = (g1[...], b1[...], bqv[0:1, :], bqv[1:2, :], bproj[...])
    rows = [place(v, D, me) for v in vectors]
    held, entries = table.shape
    lane = iota((entries, TAB), 1)
    spot = iota((entries, TAB), 0) * GROUP + TAB - (WIN - 1) * 2 * WIN * GROUP
    spot = jnp.where(spot >= TAB, spot - TAB, spot)
    values = table[...].astype(F32).T
    groups = [jnp.zeros((1, TAB), F32) for _ in range(GROUPS)]
    for h in range(held):
        head = me * held + h
        inside = lane == spot + (head & (GROUP - 1))
        row = jnp.sum(jnp.where(inside, values[:, h : h + 1], 0.0), 0, keepdims=True)
        for g in range(GROUPS):
            groups[g] = groups[g] + jnp.where((head >> 3) == g, row, 0.0)
    for g in range(GROUPS):
        rows += [groups[g][:, c * D : (c + 1) * D] for c in range(TAB // D)]
    attn[4 * depth :, :] = padded(rows, SMALL)
    for c in range(FF // D):
        mlp[c * depth : (c + 1) * depth, :] = win[:, c * D : (c + 1) * D]
    out[...] = wout[...]
    held = jnp.concatenate([bin_[r : r + 1] for r in range(bin_.shape[0])], 1)
    hidden_bias = place(held, FF, me)
    rows = [place(v, D, me) for v in (g2[...], b2[...], bout[...])]
    rows += [hidden_bias[:, c * D : (c + 1) * D] for c in range(FF // D)]
    mlp[4 * depth :, :] = padded(rows, SMALL)


def join_halves(late, half, back, both, sems):
    rows = half.shape[0]
    copies = []
    for n, (part, at) in enumerate(((half, late), (back, 1 - late))):
        to = both.at[pl.ds(pl.multiple_of(at * rows, 16), rows), :]
        copies.append(pltpu.make_async_copy(part, to, sems.at[n]))
    for copy in copies:
        copy.start()
    for copy in copies:
        copy.wait()


def unpack_attn_body(half, back, g1, b1, wqkv, bqv, table, attn, sems):
    depth = wqkv.shape[0]
    me = shard_place()
    join_halves(late_place(), half, back, attn, sems)
    for c in range(3):
        wqkv[:, c * D : (c + 1) * D] = attn[c * depth : (c + 1) * depth, :].astype(F32)
    small = attn[3 * depth :, :].astype(F32)
    g1[...] = mine(small[0:1], depth, me)
    b1[...] = mine(small[1:2], depth, me)
    bqv[0:1, :] = mine(small[2:3], depth, me)
    bqv[1:2, :] = mine(small[3:4], depth, me)
    held, entries = table.shape
    lane = iota((entries, TAB), 1)
    spot = (entries - 1 - iota((entries, TAB), 0)) * GROUP
    parts = TAB // D
    rows = [
        jnp.concatenate([small[4 + g * parts + c : 5 + g * parts + c] for c in range(parts)], 1)
        for g in range(GROUPS)
    ]
    which = iota((entries, held), 1)
    total = jnp.zeros((entries, held), F32)
    for h in range(held):
        head = me * held + h
        row = rows[0]
        for g in range(1, GROUPS):
            row = jnp.where((head >> 3) == g, rows[g], row)
        inside = lane == spot + (head & (GROUP - 1))
        column = jnp.sum(jnp.where(inside, row, 0.0), 1, keepdims=True)
        total = jnp.where(which == h, column, total)
    table[...] = total.T


def unpack_in_body(half, back, win, bin_, both, sems):
    depth = win.shape[0]
    join_halves(late_place(), half, back, both, sems)
    for c in range(FF // D):
        win[:, c * D : (c + 1) * D] = both[c * depth : (c + 1) * depth, :].astype(F32)
    small = both[4 * depth :, :].astype(F32)
    hidden = jnp.concatenate([small[c : c + 1] for c in range(FF // D)], 1)
    hidden = mine(hidden, depth * FF // D, shard_place())
    for r in range(bin_.shape[0]):
        bin_[r : r + 1] = hidden[:, r * 128 : (r + 1) * 128]


def unpack_out_body(half, back, wout, wproj, g2, b2, bout, bproj, both, sems):
    depth = wproj.shape[0]
    me = shard_place()
    join_halves(late_place(), half, back, both, sems)
    wout[...] = both[: 4 * depth, :].astype(F32)
    wproj[...] = both[4 * depth : 5 * depth, :].astype(F32)
    small = both[5 * depth :, :].astype(F32)
    g2[...] = mine(small[0:1], depth, me)
    b2[...] = mine(small[1:2], depth, me)
    bout[...] = mine(small[2:3], depth, me)
    bproj[...] = mine(small[3:4], depth, me)


def put_shares(me, same, other, start, values, first=0):
    core, chip = me & 1, me >> 1
    rows = values.shape[1]
    for c in range(values.shape[0] // 2):
        one, two = values[2 * c], values[2 * c + 1]
        q = (first // 2 + c) ^ chip
        same[q, start : start + rows, :] = jnp.where(core == 0, one, two).astype(BF)
        other[q, start : start + rows, :] = jnp.where(core == 0, two, one).astype(BF)


def put_smalls(same, other, start, rows):
    block = padded(rows, SMALL)
    for q in range(same.shape[0]):
        same[q, start:, :] = block
        other[q, start:, :] = block


def exchange(value, axis, mask):
    peers = lax.axis_size(axis)
    return lax.ppermute(value, axis, [(i, i ^ mask) for i in range(peers)])


def gather_pieces(slab):
    chips = lax.axis_size("shard") // 2
    pieces = [None] * (2 * chips)
    for q in range(chips):
        pieces[2 * q] = exchange(slab, "shard", 2 * q) if q else slab
    for q in range(chips):
        pieces[2 * q + 1] = exchange(pieces[2 * q], "shard", 1)
    return pieces


def add_pair(here, came):
    return (here.astype(F32) + came.astype(F32)).astype(BF)


def add_cores(same, came):
    return [add_pair(same[q], came[q]) for q in range(1, same.shape[0])]


def to_chips(sums):
    return [exchange(s, "shard", 2 * q + 2) for q, s in enumerate(sums)]


def add_chips_body(same, came, *refs):
    parts, (keep, send) = refs[:-2], refs[-2:]
    half = keep.shape[0]
    for at, target in ((late_place(), keep), (1 - late_place(), send)):
        rows = pl.ds(pl.multiple_of(at * half, 16), half)
        total = same[0, rows, :].astype(F32) + came[0, rows, :].astype(F32)
        for part in parts:
            total += part[rows, :].astype(F32)
        target[...] = total.astype(BF)


def add_chips(same, came, parts, flops=1024):
    half = like((same.shape[1] // 2, D), BF)
    return kernel_call(add_chips_body, [half, half], (same, came, *parts), flops=flops)


def seq_rest(half):
    reach = 4
    while reach < lax.axis_size("seq"):
        half = add_pair(half, exchange(half, "seq", reach))
        reach *= 2
    return half


def tie(first, second):
    first, second = list(first), list(second)
    out = lax.optimization_barrier((*first, *second))
    return list(out[: len(first)]), list(out[len(first) :])


def after(first, second):
    return list(first), tie(first, second)[1]


def block_of(slab, c, depth):
    me = shard_place()
    rows = [slab[k ^ me, c * depth : (c + 1) * depth, :] for k in range(slab.shape[0])]
    return jnp.concatenate(rows, 0)


def smalls_of(slab, start):
    return jnp.sum(slab[:, start:, :].astype(F32), 0)


def project_body(tokens, halo, slab, normed_win, query, key, value, wide):
    columns = column_places()
    own = WIN - SHIFT
    depth = (slab.shape[1] - SMALL) // 4
    small = smalls_of(slab, 4 * depth)
    gain, offset, bias_q, bias_v = (small[r : r + 1] for r in range(4))
    for r in range(WIN):
        x = (tokens[SHIFT + r] if r < own else halo[r - own]).astype(F32)
        normed, _ = norm_stats(x)
        low = (normed * gain + offset).astype(BF)
        wide[:, r] = dot(columns, low).reshape(WINDOWS, SLOT, D)
    normed_win[...] = wide[...].reshape(PADDED, D).astype(BF)
    query[...] = (dot(normed_win[...], block_of(slab, 0, depth)) + bias_q).astype(BF)
    key[...] = dot(normed_win[...], block_of(slab, 1, depth)).astype(BF)
    value[...] = (dot(normed_win[...], block_of(slab, 2, depth)) + bias_v).astype(BF)


def attn_forward_body(
    slab, reg_rows, reg_lanes, tokens, halo, query, key, value, probs, restored, mixed, wide, bias
):
    n = pl.program_id(0)
    depth = (slab.shape[1] - SMALL) // 4

    @pl.when(n == 0)
    def _():
        small = smalls_of(slab, 4 * depth)
        parts = TAB // D
        empty = (iota((PLACES, LANES), 0) & (SLOT - 1)) == WIN
        turned = []
        for g in range(GROUPS):
            first = 5 + g * parts
            row = jnp.concatenate([small[first + c : first + c + 1] for c in range(parts)], 1)
            row = jnp.broadcast_to(row, (SLOT, TAB))
            row = pltpu.roll(row, 0, 1, stride=GROUP, stride_axis=0)
            rows = [pltpu.roll(row, (2 * WIN - 1) * GROUP * r, 1)[:, :TAB_USED] for r in range(WIN)]
            turned.append(jnp.concatenate(rows, 0).astype(BF))
        for half in range(GROUP // QUAD):
            pick = table_pick(0, half, False)
            for g in range(GROUPS):
                picked = dot(turned[g], pick)
                bias[g * (GROUP // QUAD) + half] = jnp.where(empty, -1e30, picked)

    masks = head_masks()
    penalty = [
        jnp.where(reg_rows[s][:, 0:1] != reg_lanes[s], -100.0, 0.0) for s in range(2)
    ]
    parts = [slice(s * PLACES, (s + 1) * PLACES) for s in range(2)]
    units = [(u, s) for u in range(QUADS) for s in range(2)]
    feats = [slice(u * FEAT, (u + 1) * FEAT) for u in range(QUADS)]
    values, scores = [], []
    for u in range(QUADS):
        q2 = query[:, feats[u]].astype(F32)
        k2 = key[:, feats[u]].astype(F32)
        v2 = value[:, feats[u]].astype(F32)
        for s in range(2):
            values.append(v2[parts[s]].astype(BF))
            scores.append(dot_nt(k2[parts[s]].astype(BF), spread(q2[parts[s]], masks)))
    shares = []
    for (u, s), score in zip(units, scores):
        logits = score * SCALE + bias[u] + penalty[s]
        powers = jnp.exp(logits - jnp.max(logits, 0, keepdims=True))
        shares.append(powers * (1.0 / jnp.sum(powers, 0, keepdims=True)))
    wholes = [dot_tn(p.astype(BF), v) for p, v in zip(shares, values)]
    for (u, s), o in zip(units, wholes):
        wide[2 * n + s, :, :, feats[u]] = own_heads(o).reshape(WIN, SLOT, FEAT)
    for u in range(QUADS):
        probs[0, u] = jnp.concatenate(shares[2 * u : 2 * u + 2], 0).astype(BF)

    @pl.when(n == pl.num_programs(0) - 1)
    def _():
        bias_proj = smalls_of(slab, 4 * depth)[4:5]
        back = places_column()
        own = WIN - SHIFT
        for r in range(WIN):
            here = wide[:, r].reshape(WINDOWS * SLOT, D).astype(BF)
            restored[r * WIDTH : (r + 1) * WIDTH, :] = dot(back, here).astype(BF)
        branch = dot(restored[...], block_of(slab, 3, depth)) + bias_proj
        for r in range(WIN):
            x = (tokens[SHIFT + r] if r < own else halo[r - own]).astype(F32)
            mixed[r * WIDTH : (r + 1) * WIDTH, :] = x + branch[r * WIDTH : (r + 1) * WIDTH]


def gelu_parts(h):
    under = 1.0 + (0.3275911 * 0.5**0.5) * jnp.abs(h)
    t = pl.reciprocal(under, approx=True)
    t = t * (2.0 - under * t)
    bell = jnp.exp2(h * h * (-0.5 / math.log(2.0)))
    poly = t * (
        0.127414796
        + t * (-0.142248368 + t * (0.7107068705 + t * (-0.7265760135 + t * 0.5307027145)))
    )
    tail = poly * bell
    upto = jnp.where(h >= 0, 1.0 - tail, tail)
    return upto, bell * 0.3989422804014327


def mlp_forward_body(
    mixed,
    cotangent,
    cot_halo,
    slab,
    out_slab,
    kept,
    sent,
    cot,
    actives,
    back_sum,
    vectors,
    same,
    other,
):
    me = shard_place()
    shards, height = slab.shape[:2]
    depth = (height - SMALL) // 4
    span = shards * D // FF
    chunks = FF // D
    small = smalls_of(slab, 4 * depth)
    vectors[...] = small
    gain, offset, bias_o = (small[r : r + 1] for r in range(3))
    own = WIN - SHIFT
    parts = [slice(r * WIDTH, (r + 1) * WIDTH) for r in range(WIN)]
    lows = []
    for r, part in enumerate(parts):
        cot[part, :] = cotangent[SHIFT + r] if r < own else cot_halo[r - own]
        normed, _ = norm_stats(mixed[part, :])
        lows.append((normed * gain + offset).astype(BF))
    normed_low = jnp.concatenate(lows, 0)

    def w_in(c):
        return slab[:, c * depth : (c + 1) * depth, :].reshape(D, D)

    def w_out(c):
        rows = [out_slab[k ^ me] for k in range(c * span, (c + 1) * span)]
        return jnp.concatenate(rows, 0)

    hiddens, slopes, grads, forward, backward, bias_sums = {}, {}, {}, None, None, []
    for step in range(-1, chunks + 1):
        ahead, behind = step + 1, step - 1
        products = []
        if ahead < chunks:
            products.append(lambda: hiddens.update({ahead: dot(normed_low, w_in(ahead))}))
            products.append(lambda: slopes.update({ahead: dot_nt(cot[...], w_out(ahead))}))
        if behind >= 0:
            active = actives[:, behind * D : (behind + 1) * D]
            grad = grads.pop(behind)

            def add_forward():
                nonlocal forward
                one = dot(active, w_out(behind))
                forward = one if forward is None else forward + one

            def add_backward():
                nonlocal backward
                one = dot_nt(grad, w_in(behind))
                backward = one if backward is None else backward + one

            def weight():
                one = dot_tn(normed_low, grad).reshape(shards, depth, D)
                put_shares(me, same, other, behind * depth, one)

            products += [add_forward, add_backward, weight]
        rows = []
        if 0 <= step < chunks:
            hidden, slope = hiddens.pop(step), slopes.pop(step)
            bias_sum = 0.0
            for r, part in enumerate(parts):
                h = hidden[part] + small[3 + step : 4 + step]
                upto, density = gelu_parts(h)
                actives[part, step * D : (step + 1) * D] = (h * upto).astype(BF)
                rows.append((slope[part] * (upto + h * density)).astype(BF))
                bias_sum += jnp.sum(rows[-1].astype(F32), 0, keepdims=True)
                if r < len(products):
                    products[r]()
            bias_sums.append(bias_sum)
            grads[step] = jnp.concatenate(rows, 0)
        else:
            for product in products:
                product()
    back_sum[...] = backward
    result = mixed[...] + forward + bias_o
    kept[...] = result[: own * WIDTH]
    sent[...] = result[own * WIDTH :].astype(BF)
    put_smalls(same, other, 4 * depth, bias_sums)


def mlp_backward_body(
    mixed,
    cot,
    actives,
    back_sum,
    vectors,
    attn_slab,
    restored,
    grad_mixed,
    grad_win,
    same,
    other,
    wide,
):
    me = shard_place()
    shards, height = attn_slab.shape[:2]
    depth = (height - SMALL) // 4
    span = shards * D // FF
    gain = vectors[0:1]
    parts = [slice(r * WIDTH, (r + 1) * WIDTH) for r in range(WIN)]
    columns = column_places()
    w_proj = block_of(attn_slab, 3, depth)
    sums = [0.0] * 4
    branches = []
    for r, part in enumerate(parts):
        if r < FF // D:
            one = dot_tn(actives[:, r * D : (r + 1) * D], cot[...])
            put_shares(me, same, other, 0, one.reshape(span, 4 * depth, D), r * span)
        normed, scale = norm_stats(mixed[part, :])
        g = back_sum[part, :]
        c = cot[part, :].astype(F32)
        grad = c + norm_back(g, normed, scale, gain)
        grad_mixed[part, :] = grad
        branch = grad.astype(BF)
        branches.append(branch)
        for n, one in enumerate((g * normed, g, c, branch.astype(F32))):
            sums[n] += jnp.sum(one, 0, keepdims=True)
        grad_att = dot_nt(branch, w_proj).astype(BF)
        wide[:, r] = dot(columns, grad_att).reshape(WINDOWS, SLOT, D)
    proj = dot_tn(restored[...], jnp.concatenate(branches, 0)).reshape(shards, depth, D)
    put_shares(me, same, other, 4 * depth, proj)
    put_smalls(same, other, 5 * depth, sums)
    grad_win[...] = wide[...].reshape(PADDED, D).astype(BF)


def attn_backward_body(query, key, value, probs, grad_win, came, out, pairs):
    @pl.when(pl.program_id(0) == 0)
    def _():
        pairs[...] = came[...]

    masks = head_masks()
    parts = [slice(s * PLACES, (s + 1) * PLACES) for s in range(2)]
    feats = [slice(u * FEAT, (u + 1) * FEAT) for u in range(QUADS)]
    keys, shares, grads, queries, slopes = [], [], [], [], []
    for u in range(QUADS):
        q2 = query[:, feats[u]].astype(F32)
        k2 = key[:, feats[u]].astype(F32)
        v2 = value[:, feats[u]].astype(F32)
        go2 = grad_win[:, feats[u]].astype(F32)
        p2 = probs[0, u].astype(F32)
        for part in parts:
            keys.append(k2[part].astype(BF))
            shares.append(p2[part])
            grads.append(spread(go2[part], masks))
            queries.append(spread(q2[part], masks))
            slopes.append(dot_nt(v2[part].astype(BF), grads[-1]))
    lows = []
    for p, dp in zip(shares, slopes):
        inner = jnp.sum(p * dp, 0, keepdims=True)
        lows.append((p * (dp - inner)).astype(BF))
    dvs = [dot(p.astype(BF), go) for p, go in zip(shares, grads)]
    dks = [dot(ds, q) for ds, q in zip(lows, queries)]
    dqs = [dot_tn(ds, k) for ds, k in zip(lows, keys)]
    for u in range(QUADS):
        two = slice(2 * u, 2 * u + 2)
        pairs[u] += lows[2 * u].astype(F32) + lows[2 * u + 1].astype(F32)
        for c, held in enumerate(
            (
                [own_heads(dq) * SCALE for dq in dqs[two]],
                [dk * SCALE for dk in dks[two]],
                dvs[two],
            )
        ):
            both = jnp.concatenate(held, 0).astype(BF)
            out[:, c * D + u * FEAT : c * D + (u + 1) * FEAT] = both


def attn_last_body(
    grad_mixed,
    tokens,
    halo,
    slab,
    normed_win,
    pairs,
    *refs,
):
    grads = refs[:-5]
    kept, sent, same, other, wide = refs[-5:]
    me = shard_place()
    shards = slab.shape[0]
    depth = (slab.shape[1] - SMALL) // 4
    small = smalls_of(slab, 4 * depth)
    gain = small[0:1]
    own = WIN - SHIFT
    vectors = []
    for c in range(3):
        cols = slice(c * D, (c + 1) * D)
        g = jnp.concatenate([part[:, cols] for part in grads], 0)
        if c != 1:
            vectors.append(jnp.sum(g.astype(F32), 0, keepdims=True))
        put_shares(
            me, same, other, c * depth, dot_tn(normed_win[...], g).reshape(shards, depth, D)
        )
        part = dot_nt(g, block_of(slab, c, depth))
        total = part if c == 0 else total + part
    wide[...] = total.reshape(WINDOWS, WIN, SLOT, D)
    back = places_column()
    gain_sum = jnp.zeros((1, D), F32)
    bias_sum = jnp.zeros((1, D), F32)
    for r in range(WIN):
        here = wide[:, r].reshape(WINDOWS * SLOT, D).astype(BF)
        g = dot(back, here)
        x = (tokens[SHIFT + r] if r < own else halo[r - own]).astype(F32)
        normed, scale = norm_stats(x)
        gain_sum += jnp.sum(g * normed, 0, keepdims=True)
        bias_sum += jnp.sum(g, 0, keepdims=True)
        grad = grad_mixed[r * WIDTH : (r + 1) * WIDTH, :] + norm_back(g, normed, scale, gain)
        if r < own:
            kept[r * WIDTH : (r + 1) * WIDTH, :] = grad
        else:
            sent[(r - own) * WIDTH : (r - own + 1) * WIDTH, :] = grad.astype(BF)

    rows = [gain_sum, bias_sum, vectors[0], vectors[1]]
    halves = GROUP // QUAD
    picks = [table_pick(1, half, True) for half in range(halves)]
    for g in range(GROUPS):
        laid = jnp.zeros((PLACES, TAB_USED), F32)
        for half in range(halves):
            total = pairs[g * halves + half]
            high = total.astype(BF)
            low = (total - high.astype(F32)).astype(BF)
            laid += dot(high, picks[half]) + dot(low, picks[half])
        laid = jnp.concatenate([laid, jnp.zeros((PLACES, TAB - TAB_USED), F32)], 1)
        total = jnp.zeros((SLOT, TAB), F32)
        for r in range(WIN):
            total += pltpu.roll(
                laid[r * SLOT : (r + 1) * SLOT], (2 * WIN - 1) * GROUP * r, 1
            )
        total = pltpu.roll(total, 0, 1, stride=GROUP, stride_axis=0)
        row = jnp.sum(total, 0, keepdims=True)
        rows += [row[:, c * D : (c + 1) * D] for c in range(TAB // D)]
    put_smalls(same, other, 3 * depth, rows)


def region_views(regions, rows, place):
    here = lax.dynamic_slice_in_dim(regions[0], place * rows, rows, 0)
    windows = here.reshape(WIN, WINDOWS, WIN).transpose(1, 0, 2)
    windows = jnp.pad(windows, ((0, 0), (0, 0), (0, SLOT - WIN))).astype(F32)
    windows = windows.reshape(WINDOWS, PLACES)
    by_row = jnp.broadcast_to(windows[:, :, None], (WINDOWS, PLACES, 128))
    by_lane = jnp.tile(jnp.pad(windows, ((0, 0), (0, HOLD - PLACES))), (1, QUAD))
    return by_row, by_lane[:, None, :]


def per_device(
    tokens,
    regions,
    cotangent,
    gain_one,
    bias_one,
    w_qkv,
    bias_qv,
    table,
    w_proj,
    bias_proj,
    gain_two,
    bias_two,
    w_in,
    bias_in,
    w_out,
    bias_out,
):
    images, local_rows, columns, _ = tokens.shape
    assert images == 1 and local_rows == WIN and columns == WIDTH
    shards = lax.axis_size("shard")
    seq = lax.axis_index("seq").astype(jnp.int32)
    chips = shards // 2
    depth = D // shards
    own = WIN - SHIFT
    attn_params = (gain_one[None], bias_one[None], w_qkv, bias_qv, table.T)
    bin_rows = bias_in.reshape(-1, 128)
    mlp_params = (
        w_proj,
        bias_proj[None],
        gain_two[None],
        bias_two[None],
        w_in,
        bin_rows,
        w_out,
        bias_out[None],
    )
    attn_slab, mlp_slab, out_slab = kernel_call(
        pack_body,
        [like((4 * depth + SMALL, D), BF)] * 2 + [like((4 * depth, D), BF)],
        (*attn_params, *mlp_params),
        vmem=60,
    )
    pieces = gather_pieces(attn_slab)
    pieces, (out_slab,) = tie(pieces, [out_slab])
    attn_all = jnp.stack(pieces)
    out_pieces = gather_pieces(out_slab)
    mlp_all = lax.all_gather(mlp_slab, "shard")
    tokens_here = tokens[0]
    token_halo = shifted_2(tokens_here[:SHIFT], "seq", -1)
    cot_here = cotangent[0]
    cot_halo = shifted_2(cot_here[:SHIFT], "seq", -1)
    by_row, by_lane = region_views(regions, local_rows, seq)

    normed_win, query, key, value = kernel_call(
        project_body,
        [like((PADDED, D), BF)] * 4,
        (tokens_here, token_halo, attn_all),
        scratch=[pltpu.VMEM((WINDOWS, WIN, SLOT, D), F32)],
    )
    pair_rows = 2 * PLACES
    steps = WINDOWS // 2

    def rows_from(first, width=D):
        return pl.BlockSpec((pair_rows, width), lambda i: (first + i, 0))

    def probs_from(first):
        return pl.BlockSpec((1, QUADS, pair_rows, LANES), lambda i: (first + i, 0, 0, 0))

    def fixed(shape):
        return pl.BlockSpec(shape, lambda i: (0,) * len(shape))

    probs, restored, mixed = kernel_call(
        attn_forward_body,
        [
            like((steps, QUADS, pair_rows, LANES), BF),
            like((TOKENS, D), BF),
            like((TOKENS, D), F32),
        ],
        (attn_all, by_row, by_lane, tokens_here, token_halo, query, key, value),
        grid=(steps,),
        in_blocks=[
            fixed(attn_all.shape),
            pl.BlockSpec((2, *by_row.shape[1:]), lambda i: (i, 0, 0)),
            pl.BlockSpec((2, *by_lane.shape[1:]), lambda i: (i, 0, 0)),
            fixed(tokens_here.shape),
            fixed(token_halo.shape),
            rows_from(0),
            rows_from(0),
            rows_from(0),
        ],
        out_blocks=[probs_from(0), fixed((TOKENS, D)), fixed((TOKENS, D))],
        scratch=[
            pltpu.VMEM((WINDOWS, WIN, SLOT, D), F32),
            pltpu.VMEM((QUADS, PLACES, LANES), F32),
        ],
    )
    share_a = like((chips, 4 * depth + SMALL, D), BF)
    share_b = like((chips, 5 * depth + SMALL, D), BF)
    out_kept, out_sent, cot, actives, back_sum, vectors, same_a, other_a = kernel_call(
        mlp_forward_body,
        [
            like((own * WIDTH, D), F32),
            like((SHIFT * WIDTH, D), BF),
            like((TOKENS, D), BF),
            like((TOKENS, FF), BF),
            like((TOKENS, D), F32),
            like((SMALL, D), F32),
            share_a,
            share_a,
        ],
        (mixed, cot_here, cot_halo, mlp_all, jnp.stack(out_pieces)),
    )
    grad_mixed, grad_win, same_b, other_b = kernel_call(
        mlp_backward_body,
        [like((TOKENS, D), F32), like((PADDED, D), BF), share_b, share_b],
        (mixed, cot, actives, back_sum, vectors, attn_all, restored),
        scratch=[pltpu.VMEM((WINDOWS, WIN, SLOT, D), F32)],
    )

    def backward(first, count, grad_win, came):
        sums = like((QUADS, PLACES, LANES), F32)
        return kernel_call(
            attn_backward_body,
            [like((count * pair_rows, 3 * D), BF), sums],
            (query, key, value, probs, grad_win, came),
            grid=(count,),
            in_blocks=[rows_from(first)] * 3
            + [probs_from(first), rows_from(first), fixed(sums.shape)],
            out_blocks=[rows_from(0, 3 * D), fixed(sums.shape)],
            )

    none = jnp.zeros((QUADS, PLACES, LANES), F32)
    count = steps // 2
    came_a = exchange(other_a, "shard", 1)
    sums, (grad_win,) = tie(add_cores(same_a, came_a), [grad_win])
    parts_a = to_chips(sums)
    came_b = exchange(other_b, "shard", 1)
    early, pairs = backward(0, count, grad_win, none)
    sums, (pairs,) = tie(add_cores(same_b, came_b), [pairs])
    parts_b = to_chips(sums)
    late_part, pairs = backward(count, count, grad_win, pairs)
    keep_a, send = add_chips(same_a, came_a, parts_a)
    (send,), (pairs,) = tie([send], [pairs])
    near_a = exchange(send, "seq", 1)
    (out_halo,), (pairs,) = tie([shifted_2(out_sent, "seq", 1)], [pairs])
    tok_kept, tok_sent, attn_same, attn_other = kernel_call(
        attn_last_body,
        [
            like((own * WIDTH, D), F32),
            like((SHIFT * WIDTH, D), BF),
            like((chips, 3 * depth + SMALL, D), BF),
            like((chips, 3 * depth + SMALL, D), BF),
        ],
        (grad_mixed, tokens_here, token_halo, attn_all, normed_win, pairs, early, late_part),
        scratch=[pltpu.VMEM((WINDOWS, WIN, SLOT, D), F32)],
    )
    half_a = add_pair(keep_a, near_a)
    (half_a,), (attn_other, tok_sent) = after([half_a], [attn_other, tok_sent])
    far_a = exchange(half_a, "seq", 2)
    attn_came = exchange(attn_other, "shard", 1)
    keep_b, send = add_chips(same_b, came_b, parts_b, 10_000_000_000)
    (send,), (attn_came,) = after([send], [attn_came])
    near_b = exchange(send, "seq", 1)
    sums, (far_a,) = after(add_cores(attn_same, attn_came), [far_a])
    attn_parts = to_chips(sums)
    half_a = seq_rest(add_pair(half_a, far_a))
    (half_a,), (near_b, tok_sent) = after([half_a], [near_b, tok_sent])
    tok_halo = shifted_2(tok_sent, "seq", 1)
    half_b = add_pair(keep_b, near_b)
    far_b = exchange(half_b, "seq", 2)
    attn_parts, (far_b,) = after(attn_parts, [far_b])
    half_b = seq_rest(add_pair(half_b, far_b))
    (half_b,), attn_parts = after([half_b], attn_parts)
    keep, send = add_chips(attn_same, attn_came, attn_parts)
    def unpack(body, params, half, back):
        return kernel_call(
            body,
            [like(p.shape, F32) for p in params],
            (half, back),
            scratch=[
                pltpu.VMEM((2 * half.shape[0], D), BF),
                pltpu.SemaphoreType.DMA((2,)),
            ],
                apart=2,
        )

    def joined(halo, kept):
        return jnp.concatenate([halo.astype(F32), kept], 0).reshape(tokens.shape)

    near = exchange(send, "seq", 1)
    back_b = exchange(half_b, "seq", 1)
    half = add_pair(keep, near)
    far = exchange(half, "seq", 2)
    back_a = exchange(half_a, "seq", 1)
    half = seq_rest(add_pair(half, far))
    back = exchange(half, "seq", 1)
    in_grads = unpack(unpack_in_body, (w_in, bin_rows), half_a, back_a)
    column = gain_two[None]
    out_grads = unpack(unpack_out_body, (w_out, w_proj, *[column] * 4), half_b, back_b)
    grad_tokens = joined(tok_halo, tok_kept)
    output = joined(out_halo, out_kept)
    early, (back,) = after([*in_grads, *out_grads, grad_tokens, output], [back])
    in_grads, out_grads, (grad_tokens, output) = early[:2], early[2:8], early[8:]
    attn_grads = unpack(unpack_attn_body, attn_params, half, back)
    g_wout, g_wproj, g_gain, g_offset, g_bout, g_bproj = out_grads
    summed = [*attn_grads[:4], attn_grads[4].T, g_wproj, g_bproj, g_gain, g_offset]
    summed += [*in_grads, g_wout, g_bout]

    targets = (
        gain_one,
        bias_one,
        w_qkv,
        bias_qv,
        table,
        w_proj,
        bias_proj,
        gain_two,
        bias_two,
        w_in,
        bias_in,
        w_out,
        bias_out,
    )
    grads = [g.reshape(p.shape) for g, p in zip(summed, targets)]
    return (output, grad_tokens, *grads)


def solution(mesh):
    return jax.shard_map(
        per_device,
        mesh=mesh,
        in_specs=(
            P("shard", "seq", None, None),
            P("shard", None, None),
            P("shard", "seq", None, None),
            P("shard"),
            P("shard"),
            P("shard", None),
            P(None, "shard"),
            P(None, "shard"),
            P("shard", None),
            P("shard"),
            P("shard"),
            P("shard"),
            P("shard", None),
            P("shard"),
            P("shard", None),
            P("shard"),
        ),
        out_specs=(
            P("shard", "seq", None, None),
            P("shard", "seq", None, None),
            P("shard"),
            P("shard"),
            P("shard", None),
            P(None, "shard"),
            P(None, "shard"),
            P("shard", None),
            P("shard"),
            P("shard"),
            P("shard"),
            P("shard", None),
            P("shard"),
            P("shard", None),
            P("shard"),
        ),
        check_vma=False,
    )
```

```python
import math

import jax
import jax.numpy as jnp
from jax import lax
from jax.experimental import pallas as pl
from jax.experimental.pallas import tpu as pltpu
from jax.sharding import PartitionSpec as P

D = 512
HEADS = 16
HEAD = 32
WIN = 7
SHIFT = 3
FF = 2048
WIDTH = 112
WINDOWS = WIDTH // WIN
SLOT = 8
PLACES = WIN * SLOT
GROUP = 8
GROUPS = HEADS // GROUP
QUAD = 4
QUADS = HEADS // QUAD
FEAT = QUAD * HEAD
HOLD = 64
LANES = QUAD * HOLD
TOKENS = WIN * WIDTH
PADDED = WINDOWS * PLACES
TAB = 1536
TAB_USED = 768
SMALL = 32
EPS = 1e-05
SCALE = HEAD**-0.5
BF = jnp.bfloat16
F32 = jnp.float32


def shifted_2(value, axis, by):
    peers = lax.axis_size(axis)
    return lax.ppermute(value, axis, [(i, (i + by) % peers) for i in range(peers)])


def dot(left, right, dims=((1,), (0,))):
    return lax.dot_general(left, right, (dims, ((), ())), preferred_element_type=F32)


def dot_nt(left, right):
    return dot(left, right, ((1,), (1,)))


def dot_tn(left, right):
    return dot(left, right, ((0,), (0,)))


def iota(shape, axis):
    return lax.broadcasted_iota(jnp.int32, shape, axis)


def shard_place():
    return lax.axis_index("shard").astype(jnp.int32)


def late_place():
    return lax.axis_index("seq").astype(jnp.int32) & 1


def one_hot(condition):
    return jnp.where(condition, 1.0, 0.0).astype(BF)


def column_places():
    slot = iota((WINDOWS * SLOT, WIDTH), 0)
    column = iota((WINDOWS * SLOT, WIDTH), 1)
    place = slot & (SLOT - 1)
    wanted = (slot >> 3) * WIN + place + SHIFT
    wanted = jnp.where(wanted >= WIDTH, wanted - WIDTH, wanted)
    return one_hot((wanted == column) & (place < WIN))


def places_column():
    slot = iota((WIDTH, WINDOWS * SLOT), 1)
    column = iota((WIDTH, WINDOWS * SLOT), 0)
    place = slot & (SLOT - 1)
    wanted = (slot >> 3) * WIN + place + SHIFT
    wanted = jnp.where(wanted >= WIDTH, wanted - WIDTH, wanted)
    return one_hot((wanted == column) & (place < WIN))


def head_masks():
    feature = iota((1, FEAT), 1) >> 5
    return [jnp.where(feature == h, 1.0, 0.0).astype(F32) for h in range(QUAD)]


def spread(values, masks):
    empty = jnp.zeros((HOLD - PLACES, FEAT), F32)
    rows = []
    for mask in masks:
        rows += [values * mask, empty]
    return jnp.concatenate(rows, 0).astype(BF)


def own_heads(values):
    feature = iota((PLACES, FEAT), 1) >> 5
    out = values[:PLACES]
    for h in range(1, QUAD):
        out = jnp.where(feature == h, values[h * HOLD : h * HOLD + PLACES], out)
    return out


def table_pick(row_axis, quad, backwards):
    shape = (TAB_USED, LANES) if row_axis == 0 else (LANES, TAB_USED)
    lane = iota(shape, row_axis)
    pair = iota(shape, 1 - row_axis)
    head, place = pair >> 6, pair & (HOLD - 1)
    row, column = place >> 3, place & (SLOT - 1)
    entry = row * (2 * WIN - 1) + column
    if backwards:
        entry = (WIN - 1) * 2 * WIN - entry
    held = head + quad % (GROUP // QUAD) * QUAD
    match = ((lane >> 3) == entry) & ((lane & 7) == held)
    return one_hot(match & (column < WIN) & (row < WIN))


def norm_stats(values):
    average = jnp.mean(values, -1, keepdims=True)
    centered = values - average
    variance = jnp.mean(centered * centered, -1, keepdims=True)
    scale = lax.rsqrt(variance + EPS)
    return centered * scale, scale


def norm_back(grad, normed, scale, gain):
    scaled = grad * gain
    first = jnp.mean(scaled, -1, keepdims=True)
    second = jnp.mean(scaled * normed, -1, keepdims=True)
    return scale * (scaled - first - normed * second)


def whole(memory=pltpu.VMEM):
    return pl.BlockSpec(memory_space=memory)


def kernel_call(
    body, outs, ins, scratch=(), apart=0, grid=None, in_blocks=None, out_blocks=None,
    vmem=16,
    flops=1024,
):
    in_specs = in_blocks or [whole()] * (len(ins) - apart) + [whole(pl.ANY)] * apart
    options = {"grid": grid} if grid else {}
    return pl.pallas_call(
        body,
        out_shape=tuple(outs),
        in_specs=in_specs,
        out_specs=tuple(out_blocks or [whole()] * len(outs)),
        scratch_shapes=list(scratch),
        cost_estimate=pl.CostEstimate(flops=flops, bytes_accessed=1024, transcendentals=0),
        compiler_params=pltpu.CompilerParams(vmem_limit_bytes=vmem * 1024 * 1024),
        **options,
    )(*ins)


def like(shape, dtype):
    return jax.ShapeDtypeStruct(shape, dtype)


def place(vector, lanes, me):
    w = vector.shape[1]
    pick = one_hot(iota((w, lanes), 1) == iota((w, lanes), 0) + me * w)
    wide = jnp.broadcast_to(vector, (8, w))
    return dot(wide.astype(BF), pick)[0:1]


def mine(row, w, me):
    lanes = row.shape[1]
    pick = one_hot(iota((lanes, w), 0) == iota((lanes, w), 1) + me * w)
    wide = jnp.broadcast_to(row, (8, lanes))
    return dot(wide.astype(BF), pick)[0:1]


def padded(rows, height):
    total = sum(r.shape[0] for r in rows)
    return jnp.concatenate(rows + [jnp.zeros((height - total, D), F32)], 0).astype(BF)


def pack_body(
    g1, b1, wqkv, bqv, table, wproj, bproj, g2, b2, win, bin_, wout, bout, attn, mlp, out
):
    depth = wqkv.shape[0]
    me = shard_place()
    for c in range(3):
        attn[c * depth : (c + 1) * depth, :] = wqkv[:, c * D : (c + 1) * D]
    attn[3 * depth : 4 * depth, :] = wproj[...]
    vectors = (g1[...], b1[...], bqv[0:1, :], bqv[1:2, :], bproj[...])
    rows = [place(v, D, me) for v in vectors]
    held, entries = table.shape
    lane = iota((entries, TAB), 1)
    spot = iota((entries, TAB), 0) * GROUP + TAB - (WIN - 1) * 2 * WIN * GROUP
    spot = jnp.where(spot >= TAB, spot - TAB, spot)
    values = table[...].astype(F32).T
    groups = [jnp.zeros((1, TAB), F32) for _ in range(GROUPS)]
    for h in range(held):
        head = me * held + h
        inside = lane == spot + (head & (GROUP - 1))
        row = jnp.sum(jnp.where(inside, values[:, h : h + 1], 0.0), 0, keepdims=True)
        for g in range(GROUPS):
            groups[g] = groups[g] + jnp.where((head >> 3) == g, row, 0.0)
    for g in range(GROUPS):
        rows += [groups[g][:, c * D : (c + 1) * D] for c in range(TAB // D)]
    attn[4 * depth :, :] = padded(rows, SMALL)
    for c in range(FF // D):
        mlp[c * depth : (c + 1) * depth, :] = win[:, c * D : (c + 1) * D]
    out[...] = wout[...]
    held = jnp.concatenate([bin_[r : r + 1] for r in range(bin_.shape[0])], 1)
    hidden_bias = place(held, FF, me)
    rows = [place(v, D, me) for v in (g2[...], b2[...], bout[...])]
    rows += [hidden_bias[:, c * D : (c + 1) * D] for c in range(FF // D)]
    mlp[4 * depth :, :] = padded(rows, SMALL)


def join_halves(late, half, back, both, sems):
    rows = half.shape[0]
    copies = []
    for n, (part, at) in enumerate(((half, late), (back, 1 - late))):
        to = both.at[pl.ds(pl.multiple_of(at * rows, 16), rows), :]
        copies.append(pltpu.make_async_copy(part, to, sems.at[n]))
    for copy in copies:
        copy.start()
    for copy in copies:
        copy.wait()


def unpack_attn_body(half, back, g1, b1, wqkv, bqv, table, attn, sems):
    depth = wqkv.shape[0]
    me = shard_place()
    join_halves(late_place(), half, back, attn, sems)
    for c in range(3):
        wqkv[:, c * D : (c + 1) * D] = attn[c * depth : (c + 1) * depth, :].astype(F32)
    small = attn[3 * depth :, :].astype(F32)
    g1[...] = mine(small[0:1], depth, me)
    b1[...] = mine(small[1:2], depth, me)
    bqv[0:1, :] = mine(small[2:3], depth, me)
    bqv[1:2, :] = mine(small[3:4], depth, me)
    held, entries = table.shape
    lane = iota((entries, TAB), 1)
    spot = (entries - 1 - iota((entries, TAB), 0)) * GROUP
    parts = TAB // D
    rows = [
        jnp.concatenate([small[4 + g * parts + c : 5 + g * parts + c] for c in range(parts)], 1)
        for g in range(GROUPS)
    ]
    which = iota((entries, held), 1)
    total = jnp.zeros((entries, held), F32)
    for h in range(held):
        head = me * held + h
        row = rows[0]
        for g in range(1, GROUPS):
            row = jnp.where((head >> 3) == g, rows[g], row)
        inside = lane == spot + (head & (GROUP - 1))
        column = jnp.sum(jnp.where(inside, row, 0.0), 1, keepdims=True)
        total = jnp.where(which == h, column, total)
    table[...] = total.T


def unpack_in_body(half, back, win, bin_, both, sems):
    depth = win.shape[0]
    join_halves(late_place(), half, back, both, sems)
    for c in range(FF // D):
        win[:, c * D : (c + 1) * D] = both[c * depth : (c + 1) * depth, :].astype(F32)
    small = both[4 * depth :, :].astype(F32)
    hidden = jnp.concatenate([small[c : c + 1] for c in range(FF // D)], 1)
    hidden = mine(hidden, depth * FF // D, shard_place())
    for r in range(bin_.shape[0]):
        bin_[r : r + 1] = hidden[:, r * 128 : (r + 1) * 128]


def unpack_out_body(half, back, wout, wproj, g2, b2, bout, bproj, both, sems):
    depth = wproj.shape[0]
    me = shard_place()
    join_halves(late_place(), half, back, both, sems)
    wout[...] = both[: 4 * depth, :].astype(F32)
    wproj[...] = both[4 * depth : 5 * depth, :].astype(F32)
    small = both[5 * depth :, :].astype(F32)
    g2[...] = mine(small[0:1], depth, me)
    b2[...] = mine(small[1:2], depth, me)
    bout[...] = mine(small[2:3], depth, me)
    bproj[...] = mine(small[3:4], depth, me)


def put_shares(me, same, other, start, values, first=0):
    core, chip = me & 1, me >> 1
    rows = values.shape[1]
    for c in range(values.shape[0] // 2):
        one, two = values[2 * c], values[2 * c + 1]
        q = (first // 2 + c) ^ chip
        same[q, start : start + rows, :] = jnp.where(core == 0, one, two).astype(BF)
        other[q, start : start + rows, :] = jnp.where(core == 0, two, one).astype(BF)


def put_smalls(same, other, start, rows):
    block = padded(rows, SMALL)
    for q in range(same.shape[0]):
        same[q, start:, :] = block
        other[q, start:, :] = block


def exchange(value, axis, mask):
    peers = lax.axis_size(axis)
    return lax.ppermute(value, axis, [(i, i ^ mask) for i in range(peers)])


def gather_pieces(slab):
    chips = lax.axis_size("shard") // 2
    pieces = [None] * (2 * chips)
    for q in range(chips):
        pieces[2 * q] = exchange(slab, "shard", 2 * q) if q else slab
    for q in range(chips):
        pieces[2 * q + 1] = exchange(pieces[2 * q], "shard", 1)
    return pieces


def add_pair(here, came):
    return (here.astype(F32) + came.astype(F32)).astype(BF)


def add_cores(same, came):
    return [add_pair(same[q], came[q]) for q in range(1, same.shape[0])]


def to_chips(sums):
    return [exchange(s, "shard", 2 * q + 2) for q, s in enumerate(sums)]


def add_chips_body(same, came, *refs):
    parts, (keep, send) = refs[:-2], refs[-2:]
    half = keep.shape[0]
    for at, target in ((late_place(), keep), (1 - late_place(), send)):
        rows = pl.ds(pl.multiple_of(at * half, 16), half)
        total = same[0, rows, :].astype(F32) + came[0, rows, :].astype(F32)
        for part in parts:
            total += part[rows, :].astype(F32)
        target[...] = total.astype(BF)


def add_chips(same, came, parts, flops=1024):
    half = like((same.shape[1] // 2, D), BF)
    return kernel_call(add_chips_body, [half, half], (same, came, *parts), flops=flops)


def seq_rest(half):
    reach = 4
    while reach < lax.axis_size("seq"):
        half = add_pair(half, exchange(half, "seq", reach))
        reach *= 2
    return half


def tie(first, second):
    first, second = list(first), list(second)
    out = lax.optimization_barrier((*first, *second))
    return list(out[: len(first)]), list(out[len(first) :])


def after(first, second):
    return list(first), tie(first, second)[1]


def block_of(slab, c, depth):
    me = shard_place()
    rows = [slab[k ^ me, c * depth : (c + 1) * depth, :] for k in range(slab.shape[0])]
    return jnp.concatenate(rows, 0)


def smalls_of(slab, start):
    return jnp.sum(slab[:, start:, :].astype(F32), 0)


def project_body(tokens, halo, slab, normed_win, query, key, value, wide):
    columns = column_places()
    own = WIN - SHIFT
    depth = (slab.shape[1] - SMALL) // 4
    small = smalls_of(slab, 4 * depth)
    gain, offset, bias_q, bias_v = (small[r : r + 1] for r in range(4))
    for r in range(WIN):
        x = (tokens[SHIFT + r] if r < own else halo[r - own]).astype(F32)
        normed, _ = norm_stats(x)
        low = (normed * gain + offset).astype(BF)
        wide[:, r] = dot(columns, low).reshape(WINDOWS, SLOT, D)
    normed_win[...] = wide[...].reshape(PADDED, D).astype(BF)
    query[...] = (dot(normed_win[...], block_of(slab, 0, depth)) + bias_q).astype(BF)
    key[...] = dot(normed_win[...], block_of(slab, 1, depth)).astype(BF)
    value[...] = (dot(normed_win[...], block_of(slab, 2, depth)) + bias_v).astype(BF)


def attn_forward_body(
    slab, reg_rows, reg_lanes, tokens, halo, query, key, value, probs, restored, mixed, wide, bias
):
    n = pl.program_id(0)
    depth = (slab.shape[1] - SMALL) // 4

    @pl.when(n == 0)
    def _():
        small = smalls_of(slab, 4 * depth)
        parts = TAB // D
        empty = (iota((PLACES, LANES), 0) & (SLOT - 1)) == WIN
        turned = []
        for g in range(GROUPS):
            first = 5 + g * parts
            row = jnp.concatenate([small[first + c : first + c + 1] for c in range(parts)], 1)
            row = jnp.broadcast_to(row, (SLOT, TAB))
            row = pltpu.roll(row, 0, 1, stride=GROUP, stride_axis=0)
            rows = [pltpu.roll(row, (2 * WIN - 1) * GROUP * r, 1)[:, :TAB_USED] for r in range(WIN)]
            turned.append(jnp.concatenate(rows, 0).astype(BF))
        for half in range(GROUP // QUAD):
            pick = table_pick(0, half, False)
            for g in range(GROUPS):
                picked = dot(turned[g], pick)
                bias[g * (GROUP // QUAD) + half] = jnp.where(empty, -1e30, picked)

    masks = head_masks()
    penalty = [
        jnp.where(reg_rows[s][:, 0:1] != reg_lanes[s], -100.0, 0.0) for s in range(2)
    ]
    parts = [slice(s * PLACES, (s + 1) * PLACES) for s in range(2)]
    units = [(u, s) for u in range(QUADS) for s in range(2)]
    feats = [slice(u * FEAT, (u + 1) * FEAT) for u in range(QUADS)]
    values, scores = [], []
    for u in range(QUADS):
        q2 = query[:, feats[u]].astype(F32)
        k2 = key[:, feats[u]].astype(F32)
        v2 = value[:, feats[u]].astype(F32)
        for s in range(2):
            values.append(v2[parts[s]].astype(BF))
            scores.append(dot_nt(k2[parts[s]].astype(BF), spread(q2[parts[s]], masks)))
    shares = []
    for (u, s), score in zip(units, scores):
        logits = score * SCALE + bias[u] + penalty[s]
        powers = jnp.exp(logits - jnp.max(logits, 0, keepdims=True))
        shares.append(powers * (1.0 / jnp.sum(powers, 0, keepdims=True)))
    wholes = [dot_tn(p.astype(BF), v) for p, v in zip(shares, values)]
    for (u, s), o in zip(units, wholes):
        wide[2 * n + s, :, :, feats[u]] = own_heads(o).reshape(WIN, SLOT, FEAT)
    for u in range(QUADS):
        probs[0, u] = jnp.concatenate(shares[2 * u : 2 * u + 2], 0).astype(BF)

    @pl.when(n == pl.num_programs(0) - 1)
    def _():
        bias_proj = smalls_of(slab, 4 * depth)[4:5]
        back = places_column()
        own = WIN - SHIFT
        for r in range(WIN):
            here = wide[:, r].reshape(WINDOWS * SLOT, D).astype(BF)
            restored[r * WIDTH : (r + 1) * WIDTH, :] = dot(back, here).astype(BF)
        branch = dot(restored[...], block_of(slab, 3, depth)) + bias_proj
        for r in range(WIN):
            x = (tokens[SHIFT + r] if r < own else halo[r - own]).astype(F32)
            mixed[r * WIDTH : (r + 1) * WIDTH, :] = x + branch[r * WIDTH : (r + 1) * WIDTH]


def gelu_parts(h):
    under = 1.0 + (0.3275911 * 0.5**0.5) * jnp.abs(h)
    t = pl.reciprocal(under, approx=True)
    t = t * (2.0 - under * t)
    bell = jnp.exp2(h * h * (-0.5 / math.log(2.0)))
    poly = t * (
        0.127414796
        + t * (-0.142248368 + t * (0.7107068705 + t * (-0.7265760135 + t * 0.5307027145)))
    )
    tail = poly * bell
    upto = jnp.where(h >= 0, 1.0 - tail, tail)
    return upto, bell * 0.3989422804014327


def mlp_forward_body(
    mixed,
    cot,
    slab,
    out_slab,
    kept,
    sent,
    actives,
    back_sum,
    vectors,
    same,
    other,
):
    me = shard_place()
    shards, height = slab.shape[:2]
    depth = (height - SMALL) // 4
    span = shards * D // FF
    chunks = FF // D
    small = smalls_of(slab, 4 * depth)
    vectors[...] = small
    gain, offset, bias_o = (small[r : r + 1] for r in range(3))
    own = WIN - SHIFT
    parts = [slice(r * WIDTH, (r + 1) * WIDTH) for r in range(WIN)]
    lows = []
    for part in parts:
        normed, _ = norm_stats(mixed[part, :])
        lows.append((normed * gain + offset).astype(BF))
    normed_low = jnp.concatenate(lows, 0)

    def w_in(c):
        return slab[:, c * depth : (c + 1) * depth, :].reshape(D, D)

    def w_out(c):
        rows = [out_slab[k ^ me] for k in range(c * span, (c + 1) * span)]
        return jnp.concatenate(rows, 0)

    hiddens, slopes, grads, forward, backward, bias_sums = {}, {}, {}, None, None, []
    for step in range(-1, chunks + 1):
        ahead, behind = step + 1, step - 1
        products = []
        if ahead < chunks:
            products.append(lambda: hiddens.update({ahead: dot(normed_low, w_in(ahead))}))
            products.append(lambda: slopes.update({ahead: dot_nt(cot[...], w_out(ahead))}))
        if behind >= 0:
            active = actives[:, behind * D : (behind + 1) * D]
            grad = grads.pop(behind)

            def add_forward():
                nonlocal forward
                one = dot(active, w_out(behind))
                forward = one if forward is None else forward + one

            def add_backward():
                nonlocal backward
                one = dot_nt(grad, w_in(behind))
                backward = one if backward is None else backward + one

            def weight():
                one = dot_tn(normed_low, grad).reshape(shards, depth, D)
                put_shares(me, same, other, behind * depth, one)

            products += [add_forward, add_backward, weight]
        rows = []
        if 0 <= step < chunks:
            hidden, slope = hiddens.pop(step), slopes.pop(step)
            bias_sum = 0.0
            for r, part in enumerate(parts):
                h = hidden[part] + small[3 + step : 4 + step]
                upto, density = gelu_parts(h)
                actives[part, step * D : (step + 1) * D] = (h * upto).astype(BF)
                rows.append((slope[part] * (upto + h * density)).astype(BF))
                bias_sum += jnp.sum(rows[-1].astype(F32), 0, keepdims=True)
                if r < len(products):
                    products[r]()
            bias_sums.append(bias_sum)
            grads[step] = jnp.concatenate(rows, 0)
        else:
            for product in products:
                product()
    back_sum[...] = backward
    result = mixed[...] + forward + bias_o
    kept[...] = result[: own * WIDTH]
    sent[...] = result[own * WIDTH :].astype(BF)
    put_smalls(same, other, 4 * depth, bias_sums)


def mlp_backward_body(
    mixed,
    cot,
    actives,
    back_sum,
    vectors,
    attn_slab,
    restored,
    grad_mixed,
    grad_win,
    same,
    other,
    wide,
):
    me = shard_place()
    shards, height = attn_slab.shape[:2]
    depth = (height - SMALL) // 4
    span = shards * D // FF
    gain = vectors[0:1]
    parts = [slice(r * WIDTH, (r + 1) * WIDTH) for r in range(WIN)]
    columns = column_places()
    w_proj = block_of(attn_slab, 3, depth)
    sums = [0.0] * 4
    branches = []
    for r, part in enumerate(parts):
        if r < FF // D:
            one = dot_tn(actives[:, r * D : (r + 1) * D], cot[...])
            put_shares(me, same, other, 0, one.reshape(span, 4 * depth, D), r * span)
        normed, scale = norm_stats(mixed[part, :])
        g = back_sum[part, :]
        c = cot[part, :].astype(F32)
        grad = c + norm_back(g, normed, scale, gain)
        grad_mixed[part, :] = grad
        branch = grad.astype(BF)
        branches.append(branch)
        for n, one in enumerate((g * normed, g, c, branch.astype(F32))):
            sums[n] += jnp.sum(one, 0, keepdims=True)
        grad_att = dot_nt(branch, w_proj).astype(BF)
        wide[:, r] = dot(columns, grad_att).reshape(WINDOWS, SLOT, D)
    proj = dot_tn(restored[...], jnp.concatenate(branches, 0)).reshape(shards, depth, D)
    put_shares(me, same, other, 4 * depth, proj)
    put_smalls(same, other, 5 * depth, sums)
    grad_win[...] = wide[...].reshape(PADDED, D).astype(BF)


def attn_backward_body(query, key, value, probs, grad_win, came, out, pairs):
    @pl.when(pl.program_id(0) == 0)
    def _():
        pairs[...] = came[...]

    masks = head_masks()
    parts = [slice(s * PLACES, (s + 1) * PLACES) for s in range(2)]
    feats = [slice(u * FEAT, (u + 1) * FEAT) for u in range(QUADS)]
    keys, shares, grads, queries, slopes = [], [], [], [], []
    for u in range(QUADS):
        q2 = query[:, feats[u]].astype(F32)
        k2 = key[:, feats[u]].astype(F32)
        v2 = value[:, feats[u]].astype(F32)
        go2 = grad_win[:, feats[u]].astype(F32)
        p2 = probs[0, u].astype(F32)
        for part in parts:
            keys.append(k2[part].astype(BF))
            shares.append(p2[part])
            grads.append(spread(go2[part], masks))
            queries.append(spread(q2[part], masks))
            slopes.append(dot_nt(v2[part].astype(BF), grads[-1]))
    lows = []
    for p, dp in zip(shares, slopes):
        inner = jnp.sum(p * dp, 0, keepdims=True)
        lows.append((p * (dp - inner)).astype(BF))
    dvs = [dot(p.astype(BF), go) for p, go in zip(shares, grads)]
    dks = [dot(ds, q) for ds, q in zip(lows, queries)]
    dqs = [dot_tn(ds, k) for ds, k in zip(lows, keys)]
    for u in range(QUADS):
        two = slice(2 * u, 2 * u + 2)
        pairs[u] += lows[2 * u].astype(F32) + lows[2 * u + 1].astype(F32)
        for c, held in enumerate(
            (
                [own_heads(dq) * SCALE for dq in dqs[two]],
                [dk * SCALE for dk in dks[two]],
                dvs[two],
            )
        ):
            both = jnp.concatenate(held, 0).astype(BF)
            out[:, c * D + u * FEAT : c * D + (u + 1) * FEAT] = both


def attn_last_body(
    grad_mixed,
    tokens,
    halo,
    slab,
    normed_win,
    pairs,
    *refs,
):
    grads = refs[:-5]
    kept, sent, same, other, wide = refs[-5:]
    me = shard_place()
    shards = slab.shape[0]
    depth = (slab.shape[1] - SMALL) // 4
    small = smalls_of(slab, 4 * depth)
    gain = small[0:1]
    own = WIN - SHIFT
    vectors = []
    for c in range(3):
        cols = slice(c * D, (c + 1) * D)
        g = jnp.concatenate([part[:, cols] for part in grads], 0)
        if c != 1:
            vectors.append(jnp.sum(g.astype(F32), 0, keepdims=True))
        put_shares(
            me, same, other, c * depth, dot_tn(normed_win[...], g).reshape(shards, depth, D)
        )
        part = dot_nt(g, block_of(slab, c, depth))
        total = part if c == 0 else total + part
    wide[...] = total.reshape(WINDOWS, WIN, SLOT, D)
    back = places_column()
    gain_sum = jnp.zeros((1, D), F32)
    bias_sum = jnp.zeros((1, D), F32)
    for r in range(WIN):
        here = wide[:, r].reshape(WINDOWS * SLOT, D).astype(BF)
        g = dot(back, here)
        x = (tokens[SHIFT + r] if r < own else halo[r - own]).astype(F32)
        normed, scale = norm_stats(x)
        gain_sum += jnp.sum(g * normed, 0, keepdims=True)
        bias_sum += jnp.sum(g, 0, keepdims=True)
        grad = grad_mixed[r * WIDTH : (r + 1) * WIDTH, :] + norm_back(g, normed, scale, gain)
        if r < own:
            kept[r * WIDTH : (r + 1) * WIDTH, :] = grad
        else:
            sent[(r - own) * WIDTH : (r - own + 1) * WIDTH, :] = grad.astype(BF)

    rows = [gain_sum, bias_sum, vectors[0], vectors[1]]
    halves = GROUP // QUAD
    picks = [table_pick(1, half, True) for half in range(halves)]
    for g in range(GROUPS):
        laid = jnp.zeros((PLACES, TAB_USED), F32)
        for half in range(halves):
            total = pairs[g * halves + half]
            high = total.astype(BF)
            low = (total - high.astype(F32)).astype(BF)
            laid += dot(high, picks[half]) + dot(low, picks[half])
        laid = jnp.concatenate([laid, jnp.zeros((PLACES, TAB - TAB_USED), F32)], 1)
        total = jnp.zeros((SLOT, TAB), F32)
        for r in range(WIN):
            total += pltpu.roll(
                laid[r * SLOT : (r + 1) * SLOT], (2 * WIN - 1) * GROUP * r, 1
            )
        total = pltpu.roll(total, 0, 1, stride=GROUP, stride_axis=0)
        row = jnp.sum(total, 0, keepdims=True)
        rows += [row[:, c * D : (c + 1) * D] for c in range(TAB // D)]
    put_smalls(same, other, 3 * depth, rows)


def region_views(regions, rows, place):
    here = lax.dynamic_slice_in_dim(regions[0], place * rows, rows, 0)
    windows = here.reshape(WIN, WINDOWS, WIN).transpose(1, 0, 2)
    windows = jnp.pad(windows, ((0, 0), (0, 0), (0, SLOT - WIN))).astype(F32)
    windows = windows.reshape(WINDOWS, PLACES)
    by_row = jnp.broadcast_to(windows[:, :, None], (WINDOWS, PLACES, 128))
    by_lane = jnp.tile(jnp.pad(windows, ((0, 0), (0, HOLD - PLACES))), (1, QUAD))
    return by_row, by_lane[:, None, :]


def per_device(
    tokens,
    regions,
    cotangent,
    gain_one,
    bias_one,
    w_qkv,
    bias_qv,
    table,
    w_proj,
    bias_proj,
    gain_two,
    bias_two,
    w_in,
    bias_in,
    w_out,
    bias_out,
):
    images, local_rows, columns, _ = tokens.shape
    assert images == 1 and local_rows == WIN and columns == WIDTH
    shards = lax.axis_size("shard")
    seq = lax.axis_index("seq").astype(jnp.int32)
    chips = shards // 2
    depth = D // shards
    own = WIN - SHIFT
    attn_params = (gain_one[None], bias_one[None], w_qkv, bias_qv, table.T)
    bin_rows = bias_in.reshape(-1, 128)
    mlp_params = (
        w_proj,
        bias_proj[None],
        gain_two[None],
        bias_two[None],
        w_in,
        bin_rows,
        w_out,
        bias_out[None],
    )
    attn_slab, mlp_slab, out_slab = kernel_call(
        pack_body,
        [like((4 * depth + SMALL, D), BF)] * 2 + [like((4 * depth, D), BF)],
        (*attn_params, *mlp_params),
        vmem=60,
    )
    pieces = gather_pieces(attn_slab)
    pieces, (out_slab,) = tie(pieces, [out_slab])
    attn_all = jnp.stack(pieces)
    out_pieces = gather_pieces(out_slab)
    mlp_all = lax.all_gather(mlp_slab, "shard")
    tokens_here = tokens[0]
    token_halo = shifted_2(tokens_here[:SHIFT], "seq", -1)
    cot_here = cotangent[0]
    cot_halo = shifted_2(cot_here[:SHIFT], "seq", -1)
    by_row, by_lane = region_views(regions, local_rows, seq)

    normed_win, query, key, value = kernel_call(
        project_body,
        [like((PADDED, D), BF)] * 4,
        (tokens_here, token_halo, attn_all),
        scratch=[pltpu.VMEM((WINDOWS, WIN, SLOT, D), F32)],
    )
    pair_rows = 2 * PLACES
    steps = WINDOWS // 2

    def rows_from(first, width=D):
        return pl.BlockSpec((pair_rows, width), lambda i: (first + i, 0))

    def probs_from(first):
        return pl.BlockSpec((1, QUADS, pair_rows, LANES), lambda i: (first + i, 0, 0, 0))

    def fixed(shape):
        return pl.BlockSpec(shape, lambda i: (0,) * len(shape))

    probs, restored, mixed = kernel_call(
        attn_forward_body,
        [
            like((steps, QUADS, pair_rows, LANES), BF),
            like((TOKENS, D), BF),
            like((TOKENS, D), F32),
        ],
        (attn_all, by_row, by_lane, tokens_here, token_halo, query, key, value),
        grid=(steps,),
        in_blocks=[
            fixed(attn_all.shape),
            pl.BlockSpec((2, *by_row.shape[1:]), lambda i: (i, 0, 0)),
            pl.BlockSpec((2, *by_lane.shape[1:]), lambda i: (i, 0, 0)),
            fixed(tokens_here.shape),
            fixed(token_halo.shape),
            rows_from(0),
            rows_from(0),
            rows_from(0),
        ],
        out_blocks=[probs_from(0), fixed((TOKENS, D)), fixed((TOKENS, D))],
        scratch=[
            pltpu.VMEM((WINDOWS, WIN, SLOT, D), F32),
            pltpu.VMEM((QUADS, PLACES, LANES), F32),
        ],
    )
    share_a = like((chips, 4 * depth + SMALL, D), BF)
    share_b = like((chips, 5 * depth + SMALL, D), BF)
    _, (cot_halo,) = after([mixed], [cot_halo])
    cot = jnp.concatenate([cot_here[SHIFT:], cot_halo], 0).reshape(TOKENS, D)
    out_kept, out_sent, actives, back_sum, vectors, same_a, other_a = kernel_call(
        mlp_forward_body,
        [
            like((own * WIDTH, D), F32),
            like((SHIFT * WIDTH, D), BF),
            like((TOKENS, FF), BF),
            like((TOKENS, D), F32),
            like((SMALL, D), F32),
            share_a,
            share_a,
        ],
        (mixed, cot, mlp_all, jnp.stack(out_pieces)),
    )
    grad_mixed, grad_win, same_b, other_b = kernel_call(
        mlp_backward_body,
        [like((TOKENS, D), F32), like((PADDED, D), BF), share_b, share_b],
        (mixed, cot, actives, back_sum, vectors, attn_all, restored),
        scratch=[pltpu.VMEM((WINDOWS, WIN, SLOT, D), F32)],
    )

    def backward(first, count, grad_win, came):
        sums = like((QUADS, PLACES, LANES), F32)
        return kernel_call(
            attn_backward_body,
            [like((count * pair_rows, 3 * D), BF), sums],
            (query, key, value, probs, grad_win, came),
            grid=(count,),
            in_blocks=[rows_from(first)] * 3
            + [probs_from(first), rows_from(first), fixed(sums.shape)],
            out_blocks=[rows_from(0, 3 * D), fixed(sums.shape)],
            )

    none = jnp.zeros((QUADS, PLACES, LANES), F32)
    count = steps // 2
    came_a = exchange(other_a, "shard", 1)
    sums, (grad_win,) = tie(add_cores(same_a, came_a), [grad_win])
    parts_a = to_chips(sums)
    came_b = exchange(other_b, "shard", 1)
    early, pairs = backward(0, count, grad_win, none)
    sums, (pairs,) = tie(add_cores(same_b, came_b), [pairs])
    parts_b = to_chips(sums)
    late_part, pairs = backward(count, count, grad_win, pairs)
    keep_a, send = add_chips(same_a, came_a, parts_a)
    (send,), (pairs,) = tie([send], [pairs])
    near_a = exchange(send, "seq", 1)
    (out_halo,), (pairs,) = tie([shifted_2(out_sent, "seq", 1)], [pairs])
    tok_kept, tok_sent, attn_same, attn_other = kernel_call(
        attn_last_body,
        [
            like((own * WIDTH, D), F32),
            like((SHIFT * WIDTH, D), BF),
            like((chips, 3 * depth + SMALL, D), BF),
            like((chips, 3 * depth + SMALL, D), BF),
        ],
        (grad_mixed, tokens_here, token_halo, attn_all, normed_win, pairs, early, late_part),
        scratch=[pltpu.VMEM((WINDOWS, WIN, SLOT, D), F32)],
    )
    half_a = add_pair(keep_a, near_a)
    (half_a,), (attn_other, tok_sent) = after([half_a], [attn_other, tok_sent])
    far_a = exchange(half_a, "seq", 2)
    attn_came = exchange(attn_other, "shard", 1)
    keep_b, send = add_chips(same_b, came_b, parts_b, 10_000_000_000)
    (send,), (attn_came,) = after([send], [attn_came])
    near_b = exchange(send, "seq", 1)
    sums, (far_a,) = after(add_cores(attn_same, attn_came), [far_a])
    attn_parts = to_chips(sums)
    half_a = seq_rest(add_pair(half_a, far_a))
    (half_a,), (near_b, tok_sent) = after([half_a], [near_b, tok_sent])
    tok_halo = shifted_2(tok_sent, "seq", 1)
    half_b = add_pair(keep_b, near_b)
    far_b = exchange(half_b, "seq", 2)
    attn_parts, (far_b,) = after(attn_parts, [far_b])
    half_b = seq_rest(add_pair(half_b, far_b))
    (half_b,), attn_parts = after([half_b], attn_parts)
    keep, send = add_chips(attn_same, attn_came, attn_parts)
    def unpack(body, params, half, back):
        return kernel_call(
            body,
            [like(p.shape, F32) for p in params],
            (half, back),
            scratch=[
                pltpu.VMEM((2 * half.shape[0], D), BF),
                pltpu.SemaphoreType.DMA((2,)),
            ],
                apart=2,
        )

    def joined(halo, kept):
        return jnp.concatenate([halo.astype(F32), kept], 0).reshape(tokens.shape)

    near = exchange(send, "seq", 1)
    back_b = exchange(half_b, "seq", 1)
    half = add_pair(keep, near)
    far = exchange(half, "seq", 2)
    back_a = exchange(half_a, "seq", 1)
    half = seq_rest(add_pair(half, far))
    back = exchange(half, "seq", 1)
    in_grads = unpack(unpack_in_body, (w_in, bin_rows), half_a, back_a)
    column = gain_two[None]
    out_grads = unpack(unpack_out_body, (w_out, w_proj, *[column] * 4), half_b, back_b)
    grad_tokens = joined(tok_halo, tok_kept)
    output = joined(out_halo, out_kept)
    early, (back,) = after([*in_grads, *out_grads, grad_tokens, output], [back])
    in_grads, out_grads, (grad_tokens, output) = early[:2], early[2:8], early[8:]
    attn_grads = unpack(unpack_attn_body, attn_params, half, back)
    g_wout, g_wproj, g_gain, g_offset, g_bout, g_bproj = out_grads
    summed = [*attn_grads[:4], attn_grads[4].T, g_wproj, g_bproj, g_gain, g_offset]
    summed += [*in_grads, g_wout, g_bout]

    targets = (
        gain_one,
        bias_one,
        w_qkv,
        bias_qv,
        table,
        w_proj,
        bias_proj,
        gain_two,
        bias_two,
        w_in,
        bias_in,
        w_out,
        bias_out,
    )
    grads = [g.reshape(p.shape) for g, p in zip(summed, targets)]
    return (output, grad_tokens, *grads)


def solution(mesh):
    return jax.shard_map(
        per_device,
        mesh=mesh,
        in_specs=(
            P("shard", "seq", None, None),
            P("shard", None, None),
            P("shard", "seq", None, None),
            P("shard"),
            P("shard"),
            P("shard", None),
            P(None, "shard"),
            P(None, "shard"),
            P("shard", None),
            P("shard"),
            P("shard"),
            P("shard"),
            P("shard", None),
            P("shard"),
            P("shard", None),
            P("shard"),
        ),
        out_specs=(
            P("shard", "seq", None, None),
            P("shard", "seq", None, None),
            P("shard"),
            P("shard"),
            P("shard", None),
            P(None, "shard"),
            P(None, "shard"),
            P("shard", None),
            P("shard"),
            P("shard"),
            P("shard"),
            P("shard", None),
            P("shard"),
            P("shard", None),
            P("shard"),
        ),
        check_vma=False,
    )
```
